32 devices in a mesh: groups: 2 (over y), expert: 4 (over z), etp: 4 (over x, core).
Axes of the slice: x: 2, y: 2, z: 4, core: 2. Of those that a mesh axis runs over, the one named last changes fastest.
Arguments:
- hidden_in: bfloat16 [1024, 1024], P(('groups', 'expert'), 'etp'), parts along dimension 0, may hold values from -6 to 6
- out_grad: bfloat16 [1024, 1024], P(('groups', 'expert'), 'etp'), parts along dimension 0, may hold values from -3 to 3
- expert_ids: int32 [1024, 6], P(('groups', 'expert')), parts along dimension 0, may hold values from 0 to 63, all different within a row; in each aligned block of 128 rows (0 to 127, 128 to 255, ...) at most 16 rows name the same one
- gate_values: float32 [1024, 6], P(('groups', 'expert')), parts along dimension 0, may hold values from 0.1 to 1
- capacity_blocks: int32 [128], P('groups'), parts along dimension 0, may hold values from 1 to 4
- gate_weight: bfloat16 [64, 1024, 1408], P('expert', None, 'etp'), may hold values from -0.1875 to 0.1875
- up_weight: bfloat16 [64, 1024, 1408], P('expert', None, 'etp'), may hold values from -0.1875 to 0.1875
- down_weight: bfloat16 [64, 1408, 1024], P('expert', 'etp'), may hold values from -0.15625 to 0.15625
Outputs:
- layer_out: bfloat16 [1024, 1024], P(('groups', 'expert'), 'etp'), parts along dimension 0
- input_grad: bfloat16 [1024, 1024], P(('groups', 'expert'), 'etp'), parts along dimension 0
- gate_value_grad: float32 [1024, 6], P(('groups', 'expert')), parts along dimension 0
- gate_weight_grad: bfloat16 [128, 1024, 1408], P(('groups', 'expert'), None, 'etp'), parts along dimension 0
- up_weight_grad: bfloat16 [128, 1024, 1408], P(('groups', 'expert'), None, 'etp'), parts along dimension 0
- down_weight_grad: bfloat16 [128, 1408, 1024], P(('groups', 'expert'), 'etp'), parts along dimension 0
The draws below stay inside these ranges and needn't reach their ends.
There are 2 independent parts, one for each index of `groups`. The reference program is written for one: setup_inputs(seed, part) draws one part's arguments, and reference() takes and returns one part's arrays. A program takes and returns all parts, laid end to end along the dimension named above; an argument that names none is the same for every part. Nothing has to cross between parts.
Inputs may be any that keep to these rules, and one draw needn't show every extreme that they name: `expert_ids`: each row names 6 different experts; within each aligned block of 128 rows no expert is named more than 16 times.
All inputs are finite; a program needn't handle non-finite values.
Results may differ from the reference program's by a relative error of at most 0.013.
Values may be sent and summed in bfloat16 or wider, within the bound.
No kernel may reach another device: no remote copies, remote signals or barrier semaphores. Data moves between devices by JAX's collectives and lax.ppermute only.
A program may use at most 192 MiB of HBM per device.

```python
import math
import jax
import jax.numpy as jnp
import numpy as np
from jax import lax

D = 1024
FF = 1408
EXPERTS = 64
TOPK = 6
MAXB = 4
TOK_DEV = 128
TOKENS = 512
CAP = 16
BLK = 4
FF_DEV = 352
N_EXPERT = 4
N_ETP = 4


def draw_capacity_blocks(key, part):
    key = jax.random.fold_in(key, 7)
    first, second = jax.random.split(key)
    values = jax.random.randint(first, (EXPERTS,), 1, MAXB + 1)
    chosen = jax.random.randint(second, (), 0, EXPERTS)
    return jnp.where(jnp.arange(EXPERTS) == chosen, MAXB, values).astype(jnp.int32)


def block_levels(own_key, extent, shards, low, largest):
    def one(dim, shards_of):
        draws = jax.random.uniform(jax.random.fold_in(jax.random.fold_in(own_key, 6), dim), (shards_of,), jnp.float32, low / len(shards), largest / len(shards))
        return jnp.repeat(jnp.exp(draws), extent[dim] // shards_of).reshape((-1,) + (1,) * (len(extent) - dim - 1))

    loudness = one(*shards[0])
    for cut in shards[1:]:
        loudness = loudness * one(*cut)
    return loudness


def assign_block(key, own, number, rows, count, top, limit, slope):
    ranking = jax.random.permutation(key, count)
    packed, common = shares(count, rows * top, limit, slope, True), shares(count, rows * top, limit, slope, False)
    places = jnp.arange(count)

    def named(tallies, turn):
        used = int((tallies > 0).sum())
        fixed = max(1, used // 4)
        passed = fixed + (places - fixed + turn * (used - fixed)) % max(1, count - fixed)
        return jnp.zeros((count,), jnp.int32).at[ranking[jnp.where(places < fixed, places, passed)]].set(jnp.asarray(tallies, jnp.int32))

    tallies = jnp.where(number % 4 == 0, named(packed, number // 4), named(common, number - number // 4 - 1))
    mixed = jax.random.permutation(jax.random.fold_in(own, 3), count)
    donor, sink = mixed[0:count // 2 * 2:2], mixed[1:count // 2 * 2:2]
    slack = jnp.minimum(tallies[donor] - 1, limit - tallies[sink]) // 2
    slack = jnp.where((donor == ranking[0]) | (sink == ranking[0]) | (tallies[sink] == 0), 0, jnp.maximum(slack, 0))
    passed = jax.random.randint(jax.random.fold_in(own, 4), (count // 2,), 0, 1 << 20) % (slack + 1)
    tallies = tallies.at[donor].add(-passed).at[sink].add(passed)
    labels = jnp.searchsorted(jnp.cumsum(tallies), jnp.arange(rows * top), side="right").astype(jnp.int32)
    grid = labels.reshape(top, rows).T
    grid = grid[jax.random.permutation(jax.random.fold_in(own, 1), rows)]
    turn = jax.random.randint(jax.random.fold_in(own, 2), (rows, 1), 0, top)
    return jnp.take_along_axis(grid, (jnp.arange(top)[None, :] + turn) % top, axis=1)


def shares(amount, total, most, slope, full):
    weights = [(1 << 20) // math.isqrt(grade ** slope) + 1 for grade in range(1, amount + 1)]
    largest = most if full else min(most, max(-(-total // amount), total * weights[0] // sum(weights)))
    least = 1 if total - largest >= amount - 1 else 0
    counts, surplus = [largest] + [least] * (amount - 1), total - largest - least * (amount - 1)
    while surplus > 0:
        movable = [i for i in range(1, amount) if counts[i] < largest] or [i for i in range(1, amount) if counts[i] < most]
        whole, left = sum([weights[i] for i in movable]), surplus
        for i in movable:
            extra = min(most - counts[i], max(1, left * weights[i] // whole), surplus)
            counts[i] = counts[i] + extra
            surplus = surplus - extra
    return np.array(counts)


def bell_draw(rng, dims, spread, reach, pieces=(), kind=jnp.bfloat16):
    entries = spread * jax.random.normal(rng, dims, jnp.float32)
    if pieces:
        entries = entries * block_levels(rng, dims, pieces, -0.22, 0.18)
    return jnp.clip(entries, -reach, reach).astype(kind)


def setup_inputs(seed: int = 0, part: int = 0) -> dict:
    streams_of = jax.random.split(jax.random.key(seed), 9)
    own_keys = jax.random.split(jax.random.fold_in(streams_of[8], part), 9)
    hidden_in = bell_draw(own_keys[0], (TOKENS, D), 1.0, 6.0, ((0, 4), (1, 4)))
    out_grad = bell_draw(own_keys[1], (TOKENS, D), 0.5, 3.0, ((0, 4), (1, 4)))
    expert_ids_keys = jax.random.split(jax.random.fold_in(own_keys[2], 1), TOKENS // TOK_DEV)
    expert_ids_turns = jax.random.permutation(jax.random.fold_in(own_keys[2], 3), TOKENS // TOK_DEV)
    expert_ids = jax.vmap(lambda own, number: assign_block(jax.random.fold_in(own_keys[2], 2), own, number, TOK_DEV, EXPERTS, TOPK, CAP, 2))(expert_ids_keys, expert_ids_turns).reshape((TOKENS, TOPK))
    gate_values = jnp.clip(0.1 + 0.9 * jax.random.uniform(own_keys[3], (TOKENS, TOPK), jnp.float32) ** block_levels(own_keys[3], (TOKENS, TOPK), ((0, 4),), -0.2, 0.2), 0.1, 1.0)
    capacity_blocks = draw_capacity_blocks(jax.random.fold_in(jax.random.fold_in(streams_of[8], part), 71), part)
    gate_weight = bell_draw(streams_of[5], (EXPERTS, D, FF), D ** -0.5, 0.1875, ((0, 4), (2, 4)))
    up_weight = bell_draw(streams_of[6], (EXPERTS, D, FF), D ** -0.5, 0.1875, ((0, 4), (2, 4)))
    down_weight = bell_draw(streams_of[7], (EXPERTS, FF, D), FF ** -0.5, 0.15625, ((0, 4), (1, 4)))
    return dict(hidden_in=hidden_in, out_grad=out_grad, expert_ids=expert_ids, gate_values=gate_values, capacity_blocks=capacity_blocks, gate_weight=gate_weight, up_weight=up_weight, down_weight=down_weight)


def ranks_of(block_ids):
    onehot = (block_ids[:, None] == jnp.arange(EXPERTS, dtype=jnp.int32)[None, :]).astype(jnp.int32)
    before = jnp.cumsum(onehot, axis=0) - onehot
    return jnp.sum(before * onehot, axis=1).astype(jnp.int32)


def grouped_sum(parts):
    rounded = lax.optimization_barrier(parts.astype(jnp.bfloat16))
    return jnp.sum(rounded.astype(jnp.float32), axis=1).astype(jnp.bfloat16)


def expert_pass(operands):
    gate_w, up_w, down_w, rows_in, rows_grad = operands
    count = rows_in.shape[0]
    hidden_gate = jnp.dot(rows_in, gate_w, preferred_element_type=jnp.float32)
    hidden_up = jnp.dot(rows_in, up_w, preferred_element_type=jnp.float32)
    activ = (jax.nn.silu(hidden_gate) * hidden_up).astype(jnp.bfloat16)
    out_parts = jnp.einsum("rgf,gfd->rgd", activ.reshape(count, N_ETP, FF_DEV).astype(jnp.float32),
                           down_w.reshape(N_ETP, FF_DEV, D).astype(jnp.float32))
    expert_out = grouped_sum(out_parts)
    act_grad = jnp.dot(rows_grad, down_w.T, preferred_element_type=jnp.float32)
    down_grad = jnp.dot(activ.T, rows_grad, preferred_element_type=jnp.float32).astype(jnp.bfloat16)
    sigma = jax.nn.sigmoid(hidden_gate)
    gate_part = (act_grad * hidden_up * sigma * (1.0 + hidden_gate * (1.0 - sigma))).astype(jnp.bfloat16)
    up_part = (act_grad * jax.nn.silu(hidden_gate)).astype(jnp.bfloat16)
    gate_grad = jnp.dot(rows_in.T, gate_part, preferred_element_type=jnp.float32).astype(jnp.bfloat16)
    up_grad = jnp.dot(rows_in.T, up_part, preferred_element_type=jnp.float32).astype(jnp.bfloat16)
    back_parts = jnp.einsum("rgf,dgf->rgd", gate_part.reshape(count, N_ETP, FF_DEV).astype(jnp.float32),
                            gate_w.reshape(D, N_ETP, FF_DEV).astype(jnp.float32))
    back_parts = back_parts + jnp.einsum("rgf,dgf->rgd", up_part.reshape(count, N_ETP, FF_DEV).astype(jnp.float32),
                                         up_w.reshape(D, N_ETP, FF_DEV).astype(jnp.float32))
    slot_grad = grouped_sum(back_parts)
    return expert_out, slot_grad, gate_grad, up_grad, down_grad


def reference(hidden_in, out_grad, expert_ids, gate_values, capacity_blocks, gate_weight, up_weight, down_weight):
    block_ids = expert_ids.reshape(N_EXPERT, TOK_DEV * TOPK)
    ranks = jax.vmap(ranks_of)(block_ids).reshape(TOKENS, TOPK)
    limits = capacity_blocks[expert_ids] * BLK
    kept = ranks < limits
    source = (jnp.arange(TOKENS, dtype=jnp.int32) // TOK_DEV)[:, None]
    rows_all = EXPERTS * N_EXPERT * CAP
    slots = jnp.where(kept, expert_ids * (N_EXPERT * CAP) + source * CAP + ranks, rows_all).astype(jnp.int32)
    token_index = jnp.broadcast_to(jnp.arange(TOKENS, dtype=jnp.int32)[:, None], (TOKENS, TOPK))
    owners = jnp.full((rows_all,), TOKENS, jnp.int32).at[slots.reshape(-1)].set(token_index.reshape(-1), mode="drop")
    weights = jnp.where(kept, gate_values, 0.0).astype(jnp.float32)
    slot_gates = jnp.zeros((rows_all,), jnp.float32).at[slots.reshape(-1)].set(weights.reshape(-1), mode="drop")
    padded_in = jnp.concatenate([hidden_in, jnp.zeros((1, D), jnp.bfloat16)], 0)
    padded_grad = jnp.concatenate([out_grad, jnp.zeros((1, D), jnp.bfloat16)], 0)
    rows_in = padded_in[owners].reshape(EXPERTS, N_EXPERT * CAP, D)
    rows_grad = (slot_gates[:, None] * padded_grad[owners].astype(jnp.float32)).astype(jnp.bfloat16)
    rows_grad = rows_grad.reshape(EXPERTS, N_EXPERT * CAP, D)
    expert_out, slot_grad, gate_grad, up_grad, down_grad = lax.map(
        expert_pass, (gate_weight, up_weight, down_weight, rows_in, rows_grad))
    out_flat = jnp.concatenate([expert_out.reshape(rows_all, D), jnp.zeros((1, D), jnp.bfloat16)], 0)
    back_flat = jnp.concatenate([slot_grad.reshape(rows_all, D), jnp.zeros((1, D), jnp.bfloat16)], 0)
    layer_sum = jnp.zeros((TOKENS, D), jnp.float32)
    input_sum = jnp.zeros((TOKENS, D), jnp.float32)
    dots = []
    for column in range(TOPK):
        picked = out_flat[slots[:, column]].astype(jnp.float32)
        layer_sum = layer_sum + weights[:, column:column + 1] * picked
        dots.append(jnp.sum(out_grad.astype(jnp.float32) * picked, axis=1))
        returned = back_flat[slots[:, column]].astype(jnp.float32)
        input_sum = input_sum + weights[:, column:column + 1] * returned
    gate_value_grad = jnp.stack(dots, axis=1) * kept.astype(jnp.float32)
    return (layer_sum.astype(jnp.bfloat16), input_sum.astype(jnp.bfloat16), gate_value_grad,
            gate_grad, up_grad, down_grad)
```

```python
import functools

import jax
import jax.numpy as jnp
from jax import lax
from jax.experimental import pallas as pl
from jax.experimental.pallas import tpu as pltpu
from jax.sharding import PartitionSpec as P

CAP = 16
BLK = 4
EXTRA = 16
F32 = jnp.float32
BF16 = jnp.bfloat16


def nn(a, b):
    return lax.dot_general(a, b, (((1,), (0,)), ((), ())), preferred_element_type=F32)


def nt(a, b):
    return lax.dot_general(a, b, (((1,), (1,)), ((), ())), preferred_element_type=F32)


def tn(a, b):
    return lax.dot_general(a, b, (((0,), (0,)), ((), ())), preferred_element_type=F32)


def routing_rows(expert_ids, gate_values):
    choose = expert_ids.shape[1]
    high = lax.reduce_precision(gate_values, exponent_bits=8, mantissa_bits=7)
    low = lax.reduce_precision(gate_values - high, exponent_bits=8, mantissa_bits=7)
    pad = ((0, 8 - choose), (0, 0))
    top = jnp.concatenate([jnp.pad(expert_ids.T.astype(F32), pad), jnp.pad(high.T, pad)], axis=1)
    bottom = jnp.concatenate([jnp.pad(low.T, pad), jnp.zeros_like(jnp.pad(low.T, pad))], axis=1)
    return jnp.concatenate([top, bottom], axis=0).astype(BF16)


def forward_kernel(
    choose, block_ref, limit_ref, expert_ref, gate_ref, up_ref, down_ref,
    home_ref, rows_ref, grads_ref, p_ref, q_ref, a_ref,
    onehot, slot_gate, out_rows, back_rows, dots,
):
    step = pl.program_id(0)
    experts = pl.num_programs(0)
    sources, slots, tokens = onehot.shape
    shares = block_ref.shape[0] // sources
    width = block_ref.shape[2]

    def routing(s):
        info = block_ref[s * shares, 2 * tokens:2 * tokens + EXTRA, :].astype(F32)
        ids = info[0:choose, 0:tokens]
        gates = info[0:choose, tokens:2 * tokens] + info[8:8 + choose, 0:tokens]
        return ids, gates

    @pl.when(step == 0)
    def _():
        row = lax.broadcasted_iota(jnp.int32, (tokens, tokens), 0)
        col = lax.broadcasted_iota(jnp.int32, (tokens, tokens), 1)
        before = jnp.where(row < col, 1.0, 0.0).astype(BF16)
        mine = expert_ref[...]
        limit = limit_ref[...]
        place = lax.broadcasted_iota(jnp.int32, (slots // CAP, CAP, tokens), 1).astype(F32)
        for s in range(sources):
            ids, gates = routing(s)
            named = jnp.zeros((slots // CAP, tokens), F32)
            gate = jnp.zeros((slots // CAP, tokens), F32)
            for k in range(choose):
                hit = ids[k:k + 1, :] == mine
                named = named + jnp.where(hit, 1.0, 0.0)
                gate = gate + jnp.where(hit, gates[k:k + 1, :], 0.0)
            rank = nn(named.astype(BF16), before)
            rank = jnp.where((named > 0.5) & (rank < limit), rank, -1.0)
            chosen = jnp.where(rank[:, None, :] == place, 1.0, 0.0)
            gate_of = jnp.sum(chosen * gate[:, None, :], axis=2, keepdims=True)
            slot_gate[:, s * CAP:(s + 1) * CAP, :] = jnp.broadcast_to(gate_of, chosen.shape)
            table = chosen.reshape(slots, tokens).astype(BF16)
            onehot[s] = table
            for q in range(shares):
                for half, ref in ((0, rows_ref), (1, grads_ref)):
                    part = block_ref[s * shares + q, half * tokens:(half + 1) * tokens, :]
                    picked = nn(table, part).astype(BF16).reshape(slots // CAP, CAP, width)
                    ref[:, s * CAP:(s + 1) * CAP, q * width:(q + 1) * width] = picked

    x = rows_ref[step]
    y = grads_ref[step]
    gate = slot_gate[step][:, 0:1]
    hidden_gate = nt(x, gate_ref[0])
    hidden_up = nt(x, up_ref[0])
    grad = nt(y, down_ref[0])
    sigma = jax.nn.sigmoid(hidden_gate)
    silu = hidden_gate * sigma
    activ = (silu * hidden_up).astype(BF16).astype(F32)
    dots[step] = jnp.broadcast_to(jnp.sum(activ * grad, axis=1, keepdims=True), dots.shape[1:])
    scaled = (activ * gate).astype(BF16)
    grad = grad * gate
    gate_part = (grad * hidden_up * sigma * (1.0 + hidden_gate * (1.0 - sigma))).astype(BF16)
    up_part = (grad * silu).astype(BF16)
    a_ref[0] = scaled
    p_ref[0] = gate_part
    q_ref[0] = up_part
    out = nn(scaled, down_ref[0]).astype(BF16)
    back = ((nn(gate_part, gate_ref[0]) + nn(up_part, up_ref[0])) * gate).astype(BF16)
    for s in range(sources):
        at = pl.ds(pl.multiple_of(step * CAP, CAP), CAP)
        out_rows[s, at, :] = out[s * CAP:(s + 1) * CAP]
        back_rows[s, at, :] = back[s * CAP:(s + 1) * CAP]

    @pl.when(step == experts - 1)
    def _():
        mine = expert_ref[...]
        for s in range(sources):
            table = onehot[s]
            for half, ref in ((0, out_rows), (1, back_rows)):
                total = tn(table, ref[s]).astype(BF16)
                for q in range(shares):
                    home_ref[s * shares + q, half * tokens:(half + 1) * tokens, :] = total[:, q * width:(q + 1) * width]
            ids, _ = routing(s)
            chosen = table.astype(F32).reshape(slots // CAP, CAP, tokens)
            share = jnp.sum(chosen * dots[:, s * CAP:(s + 1) * CAP, :], axis=1)
            rows = [jnp.sum(jnp.where(ids[k:k + 1, :] == mine, share, 0.0), axis=0, keepdims=True) for k in range(choose)]
            rows = jnp.concatenate(rows + [jnp.zeros((8 - choose, tokens), F32)], axis=0)
            rows = jnp.concatenate([rows, jnp.zeros_like(rows)], axis=0)
            rows = jnp.concatenate([rows, jnp.zeros((EXTRA, width - tokens), F32)], axis=1).astype(BF16)
            for q in range(shares):
                home_ref[s * shares + q, 2 * tokens:2 * tokens + EXTRA, :] = rows


def grads_kernel(rows_ref, grads_ref, p_ref, q_ref, a_ref, gate_grad, up_grad, down_grad):
    x = rows_ref[0]
    gate_grad[0] = tn(p_ref[0], x).astype(BF16)
    up_grad[0] = tn(q_ref[0], x).astype(BF16)
    down_grad[0] = tn(a_ref[0], grads_ref[0]).astype(BF16)


def gathered_body(
    hidden_in, out_grad, expert_ids, gate_values, capacity_blocks, gate_weight, up_weight, down_weight
):
    sources = lax.axis_size("expert")
    shares = lax.axis_size("etp")
    tokens, width = hidden_in.shape
    choose = expert_ids.shape[1]
    local_experts, units, model = down_weight.shape
    slots = local_experts * CAP
    rows = sources * CAP
    first = lax.axis_index("expert") * local_experts
    limit = lax.dynamic_slice(capacity_blocks, (first,), (local_experts,)).astype(F32)[:, None] * BLK
    mine = (first + jnp.arange(local_experts, dtype=jnp.int32)).astype(F32)[:, None]
    gate_t = jnp.swapaxes(gate_weight, 1, 2)
    up_t = jnp.swapaxes(up_weight, 1, 2)
    packed = jnp.concatenate([hidden_in, out_grad, routing_rows(expert_ids, gate_values)], axis=0)
    blocks = lax.all_gather(packed, ("expert", "etp"), axis=0, tiled=False)

    per_expert = lambda *shape: pl.BlockSpec((1,) + shape, lambda e: (e, 0, 0))
    whole = lambda *shape: pl.BlockSpec(shape, lambda e: (0,) * len(shape))
    height = 2 * tokens + EXTRA
    home, x_rows, y_rows, gate_part, up_part, scaled = pl.pallas_call(
        functools.partial(forward_kernel, choose),
        grid=(local_experts,),
        in_specs=[
            whole(sources * shares, height, width),
            whole(local_experts, 1),
            whole(local_experts, 1),
            per_expert(units, model),
            per_expert(units, model),
            per_expert(units, model),
        ],
        out_specs=[
            whole(sources * shares, height, width),
            whole(local_experts, rows, model),
            whole(local_experts, rows, model),
            per_expert(rows, units),
            per_expert(rows, units),
            per_expert(rows, units),
        ],
        out_shape=[
            jax.ShapeDtypeStruct((sources * shares, height, width), BF16),
            jax.ShapeDtypeStruct((local_experts, rows, model), BF16),
            jax.ShapeDtypeStruct((local_experts, rows, model), BF16),
            jax.ShapeDtypeStruct((local_experts, rows, units), BF16),
            jax.ShapeDtypeStruct((local_experts, rows, units), BF16),
            jax.ShapeDtypeStruct((local_experts, rows, units), BF16),
        ],
        scratch_shapes=[
            pltpu.VMEM((sources, slots, tokens), BF16),
            pltpu.VMEM((local_experts, rows, tokens), F32),
            pltpu.VMEM((sources, slots, model), BF16),
            pltpu.VMEM((sources, slots, model), BF16),
            pltpu.VMEM((local_experts, rows, tokens), F32),
        ],
        compiler_params=pltpu.CompilerParams(vmem_limit_bytes=48 * 1024 * 1024),
        cost_estimate=pl.CostEstimate(
            flops=2 * 6 * local_experts * rows * units * model,
            bytes_accessed=3 * 2 * local_experts * units * model,
            transcendentals=local_experts * rows * units,
        ),
    )(blocks, limit, mine, gate_t, up_t, down_weight)

    total = lax.psum_scatter(home, ("expert", "etp"), scatter_dimension=0, tiled=False)

    gate_grad, up_grad, down_grad = pl.pallas_call(
        grads_kernel,
        grid=(local_experts,),
        in_specs=[
            per_expert(rows, model),
            per_expert(rows, model),
            per_expert(rows, units),
            per_expert(rows, units),
            per_expert(rows, units),
        ],
        out_specs=[per_expert(units, model)] * 3,
        out_shape=[jax.ShapeDtypeStruct((local_experts, units, model), BF16)] * 3,
        compiler_params=pltpu.CompilerParams(vmem_limit_bytes=32 * 1024 * 1024),
        cost_estimate=pl.CostEstimate(
            flops=2 * 3 * local_experts * rows * units * model,
            bytes_accessed=3 * 2 * local_experts * units * model,
            transcendentals=0,
        ),
    )(x_rows, y_rows, gate_part, up_part, scaled)

    return (
        total[0:tokens],
        total[tokens:2 * tokens],
        total[2 * tokens:2 * tokens + choose, 0:tokens].astype(F32).T,
        jnp.swapaxes(gate_grad, 1, 2),
        jnp.swapaxes(up_grad, 1, 2),
        down_grad,
    )


def slot_layout(expert_ids, capacity_blocks):
    tokens_here, choose = expert_ids.shape
    experts = capacity_blocks.shape[0]
    flat_ids = expert_ids.reshape(-1)
    onehot = (flat_ids[:, None] == jnp.arange(experts, dtype=jnp.int32)[None, :]).astype(jnp.int32)
    before = jnp.cumsum(onehot, axis=0) - onehot
    ranks = jnp.sum(before * onehot, axis=1)
    limits = jnp.sum(onehot * capacity_blocks[None, :], axis=1) * BLK
    kept = ranks < limits
    slots = jnp.where(kept, flat_ids * CAP + ranks, experts * CAP)
    token_index = jnp.arange(tokens_here * choose, dtype=jnp.int32) // choose
    owners = (
        jnp.full((experts * CAP,), tokens_here, jnp.int32).at[slots].set(token_index, mode="drop")
    )
    return (kept.reshape(tokens_here, choose), slots.reshape(tokens_here, choose), owners)


def outgoing(rows, owners, experts, scale):
    padded = jnp.concatenate([rows, jnp.zeros((1, rows.shape[1]), rows.dtype)], 0)
    picked = padded[owners]
    if scale is not None:
        picked = (scale[:, None] * picked.astype(jnp.float32)).astype(jnp.bfloat16)
    return picked.reshape(experts, CAP, rows.shape[1])


def local_grads(hidden_gate, hidden_up, act_grad):
    sigma = jax.nn.sigmoid(hidden_gate)
    gate_part = (act_grad * hidden_up * sigma * (1.0 + hidden_gate * (1.0 - sigma))).astype(
        jnp.bfloat16
    )
    up_part = (act_grad * jax.nn.silu(hidden_gate)).astype(jnp.bfloat16)
    return (gate_part, up_part)


def combine(back, slots, weights):
    padded = jnp.concatenate([back, jnp.zeros((1, back.shape[1]), back.dtype)], 0)
    picked = padded[slots].astype(jnp.float32)
    return (jnp.einsum("tk,tkw->tw", weights, picked), picked)


def dispatched_body(
    hidden_in,
    out_grad,
    expert_ids,
    gate_values,
    capacity_blocks,
    gate_weight,
    up_weight,
    down_weight,
):
    experts = capacity_blocks.shape[0]
    sources = lax.axis_size("expert")
    local_experts = gate_weight.shape[0]
    kept, slots, owners = slot_layout(expert_ids, capacity_blocks)
    weights = jnp.where(kept, gate_values, 0.0)
    slot_gates = (
        jnp.zeros((experts * CAP,), jnp.float32)
        .at[slots.reshape(-1)]
        .set(weights.reshape(-1), mode="drop")
    )
    send_in = outgoing(hidden_in, owners, experts, None)
    send_grad = outgoing(out_grad, owners, experts, slot_gates)
    recv_in, recv_grad = (
        lax.all_to_all(send_in, "expert", split_axis=0, concat_axis=0, tiled=True),
        lax.all_to_all(send_grad, "expert", split_axis=0, concat_axis=0, tiled=True),
    )
    share = recv_in.shape[2]
    share_in = recv_in.reshape(sources, local_experts, CAP, share)
    share_grad = recv_grad.reshape(sources, local_experts, CAP, share)
    piece = lax.all_gather(share_in, "etp", axis=3, tiled=True)
    hidden_gate = jnp.einsum(
        "secn,enf->secf", piece, gate_weight, preferred_element_type=jnp.float32
    )
    hidden_up = jnp.einsum("secn,enf->secf", piece, up_weight, preferred_element_type=jnp.float32)
    activ = (jax.nn.silu(hidden_gate) * hidden_up).astype(jnp.bfloat16)
    piece = lax.all_gather(share_grad, "etp", axis=3, tiled=True)
    act_grad = jnp.einsum("secn,efn->secf", piece, down_weight, preferred_element_type=jnp.float32)
    columns = jnp.einsum("secf,secn->efn", activ, piece, preferred_element_type=jnp.float32)
    act_grad, down_grad = (act_grad, columns)
    gate_part, up_part = local_grads(hidden_gate, hidden_up, act_grad)
    stacked = jnp.stack([gate_part, up_part])
    weight_grads = jnp.einsum(
        "secn,gsecf->genf",
        lax.all_gather(share_in, "etp", axis=3, tiled=True),
        stacked,
        preferred_element_type=jnp.float32,
    )
    out_part = jnp.einsum("secf,efd->secd", activ, down_weight, preferred_element_type=jnp.float32)
    back_part = jnp.einsum(
        "secf,edf->secd", gate_part, gate_weight, preferred_element_type=jnp.float32
    )
    back_part = back_part + jnp.einsum(
        "secf,edf->secd", up_part, up_weight, preferred_element_type=jnp.float32
    )
    out_rows = lax.psum_scatter(
        out_part.astype(jnp.bfloat16), "etp", scatter_dimension=3, tiled=True
    )
    home_out = lax.all_to_all(out_rows, "expert", split_axis=0, concat_axis=0, tiled=True)
    share_width = home_out.shape[3]
    layer_sum, picked = combine(home_out.reshape(experts * CAP, share_width), slots, weights)
    dot_part = jnp.einsum("tw,tkw->tk", out_grad.astype(jnp.float32), picked) * kept.astype(
        jnp.float32
    )
    gate_value_grad = lax.psum(dot_part, "etp")
    back_rows = lax.psum_scatter(
        back_part.astype(jnp.bfloat16), "etp", scatter_dimension=3, tiled=True
    )
    home_back = lax.all_to_all(back_rows, "expert", split_axis=0, concat_axis=0, tiled=True)
    input_sum, returned = combine(home_back.reshape(experts * CAP, share_width), slots, weights)
    return (
        layer_sum.astype(jnp.bfloat16),
        input_sum.astype(jnp.bfloat16),
        gate_value_grad,
        weight_grads[0].astype(jnp.bfloat16),
        weight_grads[1].astype(jnp.bfloat16),
        down_grad.astype(jnp.bfloat16),
    )


def body(*operands):
    hidden_in, gate_weight = operands[0], operands[5]
    if hidden_in.shape[0] <= gate_weight.shape[0] * CAP:
        return gathered_body(*operands)
    return dispatched_body(*operands)


def solution(mesh):
    in_specs = (
        P(("groups", "expert"), "etp"),
        P(("groups", "expert"), "etp"),
        P(("groups", "expert"), None),
        P(("groups", "expert"), None),
        P("groups"),
        P("expert", None, "etp"),
        P("expert", None, "etp"),
        P("expert", "etp", None),
    )
    out_specs = (
        P(("groups", "expert"), "etp"),
        P(("groups", "expert"), "etp"),
        P(("groups", "expert"), None),
        P(("groups", "expert"), None, "etp"),
        P(("groups", "expert"), None, "etp"),
        P(("groups", "expert"), "etp", None),
    )
    return jax.shard_map(body, mesh=mesh, in_specs=in_specs, out_specs=out_specs, check_vma=False)
```

```python
import functools

import jax
import jax.numpy as jnp
from jax import lax
from jax.experimental import pallas as pl
from jax.experimental.pallas import tpu as pltpu
from jax.sharding import PartitionSpec as P

CAP = 16
BLK = 4
EXTRA = 16
F32 = jnp.float32
BF16 = jnp.bfloat16


def nn(a, b):
    return lax.dot_general(a, b, (((1,), (0,)), ((), ())), preferred_element_type=F32)


def nt(a, b):
    return lax.dot_general(a, b, (((1,), (1,)), ((), ())), preferred_element_type=F32)


def tn(a, b):
    return lax.dot_general(a, b, (((0,), (0,)), ((), ())), preferred_element_type=F32)


def routing_rows(expert_ids, gate_values):
    choose = expert_ids.shape[1]
    high = lax.reduce_precision(gate_values, exponent_bits=8, mantissa_bits=7)
    low = lax.reduce_precision(gate_values - high, exponent_bits=8, mantissa_bits=7)
    pad = ((0, 8 - choose), (0, 0))
    top = jnp.concatenate([jnp.pad(expert_ids.T.astype(F32), pad), jnp.pad(high.T, pad)], axis=1)
    bottom = jnp.concatenate([jnp.pad(low.T, pad), jnp.zeros_like(jnp.pad(low.T, pad))], axis=1)
    return jnp.concatenate([top, bottom], axis=0).astype(BF16)


def forward_kernel(
    choose, sources, shares, pair, me_ref, limit_ref, expert_ref, *refs,
):
    blocks, refs = refs[:sources * shares], refs[sources * shares:]
    (
        gate_ref, up_ref, down_ref,
        out_keep, out_send, back_keep, back_send, rows_ref, grads_ref, p_ref, q_ref, a_ref,
        onehot, slot_gate, out_rows, back_rows, dots,
    ) = refs
    step = pl.program_id(0)
    slots, tokens = onehot.shape[1:]
    width = blocks[0].shape[1]
    me = me_ref[0]

    def columns(mask):
        return pl.ds(pl.multiple_of(lax.bitwise_xor(me, mask) * width, width), width)

    def routing(s):
        info = blocks[s * shares][2 * tokens:2 * tokens + EXTRA, :].astype(F32)
        ids = info[0:choose, 0:tokens]
        gates = info[0:choose, tokens:2 * tokens] + info[8:8 + choose, 0:tokens]
        return ids, gates

    @pl.when(step == 0)
    def _():
        row = lax.broadcasted_iota(jnp.int32, (tokens, tokens), 0)
        col = lax.broadcasted_iota(jnp.int32, (tokens, tokens), 1)
        before = jnp.where(row < col, 1.0, 0.0).astype(BF16)
        mine = expert_ref[...]
        limit = limit_ref[...]
        place = lax.broadcasted_iota(jnp.int32, (slots // CAP, CAP, tokens), 1).astype(F32)
        for s in range(sources):
            ids, gates = routing(s)
            named = jnp.zeros((slots // CAP, tokens), F32)
            gate = jnp.zeros((slots // CAP, tokens), F32)
            for k in range(choose):
                hit = ids[k:k + 1, :] == mine
                named = named + jnp.where(hit, 1.0, 0.0)
                gate = gate + jnp.where(hit, gates[k:k + 1, :], 0.0)
            rank = nn(named.astype(BF16), before)
            rank = jnp.where((named > 0.5) & (rank < limit), rank, -1.0)
            chosen = jnp.where(rank[:, None, :] == place, 1.0, 0.0)
            gate_of = jnp.sum(chosen * gate[:, None, :], axis=2, keepdims=True)
            slot_gate[:, s * CAP:(s + 1) * CAP, :] = jnp.broadcast_to(gate_of, chosen.shape)
            table = chosen.reshape(slots, tokens).astype(BF16)
            onehot[s] = table
            for q in range(shares):
                for half, ref in ((0, rows_ref), (1, grads_ref)):
                    part = blocks[s * shares + q][half * tokens:(half + 1) * tokens, :]
                    picked = nn(table, part).astype(BF16).reshape(slots // CAP, CAP, width)
                    ref[:, s * CAP:(s + 1) * CAP, columns(q)] = picked

    for turn in range(pair):
        e = step * pair + turn
        x = rows_ref[e]
        y = grads_ref[e]
        gate = slot_gate[e][:, 0:1]
        hidden_gate = nt(x, gate_ref[turn])
        hidden_up = nt(x, up_ref[turn])
        grad = nt(y, down_ref[turn])
        sigma = jax.nn.sigmoid(hidden_gate)
        silu = hidden_gate * sigma
        activ = (silu * hidden_up).astype(BF16).astype(F32)
        dots[e] = jnp.broadcast_to(jnp.sum(activ * grad, axis=1, keepdims=True), dots.shape[1:])
        scaled = (activ * gate).astype(BF16)
        grad = grad * gate
        gate_part = (grad * hidden_up * sigma * (1.0 + hidden_gate * (1.0 - sigma))).astype(BF16)
        up_part = (grad * silu).astype(BF16)
        a_ref[turn] = scaled
        p_ref[turn] = gate_part
        q_ref[turn] = up_part
        out = nn(scaled, down_ref[turn]).astype(BF16)
        back = ((nn(gate_part, gate_ref[turn]) + nn(up_part, up_ref[turn])) * gate).astype(BF16)
        for s in range(sources):
            at = pl.ds(pl.multiple_of(e * CAP, CAP), CAP)
            out_rows[s, at, :] = out[s * CAP:(s + 1) * CAP]
            back_rows[s, at, :] = back[s * CAP:(s + 1) * CAP]

    @pl.when(step == pl.num_programs(0) - 1)
    def _():
        mine = expert_ref[...]
        for s in range(sources):
            table = onehot[s]
            ids, _ = routing(s)
            chosen = table.astype(F32).reshape(slots // CAP, CAP, tokens)
            share = jnp.sum(chosen * dots[:, s * CAP:(s + 1) * CAP, :], axis=1)
            rows = [jnp.sum(jnp.where(ids[k:k + 1, :] == mine, share, 0.0), axis=0, keepdims=True) for k in range(choose)]
            rows = jnp.concatenate(rows + [jnp.zeros((EXTRA - choose, tokens), F32)], axis=0)
            rows = jnp.concatenate([rows, jnp.zeros((EXTRA, width - tokens), F32)], axis=1).astype(BF16)
            for q in range(shares):
                out_home, back_home = (out_send, back_send) if q % 2 else (out_keep, back_keep)
                out_home[q // 2, s, 0:tokens, :] = tn(table, out_rows[s, :, columns(q)]).astype(BF16)
                out_home[q // 2, s, tokens:tokens + EXTRA, :] = rows
                back_home[q // 2, s] = tn(table, back_rows[s, :, columns(q)]).astype(BF16)


def product_kernel(left_ref, right_ref, out_ref):
    for turn in range(out_ref.shape[0]):
        out_ref[turn] = tn(left_ref[turn], right_ref[turn]).astype(BF16)


def weight_grad(left, right, pair):
    experts, rows, units = left.shape
    model = right.shape[2]
    block = lambda *shape: pl.BlockSpec((pair,) + shape, lambda e: (e, 0, 0))
    return pl.pallas_call(
        product_kernel,
        grid=(experts // pair,),
        in_specs=[block(rows, units), block(rows, model)],
        out_specs=block(units, model),
        out_shape=jax.ShapeDtypeStruct((experts, units, model), BF16),
        compiler_params=pltpu.CompilerParams(vmem_limit_bytes=56 * 1024 * 1024),
        cost_estimate=pl.CostEstimate(
            flops=2 * experts * rows * units * model,
            bytes_accessed=2 * experts * (units * model + rows * model + rows * units),
            transcendentals=0,
        ),
    )(left, right)


def swap(array, bit):
    count = lax.axis_size("etp")
    return lax.ppermute(array, "etp", [(i, i ^ bit) for i in range(count)])


def shift(array, by):
    count = lax.axis_size("expert")
    return lax.ppermute(array, "expert", [(i, (i + by) % count) for i in range(count)])


def gather_blocks(block):
    sources = lax.axis_size("expert")
    blocks = []
    for s in range(sources):
        held = shift(block, s) if s else block
        across = swap(held, 2)
        blocks = blocks + [held, swap(held, 1), across, swap(across, 1)]
    return blocks


def add(a, b):
    return (a.astype(F32) + b.astype(F32)).astype(BF16)


def gathered_body(
    hidden_in, out_grad, expert_ids, gate_values, capacity_blocks, gate_weight, up_weight, down_weight
):
    sources = lax.axis_size("expert")
    shares = lax.axis_size("etp")
    tokens, width = hidden_in.shape
    choose = expert_ids.shape[1]
    local_experts, units, model = down_weight.shape
    slots = local_experts * CAP
    rows = sources * CAP
    pair = 2 if local_experts % 2 == 0 else 1
    me = lax.axis_index("etp").astype(jnp.int32)[None]
    first = lax.axis_index("expert") * local_experts
    limit = lax.dynamic_slice(capacity_blocks, (first,), (local_experts,)).astype(F32)[:, None] * BLK
    mine = (first + jnp.arange(local_experts, dtype=jnp.int32)).astype(F32)[:, None]
    gate_t = jnp.swapaxes(gate_weight, 1, 2)
    up_t = jnp.swapaxes(up_weight, 1, 2)
    packed = jnp.concatenate([hidden_in, out_grad, routing_rows(expert_ids, gate_values)], axis=0)
    blocks = gather_blocks(packed)

    per_expert = lambda *shape: pl.BlockSpec((pair,) + shape, lambda e: (e, 0, 0))
    whole = lambda *shape: pl.BlockSpec(shape, lambda e: (0,) * len(shape))
    out_shapes = [
        (2, sources, tokens + EXTRA, width),
        (2, sources, tokens + EXTRA, width),
        (2, sources, tokens, width),
        (2, sources, tokens, width),
        (local_experts, rows, model),
        (local_experts, rows, model),
    ]
    out_keep, out_send, back_keep, back_send, x_rows, y_rows, gate_part, up_part, scaled = pl.pallas_call(
        functools.partial(forward_kernel, choose, sources, shares, pair),
        grid=(local_experts // pair,),
        in_specs=[
            pl.BlockSpec(memory_space=pltpu.SMEM),
            whole(local_experts, 1),
            whole(local_experts, 1),
        ]
        + [whole(2 * tokens + EXTRA, width)] * (sources * shares)
        + [per_expert(units, model)] * 3,
        out_specs=[whole(*shape) for shape in out_shapes] + [per_expert(rows, units)] * 3,
        out_shape=[jax.ShapeDtypeStruct(shape, BF16) for shape in out_shapes]
        + [jax.ShapeDtypeStruct((local_experts, rows, units), BF16)] * 3,
        scratch_shapes=[
            pltpu.VMEM((sources, slots, tokens), BF16),
            pltpu.VMEM((local_experts, rows, tokens), F32),
            pltpu.VMEM((sources, slots, model), BF16),
            pltpu.VMEM((sources, slots, model), BF16),
            pltpu.VMEM((local_experts, rows, tokens), F32),
        ],
        compiler_params=pltpu.CompilerParams(vmem_limit_bytes=48 * 1024 * 1024),
        cost_estimate=pl.CostEstimate(
            flops=2 * 6 * local_experts * rows * units * model,
            bytes_accessed=3 * 2 * local_experts * units * model,
            transcendentals=local_experts * rows * units,
        ),
    )(me, limit, mine, *blocks, gate_t, up_t, down_weight)

    out_came, back_came = swap(out_send, 1), swap(back_send, 1)
    down_grad = weight_grad(scaled, y_rows, pair)
    out_far, back_far = add(out_keep[1], out_came[1]), add(back_keep[1], back_came[1])
    out_far, back_far, up_part = lax.optimization_barrier((out_far, back_far, up_part))
    out_came, back_came = add(out_keep[0], out_came[0]), add(back_keep[0], back_came[0])
    up_grad = weight_grad(up_part, x_rows, pair)
    out_near, back_near = add(out_came, swap(out_far, 2)), add(back_came, swap(back_far, 2))
    out_near, back_near, gate_part = lax.optimization_barrier((out_near, back_near, gate_part))
    gate_grad = weight_grad(gate_part, x_rows, pair)
    out_total, back_total = out_near[0].astype(F32), back_near[0].astype(F32)
    for s in range(1, sources):
        out_total = out_total + shift(out_near[s], -s).astype(F32)
        back_total = back_total + shift(back_near[s], -s).astype(F32)
    return (
        out_total[0:tokens].astype(BF16),
        back_total.astype(BF16),
        out_total[tokens:tokens + choose, 0:tokens].T,
        jnp.swapaxes(gate_grad, 1, 2),
        jnp.swapaxes(up_grad, 1, 2),
        down_grad,
    )


def slot_layout(expert_ids, capacity_blocks):
    tokens_here, choose = expert_ids.shape
    experts = capacity_blocks.shape[0]
    flat_ids = expert_ids.reshape(-1)
    onehot = (flat_ids[:, None] == jnp.arange(experts, dtype=jnp.int32)[None, :]).astype(jnp.int32)
    before = jnp.cumsum(onehot, axis=0) - onehot
    ranks = jnp.sum(before * onehot, axis=1)
    limits = jnp.sum(onehot * capacity_blocks[None, :], axis=1) * BLK
    kept = ranks < limits
    slots = jnp.where(kept, flat_ids * CAP + ranks, experts * CAP)
    token_index = jnp.arange(tokens_here * choose, dtype=jnp.int32) // choose
    owners = (
        jnp.full((experts * CAP,), tokens_here, jnp.int32).at[slots].set(token_index, mode="drop")
    )
    return (kept.reshape(tokens_here, choose), slots.reshape(tokens_here, choose), owners)


def outgoing(rows, owners, experts, scale):
    padded = jnp.concatenate([rows, jnp.zeros((1, rows.shape[1]), rows.dtype)], 0)
    picked = padded[owners]
    if scale is not None:
        picked = (scale[:, None] * picked.astype(jnp.float32)).astype(jnp.bfloat16)
    return picked.reshape(experts, CAP, rows.shape[1])


def local_grads(hidden_gate, hidden_up, act_grad):
    sigma = jax.nn.sigmoid(hidden_gate)
    gate_part = (act_grad * hidden_up * sigma * (1.0 + hidden_gate * (1.0 - sigma))).astype(
        jnp.bfloat16
    )
    up_part = (act_grad * jax.nn.silu(hidden_gate)).astype(jnp.bfloat16)
    return (gate_part, up_part)


def combine(back, slots, weights):
    padded = jnp.concatenate([back, jnp.zeros((1, back.shape[1]), back.dtype)], 0)
    picked = padded[slots].astype(jnp.float32)
    return (jnp.einsum("tk,tkw->tw", weights, picked), picked)


def dispatched_body(
    hidden_in,
    out_grad,
    expert_ids,
    gate_values,
    capacity_blocks,
    gate_weight,
    up_weight,
    down_weight,
):
    experts = capacity_blocks.shape[0]
    sources = lax.axis_size("expert")
    local_experts = gate_weight.shape[0]
    kept, slots, owners = slot_layout(expert_ids, capacity_blocks)
    weights = jnp.where(kept, gate_values, 0.0)
    slot_gates = (
        jnp.zeros((experts * CAP,), jnp.float32)
        .at[slots.reshape(-1)]
        .set(weights.reshape(-1), mode="drop")
    )
    send_in = outgoing(hidden_in, owners, experts, None)
    send_grad = outgoing(out_grad, owners, experts, slot_gates)
    recv_in, recv_grad = (
        lax.all_to_all(send_in, "expert", split_axis=0, concat_axis=0, tiled=True),
        lax.all_to_all(send_grad, "expert", split_axis=0, concat_axis=0, tiled=True),
    )
    share = recv_in.shape[2]
    share_in = recv_in.reshape(sources, local_experts, CAP, share)
    share_grad = recv_grad.reshape(sources, local_experts, CAP, share)
    piece = lax.all_gather(share_in, "etp", axis=3, tiled=True)
    hidden_gate = jnp.einsum(
        "secn,enf->secf", piece, gate_weight, preferred_element_type=jnp.float32
    )
    hidden_up = jnp.einsum("secn,enf->secf", piece, up_weight, preferred_element_type=jnp.float32)
    activ = (jax.nn.silu(hidden_gate) * hidden_up).astype(jnp.bfloat16)
    piece = lax.all_gather(share_grad, "etp", axis=3, tiled=True)
    act_grad = jnp.einsum("secn,efn->secf", piece, down_weight, preferred_element_type=jnp.float32)
    columns = jnp.einsum("secf,secn->efn", activ, piece, preferred_element_type=jnp.float32)
    act_grad, down_grad = (act_grad, columns)
    gate_part, up_part = local_grads(hidden_gate, hidden_up, act_grad)
    stacked = jnp.stack([gate_part, up_part])
    weight_grads = jnp.einsum(
        "secn,gsecf->genf",
        lax.all_gather(share_in, "etp", axis=3, tiled=True),
        stacked,
        preferred_element_type=jnp.float32,
    )
    out_part = jnp.einsum("secf,efd->secd", activ, down_weight, preferred_element_type=jnp.float32)
    back_part = jnp.einsum(
        "secf,edf->secd", gate_part, gate_weight, preferred_element_type=jnp.float32
    )
    back_part = back_part + jnp.einsum(
        "secf,edf->secd", up_part, up_weight, preferred_element_type=jnp.float32
    )
    out_rows = lax.psum_scatter(
        out_part.astype(jnp.bfloat16), "etp", scatter_dimension=3, tiled=True
    )
    home_out = lax.all_to_all(out_rows, "expert", split_axis=0, concat_axis=0, tiled=True)
    share_width = home_out.shape[3]
    layer_sum, picked = combine(home_out.reshape(experts * CAP, share_width), slots, weights)
    dot_part = jnp.einsum("tw,tkw->tk", out_grad.astype(jnp.float32), picked) * kept.astype(
        jnp.float32
    )
    gate_value_grad = lax.psum(dot_part, "etp")
    back_rows = lax.psum_scatter(
        back_part.astype(jnp.bfloat16), "etp", scatter_dimension=3, tiled=True
    )
    home_back = lax.all_to_all(back_rows, "expert", split_axis=0, concat_axis=0, tiled=True)
    input_sum, returned = combine(home_back.reshape(experts * CAP, share_width), slots, weights)
    return (
        layer_sum.astype(jnp.bfloat16),
        input_sum.astype(jnp.bfloat16),
        gate_value_grad,
        weight_grads[0].astype(jnp.bfloat16),
        weight_grads[1].astype(jnp.bfloat16),
        down_grad.astype(jnp.bfloat16),
    )


def body(*operands):
    hidden_in, gate_weight = operands[0], operands[5]
    if lax.axis_size("etp") == 4 and hidden_in.shape[0] <= gate_weight.shape[0] * CAP:
        return gathered_body(*operands)
    return dispatched_body(*operands)


def solution(mesh):
    in_specs = (
        P(("groups", "expert"), "etp"),
        P(("groups", "expert"), "etp"),
        P(("groups", "expert"), None),
        P(("groups", "expert"), None),
        P("groups"),
        P("expert", None, "etp"),
        P("expert", None, "etp"),
        P("expert", "etp", None),
    )
    out_specs = (
        P(("groups", "expert"), "etp"),
        P(("groups", "expert"), "etp"),
        P(("groups", "expert"), None),
        P(("groups", "expert"), None, "etp"),
        P(("groups", "expert"), None, "etp"),
        P(("groups", "expert"), "etp", None),
    )
    return jax.shard_map(body, mesh=mesh, in_specs=in_specs, out_specs=out_specs, check_vma=False)
```

```python
import functools

import jax
import jax.numpy as jnp
from jax import lax
from jax.experimental import pallas as pl
from jax.experimental.pallas import tpu as pltpu
from jax.sharding import PartitionSpec as P

CAP = 16
BLK = 4
EXTRA = 16
F32 = jnp.float32
BF16 = jnp.bfloat16


def nn(a, b):
    return lax.dot_general(a, b, (((1,), (0,)), ((), ())), preferred_element_type=F32)


def nt(a, b):
    return lax.dot_general(a, b, (((1,), (1,)), ((), ())), preferred_element_type=F32)


def tn(a, b):
    return lax.dot_general(a, b, (((0,), (0,)), ((), ())), preferred_element_type=F32)


def routing_rows(expert_ids, gate_values):
    choose = expert_ids.shape[1]
    high = lax.reduce_precision(gate_values, exponent_bits=8, mantissa_bits=7)
    low = lax.reduce_precision(gate_values - high, exponent_bits=8, mantissa_bits=7)
    pad = ((0, 8 - choose), (0, 0))
    top = jnp.concatenate([jnp.pad(expert_ids.T.astype(F32), pad), jnp.pad(high.T, pad)], axis=1)
    bottom = jnp.concatenate([jnp.pad(low.T, pad), jnp.zeros_like(jnp.pad(low.T, pad))], axis=1)
    return jnp.concatenate([top, bottom], axis=0).astype(BF16)


def routing(info, choose, tokens):
    info = info.astype(F32)
    return info[0:choose, 0:tokens], info[0:choose, tokens:2 * tokens] + info[8:8 + choose, 0:tokens]


def columns(me, mask, width):
    return pl.ds(pl.multiple_of(lax.bitwise_xor(me, mask) * width, width), width)


def send_home(home_keep, home_send, me, onehot, rows, tokens, width):
    for s in range(onehot.shape[0]):
        for q in range(4):
            home = home_send if q % 2 else home_keep
            home[q // 2, s, 0:tokens, :] = tn(onehot[s], rows[s, :, columns(me, q, width)]).astype(BF16)


RING = 8


def ring(weight, slots, sems):
    def load(e):
        slot = lax.rem(e, RING)
        return pltpu.make_async_copy(weight.at[e], slots.at[slot], sems.at[slot])

    def start(e):
        @pl.when(e < weight.shape[0])
        def _():
            load(e).start()

    return start, lambda e: load(e).wait()


def forward_kernel(
    choose, capacity_ref, o0, o1, o2, o3, b0, b1, b2, b3, gate_ref, up_ref, down_hbm, later_ref,
    out_rows, rows_ref, act_ref, slope_ref, silu_ref, onehot, slot_gate,
    down_ref, sems,
):
    sources, slots, tokens = onehot.shape
    experts = slots // CAP
    width = b0.shape[2]
    me = lax.axis_index("etp")
    first = lax.axis_index("expert") * experts

    start, wait = ring(down_hbm, down_ref, sems)
    for e in range(RING):
        start(jnp.int32(e))
    row = lax.broadcasted_iota(jnp.int32, (tokens, tokens), 0)
    col = lax.broadcasted_iota(jnp.int32, (tokens, tokens), 1)
    before = jnp.where(row < col, 1.0, 0.0).astype(BF16)
    expert = lax.broadcasted_iota(jnp.int32, (experts, tokens), 0)
    mine = (first + expert).astype(F32)
    limit = jnp.zeros((experts, tokens), jnp.int32)
    for e in range(experts):
        limit = jnp.where(expert == e, capacity_ref[first + e] * BLK, limit)
    limit = limit.astype(F32)
    place = lax.broadcasted_iota(jnp.int32, (experts, CAP, tokens), 1).astype(F32)
    for s in range(sources):
        block = [o[...] for o in (o0, o1, o2, o3)] if s == 0 else [b[s - 1] for b in (b0, b1, b2, b3)]
        ids, gates = routing(block[0][tokens:tokens + EXTRA, :], choose, tokens)
        named = jnp.zeros((experts, tokens), F32)
        gate = jnp.zeros((experts, tokens), F32)
        for k in range(choose):
            hit = ids[k:k + 1, :] == mine
            named = named + jnp.where(hit, 1.0, 0.0)
            gate = gate + jnp.where(hit, gates[k:k + 1, :], 0.0)
        rank = nn(named.astype(BF16), before)
        rank = jnp.where((named > 0.5) & (rank < limit), rank, -1.0)
        chosen = jnp.where(rank[:, None, :] == place, 1.0, 0.0)
        gate_of = jnp.sum(chosen * gate[:, None, :], axis=2, keepdims=True)
        slot_gate[:, s * CAP:(s + 1) * CAP, :] = jnp.broadcast_to(gate_of, chosen.shape)
        table = chosen.reshape(slots, tokens).astype(BF16)
        onehot[s] = table
        for q in range(4):
            picked = nn(table, block[q][0:tokens, :]).astype(BF16).reshape(experts, CAP, width)
            rows_ref[:, s * CAP:(s + 1) * CAP, columns(me, q, width)] = picked

    def some(turn, _):
        for e in (turn * 2, turn * 2 + 1):
            wait(e)
        for e in (turn * 2, turn * 2 + 1):
            x = rows_ref[e]
            hidden_gate = nt(x, gate_ref[e])
            hidden_up = nt(x, up_ref[e])
            sigma = jax.nn.sigmoid(hidden_gate)
            silu = hidden_gate * sigma
            activ = (silu * hidden_up).astype(BF16)
            act_ref[e] = activ
            slope_ref[e] = hidden_up * sigma * (1.0 + hidden_gate * (1.0 - sigma))
            silu_ref[e] = silu
            scaled = (activ.astype(F32) * slot_gate[e][:, 0:1]).astype(BF16)
            out = nn(scaled, down_ref[lax.rem(e, RING)]).astype(BF16)
            at = pl.ds(pl.multiple_of(e * CAP, CAP), CAP)
            for s in range(sources):
                out_rows[s, at, :] = out[s * CAP:(s + 1) * CAP]
        for e in (turn * 2, turn * 2 + 1):
            start(e + RING)
        return 0

    lax.fori_loop(0, experts // 2, some, 0)


def home_kernel(onehot, rows, *refs):
    keep, send = refs[-2:]
    send_home(keep, send, lax.axis_index("etp"), onehot, rows, keep.shape[2], keep.shape[3])


def slope_kernel(
    choose, own_ref, info_ref, a0, a1, a2, a3, n0, n1, n2, n3,
    down_hbm, act_ref, slope_ref, silu_ref, onehot, slot_gate,
    rows_ref, p_ref, q_ref, a_ref, value_ref,
    dots, down_ref, sems,
):
    sources, slots, tokens = onehot.shape
    experts = slots // CAP
    start, wait = ring(down_hbm, down_ref, sems)
    for e in range(RING):
        start(jnp.int32(e))
    width = own_ref.shape[1]
    me = lax.axis_index("etp")
    for s, (here, near) in enumerate(((a0, n0), (a1, n1), (a2, n2), (a3, n3))):
        for q in range(4):
            block = (near if q % 2 else here)[q // 2]
            picked = nn(onehot[s], block).astype(BF16).reshape(experts, CAP, width)
            rows_ref[:, s * CAP:(s + 1) * CAP, columns(me, q, width)] = picked

    def some(turn, _):
        for e in (turn * 2, turn * 2 + 1):
            wait(e)
        for e in (turn * 2, turn * 2 + 1):
            grad = nt(rows_ref[e], down_ref[lax.rem(e, RING)])
            activ = act_ref[e].astype(F32)
            gate = slot_gate[e][:, 0:1]
            dots[e] = jnp.broadcast_to(jnp.sum(activ * grad, axis=1, keepdims=True), dots.shape[1:])
            a_ref[e] = (activ * gate).astype(BF16)
            grad = grad * gate
            p_ref[e] = (grad * slope_ref[e]).astype(BF16)
            q_ref[e] = (grad * silu_ref[e]).astype(BF16)
        for e in (turn * 2, turn * 2 + 1):
            start(e + RING)
        return 0

    lax.fori_loop(0, experts // 2, some, 0)
    expert = lax.broadcasted_iota(jnp.int32, (experts, tokens), 0)
    mine = (lax.axis_index("expert") * experts + expert).astype(F32)
    for s in range(sources):
        info = own_ref[tokens:tokens + EXTRA, :] if s == 0 else info_ref[s - 1, tokens:tokens + EXTRA, :]
        ids, _ = routing(info, choose, tokens)
        chosen = onehot[s].astype(F32).reshape(experts, CAP, tokens)
        share = jnp.sum(chosen * dots[:, s * CAP:(s + 1) * CAP, :], axis=1)
        rows = [jnp.sum(jnp.where(ids[k:k + 1, :] == mine, share, 0.0), axis=0, keepdims=True) for k in range(choose)]
        rows = jnp.concatenate(rows + [jnp.zeros((EXTRA - choose, tokens), F32)], axis=0)
        value_ref[s] = jnp.concatenate([rows, jnp.zeros((EXTRA, width - tokens), F32)], axis=1).astype(BF16)


def back_kernel(gate_ref, up_ref, p_ref, q_ref, onehot, slot_gate, value_ref, keep, send, back_rows):
    sources, slots, tokens = onehot.shape
    width = keep.shape[3]

    def some(turn, _):
        for e in (turn * 2, turn * 2 + 1):
            back = nn(p_ref[e], gate_ref[e]) + nn(q_ref[e], up_ref[e])
            back = (back * slot_gate[e][:, 0:1]).astype(BF16)
            at = pl.ds(pl.multiple_of(e * CAP, CAP), CAP)
            for s in range(sources):
                back_rows[s, at, :] = back[s * CAP:(s + 1) * CAP]
        return 0

    lax.fori_loop(0, slots // CAP // 2, some, 0)
    send_home(keep, send, lax.axis_index("etp"), onehot, back_rows, tokens, width)
    for s in range(sources):
        for home in (keep, send):
            home[0, s, tokens:tokens + EXTRA, :] = value_ref[s]
            home[1, s, tokens:tokens + EXTRA, :] = value_ref[s]


SLOTS = 4


def product_kernel(left_ref, right_ref, out_ref, held, sems):
    experts = out_ref.shape[0]

    def store(e):
        slot = lax.rem(e, SLOTS)
        return pltpu.make_async_copy(held.at[slot], out_ref.at[e], sems.at[slot])

    def one(e, _):
        @pl.when(e >= SLOTS)
        def _():
            store(e - SLOTS).wait()

        held[lax.rem(e, SLOTS)] = tn(left_ref[e], right_ref[e]).astype(BF16)
        store(e).start()
        return 0

    lax.fori_loop(0, experts, one, 0)

    def last(e, _):
        store(e).wait()
        return 0

    lax.fori_loop(experts - SLOTS, experts, last, 0)


def load_kernel(source, target, token, sems):
    token[...] = jnp.zeros_like(token)
    copies = [pltpu.make_async_copy(source.at[e], target.at[e], sems.at[e]) for e in range(source.shape[0])]
    for copy in copies:
        copy.start()
    for copy in copies:
        copy.wait()


def in_vmem(weight):
    return pl.pallas_call(
        load_kernel,
        in_specs=[pl.BlockSpec(memory_space=pltpu.HBM)],
        out_specs=[pl.BlockSpec(memory_space=pltpu.VMEM)] * 2,
        out_shape=[pltpu.VMEM(weight.shape, BF16), jax.ShapeDtypeStruct((8, 128), F32)],
        scratch_shapes=[pltpu.SemaphoreType.DMA((weight.shape[0],))],
        compiler_params=pltpu.CompilerParams(vmem_limit_bytes=4 * 1024 * 1024),
        cost_estimate=pl.CostEstimate(flops=0, bytes_accessed=2 * weight.size, transcendentals=0),
    )(pltpu.with_memory_space_constraint(weight, pltpu.HBM))


def join_kernel(count, *refs):
    for i in range(count):
        refs[-1][i] = refs[i][...]


def join(arrays, *there):
    return kernel_call(
        functools.partial(join_kernel, len(arrays)),
        [jax.ShapeDtypeStruct((len(arrays),) + arrays[0].shape, arrays[0].dtype)],
        [],
        0,
        limit=2,
    )(*arrays, *there)[0]


def kernel_call(kernel, out_shape, scratch, flops, out_specs=None, limit=4, in_hbm=()):
    def call(*operands):
        specs = [
            pl.BlockSpec(memory_space=pltpu.HBM if i in in_hbm else pltpu.SMEM if x.ndim == 1 else pltpu.VMEM)
            for i, x in enumerate(operands)
        ]
        operands = [
            pltpu.with_memory_space_constraint(x, pltpu.HBM) if i in in_hbm else x for i, x in enumerate(operands)
        ]
        return pl.pallas_call(
            kernel,
            in_specs=specs,
            out_specs=out_specs or [pl.BlockSpec(memory_space=pltpu.VMEM)] * len(out_shape),
            out_shape=out_shape,
            scratch_shapes=scratch,
            compiler_params=pltpu.CompilerParams(vmem_limit_bytes=limit * 1024 * 1024),
            cost_estimate=pl.CostEstimate(flops=flops, bytes_accessed=flops // 128, transcendentals=0),
        )(*operands)

    return call


def weight_grad(left, right):
    experts, rows, units = left.shape
    model = right.shape[2]
    return kernel_call(
        product_kernel,
        jax.ShapeDtypeStruct((experts, units, model), BF16),
        [pltpu.VMEM((SLOTS, units, model), BF16), pltpu.SemaphoreType.DMA((SLOTS,))],
        2 * experts * rows * units * model,
        out_specs=pl.BlockSpec(memory_space=pltpu.HBM),
        limit=6,
    )(left, right)


def swap(array, bit):
    count = lax.axis_size("etp")
    return lax.ppermute(array, "etp", [(i, i ^ bit) for i in range(count)])


def shift(array, by):
    count = lax.axis_size("expert")
    return lax.ppermute(array, "expert", [(i, (i + by) % count) for i in range(count)])


def add(a, b):
    return (a.astype(F32) + b.astype(F32)).astype(BF16)


def gathered_body(
    hidden_in, out_grad, expert_ids, gate_values, capacity_blocks, gate_weight, up_weight, down_weight
):
    sources = lax.axis_size("expert")
    tokens, width = hidden_in.shape
    choose = expert_ids.shape[1]
    local_experts, units, model = down_weight.shape
    slots = local_experts * CAP
    rows = sources * CAP
    gate_t, gate_there = in_vmem(jnp.swapaxes(gate_weight, 1, 2))
    up_t, up_there = in_vmem(jnp.swapaxes(up_weight, 1, 2))
    product = 2 * local_experts * rows * units * model
    held = lambda *shape, kind=BF16: pltpu.VMEM(shape, kind)
    sent = lambda *shape: jax.ShapeDtypeStruct(shape, BF16)

    own = jnp.concatenate([hidden_in, routing_rows(expert_ids, gate_values)], axis=0)
    came = [shift(own, s) for s in range(1, sources)]
    own_across = swap(own, 2)
    grad_across = swap(out_grad, 2)
    own_near = swap(own, 1)
    came = join(came, gate_there, up_there, own_across, own_near)
    came_across = swap(came, 2)
    across_near = swap(own_across, 1)
    grads = join([out_grad, grad_across], came, across_near)
    grads = [grads] + [shift(grads, s) for s in range(1, sources)]

    out_rows, x_rows, activ, slope, silu, onehot, slot_gate = kernel_call(
        functools.partial(forward_kernel, choose),
        [
            held(sources, slots, model),
            held(local_experts, rows, model),
            held(local_experts, rows, units),
            held(local_experts, rows, units, kind=F32),
            held(local_experts, rows, units, kind=F32),
            held(sources, slots, tokens),
            held(local_experts, rows, tokens, kind=F32),
        ],
        [pltpu.VMEM((RING, units, model), BF16), pltpu.SemaphoreType.DMA((RING,))],
        3 * product,
        limit=10,
        in_hbm=(11,),
    )(
        capacity_blocks,
        own, own_near, own_across, across_near,
        came, swap(came, 1), came_across, swap(came_across, 1),
        gate_t, up_t, down_weight, grads[0],
    )

    keep, send = kernel_call(
        home_kernel, [sent(2, sources, tokens, width)] * 2, [], 2 * slots * sources * tokens * model, limit=2,
    )(onehot, out_rows, *grads)
    out_came = swap(send, 1)
    y_rows, gate_part, up_part, scaled, values = kernel_call(
        functools.partial(slope_kernel, choose),
        [
            held(local_experts, rows, model),
            held(local_experts, rows, units),
            held(local_experts, rows, units),
            held(local_experts, rows, units),
            held(sources, EXTRA, width),
        ],
        [
            pltpu.VMEM((local_experts, rows, tokens), F32),
            pltpu.VMEM((RING, units, model), BF16),
            pltpu.SemaphoreType.DMA((RING,)),
        ],
        product,
        limit=8,
        in_hbm=(10,),
    )(own, came, *grads, *[swap(x, 1) for x in grads], down_weight, activ, slope, silu, onehot, slot_gate)

    out_far = add(keep[1], out_came[1])
    out_far, gate_part = lax.optimization_barrier((out_far, gate_part))
    out_far_came = swap(out_far, 2)
    out_near = add(keep[0], out_came[0])
    keep, send = kernel_call(
        back_kernel,
        [sent(2, sources, tokens + EXTRA, width), sent(2, sources, tokens + EXTRA, width)],
        [pltpu.VMEM((sources, slots, model), BF16)],
        2 * product,
    )(gate_t, up_t, gate_part, up_part, onehot, slot_gate, values)

    back_came = swap(send, 1)
    out_near = add(out_near, out_far_came)
    out_near, scaled = lax.optimization_barrier((out_near, scaled))
    out_total = out_near[0].astype(F32)
    for s in range(1, sources):
        out_total = out_total + shift(out_near[s], -s).astype(F32)
    down_grad = weight_grad(scaled, y_rows)
    back_far = add(keep[1], back_came[1])
    back_far, up_part = lax.optimization_barrier((back_far, up_part))
    back_far_came = swap(back_far, 2)
    back_near = add(keep[0], back_came[0])
    up_grad = weight_grad(up_part, x_rows)
    back_near = add(back_near, back_far_came)
    back_near, gate_part = lax.optimization_barrier((back_near, gate_part))
    back_total = back_near[0].astype(F32)
    for s in range(1, sources):
        back_total = back_total + shift(back_near[s], -s).astype(F32)
    gate_grad = weight_grad(gate_part, x_rows)
    return (
        out_total.astype(BF16),
        back_total[0:tokens].astype(BF16),
        back_total[tokens:tokens + choose, 0:tokens].T,
        jnp.swapaxes(gate_grad, 1, 2),
        jnp.swapaxes(up_grad, 1, 2),
        down_grad,
    )


def slot_layout(expert_ids, capacity_blocks):
    tokens_here, choose = expert_ids.shape
    experts = capacity_blocks.shape[0]
    flat_ids = expert_ids.reshape(-1)
    onehot = (flat_ids[:, None] == jnp.arange(experts, dtype=jnp.int32)[None, :]).astype(jnp.int32)
    before = jnp.cumsum(onehot, axis=0) - onehot
    ranks = jnp.sum(before * onehot, axis=1)
    limits = jnp.sum(onehot * capacity_blocks[None, :], axis=1) * BLK
    kept = ranks < limits
    slots = jnp.where(kept, flat_ids * CAP + ranks, experts * CAP)
    token_index = jnp.arange(tokens_here * choose, dtype=jnp.int32) // choose
    owners = (
        jnp.full((experts * CAP,), tokens_here, jnp.int32).at[slots].set(token_index, mode="drop")
    )
    return (kept.reshape(tokens_here, choose), slots.reshape(tokens_here, choose), owners)


def outgoing(rows, owners, experts, scale):
    padded = jnp.concatenate([rows, jnp.zeros((1, rows.shape[1]), rows.dtype)], 0)
    picked = padded[owners]
    if scale is not None:
        picked = (scale[:, None] * picked.astype(jnp.float32)).astype(jnp.bfloat16)
    return picked.reshape(experts, CAP, rows.shape[1])


def local_grads(hidden_gate, hidden_up, act_grad):
    sigma = jax.nn.sigmoid(hidden_gate)
    gate_part = (act_grad * hidden_up * sigma * (1.0 + hidden_gate * (1.0 - sigma))).astype(
        jnp.bfloat16
    )
    up_part = (act_grad * jax.nn.silu(hidden_gate)).astype(jnp.bfloat16)
    return (gate_part, up_part)


def combine(back, slots, weights):
    padded = jnp.concatenate([back, jnp.zeros((1, back.shape[1]), back.dtype)], 0)
    picked = padded[slots].astype(jnp.float32)
    return (jnp.einsum("tk,tkw->tw", weights, picked), picked)


def dispatched_body(
    hidden_in,
    out_grad,
    expert_ids,
    gate_values,
    capacity_blocks,
    gate_weight,
    up_weight,
    down_weight,
):
    experts = capacity_blocks.shape[0]
    sources = lax.axis_size("expert")
    local_experts = gate_weight.shape[0]
    kept, slots, owners = slot_layout(expert_ids, capacity_blocks)
    weights = jnp.where(kept, gate_values, 0.0)
    slot_gates = (
        jnp.zeros((experts * CAP,), jnp.float32)
        .at[slots.reshape(-1)]
        .set(weights.reshape(-1), mode="drop")
    )
    send_in = outgoing(hidden_in, owners, experts, None)
    send_grad = outgoing(out_grad, owners, experts, slot_gates)
    recv_in, recv_grad = (
        lax.all_to_all(send_in, "expert", split_axis=0, concat_axis=0, tiled=True),
        lax.all_to_all(send_grad, "expert", split_axis=0, concat_axis=0, tiled=True),
    )
    share = recv_in.shape[2]
    share_in = recv_in.reshape(sources, local_experts, CAP, share)
    share_grad = recv_grad.reshape(sources, local_experts, CAP, share)
    piece = lax.all_gather(share_in, "etp", axis=3, tiled=True)
    hidden_gate = jnp.einsum(
        "secn,enf->secf", piece, gate_weight, preferred_element_type=jnp.float32
    )
    hidden_up = jnp.einsum("secn,enf->secf", piece, up_weight, preferred_element_type=jnp.float32)
    activ = (jax.nn.silu(hidden_gate) * hidden_up).astype(jnp.bfloat16)
    piece = lax.all_gather(share_grad, "etp", axis=3, tiled=True)
    act_grad = jnp.einsum("secn,efn->secf", piece, down_weight, preferred_element_type=jnp.float32)
    columns = jnp.einsum("secf,secn->efn", activ, piece, preferred_element_type=jnp.float32)
    act_grad, down_grad = (act_grad, columns)
    gate_part, up_part = local_grads(hidden_gate, hidden_up, act_grad)
    stacked = jnp.stack([gate_part, up_part])
    weight_grads = jnp.einsum(
        "secn,gsecf->genf",
        lax.all_gather(share_in, "etp", axis=3, tiled=True),
        stacked,
        preferred_element_type=jnp.float32,
    )
    out_part = jnp.einsum("secf,efd->secd", activ, down_weight, preferred_element_type=jnp.float32)
    back_part = jnp.einsum(
        "secf,edf->secd", gate_part, gate_weight, preferred_element_type=jnp.float32
    )
    back_part = back_part + jnp.einsum(
        "secf,edf->secd", up_part, up_weight, preferred_element_type=jnp.float32
    )
    out_rows = lax.psum_scatter(
        out_part.astype(jnp.bfloat16), "etp", scatter_dimension=3, tiled=True
    )
    home_out = lax.all_to_all(out_rows, "expert", split_axis=0, concat_axis=0, tiled=True)
    share_width = home_out.shape[3]
    layer_sum, picked = combine(home_out.reshape(experts * CAP, share_width), slots, weights)
    dot_part = jnp.einsum("tw,tkw->tk", out_grad.astype(jnp.float32), picked) * kept.astype(
        jnp.float32
    )
    gate_value_grad = lax.psum(dot_part, "etp")
    back_rows = lax.psum_scatter(
        back_part.astype(jnp.bfloat16), "etp", scatter_dimension=3, tiled=True
    )
    home_back = lax.all_to_all(back_rows, "expert", split_axis=0, concat_axis=0, tiled=True)
    input_sum, returned = combine(home_back.reshape(experts * CAP, share_width), slots, weights)
    return (
        layer_sum.astype(jnp.bfloat16),
        input_sum.astype(jnp.bfloat16),
        gate_value_grad,
        weight_grads[0].astype(jnp.bfloat16),
        weight_grads[1].astype(jnp.bfloat16),
        down_grad.astype(jnp.bfloat16),
    )


def body(*operands):
    hidden_in, gate_weight = operands[0], operands[5]
    if lax.axis_size("etp") == 4 and hidden_in.shape[0] <= gate_weight.shape[0] * CAP:
        return gathered_body(*operands)
    return dispatched_body(*operands)


def solution(mesh):
    in_specs = (
        P(("groups", "expert"), "etp"),
        P(("groups", "expert"), "etp"),
        P(("groups", "expert"), None),
        P(("groups", "expert"), None),
        P("groups"),
        P("expert", None, "etp"),
        P("expert", None, "etp"),
        P("expert", "etp", None),
    )
    out_specs = (
        P(("groups", "expert"), "etp"),
        P(("groups", "expert"), "etp"),
        P(("groups", "expert"), None),
        P(("groups", "expert"), None, "etp"),
        P(("groups", "expert"), None, "etp"),
        P(("groups", "expert"), "etp", None),
    )
    return jax.shard_map(body, mesh=mesh, in_specs=in_specs, out_specs=out_specs, check_vma=False)
```

```python
import functools

import jax
import jax.numpy as jnp
from jax import lax
from jax.experimental import pallas as pl
from jax.experimental.pallas import tpu as pltpu
from jax.sharding import PartitionSpec as P

CAP = 16
BLK = 4
EXTRA = 16
F32 = jnp.float32
BF16 = jnp.bfloat16


def nn(a, b):
    return lax.dot_general(a, b, (((1,), (0,)), ((), ())), preferred_element_type=F32)


def nt(a, b):
    return lax.dot_general(a, b, (((1,), (1,)), ((), ())), preferred_element_type=F32)


def tn(a, b):
    return lax.dot_general(a, b, (((0,), (0,)), ((), ())), preferred_element_type=F32)


def pack_kernel(hidden_hbm, ids_hbm, gates_hbm, own_ref, ids_ref, gates_ref, sems):
    tokens, width = hidden_hbm.shape
    choose = ids_ref.shape[0]
    copies = [
        pltpu.make_async_copy(hidden_hbm, own_ref.at[pl.ds(0, tokens)], sems.at[0]),
        pltpu.make_async_copy(ids_hbm, ids_ref, sems.at[1]),
        pltpu.make_async_copy(gates_hbm, gates_ref, sems.at[2]),
    ]
    for copy in copies:
        copy.start()
    for copy in copies:
        copy.wait()
    gates = gates_ref[...]
    high = gates.astype(BF16).astype(F32)
    fill = jnp.zeros((8 - choose, tokens), F32)
    top = jnp.concatenate([jnp.concatenate([ids_ref[...].astype(F32), fill], axis=0), jnp.concatenate([high, fill], axis=0)], axis=1)
    low = jnp.concatenate([jnp.concatenate([gates - high, fill], axis=0), jnp.zeros((8, width - tokens), F32)], axis=1)
    own_ref[tokens:tokens + EXTRA, :] = jnp.concatenate([top, low], axis=0).astype(BF16)


def routing(info, choose, tokens):
    info = info.astype(F32)
    return info[0:choose, 0:tokens], info[0:choose, tokens:2 * tokens] + info[8:8 + choose, 0:tokens]


def columns(me, mask, width):
    return pl.ds(pl.multiple_of(lax.bitwise_xor(me, mask) * width, width), width)


def send_home(home_keep, home_send, me, onehot, rows, tokens, width):
    for s in range(onehot.shape[0]):
        for q in range(4):
            home = home_send if q % 2 else home_keep
            home[q // 2, s, 0:tokens, :] = tn(onehot[s], rows[s, :, columns(me, q, width)]).astype(BF16)


RING = 4


def ring(weight, slots, sems):
    def load(e):
        slot = lax.rem(e, RING)
        return pltpu.make_async_copy(weight.at[e], slots.at[slot], sems.at[slot])

    def start(e):
        @pl.when(e < weight.shape[0])
        def _():
            load(e).start()

    return start, lambda e: load(e).wait()


def forward_kernel(
    choose, capacity_ref, o0, o1, o2, o3, b0, b1, b2, b3, gate_ref, up_ref, down_hbm, later_ref,
    out_rows, rows_ref, act_ref, a_ref, slope_ref, silu_ref, onehot, slot_gate,
    down_ref, sems,
):
    sources, slots, tokens = onehot.shape
    experts = slots // CAP
    width = b0.shape[2]
    me = lax.axis_index("etp")
    first = lax.axis_index("expert") * experts

    start, wait = ring(down_hbm, down_ref, sems)
    for e in range(RING):
        start(jnp.int32(e))
    row = lax.broadcasted_iota(jnp.int32, (tokens, tokens), 0)
    col = lax.broadcasted_iota(jnp.int32, (tokens, tokens), 1)
    before = jnp.where(row < col, 1.0, 0.0).astype(BF16)
    expert = lax.broadcasted_iota(jnp.int32, (experts, tokens), 0)
    mine = (first + expert).astype(F32)
    limit = jnp.zeros((experts, tokens), jnp.int32)
    for e in range(experts):
        limit = jnp.where(expert == e, capacity_ref[first + e] * BLK, limit)
    limit = limit.astype(F32)
    place = lax.broadcasted_iota(jnp.int32, (experts, CAP, tokens), 1).astype(F32)
    for s in range(sources):
        block = [o[...] for o in (o0, o1, o2, o3)] if s == 0 else [b[s - 1] for b in (b0, b1, b2, b3)]
        ids, gates = routing(block[0][tokens:tokens + EXTRA, :], choose, tokens)
        named = jnp.zeros((experts, tokens), F32)
        gate = jnp.zeros((experts, tokens), F32)
        for k in range(choose):
            hit = ids[k:k + 1, :] == mine
            named = named + jnp.where(hit, 1.0, 0.0)
            gate = gate + jnp.where(hit, gates[k:k + 1, :], 0.0)
        rank = nn(named.astype(BF16), before)
        rank = jnp.where((named > 0.5) & (rank < limit), rank, -1.0)
        chosen = jnp.where(rank[:, None, :] == place, 1.0, 0.0)
        gate_of = jnp.sum(chosen * gate[:, None, :], axis=2, keepdims=True)
        slot_gate[:, s * CAP:(s + 1) * CAP, :] = jnp.broadcast_to(gate_of, chosen.shape)
        table = chosen.reshape(slots, tokens).astype(BF16)
        onehot[s] = table
        for q in range(4):
            picked = nn(table, block[q][0:tokens, :]).astype(BF16).reshape(experts, CAP, width)
            rows_ref[:, s * CAP:(s + 1) * CAP, columns(me, q, width)] = picked

    def activate(e):
        x = rows_ref[e]
        hidden_gate = nt(x, gate_ref[e])
        hidden_up = nt(x, up_ref[e])
        sigma = jax.nn.sigmoid(hidden_gate)
        silu = hidden_gate * sigma
        activ = (silu * hidden_up).astype(BF16)
        act_ref[e] = activ
        slope_ref[e] = hidden_up * sigma * (1.0 + hidden_gate * (1.0 - sigma))
        silu_ref[e] = silu
        a_ref[e] = (activ.astype(F32) * slot_gate[e][:, 0:1]).astype(BF16)

    def project(e):
        out = nn(a_ref[e], down_ref[lax.rem(e, RING)]).astype(BF16)
        at = pl.ds(pl.multiple_of(e * CAP, CAP), CAP)
        for s in range(sources):
            out_rows[s, at, :] = out[s * CAP:(s + 1) * CAP]

    def both(e):
        wait(e - 2)
        wait(e - 1)
        project(e - 2)
        project(e - 1)
        activate(e)
        activate(e + 1)
        start(e - 2 + RING)
        start(e - 1 + RING)

    skewed(experts, activate, wait, project, both)


def skewed(experts, first, wait, second, both):
    first(jnp.int32(0))
    first(jnp.int32(1))

    def turn(i, _):
        both(i * 2)
        return 0

    lax.fori_loop(1, experts // 2, turn, 0)
    for e in (experts - 2, experts - 1):
        wait(jnp.int32(e))
    for e in (experts - 2, experts - 1):
        second(jnp.int32(e))


def home_kernel(onehot, rows, *refs):
    keep, send = refs[-2:]
    send_home(keep, send, lax.axis_index("etp"), onehot, rows, keep.shape[2], keep.shape[3])


def home_values_kernel(choose, onehot, rows, dots, own_ref, info_ref, *refs):
    keep, send = refs[-2:]
    sources, slots, tokens = onehot.shape
    experts = slots // CAP
    width = keep.shape[3]
    send_home(keep, send, lax.axis_index("etp"), onehot, rows, tokens, width)
    expert = lax.broadcasted_iota(jnp.int32, (experts, tokens), 0)
    mine = (lax.axis_index("expert") * experts + expert).astype(F32)
    for s in range(sources):
        info = own_ref[tokens:tokens + EXTRA, :] if s == 0 else info_ref[s - 1, tokens:tokens + EXTRA, :]
        ids, _ = routing(info, choose, tokens)
        chosen = onehot[s].astype(F32).reshape(experts, CAP, tokens)
        share = jnp.sum(chosen * dots[:, s * CAP:(s + 1) * CAP, :], axis=1)
        values = [jnp.sum(jnp.where(ids[k:k + 1, :] == mine, share, 0.0), axis=0, keepdims=True) for k in range(choose)]
        values = jnp.concatenate(values + [jnp.zeros((EXTRA - choose, tokens), F32)], axis=0)
        values = jnp.concatenate([values, jnp.zeros((EXTRA, width - tokens), F32)], axis=1).astype(BF16)
        for home in (keep, send):
            home[0, s, tokens:tokens + EXTRA, :] = values
            home[1, s, tokens:tokens + EXTRA, :] = values


def backward_kernel(
    a0, a1, a2, a3, n0, n1, n2, n3,
    gate_ref, up_ref, down_hbm, act_ref, slope_ref, silu_ref, onehot, slot_gate, earlier_ref,
    back_rows, dots, rows_ref, p_ref, q_ref,
    down_ref, sems,
):
    sources, slots, tokens = onehot.shape
    experts = slots // CAP
    width = a0.shape[2]
    me = lax.axis_index("etp")
    start, wait = ring(down_hbm, down_ref, sems)
    for e in range(RING):
        start(jnp.int32(e))
    for s, (here, near) in enumerate(((a0, n0), (a1, n1), (a2, n2), (a3, n3))):
        for q in range(4):
            block = (near if q % 2 else here)[q // 2]
            picked = nn(onehot[s], block).astype(BF16).reshape(experts, CAP, width)
            rows_ref[:, s * CAP:(s + 1) * CAP, columns(me, q, width)] = picked

    def slopes(e):
        grad = nt(rows_ref[e], down_ref[lax.rem(e, RING)])
        activ = act_ref[e].astype(F32)
        dots[e] = jnp.broadcast_to(jnp.sum(activ * grad, axis=1, keepdims=True), dots.shape[1:])
        grad = grad * slot_gate[e][:, 0:1]
        p_ref[e] = (grad * slope_ref[e]).astype(BF16)
        q_ref[e] = (grad * silu_ref[e]).astype(BF16)

    def project(e):
        back = nn(p_ref[e], gate_ref[e]) + nn(q_ref[e], up_ref[e])
        back = (back * slot_gate[e][:, 0:1]).astype(BF16)
        at = pl.ds(pl.multiple_of(e * CAP, CAP), CAP)
        for s in range(sources):
            back_rows[s, at, :] = back[s * CAP:(s + 1) * CAP]

    def first(e):
        wait(e)
        slopes(e)
        start(e + RING)

    def both(e):
        wait(e)
        wait(e + 1)
        project(e - 2)
        project(e - 1)
        slopes(e)
        slopes(e + 1)
        start(e + RING)
        start(e + 1 + RING)

    skewed(experts, first, lambda e: None, project, both)


def add_kernel(keep, came, *refs):
    near, far = refs[-2:]
    for s in range(near.shape[0]):
        far[s] = (keep[1, s].astype(F32) + came[1, s].astype(F32)).astype(BF16)
        near[s] = (keep[0, s].astype(F32) + came[0, s].astype(F32)).astype(BF16)


def chips_kernel(near, came, *refs):
    parts = refs[-near.shape[0]:]
    for s in range(near.shape[0]):
        parts[s][...] = (near[s].astype(F32) + came[s].astype(F32)).astype(BF16)


def total_kernel(count, *refs):
    total = refs[0][...].astype(F32)
    for ref in refs[1:count]:
        total = total + ref[...].astype(F32)
    rows = refs[count]
    tokens = rows.shape[0]
    rows[...] = total[0:tokens].astype(BF16)
    for values in refs[count + 1:]:
        values[...] = total[tokens:tokens + values.shape[0], 0:values.shape[1]]


TURN = 4


def product_kernel(left_ref, right_ref, *refs):
    out_ref, held, sems = refs[-3:]
    turns = out_ref.shape[0] // TURN

    def store(turn, i):
        bank = lax.rem(turn, 2)
        return pltpu.make_async_copy(held.at[bank, i], out_ref.at[turn * TURN + i], sems.at[bank, i])

    def one(turn, _):
        @pl.when(turn >= 2)
        def _():
            for i in range(TURN):
                store(turn - 2, i).wait()

        bank = lax.rem(turn, 2)
        for i in range(TURN):
            held[bank, i] = tn(left_ref[turn * TURN + i], right_ref[turn * TURN + i]).astype(BF16)
            if i % 2:
                store(turn, i - 1).start()
                store(turn, i).start()
        return 0

    lax.fori_loop(0, turns, one, 0)
    for turn in (turns - 2, turns - 1):
        for i in range(TURN):
            store(jnp.int32(turn), i).wait()


def load_kernel(source, target, token, sems):
    token[...] = jnp.zeros_like(token)
    copies = [pltpu.make_async_copy(source.at[e], target.at[e], sems.at[e]) for e in range(source.shape[0])]
    for copy in copies:
        copy.start()
    for copy in copies:
        copy.wait()


def in_vmem(weight):
    return pl.pallas_call(
        load_kernel,
        in_specs=[pl.BlockSpec(memory_space=pltpu.HBM)],
        out_specs=[pl.BlockSpec(memory_space=pltpu.VMEM)] * 2,
        out_shape=[pltpu.VMEM(weight.shape, BF16), jax.ShapeDtypeStruct((8, 128), F32)],
        scratch_shapes=[pltpu.SemaphoreType.DMA((weight.shape[0],))],
        compiler_params=pltpu.CompilerParams(vmem_limit_bytes=4 * 1024 * 1024),
        cost_estimate=pl.CostEstimate(flops=0, bytes_accessed=2 * weight.size, transcendentals=0),
    )(pltpu.with_memory_space_constraint(weight, pltpu.HBM))


def join_kernel(count, *refs):
    for i in range(count):
        refs[-1][i] = refs[i][...]


def join(arrays, *there):
    return kernel_call(
        functools.partial(join_kernel, len(arrays)),
        [jax.ShapeDtypeStruct((len(arrays),) + arrays[0].shape, arrays[0].dtype)],
        [],
        0,
        limit=2,
    )(*arrays, *there)[0]


def kernel_call(kernel, out_shape, scratch, flops, out_specs=None, limit=4, in_hbm=()):
    def call(*operands):
        specs = [
            pl.BlockSpec(memory_space=pltpu.HBM if i in in_hbm else pltpu.SMEM if x.ndim == 1 else pltpu.VMEM)
            for i, x in enumerate(operands)
        ]
        operands = [
            pltpu.with_memory_space_constraint(x, pltpu.HBM) if i in in_hbm else x for i, x in enumerate(operands)
        ]
        return pl.pallas_call(
            kernel,
            in_specs=specs,
            out_specs=out_specs or [pl.BlockSpec(memory_space=pltpu.VMEM)] * len(out_shape),
            out_shape=out_shape,
            scratch_shapes=scratch,
            compiler_params=pltpu.CompilerParams(vmem_limit_bytes=limit * 1024 * 1024),
            cost_estimate=pl.CostEstimate(flops=flops, bytes_accessed=flops // 32, transcendentals=0),
        )(*operands)

    return call


def weight_grad(left, right, *earlier):
    experts, rows, units = left.shape
    model = right.shape[2]
    return kernel_call(
        product_kernel,
        jax.ShapeDtypeStruct((experts, units, model), BF16),
        [pltpu.VMEM((2, TURN, units, model), BF16), pltpu.SemaphoreType.DMA((2, TURN))],
        2 * experts * rows * units * model,
        out_specs=pl.BlockSpec(memory_space=pltpu.HBM),
        limit=8,
    )(left, right, *earlier)


def swap(array, bit, axis="etp"):
    count = lax.axis_size(axis)
    return lax.ppermute(array, axis, [(i, i ^ bit) for i in range(count)])


def add_cores(keep, send, *earlier):
    shape = jax.ShapeDtypeStruct(keep.shape[1:], BF16)
    hbm = range(2, 2 + len(earlier))
    return kernel_call(add_kernel, [shape, shape], [], 0, limit=2, in_hbm=hbm)(keep, swap(send, 1), *earlier)


def add_chips(near, far, *earlier):
    sources = near.shape[0]
    shape = jax.ShapeDtypeStruct(near.shape[1:], BF16)
    hbm = range(2, 2 + len(earlier))
    parts = kernel_call(chips_kernel, [shape] * sources, [], 0, limit=2, in_hbm=hbm)(near, far, *earlier)
    return parts[0], [swap(parts[s], s, "expert") for s in range(1, sources)]


def gathered_body(
    hidden_in, out_grad, expert_ids, gate_values, capacity_blocks, gate_weight, up_weight, down_weight
):
    sources = lax.axis_size("expert")
    tokens, width = hidden_in.shape
    choose = expert_ids.shape[1]
    local_experts, units, model = down_weight.shape
    slots = local_experts * CAP
    rows = sources * CAP
    gate_t, gate_there = in_vmem(jnp.swapaxes(gate_weight, 1, 2))
    up_t, up_there = in_vmem(jnp.swapaxes(up_weight, 1, 2))
    product = 2 * local_experts * rows * units * model
    held = lambda *shape, kind=BF16: pltpu.VMEM(shape, kind)
    sent = lambda *shape: jax.ShapeDtypeStruct(shape, BF16)

    own = kernel_call(
        pack_kernel,
        [sent(tokens + EXTRA, width)],
        [pltpu.VMEM((choose, tokens), jnp.int32), pltpu.VMEM((choose, tokens), F32), pltpu.SemaphoreType.DMA((3,))],
        0,
        limit=2,
        in_hbm=(0, 1, 2),
    )(hidden_in, expert_ids.T, gate_values.T)[0]
    came = [swap(own, s, "expert") for s in range(1, sources)]
    own_across = swap(own, 2)
    grad_across = swap(out_grad, 2)
    came = join(came, gate_there, own_across, grad_across)
    came_across = join([swap(came, 2)], up_there)[0]
    grads = join([out_grad, grad_across], came)
    grads = [grads] + [swap(grads, s, "expert") for s in range(1, sources)]

    out_rows, x_rows, activ, scaled, slope, silu, onehot, slot_gate = kernel_call(
        functools.partial(forward_kernel, choose),
        [
            held(sources, slots, model),
            held(local_experts, rows, model),
            held(local_experts, rows, units),
            held(local_experts, rows, units),
            held(local_experts, rows, units, kind=F32),
            held(local_experts, rows, units, kind=F32),
            held(sources, slots, tokens),
            held(local_experts, rows, tokens, kind=F32),
        ],
        [pltpu.VMEM((RING, units, model), BF16), pltpu.SemaphoreType.DMA((RING,))],
        3 * product,
        limit=6,
        in_hbm=(11,),
    )(
        capacity_blocks,
        own, swap(own, 1), own_across, swap(own_across, 1),
        came, swap(came, 1), came_across, swap(came_across, 1),
        gate_t, up_t, down_weight, grads[0],
    )

    keep, send = kernel_call(
        home_kernel, [sent(2, sources, tokens, width)] * 2, [], 2 * slots * sources * tokens * model, limit=2,
    )(onehot, out_rows, *grads)
    out_near, out_far = add_cores(keep, send)
    back_rows, dots, y_rows, gate_part, up_part = kernel_call(
        backward_kernel,
        [
            held(sources, slots, model),
            held(local_experts, rows, tokens, kind=F32),
            held(local_experts, rows, model),
            held(local_experts, rows, units),
            held(local_experts, rows, units),
        ],
        [pltpu.VMEM((RING, units, model), BF16), pltpu.SemaphoreType.DMA((RING,))],
        3 * product,
        limit=6,
        in_hbm=(10,),
    )(
        *grads, *[swap(x, 1) for x in grads],
        gate_t, up_t, down_weight, activ, slope, silu, onehot, slot_gate, out_near,
    )

    out_own, out_parts = add_chips(out_near, swap(out_far, 2))
    keep, send = kernel_call(
        functools.partial(home_values_kernel, choose),
        [sent(2, sources, tokens + EXTRA, width)] * 2,
        [],
        2 * slots * sources * tokens * model,
        limit=2,
    )(onehot, back_rows, dots, own, came, out_own)
    down_grad = weight_grad(scaled, y_rows, out_own)
    back_near, back_far = add_cores(keep, send, down_grad)
    up_grad = weight_grad(up_part, x_rows, back_near)
    layer_out = kernel_call(
        functools.partial(total_kernel, sources), [sent(tokens, width)], [], 0, limit=2
    )(out_own, *out_parts)[0]
    back_own, back_parts = add_chips(back_near, swap(back_far, 2), up_grad)
    gate_grad = weight_grad(gate_part, x_rows, back_own)
    input_grad, value_grad = kernel_call(
        functools.partial(total_kernel, sources),
        [sent(tokens, width), jax.ShapeDtypeStruct((choose, tokens), F32)],
        [],
        0,
        limit=2,
    )(back_own, *back_parts)
    return (
        layer_out,
        input_grad,
        value_grad.T,
        jnp.swapaxes(gate_grad, 1, 2),
        jnp.swapaxes(up_grad, 1, 2),
        down_grad,
    )


def slot_layout(expert_ids, capacity_blocks):
    tokens_here, choose = expert_ids.shape
    experts = capacity_blocks.shape[0]
    flat_ids = expert_ids.reshape(-1)
    onehot = (flat_ids[:, None] == jnp.arange(experts, dtype=jnp.int32)[None, :]).astype(jnp.int32)
    before = jnp.cumsum(onehot, axis=0) - onehot
    ranks = jnp.sum(before * onehot, axis=1)
    limits = jnp.sum(onehot * capacity_blocks[None, :], axis=1) * BLK
    kept = ranks < limits
    slots = jnp.where(kept, flat_ids * CAP + ranks, experts * CAP)
    token_index = jnp.arange(tokens_here * choose, dtype=jnp.int32) // choose
    owners = (
        jnp.full((experts * CAP,), tokens_here, jnp.int32).at[slots].set(token_index, mode="drop")
    )
    return (kept.reshape(tokens_here, choose), slots.reshape(tokens_here, choose), owners)


def outgoing(rows, owners, experts, scale):
    padded = jnp.concatenate([rows, jnp.zeros((1, rows.shape[1]), rows.dtype)], 0)
    picked = padded[owners]
    if scale is not None:
        picked = (scale[:, None] * picked.astype(jnp.float32)).astype(jnp.bfloat16)
    return picked.reshape(experts, CAP, rows.shape[1])


def local_grads(hidden_gate, hidden_up, act_grad):
    sigma = jax.nn.sigmoid(hidden_gate)
    gate_part = (act_grad * hidden_up * sigma * (1.0 + hidden_gate * (1.0 - sigma))).astype(
        jnp.bfloat16
    )
    up_part = (act_grad * jax.nn.silu(hidden_gate)).astype(jnp.bfloat16)
    return (gate_part, up_part)


def combine(back, slots, weights):
    padded = jnp.concatenate([back, jnp.zeros((1, back.shape[1]), back.dtype)], 0)
    picked = padded[slots].astype(jnp.float32)
    return (jnp.einsum("tk,tkw->tw", weights, picked), picked)


def dispatched_body(
    hidden_in,
    out_grad,
    expert_ids,
    gate_values,
    capacity_blocks,
    gate_weight,
    up_weight,
    down_weight,
):
    experts = capacity_blocks.shape[0]
    sources = lax.axis_size("expert")
    local_experts = gate_weight.shape[0]
    kept, slots, owners = slot_layout(expert_ids, capacity_blocks)
    weights = jnp.where(kept, gate_values, 0.0)
    slot_gates = (
        jnp.zeros((experts * CAP,), jnp.float32)
        .at[slots.reshape(-1)]
        .set(weights.reshape(-1), mode="drop")
    )
    send_in = outgoing(hidden_in, owners, experts, None)
    send_grad = outgoing(out_grad, owners, experts, slot_gates)
    recv_in, recv_grad = (
        lax.all_to_all(send_in, "expert", split_axis=0, concat_axis=0, tiled=True),
        lax.all_to_all(send_grad, "expert", split_axis=0, concat_axis=0, tiled=True),
    )
    share = recv_in.shape[2]
    share_in = recv_in.reshape(sources, local_experts, CAP, share)
    share_grad = recv_grad.reshape(sources, local_experts, CAP, share)
    piece = lax.all_gather(share_in, "etp", axis=3, tiled=True)
    hidden_gate = jnp.einsum(
        "secn,enf->secf", piece, gate_weight, preferred_element_type=jnp.float32
    )
    hidden_up = jnp.einsum("secn,enf->secf", piece, up_weight, preferred_element_type=jnp.float32)
    activ = (jax.nn.silu(hidden_gate) * hidden_up).astype(jnp.bfloat16)
    piece = lax.all_gather(share_grad, "etp", axis=3, tiled=True)
    act_grad = jnp.einsum("secn,efn->secf", piece, down_weight, preferred_element_type=jnp.float32)
    columns = jnp.einsum("secf,secn->efn", activ, piece, preferred_element_type=jnp.float32)
    act_grad, down_grad = (act_grad, columns)
    gate_part, up_part = local_grads(hidden_gate, hidden_up, act_grad)
    stacked = jnp.stack([gate_part, up_part])
    weight_grads = jnp.einsum(
        "secn,gsecf->genf",
        lax.all_gather(share_in, "etp", axis=3, tiled=True),
        stacked,
        preferred_element_type=jnp.float32,
    )
    out_part = jnp.einsum("secf,efd->secd", activ, down_weight, preferred_element_type=jnp.float32)
    back_part = jnp.einsum(
        "secf,edf->secd", gate_part, gate_weight, preferred_element_type=jnp.float32
    )
    back_part = back_part + jnp.einsum(
        "secf,edf->secd", up_part, up_weight, preferred_element_type=jnp.float32
    )
    out_rows = lax.psum_scatter(
        out_part.astype(jnp.bfloat16), "etp", scatter_dimension=3, tiled=True
    )
    home_out = lax.all_to_all(out_rows, "expert", split_axis=0, concat_axis=0, tiled=True)
    share_width = home_out.shape[3]
    layer_sum, picked = combine(home_out.reshape(experts * CAP, share_width), slots, weights)
    dot_part = jnp.einsum("tw,tkw->tk", out_grad.astype(jnp.float32), picked) * kept.astype(
        jnp.float32
    )
    gate_value_grad = lax.psum(dot_part, "etp")
    back_rows = lax.psum_scatter(
        back_part.astype(jnp.bfloat16), "etp", scatter_dimension=3, tiled=True
    )
    home_back = lax.all_to_all(back_rows, "expert", split_axis=0, concat_axis=0, tiled=True)
    input_sum, returned = combine(home_back.reshape(experts * CAP, share_width), slots, weights)
    return (
        layer_sum.astype(jnp.bfloat16),
        input_sum.astype(jnp.bfloat16),
        gate_value_grad,
        weight_grads[0].astype(jnp.bfloat16),
        weight_grads[1].astype(jnp.bfloat16),
        down_grad.astype(jnp.bfloat16),
    )


def body(*operands):
    hidden_in, gate_weight = operands[0], operands[5]
    if lax.axis_size("etp") == 4 and hidden_in.shape[0] <= gate_weight.shape[0] * CAP:
        return gathered_body(*operands)
    return dispatched_body(*operands)


def solution(mesh):
    in_specs = (
        P(("groups", "expert"), "etp"),
        P(("groups", "expert"), "etp"),
        P(("groups", "expert"), None),
        P(("groups", "expert"), None),
        P("groups"),
        P("expert", None, "etp"),
        P("expert", None, "etp"),
        P("expert", "etp", None),
    )
    out_specs = (
        P(("groups", "expert"), "etp"),
        P(("groups", "expert"), "etp"),
        P(("groups", "expert"), None),
        P(("groups", "expert"), None, "etp"),
        P(("groups", "expert"), None, "etp"),
        P(("groups", "expert"), "etp", None),
    )
    return jax.shard_map(body, mesh=mesh, in_specs=in_specs, out_specs=out_specs, check_vma=False)
```

```python
import functools

import jax
import jax.numpy as jnp
from jax import lax
from jax.experimental import pallas as pl
from jax.experimental.pallas import tpu as pltpu
from jax.sharding import PartitionSpec as P

CAP = 16
BLK = 4
EXTRA = 16
F32 = jnp.float32
BF16 = jnp.bfloat16


def nn(a, b):
    return lax.dot_general(a, b, (((1,), (0,)), ((), ())), preferred_element_type=F32)


def nt(a, b):
    return lax.dot_general(a, b, (((1,), (1,)), ((), ())), preferred_element_type=F32)


def tn(a, b):
    return lax.dot_general(a, b, (((0,), (0,)), ((), ())), preferred_element_type=F32)


def pack_kernel(hidden_hbm, ids_hbm, gates_hbm, own_ref, ids_ref, gates_ref, sems):
    tokens, width = hidden_hbm.shape
    choose = ids_ref.shape[0]
    copies = [
        pltpu.make_async_copy(hidden_hbm, own_ref.at[pl.ds(0, tokens)], sems.at[0]),
        pltpu.make_async_copy(ids_hbm, ids_ref, sems.at[1]),
        pltpu.make_async_copy(gates_hbm, gates_ref, sems.at[2]),
    ]
    for copy in copies:
        copy.start()
    for copy in copies:
        copy.wait()
    gates = gates_ref[...]
    high = gates.astype(BF16).astype(F32)
    fill = jnp.zeros((8 - choose, tokens), F32)
    top = jnp.concatenate([jnp.concatenate([ids_ref[...].astype(F32), fill], axis=0), jnp.concatenate([high, fill], axis=0)], axis=1)
    low = jnp.concatenate([jnp.concatenate([gates - high, fill], axis=0), jnp.zeros((8, width - tokens), F32)], axis=1)
    own_ref[tokens:tokens + EXTRA, :] = jnp.concatenate([top, low], axis=0).astype(BF16)


def routing(info, choose, tokens):
    info = info.astype(F32)
    return info[0:choose, 0:tokens], info[0:choose, tokens:2 * tokens] + info[8:8 + choose, 0:tokens]


def columns(me, mask, width):
    return pl.ds(pl.multiple_of(lax.bitwise_xor(me, mask) * width, width), width)


def send_home(home_keep, home_send, me, onehot, rows, tokens, width):
    for s in range(onehot.shape[0]):
        for q in range(4):
            home = home_send if q % 2 else home_keep
            home[q // 2, s, 0:tokens, :] = tn(onehot[s], rows[s, :, columns(me, q, width)]).astype(BF16)


RING = 4


def ring(weight, slots, sems, columns=None):
    def load(e):
        slot = lax.rem(e, RING)
        source = weight.at[e] if columns is None else weight.at[e, :, columns]
        return pltpu.make_async_copy(source, slots.at[slot], sems.at[slot])

    def start(e):
        @pl.when(e < weight.shape[0])
        def _():
            load(e).start()

    for e in range(RING):
        load(jnp.int32(e)).start()
    return start, lambda e: load(e).wait()


def half(me, other, size):
    return pl.ds(pl.multiple_of(lax.bitwise_xor(me // 2, other) * size, size), size)


def gather_half(me, onehot, blocks, rows_ref, experts, width, tokens, start):
    for q, block in enumerate(blocks):
        picked = nn(onehot, block).astype(BF16).reshape(experts, CAP, width)
        at = pl.multiple_of(lax.rem(lax.bitwise_xor(me, q), 2) * width, width)
        rows_ref[:, start:start + CAP, pl.ds(at, width)] = picked


def early_kernel(
    choose, capacity_ref, o0, o1, b0, b1, gate_ref, up_hbm,
    rows_ref, part_ref, onehot, slot_gate,
    up_ref, sems,
):
    sources, slots, tokens = onehot.shape
    experts = slots // CAP
    width = b0.shape[2]
    me = lax.axis_index("etp")
    first = lax.axis_index("expert") * experts

    here = half(me, 0, 2 * width)
    start, wait = ring(up_hbm, up_ref, sems, here)
    row = lax.broadcasted_iota(jnp.int32, (tokens, tokens), 0)
    col = lax.broadcasted_iota(jnp.int32, (tokens, tokens), 1)
    before = jnp.where(row < col, 1.0, 0.0).astype(BF16)
    expert = lax.broadcasted_iota(jnp.int32, (experts, tokens), 0)
    mine = (first + expert).astype(F32)
    limit = jnp.zeros((experts, tokens), jnp.int32)
    for e in range(experts):
        limit = jnp.where(expert == e, capacity_ref[first + e] * BLK, limit)
    limit = limit.astype(F32)
    place = lax.broadcasted_iota(jnp.int32, (experts, CAP, tokens), 1).astype(F32)
    for s in range(sources):
        block = [o[...] for o in (o0, o1)] if s == 0 else [b[s - 1] for b in (b0, b1)]
        ids, gates = routing(block[0][tokens:tokens + EXTRA, :], choose, tokens)
        named = jnp.zeros((experts, tokens), F32)
        gate = jnp.zeros((experts, tokens), F32)
        for k in range(choose):
            hit = ids[k:k + 1, :] == mine
            named = named + jnp.where(hit, 1.0, 0.0)
            gate = gate + jnp.where(hit, gates[k:k + 1, :], 0.0)
        rank = nn(named.astype(BF16), before)
        rank = jnp.where((named > 0.5) & (rank < limit), rank, -1.0)
        chosen = jnp.where(rank[:, None, :] == place, 1.0, 0.0)
        gate_of = jnp.sum(chosen * gate[:, None, :], axis=2, keepdims=True)
        slot_gate[:, s * CAP:(s + 1) * CAP, :] = jnp.broadcast_to(gate_of, chosen.shape)
        table = chosen.reshape(slots, tokens).astype(BF16)
        onehot[s] = table
        gather_half(me, table, [x[0:tokens, :] for x in block], rows_ref, experts, width, tokens, s * CAP)

    def some(turn, _):
        for e in (turn * 2, turn * 2 + 1):
            wait(e)
        for e in (turn * 2, turn * 2 + 1):
            part_ref[0, e] = nt(rows_ref[e], gate_ref[e, :, here])
            part_ref[1, e] = nt(rows_ref[e], up_ref[lax.rem(e, RING)])
        for e in (turn * 2, turn * 2 + 1):
            start(e + RING)
        return 0

    lax.fori_loop(0, experts // 2, some, 0)


def forward_kernel(
    o2, o3, b2, b3, gate_ref, up_hbm, down_hbm, half_ref, part_ref, onehot, slot_gate, later_ref,
    out_rows, rows_ref, act_ref, a_ref, slope_ref, silu_ref,
    there_ref, up_ref, down_ref, up_sems, down_sems,
):
    sources, slots, tokens = onehot.shape
    experts = slots // CAP
    width = b2.shape[2]
    me = lax.axis_index("etp")
    here, there = half(me, 0, 2 * width), half(me, 1, 2 * width)
    start_up, wait_up = ring(up_hbm, up_ref, up_sems, there)
    start_down, wait_down = ring(down_hbm, down_ref, down_sems)
    for s in range(sources):
        block = [o[0:tokens, :] for o in (o2, o3)] if s == 0 else [b[s - 1, 0:tokens, :] for b in (b2, b3)]
        gather_half(me, onehot[s], block, there_ref, experts, width, tokens, s * CAP)

    def activate(e):
        rows_ref[e, :, here] = half_ref[e]
        x = there_ref[e]
        rows_ref[e, :, there] = x
        hidden_gate = part_ref[0, e] + nt(x, gate_ref[e, :, there])
        hidden_up = part_ref[1, e] + nt(x, up_ref[lax.rem(e, RING)])
        sigma = jax.nn.sigmoid(hidden_gate)
        silu = hidden_gate * sigma
        activ = (silu * hidden_up).astype(BF16)
        act_ref[e] = activ
        slope_ref[e] = hidden_up * sigma * (1.0 + hidden_gate * (1.0 - sigma))
        silu_ref[e] = silu
        a_ref[e] = (activ.astype(F32) * slot_gate[e][:, 0:1]).astype(BF16)

    def project(e):
        out = nn(a_ref[e], down_ref[lax.rem(e, RING)]).astype(BF16)
        at = pl.ds(pl.multiple_of(e * CAP, CAP), CAP)
        for s in range(sources):
            out_rows[s, at, :] = out[s * CAP:(s + 1) * CAP]

    def first(e):
        wait_up(e)
        activate(e)
        start_up(e + RING)

    def both(e):
        for i in (e - 2, e - 1):
            wait_down(i)
        for i in (e, e + 1):
            wait_up(i)
        project(e - 2)
        project(e - 1)
        activate(e)
        activate(e + 1)
        for i in (e - 2, e - 1):
            start_down(i + RING)
        for i in (e, e + 1):
            start_up(i + RING)

    skewed(experts, first, wait_down, project, both)


def skewed(experts, first, wait, second, both):
    first(jnp.int32(0))
    first(jnp.int32(1))

    def turn(i, _):
        both(i * 2)
        return 0

    lax.fori_loop(1, experts // 2, turn, 0)
    for e in (experts - 2, experts - 1):
        wait(jnp.int32(e))
    for e in (experts - 2, experts - 1):
        second(jnp.int32(e))


def home_kernel(onehot, rows, *refs):
    grads, (keep, send) = refs[:-2], refs[-2:]
    send_home(keep, send, lax.axis_index("etp"), onehot, rows, keep.shape[2], keep.shape[3])
    for s, grad in enumerate(grads):
        for q in range(2):
            send[2 + q, s] = grad[q]


def home_values_kernel(choose, onehot, rows, dots, own_ref, info_ref, *refs):
    keep, send = refs[-2:]
    sources, slots, tokens = onehot.shape
    experts = slots // CAP
    width = keep.shape[3]
    send_home(keep, send, lax.axis_index("etp"), onehot, rows, tokens, width)
    expert = lax.broadcasted_iota(jnp.int32, (experts, tokens), 0)
    mine = (lax.axis_index("expert") * experts + expert).astype(F32)
    for s in range(sources):
        info = own_ref[tokens:tokens + EXTRA, :] if s == 0 else info_ref[s - 1, tokens:tokens + EXTRA, :]
        ids, _ = routing(info, choose, tokens)
        chosen = onehot[s].astype(F32).reshape(experts, CAP, tokens)
        share = jnp.sum(chosen * dots[:, s * CAP:(s + 1) * CAP, :], axis=1)
        values = [jnp.sum(jnp.where(ids[k:k + 1, :] == mine, share, 0.0), axis=0, keepdims=True) for k in range(choose)]
        values = jnp.concatenate(values + [jnp.zeros((EXTRA - choose, tokens), F32)], axis=0)
        values = jnp.concatenate([values, jnp.zeros((EXTRA, width - tokens), F32)], axis=1).astype(BF16)
        for home in (keep, send):
            home[0, s, tokens:tokens + EXTRA, :] = values
            home[1, s, tokens:tokens + EXTRA, :] = values


def backward_kernel(
    a0, a1, a2, a3, near_ref,
    gate_ref, up_hbm, down_hbm, act_ref, slope_ref, silu_ref, onehot, slot_gate, earlier_ref,
    back_rows, dots, rows_ref, p_ref, q_ref,
    up_ref, down_ref, up_sems, down_sems,
):
    sources, slots, tokens = onehot.shape
    experts = slots // CAP
    width = a0.shape[2]
    me = lax.axis_index("etp")
    start_down, wait_down = ring(down_hbm, down_ref, down_sems)
    start_up, wait_up = ring(up_hbm, up_ref, up_sems)
    for s, here in enumerate((a0, a1, a2, a3)):
        for q in range(4):
            block = near_ref[2 + q // 2, s] if q % 2 else here[q // 2]
            picked = nn(onehot[s], block).astype(BF16).reshape(experts, CAP, width)
            rows_ref[:, s * CAP:(s + 1) * CAP, columns(me, q, width)] = picked

    def slopes(e):
        grad = nt(rows_ref[e], down_ref[lax.rem(e, RING)])
        activ = act_ref[e].astype(F32)
        dots[e] = jnp.broadcast_to(jnp.sum(activ * grad, axis=1, keepdims=True), dots.shape[1:])
        grad = grad * slot_gate[e][:, 0:1]
        p_ref[e] = (grad * slope_ref[e]).astype(BF16)
        q_ref[e] = (grad * silu_ref[e]).astype(BF16)

    def project(e):
        back = nn(p_ref[e], gate_ref[e]) + nn(q_ref[e], up_ref[lax.rem(e, RING)])
        back = (back * slot_gate[e][:, 0:1]).astype(BF16)
        at = pl.ds(pl.multiple_of(e * CAP, CAP), CAP)
        for s in range(sources):
            back_rows[s, at, :] = back[s * CAP:(s + 1) * CAP]

    def first(e):
        wait_down(e)
        slopes(e)
        start_down(e + RING)

    def both(e):
        for i in (e, e + 1):
            wait_down(i)
        for i in (e - 2, e - 1):
            wait_up(i)
        project(e - 2)
        project(e - 1)
        slopes(e)
        slopes(e + 1)
        for i in (e, e + 1):
            start_down(i + RING)
        for i in (e - 2, e - 1):
            start_up(i + RING)

    skewed(experts, first, wait_up, project, both)


def add_kernel(keep, came, *refs):
    near, far = refs[-2:]
    for s in range(near.shape[0]):
        far[s] = (keep[1, s].astype(F32) + came[1, s].astype(F32)).astype(BF16)
        near[s] = (keep[0, s].astype(F32) + came[0, s].astype(F32)).astype(BF16)


def chips_kernel(near, came, *refs):
    parts = refs[-near.shape[0]:]
    for s in range(near.shape[0]):
        parts[s][...] = (near[s].astype(F32) + came[s].astype(F32)).astype(BF16)


def pairs_kernel(near, came, *refs):
    lower, upper = refs[-2:]
    count = lower.shape[0]
    for s in range(count):
        lower[s] = (near[s].astype(F32) + came[s].astype(F32)).astype(BF16)
        upper[s] = (near[count + s].astype(F32) + came[count + s].astype(F32)).astype(BF16)


def step_kernel(lower, came, *refs):
    own, other = refs[-2:]
    own[...] = (lower[0].astype(F32) + came[0].astype(F32)).astype(BF16)
    other[...] = (lower[1].astype(F32) + came[1].astype(F32)).astype(BF16)


def total_kernel(count, *refs):
    total = refs[0][...].astype(F32)
    for ref in refs[1:count]:
        total = total + ref[...].astype(F32)
    rows = refs[count]
    tokens = rows.shape[0]
    rows[...] = total[0:tokens].astype(BF16)
    for values in refs[count + 1:]:
        values[...] = total[tokens:tokens + values.shape[0], 0:values.shape[1]]


TURN = 4


def product_kernel(left_ref, right_ref, *refs):
    out_ref, held, sems = refs[-3:]
    turns = out_ref.shape[0] // TURN

    def store(turn, i):
        bank = lax.rem(turn, 2)
        return pltpu.make_async_copy(held.at[bank, i], out_ref.at[turn * TURN + i], sems.at[bank, i])

    def one(turn, _):
        @pl.when(turn >= 2)
        def _():
            for i in range(TURN):
                store(turn - 2, i).wait()

        bank = lax.rem(turn, 2)
        for i in range(TURN):
            held[bank, i] = tn(left_ref[turn * TURN + i], right_ref[turn * TURN + i]).astype(BF16)
        for i in range(TURN):
            store(turn, i).start()
        return 0

    lax.fori_loop(0, turns, one, 0)
    for turn in (turns - 2, turns - 1):
        for i in range(TURN):
            store(jnp.int32(turn), i).wait()


def load_kernel(source, target, token, sems):
    token[...] = jnp.zeros_like(token)
    copies = [pltpu.make_async_copy(source.at[e], target.at[e], sems.at[e]) for e in range(source.shape[0])]
    for copy in copies:
        copy.start()
    for copy in copies:
        copy.wait()


def in_vmem(weight):
    return pl.pallas_call(
        load_kernel,
        in_specs=[pl.BlockSpec(memory_space=pltpu.HBM)],
        out_specs=[pl.BlockSpec(memory_space=pltpu.VMEM)] * 2,
        out_shape=[pltpu.VMEM(weight.shape, BF16), jax.ShapeDtypeStruct((8, 128), F32)],
        scratch_shapes=[pltpu.SemaphoreType.DMA((weight.shape[0],))],
        compiler_params=pltpu.CompilerParams(vmem_limit_bytes=4 * 1024 * 1024),
        cost_estimate=pl.CostEstimate(flops=0, bytes_accessed=2 * weight.size, transcendentals=0),
    )(pltpu.with_memory_space_constraint(weight, pltpu.HBM))


def join_kernel(count, *refs):
    for i in range(count):
        refs[-1][i] = refs[i][...]


def join(arrays, *there):
    return kernel_call(
        functools.partial(join_kernel, len(arrays)),
        [jax.ShapeDtypeStruct((len(arrays),) + arrays[0].shape, arrays[0].dtype)],
        [],
        0,
        limit=2,
    )(*arrays, *there)[0]


def kernel_call(kernel, out_shape, scratch, flops, out_specs=None, limit=4, in_hbm=()):
    def call(*operands):
        specs = [
            pl.BlockSpec(memory_space=pltpu.HBM if i in in_hbm else pltpu.SMEM if x.ndim == 1 else pltpu.VMEM)
            for i, x in enumerate(operands)
        ]
        operands = [
            pltpu.with_memory_space_constraint(x, pltpu.HBM) if i in in_hbm else x for i, x in enumerate(operands)
        ]
        return pl.pallas_call(
            kernel,
            in_specs=specs,
            out_specs=out_specs or [pl.BlockSpec(memory_space=pltpu.VMEM)] * len(out_shape),
            out_shape=out_shape,
            scratch_shapes=scratch,
            compiler_params=pltpu.CompilerParams(vmem_limit_bytes=limit * 1024 * 1024),
            cost_estimate=pl.CostEstimate(flops=flops, bytes_accessed=flops // 32, transcendentals=0),
        )(*operands)

    return call


def weight_grad(left, right, *earlier):
    experts, rows, units = left.shape
    model = right.shape[2]
    return kernel_call(
        product_kernel,
        jax.ShapeDtypeStruct((experts, units, model), BF16),
        [pltpu.VMEM((2, TURN, units, model), BF16), pltpu.SemaphoreType.DMA((2, TURN))],
        2 * experts * rows * units * model,
        out_specs=pl.BlockSpec(memory_space=pltpu.HBM),
        limit=8,
    )(left, right, *earlier)


def swap(array, bit, axis="etp"):
    count = lax.axis_size(axis)
    return lax.ppermute(array, axis, [(i, i ^ bit) for i in range(count)])


def add_cores(keep, came, *earlier):
    shape = jax.ShapeDtypeStruct(keep.shape[1:], BF16)
    hbm = [2] if earlier else []
    return kernel_call(add_kernel, [shape, shape], [], 0, limit=2, in_hbm=hbm)(keep, came, *earlier)


def add_chips(near, far, *earlier):
    sources = near.shape[0]
    shape = jax.ShapeDtypeStruct(near.shape[1:], BF16)
    hbm = range(2, 2 + len(earlier))
    parts = kernel_call(chips_kernel, [shape] * sources, [], 0, limit=2, in_hbm=hbm)(near, far, *earlier)
    return parts[0], [swap(parts[s], s, "expert") for s in range(1, sources)]


def gathered_body(
    hidden_in, out_grad, expert_ids, gate_values, capacity_blocks, gate_weight, up_weight, down_weight
):
    sources = lax.axis_size("expert")
    tokens, width = hidden_in.shape
    choose = expert_ids.shape[1]
    local_experts, units, model = down_weight.shape
    slots = local_experts * CAP
    rows = sources * CAP
    gate_t, gate_there = in_vmem(jnp.swapaxes(gate_weight, 1, 2))
    up_t = jnp.swapaxes(up_weight, 1, 2)
    product = 2 * local_experts * rows * units * model
    held = lambda *shape, kind=BF16: pltpu.VMEM(shape, kind)
    sent = lambda *shape: jax.ShapeDtypeStruct(shape, BF16)

    own = kernel_call(
        pack_kernel,
        [sent(tokens + EXTRA, width)],
        [pltpu.VMEM((choose, tokens), jnp.int32), pltpu.VMEM((choose, tokens), F32), pltpu.SemaphoreType.DMA((3,))],
        0,
        limit=2,
        in_hbm=(0, 1, 2),
    )(hidden_in, expert_ids.T, gate_values.T)[0]
    came = [swap(own, s, "expert") for s in range(1, sources)]
    own_across = swap(own, 2)
    grad_across = swap(out_grad, 2)
    came = join(came, gate_there, own_across, grad_across)
    came_across_there = swap(came, 2)
    grads = join([out_grad, grad_across], came)
    grads = [grads] + [swap(grads, s, "expert") for s in range(1, sources)]

    half_rows, partial, onehot, slot_gate = kernel_call(
        functools.partial(early_kernel, choose),
        [
            held(local_experts, rows, model // 2),
            held(2, local_experts, rows, units, kind=F32),
            held(sources, slots, tokens),
            held(local_experts, rows, tokens, kind=F32),
        ],
        [pltpu.VMEM((RING, units, model // 2), BF16), pltpu.SemaphoreType.DMA((RING,))],
        product,
        in_hbm=(6,),
    )(capacity_blocks, own, swap(own, 1), came, swap(came, 1), gate_t, up_t)
    came_across = join([came_across_there], onehot)[0]
    out_rows, x_rows, activ, scaled, slope, silu = kernel_call(
        forward_kernel,
        [
            held(sources, slots, model),
            held(local_experts, rows, model),
            held(local_experts, rows, units),
            held(local_experts, rows, units),
            held(local_experts, rows, units, kind=F32),
            held(local_experts, rows, units, kind=F32),
        ],
        [
            pltpu.VMEM((local_experts, rows, model // 2), BF16),
            pltpu.VMEM((RING, units, model // 2), BF16),
            pltpu.VMEM((RING, units, model), BF16),
            pltpu.SemaphoreType.DMA((RING,)),
            pltpu.SemaphoreType.DMA((RING,)),
        ],
        2 * product,
        limit=9,
        in_hbm=(5, 6),
    )(
        own_across, swap(own_across, 1), came_across, swap(came_across, 1),
        gate_t, up_t, down_weight, half_rows, partial, onehot, slot_gate, grads[0],
    )

    keep, send = kernel_call(
        home_kernel,
        [sent(2, sources, tokens, width), sent(4, sources, tokens, width)],
        [],
        2 * slots * sources * tokens * model,
        limit=2,
    )(onehot, out_rows, *grads)
    near = swap(send, 1)
    out_near, out_far = add_cores(keep, near)
    back_rows, dots, y_rows, gate_part, up_part = kernel_call(
        backward_kernel,
        [
            held(sources, slots, model),
            held(local_experts, rows, tokens, kind=F32),
            held(local_experts, rows, model),
            held(local_experts, rows, units),
            held(local_experts, rows, units),
        ],
        [pltpu.VMEM((RING, units, model), BF16)] * 2 + [pltpu.SemaphoreType.DMA((RING,))] * 2,
        3 * product,
        limit=9,
        in_hbm=(6, 7),
    )(
        *grads, near,
        gate_t, up_t, down_weight, activ, slope, silu, onehot, slot_gate, out_near,
    )

    part = sent(tokens, width)
    pair = sent(2, tokens, width)
    out_lower, out_upper = kernel_call(pairs_kernel, [pair, pair], [], 0, limit=2)(out_near, swap(out_far, 2))
    keep, send = kernel_call(
        functools.partial(home_values_kernel, choose),
        [sent(2, sources, tokens + EXTRA, width)] * 2,
        [],
        2 * slots * sources * tokens * model,
        limit=2,
    )(onehot, back_rows, dots, own, came, out_lower)
    out_came = swap(out_upper, 2, "expert")
    down_grad = weight_grad(scaled, y_rows, out_lower)
    back_near, back_far = add_cores(keep, swap(send, 1), down_grad, out_came)
    out_own, out_other = kernel_call(step_kernel, [part, part], [], 0, limit=2)(out_lower, out_came, back_near)
    up_grad = weight_grad(up_part, x_rows, back_near, out_own)
    back_own, back_parts = add_chips(back_near, swap(back_far, 2), up_grad)
    layer_out = kernel_call(functools.partial(total_kernel, 2), [part], [], 0, limit=2)(
        out_own, swap(out_other, 1, "expert")
    )[0]
    gate_grad = weight_grad(gate_part, x_rows, back_own)
    input_grad, value_grad = kernel_call(
        functools.partial(total_kernel, sources),
        [part, jax.ShapeDtypeStruct((choose, tokens), F32)],
        [],
        0,
        limit=2,
    )(back_own, *back_parts)
    return (
        layer_out,
        input_grad,
        value_grad.T,
        jnp.swapaxes(gate_grad, 1, 2),
        jnp.swapaxes(up_grad, 1, 2),
        down_grad,
    )


def slot_layout(expert_ids, capacity_blocks):
    tokens_here, choose = expert_ids.shape
    experts = capacity_blocks.shape[0]
    flat_ids = expert_ids.reshape(-1)
    onehot = (flat_ids[:, None] == jnp.arange(experts, dtype=jnp.int32)[None, :]).astype(jnp.int32)
    before = jnp.cumsum(onehot, axis=0) - onehot
    ranks = jnp.sum(before * onehot, axis=1)
    limits = jnp.sum(onehot * capacity_blocks[None, :], axis=1) * BLK
    kept = ranks < limits
    slots = jnp.where(kept, flat_ids * CAP + ranks, experts * CAP)
    token_index = jnp.arange(tokens_here * choose, dtype=jnp.int32) // choose
    owners = (
        jnp.full((experts * CAP,), tokens_here, jnp.int32).at[slots].set(token_index, mode="drop")
    )
    return (kept.reshape(tokens_here, choose), slots.reshape(tokens_here, choose), owners)


def outgoing(rows, owners, experts, scale):
    padded = jnp.concatenate([rows, jnp.zeros((1, rows.shape[1]), rows.dtype)], 0)
    picked = padded[owners]
    if scale is not None:
        picked = (scale[:, None] * picked.astype(jnp.float32)).astype(jnp.bfloat16)
    return picked.reshape(experts, CAP, rows.shape[1])


def local_grads(hidden_gate, hidden_up, act_grad):
    sigma = jax.nn.sigmoid(hidden_gate)
    gate_part = (act_grad * hidden_up * sigma * (1.0 + hidden_gate * (1.0 - sigma))).astype(
        jnp.bfloat16
    )
    up_part = (act_grad * jax.nn.silu(hidden_gate)).astype(jnp.bfloat16)
    return (gate_part, up_part)


def combine(back, slots, weights):
    padded = jnp.concatenate([back, jnp.zeros((1, back.shape[1]), back.dtype)], 0)
    picked = padded[slots].astype(jnp.float32)
    return (jnp.einsum("tk,tkw->tw", weights, picked), picked)


def dispatched_body(
    hidden_in,
    out_grad,
    expert_ids,
    gate_values,
    capacity_blocks,
    gate_weight,
    up_weight,
    down_weight,
):
    experts = capacity_blocks.shape[0]
    sources = lax.axis_size("expert")
    local_experts = gate_weight.shape[0]
    kept, slots, owners = slot_layout(expert_ids, capacity_blocks)
    weights = jnp.where(kept, gate_values, 0.0)
    slot_gates = (
        jnp.zeros((experts * CAP,), jnp.float32)
        .at[slots.reshape(-1)]
        .set(weights.reshape(-1), mode="drop")
    )
    send_in = outgoing(hidden_in, owners, experts, None)
    send_grad = outgoing(out_grad, owners, experts, slot_gates)
    recv_in, recv_grad = (
        lax.all_to_all(send_in, "expert", split_axis=0, concat_axis=0, tiled=True),
        lax.all_to_all(send_grad, "expert", split_axis=0, concat_axis=0, tiled=True),
    )
    share = recv_in.shape[2]
    share_in = recv_in.reshape(sources, local_experts, CAP, share)
    share_grad = recv_grad.reshape(sources, local_experts, CAP, share)
    piece = lax.all_gather(share_in, "etp", axis=3, tiled=True)
    hidden_gate = jnp.einsum(
        "secn,enf->secf", piece, gate_weight, preferred_element_type=jnp.float32
    )
    hidden_up = jnp.einsum("secn,enf->secf", piece, up_weight, preferred_element_type=jnp.float32)
    activ = (jax.nn.silu(hidden_gate) * hidden_up).astype(jnp.bfloat16)
    piece = lax.all_gather(share_grad, "etp", axis=3, tiled=True)
    act_grad = jnp.einsum("secn,efn->secf", piece, down_weight, preferred_element_type=jnp.float32)
    columns = jnp.einsum("secf,secn->efn", activ, piece, preferred_element_type=jnp.float32)
    act_grad, down_grad = (act_grad, columns)
    gate_part, up_part = local_grads(hidden_gate, hidden_up, act_grad)
    stacked = jnp.stack([gate_part, up_part])
    weight_grads = jnp.einsum(
        "secn,gsecf->genf",
        lax.all_gather(share_in, "etp", axis=3, tiled=True),
        stacked,
        preferred_element_type=jnp.float32,
    )
    out_part = jnp.einsum("secf,efd->secd", activ, down_weight, preferred_element_type=jnp.float32)
    back_part = jnp.einsum(
        "secf,edf->secd", gate_part, gate_weight, preferred_element_type=jnp.float32
    )
    back_part = back_part + jnp.einsum(
        "secf,edf->secd", up_part, up_weight, preferred_element_type=jnp.float32
    )
    out_rows = lax.psum_scatter(
        out_part.astype(jnp.bfloat16), "etp", scatter_dimension=3, tiled=True
    )
    home_out = lax.all_to_all(out_rows, "expert", split_axis=0, concat_axis=0, tiled=True)
    share_width = home_out.shape[3]
    layer_sum, picked = combine(home_out.reshape(experts * CAP, share_width), slots, weights)
    dot_part = jnp.einsum("tw,tkw->tk", out_grad.astype(jnp.float32), picked) * kept.astype(
        jnp.float32
    )
    gate_value_grad = lax.psum(dot_part, "etp")
    back_rows = lax.psum_scatter(
        back_part.astype(jnp.bfloat16), "etp", scatter_dimension=3, tiled=True
    )
    home_back = lax.all_to_all(back_rows, "expert", split_axis=0, concat_axis=0, tiled=True)
    input_sum, returned = combine(home_back.reshape(experts * CAP, share_width), slots, weights)
    return (
        layer_sum.astype(jnp.bfloat16),
        input_sum.astype(jnp.bfloat16),
        gate_value_grad,
        weight_grads[0].astype(jnp.bfloat16),
        weight_grads[1].astype(jnp.bfloat16),
        down_grad.astype(jnp.bfloat16),
    )


def body(*operands):
    hidden_in, gate_weight = operands[0], operands[5]
    if lax.axis_size("expert") == 4 and lax.axis_size("etp") == 4 and hidden_in.shape[0] <= gate_weight.shape[0] * CAP:
        return gathered_body(*operands)
    return dispatched_body(*operands)


def solution(mesh):
    in_specs = (
        P(("groups", "expert"), "etp"),
        P(("groups", "expert"), "etp"),
        P(("groups", "expert"), None),
        P(("groups", "expert"), None),
        P("groups"),
        P("expert", None, "etp"),
        P("expert", None, "etp"),
        P("expert", "etp", None),
    )
    out_specs = (
        P(("groups", "expert"), "etp"),
        P(("groups", "expert"), "etp"),
        P(("groups", "expert"), None),
        P(("groups", "expert"), None, "etp"),
        P(("groups", "expert"), None, "etp"),
        P(("groups", "expert"), "etp", None),
    )
    return jax.shard_map(body, mesh=mesh, in_specs=in_specs, out_specs=out_specs, check_vma=False)
```

```python
import functools

import jax
import jax.numpy as jnp
from jax import lax
from jax.experimental import pallas as pl
from jax.experimental.pallas import tpu as pltpu
from jax.sharding import PartitionSpec as P

CAP = 16
BLK = 4
EXTRA = 16
F32 = jnp.float32
BF16 = jnp.bfloat16


def nn(a, b):
    return lax.dot_general(a, b, (((1,), (0,)), ((), ())), preferred_element_type=F32)


def nt(a, b):
    return lax.dot_general(a, b, (((1,), (1,)), ((), ())), preferred_element_type=F32)


def tn(a, b):
    return lax.dot_general(a, b, (((0,), (0,)), ((), ())), preferred_element_type=F32)


def pack_kernel(hidden_hbm, ids_hbm, gates_hbm, own_ref, ids_ref, gates_ref, sems):
    tokens, width = hidden_hbm.shape
    choose = ids_ref.shape[0]
    copies = [
        pltpu.make_async_copy(hidden_hbm, own_ref.at[pl.ds(0, tokens)], sems.at[0]),
        pltpu.make_async_copy(ids_hbm, ids_ref, sems.at[1]),
        pltpu.make_async_copy(gates_hbm, gates_ref, sems.at[2]),
    ]
    for copy in copies:
        copy.start()
    for copy in copies:
        copy.wait()
    gates = gates_ref[...]
    high = gates.astype(BF16).astype(F32)
    fill = jnp.zeros((8 - choose, tokens), F32)
    top = jnp.concatenate([jnp.concatenate([ids_ref[...].astype(F32), fill], axis=0), jnp.concatenate([high, fill], axis=0)], axis=1)
    low = jnp.concatenate([jnp.concatenate([gates - high, fill], axis=0), jnp.zeros((8, width - tokens), F32)], axis=1)
    own_ref[tokens:tokens + EXTRA, :] = jnp.concatenate([top, low], axis=0).astype(BF16)


def routing(info, choose, tokens):
    info = info.astype(F32)
    return info[0:choose, 0:tokens], info[0:choose, tokens:2 * tokens] + info[8:8 + choose, 0:tokens]


def columns(me, mask, width):
    return pl.ds(pl.multiple_of(lax.bitwise_xor(me, mask) * width, width), width)


def send_home(home_keep, home_send, me, onehot, rows, tokens, width):
    for s in range(onehot.shape[0]):
        for q in range(4):
            home = home_send if q % 2 else home_keep
            home[q // 2, s, 0:tokens, :] = tn(onehot[s], rows[s, :, columns(me, q, width)]).astype(BF16)


RING = 8


def ring(weight, slots, sems, columns=None):
    depth = slots.shape[0]

    def load(e):
        slot = lax.rem(e, depth)
        source = weight.at[e] if columns is None else weight.at[e, :, columns]
        return pltpu.make_async_copy(source, slots.at[slot], sems.at[slot])

    def start(e):
        @pl.when(e < weight.shape[0])
        def _():
            load(e).start()

    for e in range(min(depth, weight.shape[0])):
        load(jnp.int32(e)).start()
    if depth >= weight.shape[0]:
        return lambda e: None, lambda e: load(e).wait()
    return lambda e: start(e + depth), lambda e: load(e).wait()


def slot_of(slots, e):
    return slots[lax.rem(e, slots.shape[0])]


def half(me, other, size):
    return pl.ds(pl.multiple_of(lax.bitwise_xor(me // 2, other) * size, size), size)


def gather_half(me, onehot, blocks, rows_ref, experts, width, tokens, start):
    for q, block in enumerate(blocks):
        picked = nn(onehot, block).astype(BF16).reshape(experts, CAP, width)
        at = pl.multiple_of(lax.rem(lax.bitwise_xor(me, q), 2) * width, width)
        rows_ref[:, start:start + CAP, pl.ds(at, width)] = picked


def early_kernel(
    choose, capacity_ref, o0, o1, b0, b1, gate_ref, up_hbm,
    rows_ref, part_ref, onehot, slot_gate,
    up_ref, sems,
):
    sources, slots, tokens = onehot.shape
    experts = slots // CAP
    width = b0.shape[2]
    me = lax.axis_index("etp")
    first = lax.axis_index("expert") * experts

    here = half(me, 0, 2 * width)
    start, wait = ring(up_hbm, up_ref, sems, here)
    row = lax.broadcasted_iota(jnp.int32, (tokens, tokens), 0)
    col = lax.broadcasted_iota(jnp.int32, (tokens, tokens), 1)
    before = jnp.where(row < col, 1.0, 0.0).astype(BF16)
    expert = lax.broadcasted_iota(jnp.int32, (experts, tokens), 0)
    mine = (first + expert).astype(F32)
    limit = jnp.zeros((experts, tokens), jnp.int32)
    for e in range(experts):
        limit = jnp.where(expert == e, capacity_ref[first + e] * BLK, limit)
    limit = limit.astype(F32)
    place = lax.broadcasted_iota(jnp.int32, (experts, CAP, tokens), 1).astype(F32)
    for s in range(sources):
        block = [o[...] for o in (o0, o1)] if s == 0 else [b[s - 1] for b in (b0, b1)]
        ids, gates = routing(block[0][tokens:tokens + EXTRA, :], choose, tokens)
        named = jnp.zeros((experts, tokens), F32)
        gate = jnp.zeros((experts, tokens), F32)
        for k in range(choose):
            hit = ids[k:k + 1, :] == mine
            named = named + jnp.where(hit, 1.0, 0.0)
            gate = gate + jnp.where(hit, gates[k:k + 1, :], 0.0)
        rank = nn(named.astype(BF16), before)
        rank = jnp.where((named > 0.5) & (rank < limit), rank, -1.0)
        chosen = jnp.where(rank[:, None, :] == place, 1.0, 0.0)
        gate_of = jnp.sum(chosen * gate[:, None, :], axis=2, keepdims=True)
        slot_gate[:, s * CAP:(s + 1) * CAP, :] = jnp.broadcast_to(gate_of, chosen.shape)
        table = chosen.reshape(slots, tokens).astype(BF16)
        onehot[s] = table
        gather_half(me, table, [x[0:tokens, :] for x in block], rows_ref, experts, width, tokens, s * CAP)

    def some(turn, _):
        for e in (turn * 2, turn * 2 + 1):
            wait(e)
        for e in (turn * 2, turn * 2 + 1):
            part_ref[0, e] = nt(rows_ref[e], gate_ref[e, :, here])
            part_ref[1, e] = nt(rows_ref[e], slot_of(up_ref, e))
        for e in (turn * 2, turn * 2 + 1):
            start(e)
        return 0

    lax.fori_loop(0, experts // 2, some, 0)


def forward_kernel(
    o2, o3, b2, b3, gate_ref, up_hbm, down_hbm, half_ref, part_ref, onehot, slot_gate, later_ref,
    out_rows, rows_ref, act_ref, a_ref, slope_ref, silu_ref,
    there_ref, up_ref, down_ref, up_sems, down_sems,
):
    sources, slots, tokens = onehot.shape
    experts = slots // CAP
    width = b2.shape[2]
    me = lax.axis_index("etp")
    here, there = half(me, 0, 2 * width), half(me, 1, 2 * width)
    start_up, wait_up = ring(up_hbm, up_ref, up_sems, there)
    start_down, wait_down = ring(down_hbm, down_ref, down_sems)
    for s in range(sources):
        block = [o[0:tokens, :] for o in (o2, o3)] if s == 0 else [b[s - 1, 0:tokens, :] for b in (b2, b3)]
        gather_half(me, onehot[s], block, there_ref, experts, width, tokens, s * CAP)

    def activate(e):
        rows_ref[e, :, here] = half_ref[e]
        x = there_ref[e]
        rows_ref[e, :, there] = x
        hidden_gate = part_ref[0, e] + nt(x, gate_ref[e, :, there])
        hidden_up = part_ref[1, e] + nt(x, slot_of(up_ref, e))
        sigma = jax.nn.sigmoid(hidden_gate)
        silu = hidden_gate * sigma
        activ = (silu * hidden_up).astype(BF16)
        act_ref[e] = activ
        slope_ref[e] = hidden_up * sigma * (1.0 + hidden_gate * (1.0 - sigma))
        silu_ref[e] = silu
        a_ref[e] = (activ.astype(F32) * slot_gate[e][:, 0:1]).astype(BF16)

    def project(e):
        out = nn(a_ref[e], slot_of(down_ref, e)).astype(BF16)
        at = pl.ds(pl.multiple_of(e * CAP, CAP), CAP)
        for s in range(sources):
            out_rows[s, at, :] = out[s * CAP:(s + 1) * CAP]

    def first(e):
        wait_up(e)
        activate(e)
        start_up(e)

    def both(e):
        for i in (e - 2, e - 1):
            wait_down(i)
        for i in (e, e + 1):
            wait_up(i)
        project(e - 2)
        project(e - 1)
        activate(e)
        activate(e + 1)
        for i in (e - 2, e - 1):
            start_down(i)
        for i in (e, e + 1):
            start_up(i)

    skewed(experts, first, wait_down, project, both)


def skewed(experts, first, wait, second, both):
    first(jnp.int32(0))
    first(jnp.int32(1))

    def turn(i, _):
        both(i * 2)
        return 0

    lax.fori_loop(1, experts // 2, turn, 0)
    for e in (experts - 2, experts - 1):
        wait(jnp.int32(e))
    for e in (experts - 2, experts - 1):
        second(jnp.int32(e))


def home_kernel(onehot, rows, *refs):
    grads, (keep, send) = refs[:-2], refs[-2:]
    send_home(keep, send, lax.axis_index("etp"), onehot, rows, keep.shape[2], keep.shape[3])
    for s, grad in enumerate(grads):
        for q in range(2):
            send[2 + q, s] = grad[q]


def home_values_kernel(choose, onehot, rows, dots, own_ref, info_ref, *refs):
    keep, send = refs[-2:]
    sources, slots, tokens = onehot.shape
    experts = slots // CAP
    width = keep.shape[3]
    send_home(keep, send, lax.axis_index("etp"), onehot, rows, tokens, width)
    expert = lax.broadcasted_iota(jnp.int32, (experts, tokens), 0)
    mine = (lax.axis_index("expert") * experts + expert).astype(F32)
    for s in range(sources):
        info = own_ref[tokens:tokens + EXTRA, :] if s == 0 else info_ref[s - 1, tokens:tokens + EXTRA, :]
        ids, _ = routing(info, choose, tokens)
        chosen = onehot[s].astype(F32).reshape(experts, CAP, tokens)
        share = jnp.sum(chosen * dots[:, s * CAP:(s + 1) * CAP, :], axis=1)
        values = [jnp.sum(jnp.where(ids[k:k + 1, :] == mine, share, 0.0), axis=0, keepdims=True) for k in range(choose)]
        values = jnp.concatenate(values + [jnp.zeros((EXTRA - choose, tokens), F32)], axis=0)
        values = jnp.concatenate([values, jnp.zeros((EXTRA, width - tokens), F32)], axis=1).astype(BF16)
        for home in (keep, send):
            home[0, s, tokens:tokens + EXTRA, :] = values
            home[1, s, tokens:tokens + EXTRA, :] = values


def backward_kernel(
    a0, a1, a2, a3, near_ref,
    gate_ref, up_hbm, down_hbm, act_ref, slope_ref, silu_ref, onehot, slot_gate, earlier_ref,
    back_rows, dots, rows_ref, p_ref, q_ref,
    up_ref, down_ref, up_sems, down_sems,
):
    sources, slots, tokens = onehot.shape
    experts = slots // CAP
    width = a0.shape[2]
    me = lax.axis_index("etp")
    start_down, wait_down = ring(down_hbm, down_ref, down_sems)
    start_up, wait_up = ring(up_hbm, up_ref, up_sems)
    for s, here in enumerate((a0, a1, a2, a3)):
        for q in range(4):
            block = near_ref[2 + q // 2, s] if q % 2 else here[q // 2]
            picked = nn(onehot[s], block).astype(BF16).reshape(experts, CAP, width)
            rows_ref[:, s * CAP:(s + 1) * CAP, columns(me, q, width)] = picked

    def slopes(e):
        grad = nt(rows_ref[e], slot_of(down_ref, e))
        activ = act_ref[e].astype(F32)
        dots[e] = jnp.broadcast_to(jnp.sum(activ * grad, axis=1, keepdims=True), dots.shape[1:])
        grad = grad * slot_gate[e][:, 0:1]
        p_ref[e] = (grad * slope_ref[e]).astype(BF16)
        q_ref[e] = (grad * silu_ref[e]).astype(BF16)

    def project(e):
        back = nn(p_ref[e], gate_ref[e]) + nn(q_ref[e], slot_of(up_ref, e))
        back = (back * slot_gate[e][:, 0:1]).astype(BF16)
        at = pl.ds(pl.multiple_of(e * CAP, CAP), CAP)
        for s in range(sources):
            back_rows[s, at, :] = back[s * CAP:(s + 1) * CAP]

    def first(e):
        wait_down(e)
        slopes(e)
        start_down(e)

    def both(e):
        for i in (e, e + 1):
            wait_down(i)
        for i in (e - 2, e - 1):
            wait_up(i)
        project(e - 2)
        project(e - 1)
        slopes(e)
        slopes(e + 1)
        for i in (e, e + 1):
            start_down(i)
        for i in (e - 2, e - 1):
            start_up(i)

    skewed(experts, first, wait_up, project, both)


def add_kernel(keep, came, *refs):
    near, far = refs[-2:]
    for s in range(near.shape[0]):
        far[s] = (keep[1, s].astype(F32) + came[1, s].astype(F32)).astype(BF16)
        near[s] = (keep[0, s].astype(F32) + came[0, s].astype(F32)).astype(BF16)


def chips_kernel(out_near, out_came, back_near, back_came, *refs):
    sources, tokens = out_near.shape[:2]
    parts = refs[-sources:]
    for s in range(sources):
        parts[s][0:tokens, :] = (out_near[s].astype(F32) + out_came[s].astype(F32)).astype(BF16)
        parts[s][tokens:, :] = (back_near[s].astype(F32) + back_came[s].astype(F32)).astype(BF16)


def total_kernel(count, *refs):
    out_ref, back_ref, value_ref = refs[count:]
    tokens = out_ref.shape[0]
    total = refs[0][...].astype(F32)
    for ref in refs[1:count]:
        total = total + ref[...].astype(F32)
    out_ref[...] = total[0:tokens].astype(BF16)
    back_ref[...] = total[tokens:2 * tokens].astype(BF16)
    value_ref[...] = total[2 * tokens:2 * tokens + value_ref.shape[0], 0:value_ref.shape[1]]


BANKS = 8
TURN = 4


def product_kernel(jobs, *refs):
    lefts, rights, outs = (refs[i * len(jobs):(i + 1) * len(jobs)] for i in range(3))
    held, sems = refs[-2:]
    outs = refs[-2 - len(jobs):-2]

    def store(job, e, slot):
        return pltpu.make_async_copy(held.at[slot], outs[job].at[e], sems.at[slot])

    def turn(job, first, done, i, full):
        for pair in range(0, TURN, 2):
            places = [(first + i * TURN + j, lax.rem(done + i * TURN + j, BANKS)) for j in (pair, pair + 1)]
            if full:
                for e, slot in places:
                    store(job, e, slot).wait()
            for e, slot in places:
                held[slot] = tn(lefts[job][e], rights[job][e]).astype(BF16)
            for e, slot in places:
                store(job, e, slot).start()

    done = 0
    for job, (first, last) in enumerate(jobs):
        fresh = max(0, min(BANKS - done, last - first) // TURN)
        for i in range(fresh):
            turn(job, first, done, jnp.int32(i), False)

        def later(i, _, job=job, first=first, done=done):
            turn(job, first, done, i, True)
            return 0

        lax.fori_loop(fresh, (last - first) // TURN, later, 0)
        done = done + last - first
    for slot in range(min(done, BANKS)):
        store(0, jobs[0][0], slot).wait()


def load_kernel(source, target, token, sems):
    token[...] = jnp.zeros_like(token)
    copies = [pltpu.make_async_copy(source.at[e], target.at[e], sems.at[e]) for e in range(source.shape[0])]
    for copy in copies:
        copy.start()
    for copy in copies:
        copy.wait()


def in_vmem(weight):
    return pl.pallas_call(
        load_kernel,
        in_specs=[pl.BlockSpec(memory_space=pltpu.HBM)],
        out_specs=[pl.BlockSpec(memory_space=pltpu.VMEM)] * 2,
        out_shape=[pltpu.VMEM(weight.shape, BF16), jax.ShapeDtypeStruct((8, 128), F32)],
        scratch_shapes=[pltpu.SemaphoreType.DMA((weight.shape[0],))],
        compiler_params=pltpu.CompilerParams(vmem_limit_bytes=4 * 1024 * 1024),
        cost_estimate=pl.CostEstimate(flops=0, bytes_accessed=2 * weight.size, transcendentals=0),
    )(pltpu.with_memory_space_constraint(weight, pltpu.HBM))


def join_kernel(count, *refs):
    for i in range(count):
        refs[-1][i] = refs[i][...]


def join(arrays, *there):
    return kernel_call(
        functools.partial(join_kernel, len(arrays)),
        [jax.ShapeDtypeStruct((len(arrays),) + arrays[0].shape, arrays[0].dtype)],
        [],
        0,
        limit=2,
    )(*arrays, *there)[0]


def kernel_call(kernel, out_shape, scratch, flops, out_specs=None, limit=4, in_hbm=(), aliases={}):
    def call(*operands):
        specs = [
            pl.BlockSpec(memory_space=pltpu.HBM if i in in_hbm else pltpu.SMEM if x.ndim == 1 else pltpu.VMEM)
            for i, x in enumerate(operands)
        ]
        operands = [
            pltpu.with_memory_space_constraint(x, pltpu.HBM) if i in in_hbm else x for i, x in enumerate(operands)
        ]
        return pl.pallas_call(
            kernel,
            in_specs=specs,
            out_specs=out_specs or [pl.BlockSpec(memory_space=pltpu.VMEM)] * len(out_shape),
            out_shape=out_shape,
            scratch_shapes=scratch,
            input_output_aliases=aliases,
            compiler_params=pltpu.CompilerParams(vmem_limit_bytes=limit * 1024 * 1024),
            cost_estimate=pl.CostEstimate(flops=flops, bytes_accessed=flops // 32, transcendentals=0),
        )(*operands)

    return call


def weight_grads(jobs, begun=None, *earlier):
    count = len(jobs)
    lefts, rights = [job[0] for job in jobs], [job[1] for job in jobs]
    experts, rows, units = lefts[0].shape
    model = rights[0].shape[2]
    shape = jax.ShapeDtypeStruct((experts, units, model), BF16)
    work = sum(job[3] - job[2] for job in jobs)
    more = [] if begun is None else [begun]
    return kernel_call(
        functools.partial(product_kernel, [job[2:] for job in jobs]),
        [shape] * count,
        [pltpu.VMEM((BANKS, units, model), BF16), pltpu.SemaphoreType.DMA((BANKS,))],
        2 * work * rows * units * model,
        out_specs=[pl.BlockSpec(memory_space=pltpu.HBM)] * count,
        limit=8,
        in_hbm=(2 * count,) if more else (),
        aliases={2 * count: 0} if more else {},
    )(*lefts, *rights, *more, *earlier)


def swap(array, bit, axis="etp"):
    count = lax.axis_size(axis)
    return lax.ppermute(array, axis, [(i, i ^ bit) for i in range(count)])


def add_cores(keep, came, *earlier):
    shape = jax.ShapeDtypeStruct(keep.shape[1:], BF16)
    hbm = [2] if earlier else []
    return kernel_call(add_kernel, [shape, shape], [], 0, limit=2, in_hbm=hbm)(keep, came, *earlier)


def gathered_body(
    hidden_in, out_grad, expert_ids, gate_values, capacity_blocks, gate_weight, up_weight, down_weight
):
    sources = lax.axis_size("expert")
    tokens, width = hidden_in.shape
    choose = expert_ids.shape[1]
    local_experts, units, model = down_weight.shape
    slots = local_experts * CAP
    rows = sources * CAP
    gate_t, gate_there = in_vmem(jnp.swapaxes(gate_weight, 1, 2))
    up_t = jnp.swapaxes(up_weight, 1, 2)
    product = 2 * local_experts * rows * units * model
    held = lambda *shape, kind=BF16: pltpu.VMEM(shape, kind)
    sent = lambda *shape: jax.ShapeDtypeStruct(shape, BF16)

    own = kernel_call(
        pack_kernel,
        [sent(tokens + EXTRA, width)],
        [pltpu.VMEM((choose, tokens), jnp.int32), pltpu.VMEM((choose, tokens), F32), pltpu.SemaphoreType.DMA((3,))],
        0,
        limit=2,
        in_hbm=(0, 1, 2),
    )(hidden_in, expert_ids.T, gate_values.T)[0]
    came = [swap(own, s, "expert") for s in range(1, sources)]
    own_across = swap(own, 2)
    grad_across = swap(out_grad, 2)
    came = join(came, gate_there, own_across, grad_across)
    came_across_there = swap(came, 2)
    grads = join([out_grad, grad_across], came)
    grads = [grads] + [swap(grads, s, "expert") for s in range(1, sources)]

    half_rows, partial, onehot, slot_gate = kernel_call(
        functools.partial(early_kernel, choose),
        [
            held(local_experts, rows, model // 2),
            held(2, local_experts, rows, units, kind=F32),
            held(sources, slots, tokens),
            held(local_experts, rows, tokens, kind=F32),
        ],
        [pltpu.VMEM((local_experts, units, model // 2), BF16), pltpu.SemaphoreType.DMA((local_experts,))],
        product,
        limit=8,
        in_hbm=(6,),
    )(capacity_blocks, own, swap(own, 1), came, swap(came, 1), gate_t, up_t)
    came_across = join([came_across_there], onehot)[0]
    out_rows, x_rows, activ, scaled, slope, silu = kernel_call(
        forward_kernel,
        [
            held(sources, slots, model),
            held(local_experts, rows, model),
            held(local_experts, rows, units),
            held(local_experts, rows, units),
            held(local_experts, rows, units, kind=F32),
            held(local_experts, rows, units, kind=F32),
        ],
        [
            pltpu.VMEM((local_experts, rows, model // 2), BF16),
            pltpu.VMEM((local_experts, units, model // 2), BF16),
            pltpu.VMEM((RING, units, model), BF16),
            pltpu.SemaphoreType.DMA((local_experts,)),
            pltpu.SemaphoreType.DMA((RING,)),
        ],
        2 * product,
        limit=14,
        in_hbm=(5, 6),
    )(
        own_across, swap(own_across, 1), came_across, swap(came_across, 1),
        gate_t, up_t, down_weight, half_rows, partial, onehot, slot_gate, grads[0],
    )

    keep, send = kernel_call(
        home_kernel,
        [sent(2, sources, tokens, width), sent(4, sources, tokens, width)],
        [],
        2 * slots * sources * tokens * model,
        limit=2,
    )(onehot, out_rows, *grads)
    near = swap(send, 1)
    out_near, out_far = add_cores(keep, near)
    back_rows, dots, y_rows, gate_part, up_part = kernel_call(
        backward_kernel,
        [
            held(sources, slots, model),
            held(local_experts, rows, tokens, kind=F32),
            held(local_experts, rows, model),
            held(local_experts, rows, units),
            held(local_experts, rows, units),
        ],
        [pltpu.VMEM((RING, units, model), BF16)] * 2 + [pltpu.SemaphoreType.DMA((RING,))] * 2,
        3 * product,
        limit=14,
        in_hbm=(6, 7),
    )(
        *grads, near,
        gate_t, up_t, down_weight, activ, slope, silu, onehot, slot_gate, out_near,
    )

    out_came = swap(out_far, 2)
    keep, send = kernel_call(
        functools.partial(home_values_kernel, choose),
        [sent(2, sources, tokens + EXTRA, width)] * 2,
        [],
        2 * slots * sources * tokens * model,
        limit=2,
    )(onehot, back_rows, dots, own, came, out_came)
    some = local_experts // 2
    (down_grad,) = weight_grads([(scaled, y_rows, 0, some)])
    back_near, back_far = add_cores(keep, swap(send, 1), down_grad)
    (up_grad,) = weight_grads([(up_part, x_rows, 0, local_experts)], None, back_near)
    height = 2 * tokens + EXTRA
    parts = kernel_call(chips_kernel, [sent(height, width)] * sources, [], 0, limit=2, in_hbm=(4,))(
        out_near, out_came, back_near, swap(back_far, 2), up_grad
    )
    down_grad, gate_grad = weight_grads(
        [(scaled, y_rows, some, local_experts), (gate_part, x_rows, 0, local_experts)], down_grad, parts[0]
    )
    layer_out, input_grad, value_grad = kernel_call(
        functools.partial(total_kernel, sources),
        [sent(tokens, width), sent(tokens, width), jax.ShapeDtypeStruct((choose, tokens), F32)],
        [],
        0,
        limit=2,
    )(parts[0], *[swap(parts[s], s, "expert") for s in range(1, sources)])
    return (
        layer_out,
        input_grad,
        value_grad.T,
        jnp.swapaxes(gate_grad, 1, 2),
        jnp.swapaxes(up_grad, 1, 2),
        down_grad,
    )


def slot_layout(expert_ids, capacity_blocks):
    tokens_here, choose = expert_ids.shape
    experts = capacity_blocks.shape[0]
    flat_ids = expert_ids.reshape(-1)
    onehot = (flat_ids[:, None] == jnp.arange(experts, dtype=jnp.int32)[None, :]).astype(jnp.int32)
    before = jnp.cumsum(onehot, axis=0) - onehot
    ranks = jnp.sum(before * onehot, axis=1)
    limits = jnp.sum(onehot * capacity_blocks[None, :], axis=1) * BLK
    kept = ranks < limits
    slots = jnp.where(kept, flat_ids * CAP + ranks, experts * CAP)
    token_index = jnp.arange(tokens_here * choose, dtype=jnp.int32) // choose
    owners = (
        jnp.full((experts * CAP,), tokens_here, jnp.int32).at[slots].set(token_index, mode="drop")
    )
    return (kept.reshape(tokens_here, choose), slots.reshape(tokens_here, choose), owners)


def outgoing(rows, owners, experts, scale):
    padded = jnp.concatenate([rows, jnp.zeros((1, rows.shape[1]), rows.dtype)], 0)
    picked = padded[owners]
    if scale is not None:
        picked = (scale[:, None] * picked.astype(jnp.float32)).astype(jnp.bfloat16)
    return picked.reshape(experts, CAP, rows.shape[1])


def local_grads(hidden_gate, hidden_up, act_grad):
    sigma = jax.nn.sigmoid(hidden_gate)
    gate_part = (act_grad * hidden_up * sigma * (1.0 + hidden_gate * (1.0 - sigma))).astype(
        jnp.bfloat16
    )
    up_part = (act_grad * jax.nn.silu(hidden_gate)).astype(jnp.bfloat16)
    return (gate_part, up_part)


def combine(back, slots, weights):
    padded = jnp.concatenate([back, jnp.zeros((1, back.shape[1]), back.dtype)], 0)
    picked = padded[slots].astype(jnp.float32)
    return (jnp.einsum("tk,tkw->tw", weights, picked), picked)


def dispatched_body(
    hidden_in,
    out_grad,
    expert_ids,
    gate_values,
    capacity_blocks,
    gate_weight,
    up_weight,
    down_weight,
):
    experts = capacity_blocks.shape[0]
    sources = lax.axis_size("expert")
    local_experts = gate_weight.shape[0]
    kept, slots, owners = slot_layout(expert_ids, capacity_blocks)
    weights = jnp.where(kept, gate_values, 0.0)
    slot_gates = (
        jnp.zeros((experts * CAP,), jnp.float32)
        .at[slots.reshape(-1)]
        .set(weights.reshape(-1), mode="drop")
    )
    send_in = outgoing(hidden_in, owners, experts, None)
    send_grad = outgoing(out_grad, owners, experts, slot_gates)
    recv_in, recv_grad = (
        lax.all_to_all(send_in, "expert", split_axis=0, concat_axis=0, tiled=True),
        lax.all_to_all(send_grad, "expert", split_axis=0, concat_axis=0, tiled=True),
    )
    share = recv_in.shape[2]
    share_in = recv_in.reshape(sources, local_experts, CAP, share)
    share_grad = recv_grad.reshape(sources, local_experts, CAP, share)
    piece = lax.all_gather(share_in, "etp", axis=3, tiled=True)
    hidden_gate = jnp.einsum(
        "secn,enf->secf", piece, gate_weight, preferred_element_type=jnp.float32
    )
    hidden_up = jnp.einsum("secn,enf->secf", piece, up_weight, preferred_element_type=jnp.float32)
    activ = (jax.nn.silu(hidden_gate) * hidden_up).astype(jnp.bfloat16)
    piece = lax.all_gather(share_grad, "etp", axis=3, tiled=True)
    act_grad = jnp.einsum("secn,efn->secf", piece, down_weight, preferred_element_type=jnp.float32)
    columns = jnp.einsum("secf,secn->efn", activ, piece, preferred_element_type=jnp.float32)
    act_grad, down_grad = (act_grad, columns)
    gate_part, up_part = local_grads(hidden_gate, hidden_up, act_grad)
    stacked = jnp.stack([gate_part, up_part])
    weight_grads = jnp.einsum(
        "secn,gsecf->genf",
        lax.all_gather(share_in, "etp", axis=3, tiled=True),
        stacked,
        preferred_element_type=jnp.float32,
    )
    out_part = jnp.einsum("secf,efd->secd", activ, down_weight, preferred_element_type=jnp.float32)
    back_part = jnp.einsum(
        "secf,edf->secd", gate_part, gate_weight, preferred_element_type=jnp.float32
    )
    back_part = back_part + jnp.einsum(
        "secf,edf->secd", up_part, up_weight, preferred_element_type=jnp.float32
    )
    out_rows = lax.psum_scatter(
        out_part.astype(jnp.bfloat16), "etp", scatter_dimension=3, tiled=True
    )
    home_out = lax.all_to_all(out_rows, "expert", split_axis=0, concat_axis=0, tiled=True)
    share_width = home_out.shape[3]
    layer_sum, picked = combine(home_out.reshape(experts * CAP, share_width), slots, weights)
    dot_part = jnp.einsum("tw,tkw->tk", out_grad.astype(jnp.float32), picked) * kept.astype(
        jnp.float32
    )
    gate_value_grad = lax.psum(dot_part, "etp")
    back_rows = lax.psum_scatter(
        back_part.astype(jnp.bfloat16), "etp", scatter_dimension=3, tiled=True
    )
    home_back = lax.all_to_all(back_rows, "expert", split_axis=0, concat_axis=0, tiled=True)
    input_sum, returned = combine(home_back.reshape(experts * CAP, share_width), slots, weights)
    return (
        layer_sum.astype(jnp.bfloat16),
        input_sum.astype(jnp.bfloat16),
        gate_value_grad,
        weight_grads[0].astype(jnp.bfloat16),
        weight_grads[1].astype(jnp.bfloat16),
        down_grad.astype(jnp.bfloat16),
    )


def body(*operands):
    hidden_in, gate_weight = operands[0], operands[5]
    if lax.axis_size("expert") == 4 and lax.axis_size("etp") == 4 and hidden_in.shape[0] <= gate_weight.shape[0] * CAP:
        return gathered_body(*operands)
    return dispatched_body(*operands)


def solution(mesh):
    in_specs = (
        P(("groups", "expert"), "etp"),
        P(("groups", "expert"), "etp"),
        P(("groups", "expert"), None),
        P(("groups", "expert"), None),
        P("groups"),
        P("expert", None, "etp"),
        P("expert", None, "etp"),
        P("expert", "etp", None),
    )
    out_specs = (
        P(("groups", "expert"), "etp"),
        P(("groups", "expert"), "etp"),
        P(("groups", "expert"), None),
        P(("groups", "expert"), None, "etp"),
        P(("groups", "expert"), None, "etp"),
        P(("groups", "expert"), "etp", None),
    )
    return jax.shard_map(body, mesh=mesh, in_specs=in_specs, out_specs=out_specs, check_vma=False)
```

```python
import functools

import jax
import jax.numpy as jnp
from jax import lax
from jax.experimental import pallas as pl
from jax.experimental.pallas import tpu as pltpu
from jax.sharding import PartitionSpec as P

CAP = 16
BLK = 4
EXTRA = 16
F32 = jnp.float32
BF16 = jnp.bfloat16


def nn(a, b):
    return lax.dot_general(a, b, (((1,), (0,)), ((), ())), preferred_element_type=F32)


def nt(a, b):
    return lax.dot_general(a, b, (((1,), (1,)), ((), ())), preferred_element_type=F32)


def tn(a, b):
    return lax.dot_general(a, b, (((0,), (0,)), ((), ())), preferred_element_type=F32)


def pack_kernel(hidden_hbm, ids_hbm, gates_hbm, own_ref, ids_ref, gates_ref, sems):
    tokens, width = hidden_hbm.shape
    choose = ids_ref.shape[0]
    copies = [
        pltpu.make_async_copy(hidden_hbm, own_ref.at[pl.ds(0, tokens)], sems.at[0]),
        pltpu.make_async_copy(ids_hbm, ids_ref, sems.at[1]),
        pltpu.make_async_copy(gates_hbm, gates_ref, sems.at[2]),
    ]
    for copy in copies:
        copy.start()
    for copy in copies:
        copy.wait()
    gates = gates_ref[...]
    high = gates.astype(BF16).astype(F32)
    fill = jnp.zeros((8 - choose, tokens), F32)
    top = jnp.concatenate([jnp.concatenate([ids_ref[...].astype(F32), fill], axis=0), jnp.concatenate([high, fill], axis=0)], axis=1)
    low = jnp.concatenate([jnp.concatenate([gates - high, fill], axis=0), jnp.zeros((8, width - tokens), F32)], axis=1)
    own_ref[tokens:tokens + EXTRA, :] = jnp.concatenate([top, low], axis=0).astype(BF16)


def routing(info, choose, tokens):
    info = info.astype(F32)
    return info[0:choose, 0:tokens], info[0:choose, tokens:2 * tokens], info[8:8 + choose, 0:tokens]


def columns(me, mask, width):
    return pl.ds(pl.multiple_of(lax.bitwise_xor(me, mask) * width, width), width)


def send_home(home_keep, home_send, me, onehot, rows, tokens, width):
    for s in range(onehot.shape[0]):
        for q in range(4):
            home = home_send if q % 2 else home_keep
            home[q // 2, s, 0:tokens, :] = tn(onehot[s], rows[s, :, columns(me, q, width)]).astype(BF16)


RING = 8


def ring(weight, slots, sems, columns=None):
    depth = slots.shape[0]

    def load(e):
        slot = lax.rem(e, depth)
        source = weight.at[e] if columns is None else weight.at[e, :, columns]
        return pltpu.make_async_copy(source, slots.at[slot], sems.at[slot])

    def start(e):
        @pl.when(e < weight.shape[0])
        def _():
            load(e).start()

    for e in range(min(depth, weight.shape[0])):
        load(jnp.int32(e)).start()
    if depth >= weight.shape[0]:
        return lambda e: None, lambda e: load(e).wait()
    return lambda e: start(e + depth), lambda e: load(e).wait()


def slot_of(slots, e):
    return slots[lax.rem(e, slots.shape[0])]


def half(me, other, size):
    return pl.ds(pl.multiple_of(lax.bitwise_xor(me // 2, other) * size, size), size)


def gather_half(me, onehot, blocks, rows_ref, experts, width, tokens, start, offset):
    for q, block in enumerate(blocks):
        picked = nn(onehot, block).astype(BF16).reshape(experts, CAP, width)
        at = pl.multiple_of(lax.rem(lax.bitwise_xor(me, q), 2) * width + offset, width)
        rows_ref[:, start:start + CAP, pl.ds(at, width)] = picked


def routing_kernel(
    choose, capacity_ref, o0, o1, b0, b1, earlier_ref, rows_ref, onehot, slot_gate
):
    sources, slots, tokens = onehot.shape
    experts = slots // CAP
    width = b0.shape[2]
    me = lax.axis_index("etp")
    first = lax.axis_index("expert") * experts
    row = lax.broadcasted_iota(jnp.int32, (tokens, tokens), 0)
    col = lax.broadcasted_iota(jnp.int32, (tokens, tokens), 1)
    before = jnp.where(row < col, 1.0, 0.0).astype(BF16)
    ones = jnp.ones((tokens, tokens), BF16)
    expert = lax.broadcasted_iota(jnp.int32, (experts, tokens), 0)
    mine = (first + expert).astype(F32)
    limit = jnp.zeros((experts, tokens), jnp.int32)
    for e in range(experts):
        limit = jnp.where(expert == e, capacity_ref[first + e] * BLK, limit)
    limit = limit.astype(F32)
    place = lax.broadcasted_iota(jnp.int32, (experts, CAP, tokens), 1).astype(F32)
    for s in range(sources):
        block = [o[...] for o in (o0, o1)] if s == 0 else [b[s - 1] for b in (b0, b1)]
        ids, highs, lows = routing(block[0][tokens:tokens + EXTRA, :], choose, tokens)
        named = jnp.zeros((experts, tokens), F32)
        high, low = named, named
        for k in range(choose):
            hit = ids[k:k + 1, :] == mine
            named = named + jnp.where(hit, 1.0, 0.0)
            high = high + jnp.where(hit, highs[k:k + 1, :], 0.0)
            low = low + jnp.where(hit, lows[k:k + 1, :], 0.0)
        rank = nn(named.astype(BF16), before)
        rank = jnp.where((named > 0.5) & (rank < limit), rank, -1.0)
        taken = rank[:, None, :] == place
        spread = lambda x: jnp.where(taken, x[:, None, :], 0.0).reshape(slots, tokens).astype(BF16)
        gates = nn(spread(high), ones) + nn(spread(low), ones)
        slot_gate[:, s * CAP:(s + 1) * CAP, :] = gates.reshape(experts, CAP, tokens)
        table = jnp.where(taken, 1.0, 0.0).reshape(slots, tokens).astype(BF16)
        onehot[s] = table
        gather_half(me, table, [x[0:tokens, :] for x in block], rows_ref, experts, width, tokens, s * CAP, 0)


def forward_kernel(
    o2, o3, b2, b3, gate_ref, up_hbm, down_hbm, half_ref, onehot, slot_gate, later_ref,
    out_rows, rows_ref, act_ref, a_ref, slope_ref, silu_ref,
    up_ref, down_ref, up_sems, down_sems,
):
    sources, slots, tokens = onehot.shape
    experts = slots // CAP
    width = b2.shape[2]
    me = lax.axis_index("etp")
    start_up, wait_up = ring(up_hbm, up_ref, up_sems)
    start_down, wait_down = ring(down_hbm, down_ref, down_sems)
    rows_ref[:, :, half(me, 0, 2 * width)] = half_ref[...]
    other = lax.bitwise_xor(me // 2, 1) * 2 * width
    for s in range(sources):
        block = [o[0:tokens, :] for o in (o2, o3)] if s == 0 else [b[s - 1, 0:tokens, :] for b in (b2, b3)]
        gather_half(me, onehot[s], block, rows_ref, experts, width, tokens, s * CAP, other)

    def activate(e):
        x = rows_ref[e]
        hidden_gate = nt(x, gate_ref[e])
        hidden_up = nt(x, slot_of(up_ref, e))
        sigma = jax.nn.sigmoid(hidden_gate)
        silu = hidden_gate * sigma
        activ = (silu * hidden_up).astype(BF16)
        act_ref[e] = activ
        slope_ref[e] = hidden_up * sigma * (1.0 + hidden_gate * (1.0 - sigma))
        silu_ref[e] = silu
        a_ref[e] = (activ.astype(F32) * slot_gate[e][:, 0:1]).astype(BF16)

    def project(e):
        out = nn(a_ref[e], slot_of(down_ref, e)).astype(BF16)
        at = pl.ds(pl.multiple_of(e * CAP, CAP), CAP)
        for s in range(sources):
            out_rows[s, at, :] = out[s * CAP:(s + 1) * CAP]

    def first(e):
        wait_up(e)
        activate(e)
        start_up(e)

    def both(e):
        for i in (e - 2, e - 1):
            wait_down(i)
        for i in (e, e + 1):
            wait_up(i)
        project(e - 2)
        project(e - 1)
        activate(e)
        activate(e + 1)
        for i in (e - 2, e - 1):
            start_down(i)
        for i in (e, e + 1):
            start_up(i)

    skewed(experts, first, wait_down, project, both)


def skewed(experts, first, wait, second, both):
    first(jnp.int32(0))
    first(jnp.int32(1))

    def turn(i, _):
        both(i * 2)
        return 0

    lax.fori_loop(1, experts // 2, turn, 0)
    for e in (experts - 2, experts - 1):
        wait(jnp.int32(e))
    for e in (experts - 2, experts - 1):
        second(jnp.int32(e))


def home_kernel(onehot, rows, *refs):
    grads, (keep, send) = refs[:-2], refs[-2:]
    send_home(keep, send, lax.axis_index("etp"), onehot, rows, keep.shape[2], keep.shape[3])
    for s, grad in enumerate(grads):
        for q in range(2):
            send[2 + q, s] = grad[q]


def home_values_kernel(choose, onehot, rows, dots, own_ref, info_ref, *refs):
    keep, send = refs[-2:]
    sources, slots, tokens = onehot.shape
    experts = slots // CAP
    width = keep.shape[3]
    send_home(keep, send, lax.axis_index("etp"), onehot, rows, tokens, width)
    expert = lax.broadcasted_iota(jnp.int32, (experts, tokens), 0)
    mine = (lax.axis_index("expert") * experts + expert).astype(F32)
    for s in range(sources):
        info = own_ref[tokens:tokens + EXTRA, :] if s == 0 else info_ref[s - 1, tokens:tokens + EXTRA, :]
        ids, _, _ = routing(info, choose, tokens)
        chosen = onehot[s].astype(F32).reshape(experts, CAP, tokens)
        share = jnp.sum(chosen * dots[:, s * CAP:(s + 1) * CAP, :], axis=1)
        values = [jnp.sum(jnp.where(ids[k:k + 1, :] == mine, share, 0.0), axis=0, keepdims=True) for k in range(choose)]
        values = jnp.concatenate(values + [jnp.zeros((EXTRA - choose, tokens), F32)], axis=0)
        values = jnp.concatenate([values, jnp.zeros((EXTRA, width - tokens), F32)], axis=1).astype(BF16)
        for home in (keep, send):
            home[0, s, tokens:tokens + EXTRA, :] = values
            home[1, s, tokens:tokens + EXTRA, :] = values


def backward_kernel(
    a0, a1, a2, a3, near_ref,
    gate_ref, up_hbm, down_hbm, act_ref, a_ref, slope_ref, silu_ref, onehot, slot_gate, earlier_ref,
    back_rows, dots, rows_ref, p_ref, q_ref, down_grad,
    up_ref, down_ref, held, up_sems, down_sems, held_sems,
):
    sources, slots, tokens = onehot.shape
    experts = slots // CAP
    width = a0.shape[2]
    me = lax.axis_index("etp")
    start_down, wait_down = ring(down_hbm, down_ref, down_sems)
    start_up, wait_up = ring(up_hbm, up_ref, up_sems)
    for s, here in enumerate((a0, a1, a2, a3)):
        for q in range(4):
            block = near_ref[2 + q // 2, s] if q % 2 else here[q // 2]
            picked = nn(onehot[s], block).astype(BF16).reshape(experts, CAP, width)
            rows_ref[:, s * CAP:(s + 1) * CAP, columns(me, q, width)] = picked

    def slopes(e):
        grad = nt(rows_ref[e], slot_of(down_ref, e))
        activ = act_ref[e].astype(F32)
        dots[e] = jnp.broadcast_to(jnp.sum(activ * grad, axis=1, keepdims=True), dots.shape[1:])
        grad = grad * slot_gate[e][:, 0:1]
        p_ref[e] = (grad * slope_ref[e]).astype(BF16)
        q_ref[e] = (grad * silu_ref[e]).astype(BF16)

    def store(e):
        slot = lax.rem(e, BANKS)
        return pltpu.make_async_copy(held.at[slot], down_grad.at[e], held_sems.at[slot])

    def project(e):
        held[lax.rem(e, BANKS)] = tn(a_ref[e], rows_ref[e]).astype(BF16)
        back = nn(p_ref[e], gate_ref[e]) + nn(q_ref[e], slot_of(up_ref, e))
        back = (back * slot_gate[e][:, 0:1]).astype(BF16)
        at = pl.ds(pl.multiple_of(e * CAP, CAP), CAP)
        for s in range(sources):
            back_rows[s, at, :] = back[s * CAP:(s + 1) * CAP]

    def first(e):
        wait_down(e)
        slopes(e)
        start_down(e)

    def both(e):
        for i in (e, e + 1):
            wait_down(i)
        for i in (e - 2, e - 1):
            wait_up(i)

        @pl.when(e - 2 >= BANKS)
        def _():
            for i in (e - 2, e - 1):
                store(i - BANKS).wait()

        project(e - 2)
        project(e - 1)
        slopes(e)
        slopes(e + 1)
        for i in (e - 2, e - 1):
            store(i).start()
        for i in (e, e + 1):
            start_down(i)
        for i in (e - 2, e - 1):
            start_up(i)

    def last(e):
        wait_up(e)
        store(e - BANKS).wait()

    skewed(experts, first, last, project, both)
    for e in (experts - 2, experts - 1):
        store(jnp.int32(e)).start()
    for e in range(experts - BANKS, experts):
        store(jnp.int32(e)).wait()


def add_kernel(keep, came, *refs):
    near, far = refs[-2:]
    for s in range(near.shape[0]):
        far[s] = (keep[1, s].astype(F32) + came[1, s].astype(F32)).astype(BF16)
        near[s] = (keep[0, s].astype(F32) + came[0, s].astype(F32)).astype(BF16)


def chips_kernel(near, came, *refs):
    parts = refs[-near.shape[0]:]
    for s in range(near.shape[0]):
        parts[s][...] = (near[s].astype(F32) + came[s].astype(F32)).astype(BF16)


def total_kernel(count, *refs):
    total = refs[0][...].astype(F32)
    for ref in refs[1:count]:
        total = total + ref[...].astype(F32)
    rows = refs[count]
    tokens = rows.shape[0]
    rows[...] = total[0:tokens].astype(BF16)
    for values in refs[count + 1:]:
        values[...] = total[tokens:tokens + values.shape[0], 0:values.shape[1]]


BANKS = 8
TURN = 4


def product_kernel(jobs, *refs):
    lefts, rights, outs = (refs[i * len(jobs):(i + 1) * len(jobs)] for i in range(3))
    held, sems = refs[-2:]
    outs = refs[-2 - len(jobs):-2]

    def store(job, e, slot):
        return pltpu.make_async_copy(held.at[slot], outs[job].at[e], sems.at[slot])

    def turn(job, first, done, i, full):
        for pair in range(0, TURN, 2):
            places = [(first + i * TURN + j, lax.rem(done + i * TURN + j, BANKS)) for j in (pair, pair + 1)]
            if full:
                for e, slot in places:
                    store(job, e, slot).wait()
            for e, slot in places:
                held[slot] = tn(lefts[job][e], rights[job][e]).astype(BF16)
            for e, slot in places:
                store(job, e, slot).start()

    done = 0
    for job, (first, last) in enumerate(jobs):
        fresh = max(0, min(BANKS - done, last - first) // TURN)
        for i in range(fresh):
            turn(job, first, done, jnp.int32(i), False)

        def later(i, _, job=job, first=first, done=done):
            turn(job, first, done, i, True)
            return 0

        lax.fori_loop(fresh, (last - first) // TURN, later, 0)
        done = done + last - first
    for slot in range(min(done, BANKS)):
        store(0, jobs[0][0], slot).wait()


def load_kernel(source, target, token, sems):
    token[...] = jnp.zeros_like(token)
    copies = [pltpu.make_async_copy(source.at[e], target.at[e], sems.at[e]) for e in range(source.shape[0])]
    for copy in copies:
        copy.start()
    for copy in copies:
        copy.wait()


def in_vmem(weight):
    return pl.pallas_call(
        load_kernel,
        in_specs=[pl.BlockSpec(memory_space=pltpu.HBM)],
        out_specs=[pl.BlockSpec(memory_space=pltpu.VMEM)] * 2,
        out_shape=[pltpu.VMEM(weight.shape, BF16), jax.ShapeDtypeStruct((8, 128), F32)],
        scratch_shapes=[pltpu.SemaphoreType.DMA((weight.shape[0],))],
        compiler_params=pltpu.CompilerParams(vmem_limit_bytes=4 * 1024 * 1024),
        cost_estimate=pl.CostEstimate(flops=0, bytes_accessed=2 * weight.size, transcendentals=0),
    )(pltpu.with_memory_space_constraint(weight, pltpu.HBM))


def join_kernel(count, *refs):
    for i in range(count):
        refs[-1][i] = refs[i][...]


def join(arrays, *there):
    return kernel_call(
        functools.partial(join_kernel, len(arrays)),
        [jax.ShapeDtypeStruct((len(arrays),) + arrays[0].shape, arrays[0].dtype)],
        [],
        0,
        limit=2,
    )(*arrays, *there)[0]


def kernel_call(kernel, out_shape, scratch, flops, out_specs=None, limit=4, in_hbm=(), aliases={}):
    def call(*operands):
        specs = [
            pl.BlockSpec(memory_space=pltpu.HBM if i in in_hbm else pltpu.SMEM if x.ndim == 1 else pltpu.VMEM)
            for i, x in enumerate(operands)
        ]
        operands = [
            pltpu.with_memory_space_constraint(x, pltpu.HBM) if i in in_hbm else x for i, x in enumerate(operands)
        ]
        return pl.pallas_call(
            kernel,
            in_specs=specs,
            out_specs=out_specs or [pl.BlockSpec(memory_space=pltpu.VMEM)] * len(out_shape),
            out_shape=out_shape,
            scratch_shapes=scratch,
            input_output_aliases=aliases,
            compiler_params=pltpu.CompilerParams(vmem_limit_bytes=limit * 1024 * 1024),
            cost_estimate=pl.CostEstimate(flops=flops, bytes_accessed=flops // 32, transcendentals=0),
        )(*operands)

    return call


def weight_grads(jobs, begun=None, *earlier):
    count = len(jobs)
    lefts, rights = [job[0] for job in jobs], [job[1] for job in jobs]
    experts, rows, units = lefts[0].shape
    model = rights[0].shape[2]
    shape = jax.ShapeDtypeStruct((experts, units, model), BF16)
    work = sum(job[3] - job[2] for job in jobs)
    more = [] if begun is None else [begun]
    return kernel_call(
        functools.partial(product_kernel, [job[2:] for job in jobs]),
        [shape] * count,
        [pltpu.VMEM((BANKS, units, model), BF16), pltpu.SemaphoreType.DMA((BANKS,))],
        2 * work * rows * units * model,
        out_specs=[pl.BlockSpec(memory_space=pltpu.HBM)] * count,
        limit=8,
        in_hbm=(2 * count,) if more else (),
        aliases={2 * count: 0} if more else {},
    )(*lefts, *rights, *more, *earlier)


def swap(array, bit, axis="etp"):
    count = lax.axis_size(axis)
    return lax.ppermute(array, axis, [(i, i ^ bit) for i in range(count)])


def add_cores(keep, came, *earlier):
    shape = jax.ShapeDtypeStruct(keep.shape[1:], BF16)
    hbm = [2] if earlier else []
    return kernel_call(add_kernel, [shape, shape], [], 0, limit=2, in_hbm=hbm)(keep, came, *earlier)


def add_chips(near, far, *earlier):
    sources = near.shape[0]
    shape = jax.ShapeDtypeStruct(near.shape[1:], BF16)
    hbm = [2] if earlier else []
    parts = kernel_call(chips_kernel, [shape] * sources, [], 0, limit=2, in_hbm=hbm)(near, far, *earlier)
    return parts[0], [swap(parts[s], s, "expert") for s in range(1, sources)]


def gathered_body(
    hidden_in, out_grad, expert_ids, gate_values, capacity_blocks, gate_weight, up_weight, down_weight
):
    sources = lax.axis_size("expert")
    tokens, width = hidden_in.shape
    choose = expert_ids.shape[1]
    local_experts, units, model = down_weight.shape
    slots = local_experts * CAP
    rows = sources * CAP
    gate_t, gate_there = in_vmem(jnp.swapaxes(gate_weight, 1, 2))
    up_t = jnp.swapaxes(up_weight, 1, 2)
    product = 2 * local_experts * rows * units * model
    held = lambda *shape, kind=BF16: pltpu.VMEM(shape, kind)
    sent = lambda *shape: jax.ShapeDtypeStruct(shape, BF16)

    own = kernel_call(
        pack_kernel,
        [sent(tokens + EXTRA, width)],
        [pltpu.VMEM((choose, tokens), jnp.int32), pltpu.VMEM((choose, tokens), F32), pltpu.SemaphoreType.DMA((3,))],
        0,
        limit=2,
        in_hbm=(0, 1, 2),
    )(hidden_in, expert_ids.T, gate_values.T)[0]
    came = [swap(own, s, "expert") for s in range(1, sources)]
    own_across = swap(own, 2)
    grad_across = swap(out_grad, 2)
    came = join(came, gate_there, own_across, grad_across)
    came_across_there = swap(came, 2)
    across_near = swap(own_across, 1)
    grads = join([out_grad, grad_across], came)
    grads = [grads] + [swap(grads, s, "expert") for s in range(1, sources)]

    half_rows, onehot, slot_gate = kernel_call(
        functools.partial(routing_kernel, choose),
        [
            held(local_experts, rows, model // 2),
            held(sources, slots, tokens),
            held(local_experts, rows, tokens, kind=F32),
        ],
        [],
        product // 4,
    )(capacity_blocks, own, swap(own, 1), came, swap(came, 1), across_near)
    came_across = join([came_across_there], onehot, grads[1])[0]
    out_rows, x_rows, activ, scaled, slope, silu = kernel_call(
        forward_kernel,
        [
            held(sources, slots, model),
            held(local_experts, rows, model),
            held(local_experts, rows, units),
            held(local_experts, rows, units),
            held(local_experts, rows, units, kind=F32),
            held(local_experts, rows, units, kind=F32),
        ],
        [pltpu.VMEM((RING, units, model), BF16)] * 2 + [pltpu.SemaphoreType.DMA((RING,))] * 2,
        3 * product,
        limit=14,
        in_hbm=(5, 6),
    )(
        own_across, across_near, came_across, swap(came_across, 1),
        gate_t, up_t, down_weight, half_rows, onehot, slot_gate, grads[0],
    )

    keep, send = kernel_call(
        home_kernel,
        [sent(2, sources, tokens, width), sent(4, sources, tokens, width)],
        [],
        2 * slots * sources * tokens * model,
        limit=2,
    )(onehot, out_rows, *grads)
    near = swap(send, 1)
    out_near, out_far = add_cores(keep, near)
    back_rows, dots, y_rows, gate_part, up_part, down_grad = kernel_call(
        backward_kernel,
        [
            held(sources, slots, model),
            held(local_experts, rows, tokens, kind=F32),
            held(local_experts, rows, model),
            held(local_experts, rows, units),
            held(local_experts, rows, units),
            sent(local_experts, units, model),
        ],
        [
            pltpu.VMEM((RING, units, model), BF16),
            pltpu.VMEM((RING, units, model), BF16),
            pltpu.VMEM((BANKS, units, model), BF16),
            pltpu.SemaphoreType.DMA((RING,)),
            pltpu.SemaphoreType.DMA((RING,)),
            pltpu.SemaphoreType.DMA((BANKS,)),
        ],
        4 * product,
        out_specs=[pl.BlockSpec(memory_space=pltpu.VMEM)] * 5 + [pl.BlockSpec(memory_space=pltpu.HBM)],
        limit=20,
        in_hbm=(6, 7),
    )(
        *grads, near,
        gate_t, up_t, down_weight, activ, scaled, slope, silu, onehot, slot_gate, out_near,
    )

    out_own, out_parts = add_chips(out_near, swap(out_far, 2))
    keep, send = kernel_call(
        functools.partial(home_values_kernel, choose),
        [sent(2, sources, tokens + EXTRA, width)] * 2,
        [],
        2 * slots * sources * tokens * model,
        limit=2,
    )(onehot, back_rows, dots, own, came, out_own)
    some = local_experts // 2
    (up_grad,) = weight_grads([(up_part, x_rows, 0, some)])
    back_near, back_far = add_cores(keep, swap(send, 1), up_grad)
    (up_grad,) = weight_grads([(up_part, x_rows, some, local_experts)], up_grad, back_near)
    (layer_out,) = kernel_call(functools.partial(total_kernel, sources), [sent(tokens, width)], [], 0, limit=2)(
        out_own, *out_parts
    )
    back_own, back_parts = add_chips(back_near, swap(back_far, 2), up_grad)
    (gate_grad,) = weight_grads([(gate_part, x_rows, 0, local_experts)], None, back_own)
    input_grad, value_grad = kernel_call(
        functools.partial(total_kernel, sources),
        [sent(tokens, width), jax.ShapeDtypeStruct((choose, tokens), F32)],
        [],
        0,
        limit=2,
    )(back_own, *back_parts)
    return (
        layer_out,
        input_grad,
        value_grad.T,
        jnp.swapaxes(gate_grad, 1, 2),
        jnp.swapaxes(up_grad, 1, 2),
        down_grad,
    )


def slot_layout(expert_ids, capacity_blocks):
    tokens_here, choose = expert_ids.shape
    experts = capacity_blocks.shape[0]
    flat_ids = expert_ids.reshape(-1)
    onehot = (flat_ids[:, None] == jnp.arange(experts, dtype=jnp.int32)[None, :]).astype(jnp.int32)
    before = jnp.cumsum(onehot, axis=0) - onehot
    ranks = jnp.sum(before * onehot, axis=1)
    limits = jnp.sum(onehot * capacity_blocks[None, :], axis=1) * BLK
    kept = ranks < limits
    slots = jnp.where(kept, flat_ids * CAP + ranks, experts * CAP)
    token_index = jnp.arange(tokens_here * choose, dtype=jnp.int32) // choose
    owners = (
        jnp.full((experts * CAP,), tokens_here, jnp.int32).at[slots].set(token_index, mode="drop")
    )
    return (kept.reshape(tokens_here, choose), slots.reshape(tokens_here, choose), owners)


def outgoing(rows, owners, experts, scale):
    padded = jnp.concatenate([rows, jnp.zeros((1, rows.shape[1]), rows.dtype)], 0)
    picked = padded[owners]
    if scale is not None:
        picked = (scale[:, None] * picked.astype(jnp.float32)).astype(jnp.bfloat16)
    return picked.reshape(experts, CAP, rows.shape[1])


def local_grads(hidden_gate, hidden_up, act_grad):
    sigma = jax.nn.sigmoid(hidden_gate)
    gate_part = (act_grad * hidden_up * sigma * (1.0 + hidden_gate * (1.0 - sigma))).astype(
        jnp.bfloat16
    )
    up_part = (act_grad * jax.nn.silu(hidden_gate)).astype(jnp.bfloat16)
    return (gate_part, up_part)


def combine(back, slots, weights):
    padded = jnp.concatenate([back, jnp.zeros((1, back.shape[1]), back.dtype)], 0)
    picked = padded[slots].astype(jnp.float32)
    return (jnp.einsum("tk,tkw->tw", weights, picked), picked)


def dispatched_body(
    hidden_in,
    out_grad,
    expert_ids,
    gate_values,
    capacity_blocks,
    gate_weight,
    up_weight,
    down_weight,
):
    experts = capacity_blocks.shape[0]
    sources = lax.axis_size("expert")
    local_experts = gate_weight.shape[0]
    kept, slots, owners = slot_layout(expert_ids, capacity_blocks)
    weights = jnp.where(kept, gate_values, 0.0)
    slot_gates = (
        jnp.zeros((experts * CAP,), jnp.float32)
        .at[slots.reshape(-1)]
        .set(weights.reshape(-1), mode="drop")
    )
    send_in = outgoing(hidden_in, owners, experts, None)
    send_grad = outgoing(out_grad, owners, experts, slot_gates)
    recv_in, recv_grad = (
        lax.all_to_all(send_in, "expert", split_axis=0, concat_axis=0, tiled=True),
        lax.all_to_all(send_grad, "expert", split_axis=0, concat_axis=0, tiled=True),
    )
    share = recv_in.shape[2]
    share_in = recv_in.reshape(sources, local_experts, CAP, share)
    share_grad = recv_grad.reshape(sources, local_experts, CAP, share)
    piece = lax.all_gather(share_in, "etp", axis=3, tiled=True)
    hidden_gate = jnp.einsum(
        "secn,enf->secf", piece, gate_weight, preferred_element_type=jnp.float32
    )
    hidden_up = jnp.einsum("secn,enf->secf", piece, up_weight, preferred_element_type=jnp.float32)
    activ = (jax.nn.silu(hidden_gate) * hidden_up).astype(jnp.bfloat16)
    piece = lax.all_gather(share_grad, "etp", axis=3, tiled=True)
    act_grad = jnp.einsum("secn,efn->secf", piece, down_weight, preferred_element_type=jnp.float32)
    columns = jnp.einsum("secf,secn->efn", activ, piece, preferred_element_type=jnp.float32)
    act_grad, down_grad = (act_grad, columns)
    gate_part, up_part = local_grads(hidden_gate, hidden_up, act_grad)
    stacked = jnp.stack([gate_part, up_part])
    weight_grads = jnp.einsum(
        "secn,gsecf->genf",
        lax.all_gather(share_in, "etp", axis=3, tiled=True),
        stacked,
        preferred_element_type=jnp.float32,
    )
    out_part = jnp.einsum("secf,efd->secd", activ, down_weight, preferred_element_type=jnp.float32)
    back_part = jnp.einsum(
        "secf,edf->secd", gate_part, gate_weight, preferred_element_type=jnp.float32
    )
    back_part = back_part + jnp.einsum(
        "secf,edf->secd", up_part, up_weight, preferred_element_type=jnp.float32
    )
    out_rows = lax.psum_scatter(
        out_part.astype(jnp.bfloat16), "etp", scatter_dimension=3, tiled=True
    )
    home_out = lax.all_to_all(out_rows, "expert", split_axis=0, concat_axis=0, tiled=True)
    share_width = home_out.shape[3]
    layer_sum, picked = combine(home_out.reshape(experts * CAP, share_width), slots, weights)
    dot_part = jnp.einsum("tw,tkw->tk", out_grad.astype(jnp.float32), picked) * kept.astype(
        jnp.float32
    )
    gate_value_grad = lax.psum(dot_part, "etp")
    back_rows = lax.psum_scatter(
        back_part.astype(jnp.bfloat16), "etp", scatter_dimension=3, tiled=True
    )
    home_back = lax.all_to_all(back_rows, "expert", split_axis=0, concat_axis=0, tiled=True)
    input_sum, returned = combine(home_back.reshape(experts * CAP, share_width), slots, weights)
    return (
        layer_sum.astype(jnp.bfloat16),
        input_sum.astype(jnp.bfloat16),
        gate_value_grad,
        weight_grads[0].astype(jnp.bfloat16),
        weight_grads[1].astype(jnp.bfloat16),
        down_grad.astype(jnp.bfloat16),
    )


def body(*operands):
    hidden_in, gate_weight = operands[0], operands[5]
    if lax.axis_size("expert") == 4 and lax.axis_size("etp") == 4 and hidden_in.shape[0] <= gate_weight.shape[0] * CAP:
        return gathered_body(*operands)
    return dispatched_body(*operands)


def solution(mesh):
    in_specs = (
        P(("groups", "expert"), "etp"),
        P(("groups", "expert"), "etp"),
        P(("groups", "expert"), None),
        P(("groups", "expert"), None),
        P("groups"),
        P("expert", None, "etp"),
        P("expert", None, "etp"),
        P("expert", "etp", None),
    )
    out_specs = (
        P(("groups", "expert"), "etp"),
        P(("groups", "expert"), "etp"),
        P(("groups", "expert"), None),
        P(("groups", "expert"), None, "etp"),
        P(("groups", "expert"), None, "etp"),
        P(("groups", "expert"), "etp", None),
    )
    return jax.shard_map(body, mesh=mesh, in_specs=in_specs, out_specs=out_specs, check_vma=False)
```

```python
import functools

import jax
import jax.numpy as jnp
from jax import lax
from jax.experimental import pallas as pl
from jax.experimental.pallas import tpu as pltpu
from jax.sharding import PartitionSpec as P

CAP = 16
BLK = 4
EXTRA = 16
F32 = jnp.float32
BF16 = jnp.bfloat16


def nn(a, b):
    return lax.dot_general(a, b, (((1,), (0,)), ((), ())), preferred_element_type=F32)


def nt(a, b):
    return lax.dot_general(a, b, (((1,), (1,)), ((), ())), preferred_element_type=F32)


def tn(a, b):
    return lax.dot_general(a, b, (((0,), (0,)), ((), ())), preferred_element_type=F32)


def pack_kernel(hidden_hbm, ids_hbm, gates_hbm, own_ref, ids_ref, gates_ref, sems):
    tokens, width = hidden_hbm.shape
    choose = ids_ref.shape[0]
    copies = [
        pltpu.make_async_copy(hidden_hbm, own_ref.at[pl.ds(0, tokens)], sems.at[0]),
        pltpu.make_async_copy(ids_hbm, ids_ref, sems.at[1]),
        pltpu.make_async_copy(gates_hbm, gates_ref, sems.at[2]),
    ]
    for copy in copies:
        copy.start()
    for copy in copies:
        copy.wait()
    gates = gates_ref[...]
    high = gates.astype(BF16).astype(F32)
    fill = jnp.zeros((8 - choose, tokens), F32)
    top = jnp.concatenate([jnp.concatenate([ids_ref[...].astype(F32), fill], axis=0), jnp.concatenate([high, fill], axis=0)], axis=1)
    low = jnp.concatenate([jnp.concatenate([gates - high, fill], axis=0), jnp.zeros((8, width - tokens), F32)], axis=1)
    own_ref[tokens:tokens + EXTRA, :] = jnp.concatenate([top, low], axis=0).astype(BF16)


def routing(info, choose, tokens):
    info = info.astype(F32)
    return info[0:choose, 0:tokens], info[0:choose, tokens:2 * tokens], info[8:8 + choose, 0:tokens]


def columns(me, mask, width):
    return pl.ds(pl.multiple_of(lax.bitwise_xor(me, mask) * width, width), width)


def send_home(home_keep, home_send, me, onehot, rows, tokens, width):
    for s in range(onehot.shape[0]):
        for q in range(4):
            home = home_send if q % 2 else home_keep
            home[q // 2, s, 0:tokens, :] = tn(onehot[s], rows[s, :, columns(me, q, width)]).astype(BF16)


RING = 8


def ring(weight, slots, sems, columns=None):
    depth = slots.shape[0]

    def load(e):
        slot = lax.rem(e, depth)
        source = weight.at[e] if columns is None else weight.at[e, :, columns]
        return pltpu.make_async_copy(source, slots.at[slot], sems.at[slot])

    def start(e):
        @pl.when(e < weight.shape[0])
        def _():
            load(e).start()

    for e in range(min(depth, weight.shape[0])):
        load(jnp.int32(e)).start()
    if depth >= weight.shape[0]:
        return lambda e: None, lambda e: load(e).wait()
    return lambda e: start(e + depth), lambda e: load(e).wait()


def slot_of(slots, e):
    return slots[lax.rem(e, slots.shape[0])]


def half(me, other, size):
    return pl.ds(pl.multiple_of(lax.bitwise_xor(me // 2, other) * size, size), size)


def gather_half(me, onehot, blocks, rows_ref, experts, width, tokens, start, offset):
    for q, block in enumerate(blocks):
        picked = nn(onehot, block).astype(BF16).reshape(experts, CAP, width)
        at = pl.multiple_of(lax.rem(lax.bitwise_xor(me, q), 2) * width + offset, width)
        rows_ref[:, start:start + CAP, pl.ds(at, width)] = picked


def routing_kernel(
    choose, capacity_ref, o0, o1, b0, b1, earlier_ref, rows_ref, onehot, slot_gate
):
    sources, slots, tokens = onehot.shape
    experts = slots // CAP
    width = b0.shape[2]
    me = lax.axis_index("etp")
    first = lax.axis_index("expert") * experts
    row = lax.broadcasted_iota(jnp.int32, (tokens, tokens), 0)
    col = lax.broadcasted_iota(jnp.int32, (tokens, tokens), 1)
    before = jnp.where(row < col, 1.0, 0.0).astype(BF16)
    ones = jnp.ones((tokens, tokens), BF16)
    expert = lax.broadcasted_iota(jnp.int32, (experts, tokens), 0)
    mine = (first + expert).astype(F32)
    limit = jnp.zeros((experts, tokens), jnp.int32)
    for e in range(experts):
        limit = jnp.where(expert == e, capacity_ref[first + e] * BLK, limit)
    limit = limit.astype(F32)
    place = lax.broadcasted_iota(jnp.int32, (experts, CAP, tokens), 1).astype(F32)
    for s in range(sources):
        block = [o[...] for o in (o0, o1)] if s == 0 else [b[s - 1] for b in (b0, b1)]
        ids, highs, lows = routing(block[0][tokens:tokens + EXTRA, :], choose, tokens)
        named = jnp.zeros((experts, tokens), F32)
        high, low = named, named
        for k in range(choose):
            hit = ids[k:k + 1, :] == mine
            named = named + jnp.where(hit, 1.0, 0.0)
            high = high + jnp.where(hit, highs[k:k + 1, :], 0.0)
            low = low + jnp.where(hit, lows[k:k + 1, :], 0.0)
        rank = nn(named.astype(BF16), before)
        rank = jnp.where((named > 0.5) & (rank < limit), rank, -1.0)
        taken = rank[:, None, :] == place
        spread = lambda x: jnp.where(taken, x[:, None, :], 0.0).reshape(slots, tokens).astype(BF16)
        gates = nn(spread(high), ones) + nn(spread(low), ones)
        slot_gate[:, s * CAP:(s + 1) * CAP, :] = gates.reshape(experts, CAP, tokens)
        table = jnp.where(taken, 1.0, 0.0).reshape(slots, tokens).astype(BF16)
        onehot[s] = table
        gather_half(me, table, [x[0:tokens, :] for x in block], rows_ref, experts, width, tokens, s * CAP, 0)


def forward_kernel(
    o2, o3, b2, b3, gate_ref, up_ref, down_hbm, half_ref, onehot, slot_gate, later_ref,
    out_rows, rows_ref, act_ref, a_ref, slope_ref, silu_ref,
    down_ref, down_sems,
):
    sources, slots, tokens = onehot.shape
    experts = slots // CAP
    width = b2.shape[2]
    me = lax.axis_index("etp")
    start_down, wait_down = ring(down_hbm, down_ref, down_sems)
    rows_ref[:, :, half(me, 0, 2 * width)] = half_ref[...]
    other = lax.bitwise_xor(me // 2, 1) * 2 * width
    for s in range(sources):
        block = [o[0:tokens, :] for o in (o2, o3)] if s == 0 else [b[s - 1, 0:tokens, :] for b in (b2, b3)]
        gather_half(me, onehot[s], block, rows_ref, experts, width, tokens, s * CAP, other)

    def activate(e):
        x = rows_ref[e]
        hidden_gate = nt(x, gate_ref[e])
        hidden_up = nt(x, up_ref[e])
        sigma = jax.nn.sigmoid(hidden_gate)
        silu = hidden_gate * sigma
        activ = (silu * hidden_up).astype(BF16)
        act_ref[e] = activ
        slope_ref[e] = hidden_up * sigma * (1.0 + hidden_gate * (1.0 - sigma))
        silu_ref[e] = silu
        a_ref[e] = (activ.astype(F32) * slot_gate[e][:, 0:1]).astype(BF16)

    def project(e):
        out = nn(a_ref[e], slot_of(down_ref, e)).astype(BF16)
        at = pl.ds(pl.multiple_of(e * CAP, CAP), CAP)
        for s in range(sources):
            out_rows[s, at, :] = out[s * CAP:(s + 1) * CAP]

    def both(e):
        for i in (e - 2, e - 1):
            wait_down(i)
        project(e - 2)
        project(e - 1)
        activate(e)
        activate(e + 1)
        for i in (e - 2, e - 1):
            start_down(i)

    skewed(experts, activate, wait_down, project, both)


def skewed(experts, first, wait, second, both):
    first(jnp.int32(0))
    first(jnp.int32(1))

    def turn(i, _):
        both(i * 2)
        return 0

    lax.fori_loop(1, experts // 2, turn, 0)
    for e in (experts - 2, experts - 1):
        wait(jnp.int32(e))
    for e in (experts - 2, experts - 1):
        second(jnp.int32(e))


def home_kernel(onehot, rows, *refs):
    grads, (keep, send) = refs[:-2], refs[-2:]
    send_home(keep, send, lax.axis_index("etp"), onehot, rows, keep.shape[2], keep.shape[3])
    for s, grad in enumerate(grads):
        for q in range(2):
            send[2 + q, s] = grad[q]


def home_values_kernel(choose, onehot, rows, dots, own_ref, info_ref, *refs):
    keep, send = refs[-2:]
    sources, slots, tokens = onehot.shape
    experts = slots // CAP
    width = keep.shape[3]
    send_home(keep, send, lax.axis_index("etp"), onehot, rows, tokens, width)
    expert = lax.broadcasted_iota(jnp.int32, (experts, tokens), 0)
    mine = (lax.axis_index("expert") * experts + expert).astype(F32)
    for s in range(sources):
        info = own_ref[tokens:tokens + EXTRA, :] if s == 0 else info_ref[s - 1, tokens:tokens + EXTRA, :]
        ids, _, _ = routing(info, choose, tokens)
        chosen = onehot[s].astype(F32).reshape(experts, CAP, tokens)
        share = jnp.sum(chosen * dots[:, s * CAP:(s + 1) * CAP, :], axis=1)
        values = [jnp.sum(jnp.where(ids[k:k + 1, :] == mine, share, 0.0), axis=0, keepdims=True) for k in range(choose)]
        values = jnp.concatenate(values + [jnp.zeros((EXTRA - choose, tokens), F32)], axis=0)
        values = jnp.concatenate([values, jnp.zeros((EXTRA, width - tokens), F32)], axis=1).astype(BF16)
        for home in (keep, send):
            home[0, s, tokens:tokens + EXTRA, :] = values
            home[1, s, tokens:tokens + EXTRA, :] = values


def backward_kernel(
    a0, a1, a2, a3, near_ref,
    gate_ref, up_hbm, down_hbm, act_ref, slope_ref, silu_ref, onehot, slot_gate, earlier_ref,
    back_rows, dots, rows_ref, p_ref, q_ref,
    up_ref, down_ref, up_sems, down_sems,
):
    sources, slots, tokens = onehot.shape
    experts = slots // CAP
    width = a0.shape[2]
    me = lax.axis_index("etp")
    start_down, wait_down = ring(down_hbm, down_ref, down_sems)
    start_up, wait_up = ring(up_hbm, up_ref, up_sems)
    for s, here in enumerate((a0, a1, a2, a3)):
        for q in range(4):
            block = near_ref[2 + q // 2, s] if q % 2 else here[q // 2]
            picked = nn(onehot[s], block).astype(BF16).reshape(experts, CAP, width)
            rows_ref[:, s * CAP:(s + 1) * CAP, columns(me, q, width)] = picked

    def slopes(e):
        grad = nt(rows_ref[e], slot_of(down_ref, e))
        activ = act_ref[e].astype(F32)
        dots[e] = jnp.broadcast_to(jnp.sum(activ * grad, axis=1, keepdims=True), dots.shape[1:])
        grad = grad * slot_gate[e][:, 0:1]
        p_ref[e] = (grad * slope_ref[e]).astype(BF16)
        q_ref[e] = (grad * silu_ref[e]).astype(BF16)

    def project(e):
        back = nn(p_ref[e], gate_ref[e]) + nn(q_ref[e], slot_of(up_ref, e))
        back = (back * slot_gate[e][:, 0:1]).astype(BF16)
        at = pl.ds(pl.multiple_of(e * CAP, CAP), CAP)
        for s in range(sources):
            back_rows[s, at, :] = back[s * CAP:(s + 1) * CAP]

    def first(e):
        wait_down(e)
        slopes(e)
        start_down(e)

    def both(e):
        for i in (e, e + 1):
            wait_down(i)
        for i in (e - 2, e - 1):
            wait_up(i)
        project(e - 2)
        project(e - 1)
        slopes(e)
        slopes(e + 1)
        for i in (e, e + 1):
            start_down(i)
        for i in (e - 2, e - 1):
            start_up(i)

    skewed(experts, first, wait_up, project, both)


def add_kernel(keep, came, *refs):
    near, far = refs[-2:]
    for s in range(near.shape[0]):
        far[s] = (keep[1, s].astype(F32) + came[1, s].astype(F32)).astype(BF16)
        near[s] = (keep[0, s].astype(F32) + came[0, s].astype(F32)).astype(BF16)


def chips_kernel(near, came, *refs):
    parts = refs[-near.shape[0]:]
    for s in range(near.shape[0]):
        parts[s][...] = (near[s].astype(F32) + came[s].astype(F32)).astype(BF16)


def pairs_kernel(near, came, *refs):
    for s in range(near.shape[0]):
        refs[-2 + s % 2][s // 2] = (near[s].astype(F32) + came[s].astype(F32)).astype(BF16)


def step_kernel(even, came, *refs):
    for s in range(2):
        refs[-2 + s][...] = (even[s].astype(F32) + came[s].astype(F32)).astype(BF16)


def total_kernel(count, *refs):
    total = refs[0][...].astype(F32)
    for ref in refs[1:count]:
        total = total + ref[...].astype(F32)
    rows = refs[count]
    tokens = rows.shape[0]
    rows[...] = total[0:tokens].astype(BF16)
    for values in refs[count + 1:]:
        values[...] = total[tokens:tokens + values.shape[0], 0:values.shape[1]]


BANKS = 8
TURN = 4


def product_kernel(jobs, *refs):
    lefts, rights, outs = (refs[i * len(jobs):(i + 1) * len(jobs)] for i in range(3))
    held, sems = refs[-2:]
    outs = refs[-2 - len(jobs):-2]

    def store(job, e, slot):
        return pltpu.make_async_copy(held.at[slot], outs[job].at[e], sems.at[slot])

    def turn(job, first, done, i, full):
        for pair in range(0, TURN, 2):
            places = [(first + i * TURN + j, lax.rem(done + i * TURN + j, BANKS)) for j in (pair, pair + 1)]
            if full:
                for e, slot in places:
                    store(job, e, slot).wait()
            for e, slot in places:
                held[slot] = tn(lefts[job][e], rights[job][e]).astype(BF16)
            for e, slot in places:
                store(job, e, slot).start()

    done = 0
    for job, (first, last) in enumerate(jobs):
        fresh = max(0, min(BANKS - done, last - first) // TURN)
        for i in range(fresh):
            turn(job, first, done, jnp.int32(i), False)

        def later(i, _, job=job, first=first, done=done):
            turn(job, first, done, i, True)
            return 0

        lax.fori_loop(fresh, (last - first) // TURN, later, 0)
        done = done + last - first
    for slot in range(min(done, BANKS)):
        store(0, jobs[0][0], slot).wait()


def load_kernel(source, target, token, sems):
    token[...] = jnp.zeros_like(token)
    copies = [pltpu.make_async_copy(source.at[e], target.at[e], sems.at[e]) for e in range(source.shape[0])]
    for copy in copies:
        copy.start()
    for copy in copies:
        copy.wait()


def in_vmem(weight):
    return pl.pallas_call(
        load_kernel,
        in_specs=[pl.BlockSpec(memory_space=pltpu.HBM)],
        out_specs=[pl.BlockSpec(memory_space=pltpu.VMEM)] * 2,
        out_shape=[pltpu.VMEM(weight.shape, BF16), jax.ShapeDtypeStruct((8, 128), F32)],
        scratch_shapes=[pltpu.SemaphoreType.DMA((weight.shape[0],))],
        compiler_params=pltpu.CompilerParams(vmem_limit_bytes=4 * 1024 * 1024),
        cost_estimate=pl.CostEstimate(flops=0, bytes_accessed=2 * weight.size, transcendentals=0),
    )(pltpu.with_memory_space_constraint(weight, pltpu.HBM))


def join_kernel(count, *refs):
    for i in range(count):
        refs[-1][i] = refs[i][...]


def join(arrays, *there):
    return kernel_call(
        functools.partial(join_kernel, len(arrays)),
        [jax.ShapeDtypeStruct((len(arrays),) + arrays[0].shape, arrays[0].dtype)],
        [],
        0,
        limit=2,
    )(*arrays, *there)[0]


def kernel_call(kernel, out_shape, scratch, flops, out_specs=None, limit=4, in_hbm=(), aliases={}):
    def call(*operands):
        specs = [
            pl.BlockSpec(memory_space=pltpu.HBM if i in in_hbm else pltpu.SMEM if x.ndim == 1 else pltpu.VMEM)
            for i, x in enumerate(operands)
        ]
        operands = [
            pltpu.with_memory_space_constraint(x, pltpu.HBM) if i in in_hbm else x for i, x in enumerate(operands)
        ]
        return pl.pallas_call(
            kernel,
            in_specs=specs,
            out_specs=out_specs or [pl.BlockSpec(memory_space=pltpu.VMEM)] * len(out_shape),
            out_shape=out_shape,
            scratch_shapes=scratch,
            input_output_aliases=aliases,
            compiler_params=pltpu.CompilerParams(vmem_limit_bytes=limit * 1024 * 1024),
            cost_estimate=pl.CostEstimate(flops=flops, bytes_accessed=flops // 32, transcendentals=0),
        )(*operands)

    return call


def weight_grads(jobs, begun=None, *earlier):
    count = len(jobs)
    lefts, rights = [job[0] for job in jobs], [job[1] for job in jobs]
    experts, rows, units = lefts[0].shape
    model = rights[0].shape[2]
    shape = jax.ShapeDtypeStruct((experts, units, model), BF16)
    work = sum(job[3] - job[2] for job in jobs)
    more = [] if begun is None else [begun]
    return kernel_call(
        functools.partial(product_kernel, [job[2:] for job in jobs]),
        [shape] * count,
        [pltpu.VMEM((BANKS, units, model), BF16), pltpu.SemaphoreType.DMA((BANKS,))],
        2 * work * rows * units * model,
        out_specs=[pl.BlockSpec(memory_space=pltpu.HBM)] * count,
        limit=8,
        in_hbm=(2 * count,) if more else (),
        aliases={2 * count: 0} if more else {},
    )(*lefts, *rights, *more, *earlier)


def swap(array, bit, axis="etp"):
    count = lax.axis_size(axis)
    return lax.ppermute(array, axis, [(i, i ^ bit) for i in range(count)])


def add_cores(keep, came, *earlier):
    shape = jax.ShapeDtypeStruct(keep.shape[1:], BF16)
    hbm = [2] if earlier else []
    return kernel_call(add_kernel, [shape, shape], [], 0, limit=2, in_hbm=hbm)(keep, came, *earlier)


def add_chips(near, far, *earlier):
    sources = near.shape[0]
    shape = jax.ShapeDtypeStruct(near.shape[1:], BF16)
    hbm = [2] if earlier else []
    parts = kernel_call(chips_kernel, [shape] * sources, [], 0, limit=2, in_hbm=hbm)(near, far, *earlier)
    return parts[0], [swap(parts[s], s, "expert") for s in range(1, sources)]


def gathered_body(
    hidden_in, out_grad, expert_ids, gate_values, capacity_blocks, gate_weight, up_weight, down_weight
):
    sources = lax.axis_size("expert")
    tokens, width = hidden_in.shape
    choose = expert_ids.shape[1]
    local_experts, units, model = down_weight.shape
    slots = local_experts * CAP
    rows = sources * CAP
    gate_t, gate_there = in_vmem(jnp.swapaxes(gate_weight, 1, 2))
    up_t, up_there = in_vmem(jnp.swapaxes(up_weight, 1, 2))
    product = 2 * local_experts * rows * units * model
    held = lambda *shape, kind=BF16: pltpu.VMEM(shape, kind)
    sent = lambda *shape: jax.ShapeDtypeStruct(shape, BF16)

    own = kernel_call(
        pack_kernel,
        [sent(tokens + EXTRA, width)],
        [pltpu.VMEM((choose, tokens), jnp.int32), pltpu.VMEM((choose, tokens), F32), pltpu.SemaphoreType.DMA((3,))],
        0,
        limit=2,
        in_hbm=(0, 1, 2),
    )(hidden_in, expert_ids.T, gate_values.T)[0]
    came = [swap(own, s, "expert") for s in range(1, sources)]
    own_across = swap(own, 2)
    grad_across = swap(out_grad, 2)
    came = join(came, gate_there, own_across, grad_across)
    came_across_there = swap(came, 2)
    across_near = swap(own_across, 1)
    grads = join([out_grad, grad_across], came)
    grads = [grads] + [swap(grads, s, "expert") for s in range(1, sources)]

    half_rows, onehot, slot_gate = kernel_call(
        functools.partial(routing_kernel, choose),
        [
            held(local_experts, rows, model // 2),
            held(sources, slots, tokens),
            held(local_experts, rows, tokens, kind=F32),
        ],
        [],
        product // 4,
    )(capacity_blocks, own, swap(own, 1), came, swap(came, 1), across_near)
    came_across = join([came_across_there], onehot, up_there, grads[1])[0]
    out_rows, x_rows, activ, scaled, slope, silu = kernel_call(
        forward_kernel,
        [
            held(sources, slots, model),
            held(local_experts, rows, model),
            held(local_experts, rows, units),
            held(local_experts, rows, units),
            held(local_experts, rows, units, kind=F32),
            held(local_experts, rows, units, kind=F32),
        ],
        [pltpu.VMEM((RING, units, model), BF16), pltpu.SemaphoreType.DMA((RING,))],
        3 * product,
        limit=8,
        in_hbm=(6,),
    )(
        own_across, across_near, came_across, swap(came_across, 1),
        gate_t, up_t, down_weight, half_rows, onehot, slot_gate, grads[0],
    )

    keep, send = kernel_call(
        home_kernel,
        [sent(2, sources, tokens, width), sent(4, sources, tokens, width)],
        [],
        2 * slots * sources * tokens * model,
        limit=2,
    )(onehot, out_rows, *grads)
    near = swap(send, 1)
    out_near, out_far = add_cores(keep, near)
    back_rows, dots, y_rows, gate_part, up_part = kernel_call(
        backward_kernel,
        [
            held(sources, slots, model),
            held(local_experts, rows, tokens, kind=F32),
            held(local_experts, rows, model),
            held(local_experts, rows, units),
            held(local_experts, rows, units),
        ],
        [pltpu.VMEM((RING, units, model), BF16)] * 2 + [pltpu.SemaphoreType.DMA((RING,))] * 2,
        3 * product,
        limit=14,
        in_hbm=(6, 7),
    )(
        *grads, near,
        gate_t, jnp.swapaxes(up_weight, 1, 2), down_weight, activ, slope, silu, onehot, slot_gate, out_near,
    )

    part, pair = sent(tokens, width), sent(2, tokens, width)
    out_even, out_odd = kernel_call(pairs_kernel, [pair, pair], [], 0, limit=2)(out_near, swap(out_far, 2))
    keep, send = kernel_call(
        functools.partial(home_values_kernel, choose),
        [sent(2, sources, tokens + EXTRA, width)] * 2,
        [],
        2 * slots * sources * tokens * model,
        limit=2,
    )(onehot, back_rows, dots, own, came, out_even)
    some = local_experts // 2
    out_came = swap(out_odd, 1, "expert")
    (down_grad,) = weight_grads([(scaled, y_rows, 0, some)])
    back_near, back_far = add_cores(keep, swap(send, 1), down_grad, out_came)
    out_own, out_other = kernel_call(step_kernel, [part, part], [], 0, limit=2)(out_even, out_came, back_near)
    (up_grad,) = weight_grads([(up_part, x_rows, 0, local_experts)], None, back_near)
    (layer_out,) = kernel_call(functools.partial(total_kernel, 2), [part], [], 0, limit=2)(
        out_own, swap(out_other, 2, "expert")
    )
    back_own, back_parts = add_chips(back_near, swap(back_far, 2), up_grad)
    down_grad, gate_grad = weight_grads(
        [(scaled, y_rows, some, local_experts), (gate_part, x_rows, 0, local_experts)], down_grad, back_own
    )
    input_grad, value_grad = kernel_call(
        functools.partial(total_kernel, sources),
        [part, jax.ShapeDtypeStruct((choose, tokens), F32)],
        [],
        0,
        limit=2,
    )(back_own, *back_parts)
    return (
        layer_out,
        input_grad,
        value_grad.T,
        jnp.swapaxes(gate_grad, 1, 2),
        jnp.swapaxes(up_grad, 1, 2),
        down_grad,
    )


def slot_layout(expert_ids, capacity_blocks):
    tokens_here, choose = expert_ids.shape
    experts = capacity_blocks.shape[0]
    flat_ids = expert_ids.reshape(-1)
    onehot = (flat_ids[:, None] == jnp.arange(experts, dtype=jnp.int32)[None, :]).astype(jnp.int32)
    before = jnp.cumsum(onehot, axis=0) - onehot
    ranks = jnp.sum(before * onehot, axis=1)
    limits = jnp.sum(onehot * capacity_blocks[None, :], axis=1) * BLK
    kept = ranks < limits
    slots = jnp.where(kept, flat_ids * CAP + ranks, experts * CAP)
    token_index = jnp.arange(tokens_here * choose, dtype=jnp.int32) // choose
    owners = (
        jnp.full((experts * CAP,), tokens_here, jnp.int32).at[slots].set(token_index, mode="drop")
    )
    return (kept.reshape(tokens_here, choose), slots.reshape(tokens_here, choose), owners)


def outgoing(rows, owners, experts, scale):
    padded = jnp.concatenate([rows, jnp.zeros((1, rows.shape[1]), rows.dtype)], 0)
    picked = padded[owners]
    if scale is not None:
        picked = (scale[:, None] * picked.astype(jnp.float32)).astype(jnp.bfloat16)
    return picked.reshape(experts, CAP, rows.shape[1])


def local_grads(hidden_gate, hidden_up, act_grad):
    sigma = jax.nn.sigmoid(hidden_gate)
    gate_part = (act_grad * hidden_up * sigma * (1.0 + hidden_gate * (1.0 - sigma))).astype(
        jnp.bfloat16
    )
    up_part = (act_grad * jax.nn.silu(hidden_gate)).astype(jnp.bfloat16)
    return (gate_part, up_part)


def combine(back, slots, weights):
    padded = jnp.concatenate([back, jnp.zeros((1, back.shape[1]), back.dtype)], 0)
    picked = padded[slots].astype(jnp.float32)
    return (jnp.einsum("tk,tkw->tw", weights, picked), picked)


def dispatched_body(
    hidden_in,
    out_grad,
    expert_ids,
    gate_values,
    capacity_blocks,
    gate_weight,
    up_weight,
    down_weight,
):
    experts = capacity_blocks.shape[0]
    sources = lax.axis_size("expert")
    local_experts = gate_weight.shape[0]
    kept, slots, owners = slot_layout(expert_ids, capacity_blocks)
    weights = jnp.where(kept, gate_values, 0.0)
    slot_gates = (
        jnp.zeros((experts * CAP,), jnp.float32)
        .at[slots.reshape(-1)]
        .set(weights.reshape(-1), mode="drop")
    )
    send_in = outgoing(hidden_in, owners, experts, None)
    send_grad = outgoing(out_grad, owners, experts, slot_gates)
    recv_in, recv_grad = (
        lax.all_to_all(send_in, "expert", split_axis=0, concat_axis=0, tiled=True),
        lax.all_to_all(send_grad, "expert", split_axis=0, concat_axis=0, tiled=True),
    )
    share = recv_in.shape[2]
    share_in = recv_in.reshape(sources, local_experts, CAP, share)
    share_grad = recv_grad.reshape(sources, local_experts, CAP, share)
    piece = lax.all_gather(share_in, "etp", axis=3, tiled=True)
    hidden_gate = jnp.einsum(
        "secn,enf->secf", piece, gate_weight, preferred_element_type=jnp.float32
    )
    hidden_up = jnp.einsum("secn,enf->secf", piece, up_weight, preferred_element_type=jnp.float32)
    activ = (jax.nn.silu(hidden_gate) * hidden_up).astype(jnp.bfloat16)
    piece = lax.all_gather(share_grad, "etp", axis=3, tiled=True)
    act_grad = jnp.einsum("secn,efn->secf", piece, down_weight, preferred_element_type=jnp.float32)
    columns = jnp.einsum("secf,secn->efn", activ, piece, preferred_element_type=jnp.float32)
    act_grad, down_grad = (act_grad, columns)
    gate_part, up_part = local_grads(hidden_gate, hidden_up, act_grad)
    stacked = jnp.stack([gate_part, up_part])
    weight_grads = jnp.einsum(
        "secn,gsecf->genf",
        lax.all_gather(share_in, "etp", axis=3, tiled=True),
        stacked,
        preferred_element_type=jnp.float32,
    )
    out_part = jnp.einsum("secf,efd->secd", activ, down_weight, preferred_element_type=jnp.float32)
    back_part = jnp.einsum(
        "secf,edf->secd", gate_part, gate_weight, preferred_element_type=jnp.float32
    )
    back_part = back_part + jnp.einsum(
        "secf,edf->secd", up_part, up_weight, preferred_element_type=jnp.float32
    )
    out_rows = lax.psum_scatter(
        out_part.astype(jnp.bfloat16), "etp", scatter_dimension=3, tiled=True
    )
    home_out = lax.all_to_all(out_rows, "expert", split_axis=0, concat_axis=0, tiled=True)
    share_width = home_out.shape[3]
    layer_sum, picked = combine(home_out.reshape(experts * CAP, share_width), slots, weights)
    dot_part = jnp.einsum("tw,tkw->tk", out_grad.astype(jnp.float32), picked) * kept.astype(
        jnp.float32
    )
    gate_value_grad = lax.psum(dot_part, "etp")
    back_rows = lax.psum_scatter(
        back_part.astype(jnp.bfloat16), "etp", scatter_dimension=3, tiled=True
    )
    home_back = lax.all_to_all(back_rows, "expert", split_axis=0, concat_axis=0, tiled=True)
    input_sum, returned = combine(home_back.reshape(experts * CAP, share_width), slots, weights)
    return (
        layer_sum.astype(jnp.bfloat16),
        input_sum.astype(jnp.bfloat16),
        gate_value_grad,
        weight_grads[0].astype(jnp.bfloat16),
        weight_grads[1].astype(jnp.bfloat16),
        down_grad.astype(jnp.bfloat16),
    )


def body(*operands):
    hidden_in, gate_weight = operands[0], operands[5]
    if lax.axis_size("expert") == 4 and lax.axis_size("etp") == 4 and hidden_in.shape[0] <= gate_weight.shape[0] * CAP:
        return gathered_body(*operands)
    return dispatched_body(*operands)


def solution(mesh):
    in_specs = (
        P(("groups", "expert"), "etp"),
        P(("groups", "expert"), "etp"),
        P(("groups", "expert"), None),
        P(("groups", "expert"), None),
        P("groups"),
        P("expert", None, "etp"),
        P("expert", None, "etp"),
        P("expert", "etp", None),
    )
    out_specs = (
        P(("groups", "expert"), "etp"),
        P(("groups", "expert"), "etp"),
        P(("groups", "expert"), None),
        P(("groups", "expert"), None, "etp"),
        P(("groups", "expert"), None, "etp"),
        P(("groups", "expert"), "etp", None),
    )
    return jax.shard_map(body, mesh=mesh, in_specs=in_specs, out_specs=out_specs, check_vma=False)
```

```python
import functools

import jax
import jax.numpy as jnp
from jax import lax
from jax.experimental import pallas as pl
from jax.experimental.pallas import tpu as pltpu
from jax.sharding import PartitionSpec as P

CAP = 16
BLK = 4
EXTRA = 16
F32 = jnp.float32
BF16 = jnp.bfloat16


def nn(a, b):
    return lax.dot_general(a, b, (((1,), (0,)), ((), ())), preferred_element_type=F32)


def nt(a, b):
    return lax.dot_general(a, b, (((1,), (1,)), ((), ())), preferred_element_type=F32)


def tn(a, b):
    return lax.dot_general(a, b, (((0,), (0,)), ((), ())), preferred_element_type=F32)


def pack_kernel(hidden_hbm, ids_hbm, gates_hbm, own_ref, ids_ref, gates_ref, sems):
    tokens, width = hidden_hbm.shape
    choose = ids_ref.shape[0]
    copies = [
        pltpu.make_async_copy(hidden_hbm, own_ref.at[pl.ds(0, tokens)], sems.at[0]),
        pltpu.make_async_copy(ids_hbm, ids_ref, sems.at[1]),
        pltpu.make_async_copy(gates_hbm, gates_ref, sems.at[2]),
    ]
    for copy in copies:
        copy.start()
    for copy in copies:
        copy.wait()
    gates = gates_ref[...]
    high = gates.astype(BF16).astype(F32)
    fill = jnp.zeros((8 - choose, tokens), F32)
    top = jnp.concatenate([jnp.concatenate([ids_ref[...].astype(F32), fill], axis=0), jnp.concatenate([high, fill], axis=0)], axis=1)
    low = jnp.concatenate([jnp.concatenate([gates - high, fill], axis=0), jnp.zeros((8, width - tokens), F32)], axis=1)
    own_ref[tokens:tokens + EXTRA, :] = jnp.concatenate([top, low], axis=0).astype(BF16)


def routing(info, choose, tokens):
    info = info.astype(F32)
    return info[0:choose, 0:tokens], info[0:choose, tokens:2 * tokens], info[8:8 + choose, 0:tokens]


def columns(me, mask, width):
    return pl.ds(pl.multiple_of(lax.bitwise_xor(me, mask) * width, width), width)


def send_home(home_keep, home_send, me, onehot, rows, tokens, width):
    for s in range(onehot.shape[0]):
        for q in range(4):
            home = home_send if q % 2 else home_keep
            home[q // 2, s, 0:tokens, :] = tn(onehot[s], rows[s, :, columns(me, q, width)]).astype(BF16)


RING = 6
HELD = 4


def ring(weight, slots, sems, columns=None):
    depth = slots.shape[0]

    def load(e):
        slot = lax.rem(e, depth)
        source = weight.at[e] if columns is None else weight.at[e, :, columns]
        return pltpu.make_async_copy(source, slots.at[slot], sems.at[slot])

    def start(e):
        @pl.when(e < weight.shape[0])
        def _():
            load(e).start()

    for e in range(min(depth, weight.shape[0])):
        load(jnp.int32(e)).start()
    if depth >= weight.shape[0]:
        return lambda e: None, lambda e: load(e).wait()
    return lambda e: start(e + depth), lambda e: load(e).wait()


def slot_of(slots, e):
    return slots[lax.rem(e, slots.shape[0])]


def forward_kernel(
    choose, capacity_ref, o0, o1, o2, o3, b0, b1, b2, b3, gate_ref, up_ref, down_hbm, later_ref,
    out_rows, rows_ref, act_ref, a_ref, slope_ref, silu_ref, onehot, slot_gate,
    down_ref, down_sems,
):
    sources, slots, tokens = onehot.shape
    experts = slots // CAP
    width = b0.shape[2]
    me = lax.axis_index("etp")
    first = lax.axis_index("expert") * experts
    start_down, wait_down = ring(down_hbm, down_ref, down_sems)
    row = lax.broadcasted_iota(jnp.int32, (tokens, tokens), 0)
    col = lax.broadcasted_iota(jnp.int32, (tokens, tokens), 1)
    before = jnp.where(row < col, 1.0, 0.0).astype(BF16)
    ones = jnp.ones((tokens, tokens), BF16)
    expert = lax.broadcasted_iota(jnp.int32, (experts, tokens), 0)
    mine = (first + expert).astype(F32)
    limit = jnp.zeros((experts, tokens), jnp.int32)
    for e in range(experts):
        limit = jnp.where(expert == e, capacity_ref[first + e] * BLK, limit)
    limit = limit.astype(F32)
    place = lax.broadcasted_iota(jnp.int32, (experts, CAP, tokens), 1).astype(F32)
    for s in range(sources):
        block = [o[...] for o in (o0, o1, o2, o3)] if s == 0 else [b[s - 1] for b in (b0, b1, b2, b3)]
        ids, highs, lows = routing(block[0][tokens:tokens + EXTRA, :], choose, tokens)
        named = jnp.zeros((experts, tokens), F32)
        high, low = named, named
        for k in range(choose):
            hit = ids[k:k + 1, :] == mine
            named = named + jnp.where(hit, 1.0, 0.0)
            high = high + jnp.where(hit, highs[k:k + 1, :], 0.0)
            low = low + jnp.where(hit, lows[k:k + 1, :], 0.0)
        rank = nn(named.astype(BF16), before)
        rank = jnp.where((named > 0.5) & (rank < limit), rank, -1.0)
        taken = rank[:, None, :] == place
        spread = lambda x: jnp.where(taken, x[:, None, :], 0.0).reshape(slots, tokens).astype(BF16)
        gates = nn(spread(high), ones) + nn(spread(low), ones)
        slot_gate[:, s * CAP:(s + 1) * CAP, :] = gates.reshape(experts, CAP, tokens)
        table = jnp.where(taken, 1.0, 0.0).reshape(slots, tokens).astype(BF16)
        onehot[s] = table
        for q in range(4):
            picked = nn(table, block[q][0:tokens, :]).astype(BF16).reshape(experts, CAP, width)
            rows_ref[:, s * CAP:(s + 1) * CAP, columns(me, q, width)] = picked

    def activate(e):
        x = rows_ref[e]
        hidden_gate = nt(x, gate_ref[e])
        hidden_up = nt(x, up_ref[e])
        sigma = jax.nn.sigmoid(hidden_gate)
        silu = hidden_gate * sigma
        activ = (silu * hidden_up).astype(BF16)
        act_ref[e] = activ
        slope_ref[e] = hidden_up * sigma * (1.0 + hidden_gate * (1.0 - sigma))
        silu_ref[e] = silu
        a_ref[e] = (activ.astype(F32) * slot_gate[e][:, 0:1]).astype(BF16)

    def project(e):
        out = nn(a_ref[e], slot_of(down_ref, e)).astype(BF16)
        at = pl.ds(pl.multiple_of(e * CAP, CAP), CAP)
        for s in range(sources):
            out_rows[s, at, :] = out[s * CAP:(s + 1) * CAP]

    def both(e):
        for i in (e - 2, e - 1):
            wait_down(i)
        project(e - 2)
        project(e - 1)
        activate(e)
        activate(e + 1)
        for i in (e - 2, e - 1):
            start_down(i)

    skewed(experts, activate, wait_down, project, both)


def skewed(experts, first, wait, second, both):
    first(jnp.int32(0))
    first(jnp.int32(1))

    def turn(i, _):
        both(i * 2)
        return 0

    lax.fori_loop(1, experts // 2, turn, 0)
    for e in (experts - 2, experts - 1):
        wait(jnp.int32(e))
    for e in (experts - 2, experts - 1):
        second(jnp.int32(e))


def home_kernel(onehot, rows, *refs):
    grads, (keep, send) = refs[:-2], refs[-2:]
    send_home(keep, send, lax.axis_index("etp"), onehot, rows, keep.shape[2], keep.shape[3])
    for s, grad in enumerate(grads):
        for q in range(2):
            send[2 + q, s] = grad[q]


def home_values_kernel(choose, onehot, rows, dots, own_ref, info_ref, *refs):
    keep, send = refs[-2:]
    sources, slots, tokens = onehot.shape
    experts = slots // CAP
    width = keep.shape[3]
    send_home(keep, send, lax.axis_index("etp"), onehot, rows, tokens, width)
    expert = lax.broadcasted_iota(jnp.int32, (experts, tokens), 0)
    mine = (lax.axis_index("expert") * experts + expert).astype(F32)
    for s in range(sources):
        info = own_ref[tokens:tokens + EXTRA, :] if s == 0 else info_ref[s - 1, tokens:tokens + EXTRA, :]
        ids, _, _ = routing(info, choose, tokens)
        chosen = onehot[s].astype(F32).reshape(experts, CAP, tokens)
        share = jnp.sum(chosen * dots[:, s * CAP:(s + 1) * CAP, :], axis=1)
        values = [jnp.sum(jnp.where(ids[k:k + 1, :] == mine, share, 0.0), axis=0, keepdims=True) for k in range(choose)]
        values = jnp.concatenate(values + [jnp.zeros((EXTRA - choose, tokens), F32)], axis=0)
        values = jnp.concatenate([values, jnp.zeros((EXTRA, width - tokens), F32)], axis=1).astype(BF16)
        for home in (keep, send):
            home[0, s, tokens:tokens + EXTRA, :] = values
            home[1, s, tokens:tokens + EXTRA, :] = values


def backward_kernel(
    a0, a1, a2, a3, near_ref,
    gate_ref, up_ref, down_hbm, act_ref, a_ref, slope_ref, silu_ref, onehot, slot_gate, earlier_ref,
    back_rows, dots, rows_ref, p_ref, q_ref, down_grad,
    down_ref, held, down_sems, held_sems,
):
    sources, slots, tokens = onehot.shape
    experts = slots // CAP
    width = a0.shape[2]
    me = lax.axis_index("etp")
    start_down, wait_down = ring(down_hbm, down_ref, down_sems)
    for s, here in enumerate((a0, a1, a2, a3)):
        for q in range(4):
            block = near_ref[2 + q // 2, s] if q % 2 else here[q // 2]
            picked = nn(onehot[s], block).astype(BF16).reshape(experts, CAP, width)
            rows_ref[:, s * CAP:(s + 1) * CAP, columns(me, q, width)] = picked

    def slopes(e):
        grad = nt(rows_ref[e], slot_of(down_ref, e))
        activ = act_ref[e].astype(F32)
        dots[e] = jnp.broadcast_to(jnp.sum(activ * grad, axis=1, keepdims=True), dots.shape[1:])
        grad = grad * slot_gate[e][:, 0:1]
        p_ref[e] = (grad * slope_ref[e]).astype(BF16)
        q_ref[e] = (grad * silu_ref[e]).astype(BF16)

    def store(e):
        slot = lax.rem(e, HELD)
        return pltpu.make_async_copy(held.at[slot], down_grad.at[e], held_sems.at[slot])

    def project(e):
        held[lax.rem(e, HELD)] = tn(a_ref[e], rows_ref[e]).astype(BF16)
        back = nn(p_ref[e], gate_ref[e]) + nn(q_ref[e], up_ref[e])
        back = (back * slot_gate[e][:, 0:1]).astype(BF16)
        at = pl.ds(pl.multiple_of(e * CAP, CAP), CAP)
        for s in range(sources):
            back_rows[s, at, :] = back[s * CAP:(s + 1) * CAP]

    def first(e):
        wait_down(e)
        slopes(e)
        start_down(e)

    def both(e):
        for i in (e, e + 1):
            wait_down(i)

        @pl.when(e - 2 >= HELD)
        def _():
            for i in (e - 2, e - 1):
                store(i - HELD).wait()

        project(e - 2)
        project(e - 1)
        slopes(e)
        slopes(e + 1)
        for i in (e - 2, e - 1):
            store(i).start()
        for i in (e, e + 1):
            start_down(i)

    skewed(experts, first, lambda e: store(e - HELD).wait(), project, both)
    for e in (experts - 2, experts - 1):
        store(jnp.int32(e)).start()
    for e in range(experts - HELD, experts):
        store(jnp.int32(e)).wait()


def add_kernel(keep, came, *refs):
    near, far = refs[-2:]
    for s in range(near.shape[0]):
        far[s] = (keep[1, s].astype(F32) + came[1, s].astype(F32)).astype(BF16)
        near[s] = (keep[0, s].astype(F32) + came[0, s].astype(F32)).astype(BF16)


def chips_kernel(near, came, *refs):
    parts = refs[-near.shape[0]:]
    for s in range(near.shape[0]):
        parts[s][...] = (near[s].astype(F32) + came[s].astype(F32)).astype(BF16)


def total_kernel(count, *refs):
    total = refs[0][...].astype(F32)
    for ref in refs[1:count]:
        total = total + ref[...].astype(F32)
    rows = refs[count]
    tokens = rows.shape[0]
    rows[...] = total[0:tokens].astype(BF16)
    for values in refs[count + 1:]:
        values[...] = total[tokens:tokens + values.shape[0], 0:values.shape[1]]


BANKS = 8
TURN = 4


def product_kernel(jobs, *refs):
    lefts, rights, outs = (refs[i * len(jobs):(i + 1) * len(jobs)] for i in range(3))
    held, sems = refs[-2:]
    outs = refs[-2 - len(jobs):-2]

    def store(job, e, slot):
        return pltpu.make_async_copy(held.at[slot], outs[job].at[e], sems.at[slot])

    def turn(job, first, done, i, full):
        for pair in range(0, TURN, 2):
            places = [(first + i * TURN + j, lax.rem(done + i * TURN + j, BANKS)) for j in (pair, pair + 1)]
            if full:
                for e, slot in places:
                    store(job, e, slot).wait()
            for e, slot in places:
                held[slot] = tn(lefts[job][e], rights[job][e]).astype(BF16)
            for e, slot in places:
                store(job, e, slot).start()

    done = 0
    for job, (first, last) in enumerate(jobs):
        fresh = max(0, min(BANKS - done, last - first) // TURN)
        for i in range(fresh):
            turn(job, first, done, jnp.int32(i), False)

        def later(i, _, job=job, first=first, done=done):
            turn(job, first, done, i, True)
            return 0

        lax.fori_loop(fresh, (last - first) // TURN, later, 0)
        done = done + last - first
    for slot in range(min(done, BANKS)):
        store(0, jobs[0][0], slot).wait()


def load_kernel(source, target, token, sems):
    token[...] = jnp.zeros_like(token)
    copies = [pltpu.make_async_copy(source.at[e], target.at[e], sems.at[e]) for e in range(source.shape[0])]
    for copy in copies:
        copy.start()
    for copy in copies:
        copy.wait()


def in_vmem(weight):
    return pl.pallas_call(
        load_kernel,
        in_specs=[pl.BlockSpec(memory_space=pltpu.HBM)],
        out_specs=[pl.BlockSpec(memory_space=pltpu.VMEM)] * 2,
        out_shape=[pltpu.VMEM(weight.shape, BF16), jax.ShapeDtypeStruct((8, 128), F32)],
        scratch_shapes=[pltpu.SemaphoreType.DMA((weight.shape[0],))],
        compiler_params=pltpu.CompilerParams(vmem_limit_bytes=4 * 1024 * 1024),
        cost_estimate=pl.CostEstimate(flops=0, bytes_accessed=2 * weight.size, transcendentals=0),
    )(pltpu.with_memory_space_constraint(weight, pltpu.HBM))


def join_kernel(count, *refs):
    for i in range(count):
        refs[-1][i] = refs[i][...]


def join(arrays, *there):
    return kernel_call(
        functools.partial(join_kernel, len(arrays)),
        [jax.ShapeDtypeStruct((len(arrays),) + arrays[0].shape, arrays[0].dtype)],
        [],
        0,
        limit=2,
    )(*arrays, *there)[0]


def kernel_call(kernel, out_shape, scratch, flops, out_specs=None, limit=4, in_hbm=(), aliases={}):
    def call(*operands):
        specs = [
            pl.BlockSpec(memory_space=pltpu.HBM if i in in_hbm else pltpu.SMEM if x.ndim == 1 else pltpu.VMEM)
            for i, x in enumerate(operands)
        ]
        operands = [
            pltpu.with_memory_space_constraint(x, pltpu.HBM) if i in in_hbm else x for i, x in enumerate(operands)
        ]
        return pl.pallas_call(
            kernel,
            in_specs=specs,
            out_specs=out_specs or [pl.BlockSpec(memory_space=pltpu.VMEM)] * len(out_shape),
            out_shape=out_shape,
            scratch_shapes=scratch,
            input_output_aliases=aliases,
            compiler_params=pltpu.CompilerParams(vmem_limit_bytes=limit * 1024 * 1024),
            cost_estimate=pl.CostEstimate(flops=flops, bytes_accessed=flops // 32, transcendentals=0),
        )(*operands)

    return call


def weight_grads(jobs, begun=None, *earlier):
    count = len(jobs)
    lefts, rights = [job[0] for job in jobs], [job[1] for job in jobs]
    experts, rows, units = lefts[0].shape
    model = rights[0].shape[2]
    shape = jax.ShapeDtypeStruct((experts, units, model), BF16)
    work = sum(job[3] - job[2] for job in jobs)
    more = [] if begun is None else [begun]
    return kernel_call(
        functools.partial(product_kernel, [job[2:] for job in jobs]),
        [shape] * count,
        [pltpu.VMEM((BANKS, units, model), BF16), pltpu.SemaphoreType.DMA((BANKS,))],
        2 * work * rows * units * model,
        out_specs=[pl.BlockSpec(memory_space=pltpu.HBM)] * count,
        limit=8,
        in_hbm=(2 * count,) if more else (),
        aliases={2 * count: 0} if more else {},
    )(*lefts, *rights, *more, *earlier)


def swap(array, bit, axis="etp"):
    count = lax.axis_size(axis)
    return lax.ppermute(array, axis, [(i, i ^ bit) for i in range(count)])


def add_cores(keep, came, *earlier):
    shape = jax.ShapeDtypeStruct(keep.shape[1:], BF16)
    hbm = [2] if earlier else []
    return kernel_call(add_kernel, [shape, shape], [], 0, limit=2, in_hbm=hbm)(keep, came, *earlier)


def add_chips(near, far, *earlier):
    sources = near.shape[0]
    shape = jax.ShapeDtypeStruct(near.shape[1:], BF16)
    hbm = [2] if earlier else []
    parts = kernel_call(chips_kernel, [shape] * sources, [], 0, limit=2, in_hbm=hbm)(near, far, *earlier)
    return parts[0], [swap(parts[s], s, "expert") for s in range(1, sources)]


def gathered_body(
    hidden_in, out_grad, expert_ids, gate_values, capacity_blocks, gate_weight, up_weight, down_weight
):
    sources = lax.axis_size("expert")
    tokens, width = hidden_in.shape
    choose = expert_ids.shape[1]
    local_experts, units, model = down_weight.shape
    slots = local_experts * CAP
    rows = sources * CAP
    gate_t, gate_there = in_vmem(jnp.swapaxes(gate_weight, 1, 2))
    up_t, up_there = in_vmem(jnp.swapaxes(up_weight, 1, 2))
    product = 2 * local_experts * rows * units * model
    held = lambda *shape, kind=BF16: pltpu.VMEM(shape, kind)
    sent = lambda *shape: jax.ShapeDtypeStruct(shape, BF16)

    own = kernel_call(
        pack_kernel,
        [sent(tokens + EXTRA, width)],
        [pltpu.VMEM((choose, tokens), jnp.int32), pltpu.VMEM((choose, tokens), F32), pltpu.SemaphoreType.DMA((3,))],
        0,
        limit=2,
        in_hbm=(0, 1, 2),
    )(hidden_in, expert_ids.T, gate_values.T)[0]
    came = [swap(own, s, "expert") for s in range(1, sources)]
    own_across = swap(own, 2)
    grad_across = swap(out_grad, 2)
    came = join(came, gate_there, own_across, grad_across)
    came_across_there = swap(came, 2)
    across_near = swap(own_across, 1)
    grads = join([out_grad, grad_across], came)
    grads = [grads] + [swap(grads, s, "expert") for s in range(1, sources)]

    came_across = join([came_across_there], up_there, grads[1])[0]
    out_rows, x_rows, activ, scaled, slope, silu, onehot, slot_gate = kernel_call(
        functools.partial(forward_kernel, choose),
        [
            held(sources, slots, model),
            held(local_experts, rows, model),
            held(local_experts, rows, units),
            held(local_experts, rows, units),
            held(local_experts, rows, units, kind=F32),
            held(local_experts, rows, units, kind=F32),
            held(sources, slots, tokens),
            held(local_experts, rows, tokens, kind=F32),
        ],
        [pltpu.VMEM((RING, units, model), BF16), pltpu.SemaphoreType.DMA((RING,))],
        3 * product,
        limit=9,
        in_hbm=(11,),
    )(
        capacity_blocks,
        own, swap(own, 1), own_across, across_near,
        came, swap(came, 1), came_across, swap(came_across, 1),
        gate_t, up_t, down_weight, grads[0],
    )

    keep, send = kernel_call(
        home_kernel,
        [sent(2, sources, tokens, width), sent(4, sources, tokens, width)],
        [],
        2 * slots * sources * tokens * model,
        limit=2,
    )(onehot, out_rows, *grads)
    near = swap(send, 1)
    out_near, out_far = add_cores(keep, near)
    back_rows, dots, y_rows, gate_part, up_part, down_grad = kernel_call(
        backward_kernel,
        [
            held(sources, slots, model),
            held(local_experts, rows, tokens, kind=F32),
            held(local_experts, rows, model),
            held(local_experts, rows, units),
            held(local_experts, rows, units),
            sent(local_experts, units, model),
        ],
        [
            pltpu.VMEM((RING, units, model), BF16),
            pltpu.VMEM((HELD, units, model), BF16),
            pltpu.SemaphoreType.DMA((RING,)),
            pltpu.SemaphoreType.DMA((HELD,)),
        ],
        4 * product,
        out_specs=[pl.BlockSpec(memory_space=pltpu.VMEM)] * 5 + [pl.BlockSpec(memory_space=pltpu.HBM)],
        limit=13,
        in_hbm=(7,),
    )(
        *grads, near,
        gate_t, up_t, down_weight, activ, scaled, slope, silu, onehot, slot_gate, out_near,
    )

    out_own, out_parts = add_chips(out_near, swap(out_far, 2))
    keep, send = kernel_call(
        functools.partial(home_values_kernel, choose),
        [sent(2, sources, tokens + EXTRA, width)] * 2,
        [],
        2 * slots * sources * tokens * model,
        limit=2,
    )(onehot, back_rows, dots, own, came, out_own)
    some = local_experts // 2
    (up_grad,) = weight_grads([(up_part, x_rows, 0, some)])
    back_near, back_far = add_cores(keep, swap(send, 1), up_grad)
    (up_grad,) = weight_grads([(up_part, x_rows, some, local_experts)], up_grad, back_near)
    (layer_out,) = kernel_call(functools.partial(total_kernel, sources), [sent(tokens, width)], [], 0, limit=2)(
        out_own, *out_parts
    )
    back_own, back_parts = add_chips(back_near, swap(back_far, 2), up_grad)
    (gate_grad,) = weight_grads([(gate_part, x_rows, 0, local_experts)], None, back_own)
    input_grad, value_grad = kernel_call(
        functools.partial(total_kernel, sources),
        [sent(tokens, width), jax.ShapeDtypeStruct((choose, tokens), F32)],
        [],
        0,
        limit=2,
    )(back_own, *back_parts)
    return (
        layer_out,
        input_grad,
        value_grad.T,
        jnp.swapaxes(gate_grad, 1, 2),
        jnp.swapaxes(up_grad, 1, 2),
        down_grad,
    )


def slot_layout(expert_ids, capacity_blocks):
    tokens_here, choose = expert_ids.shape
    experts = capacity_blocks.shape[0]
    flat_ids = expert_ids.reshape(-1)
    onehot = (flat_ids[:, None] == jnp.arange(experts, dtype=jnp.int32)[None, :]).astype(jnp.int32)
    before = jnp.cumsum(onehot, axis=0) - onehot
    ranks = jnp.sum(before * onehot, axis=1)
    limits = jnp.sum(onehot * capacity_blocks[None, :], axis=1) * BLK
    kept = ranks < limits
    slots = jnp.where(kept, flat_ids * CAP + ranks, experts * CAP)
    token_index = jnp.arange(tokens_here * choose, dtype=jnp.int32) // choose
    owners = (
        jnp.full((experts * CAP,), tokens_here, jnp.int32).at[slots].set(token_index, mode="drop")
    )
    return (kept.reshape(tokens_here, choose), slots.reshape(tokens_here, choose), owners)


def outgoing(rows, owners, experts, scale):
    padded = jnp.concatenate([rows, jnp.zeros((1, rows.shape[1]), rows.dtype)], 0)
    picked = padded[owners]
    if scale is not None:
        picked = (scale[:, None] * picked.astype(jnp.float32)).astype(jnp.bfloat16)
    return picked.reshape(experts, CAP, rows.shape[1])


def local_grads(hidden_gate, hidden_up, act_grad):
    sigma = jax.nn.sigmoid(hidden_gate)
    gate_part = (act_grad * hidden_up * sigma * (1.0 + hidden_gate * (1.0 - sigma))).astype(
        jnp.bfloat16
    )
    up_part = (act_grad * jax.nn.silu(hidden_gate)).astype(jnp.bfloat16)
    return (gate_part, up_part)


def combine(back, slots, weights):
    padded = jnp.concatenate([back, jnp.zeros((1, back.shape[1]), back.dtype)], 0)
    picked = padded[slots].astype(jnp.float32)
    return (jnp.einsum("tk,tkw->tw", weights, picked), picked)


def dispatched_body(
    hidden_in,
    out_grad,
    expert_ids,
    gate_values,
    capacity_blocks,
    gate_weight,
    up_weight,
    down_weight,
):
    experts = capacity_blocks.shape[0]
    sources = lax.axis_size("expert")
    local_experts = gate_weight.shape[0]
    kept, slots, owners = slot_layout(expert_ids, capacity_blocks)
    weights = jnp.where(kept, gate_values, 0.0)
    slot_gates = (
        jnp.zeros((experts * CAP,), jnp.float32)
        .at[slots.reshape(-1)]
        .set(weights.reshape(-1), mode="drop")
    )
    send_in = outgoing(hidden_in, owners, experts, None)
    send_grad = outgoing(out_grad, owners, experts, slot_gates)
    recv_in, recv_grad = (
        lax.all_to_all(send_in, "expert", split_axis=0, concat_axis=0, tiled=True),
        lax.all_to_all(send_grad, "expert", split_axis=0, concat_axis=0, tiled=True),
    )
    share = recv_in.shape[2]
    share_in = recv_in.reshape(sources, local_experts, CAP, share)
    share_grad = recv_grad.reshape(sources, local_experts, CAP, share)
    piece = lax.all_gather(share_in, "etp", axis=3, tiled=True)
    hidden_gate = jnp.einsum(
        "secn,enf->secf", piece, gate_weight, preferred_element_type=jnp.float32
    )
    hidden_up = jnp.einsum("secn,enf->secf", piece, up_weight, preferred_element_type=jnp.float32)
    activ = (jax.nn.silu(hidden_gate) * hidden_up).astype(jnp.bfloat16)
    piece = lax.all_gather(share_grad, "etp", axis=3, tiled=True)
    act_grad = jnp.einsum("secn,efn->secf", piece, down_weight, preferred_element_type=jnp.float32)
    columns = jnp.einsum("secf,secn->efn", activ, piece, preferred_element_type=jnp.float32)
    act_grad, down_grad = (act_grad, columns)
    gate_part, up_part = local_grads(hidden_gate, hidden_up, act_grad)
    stacked = jnp.stack([gate_part, up_part])
    weight_grads = jnp.einsum(
        "secn,gsecf->genf",
        lax.all_gather(share_in, "etp", axis=3, tiled=True),
        stacked,
        preferred_element_type=jnp.float32,
    )
    out_part = jnp.einsum("secf,efd->secd", activ, down_weight, preferred_element_type=jnp.float32)
    back_part = jnp.einsum(
        "secf,edf->secd", gate_part, gate_weight, preferred_element_type=jnp.float32
    )
    back_part = back_part + jnp.einsum(
        "secf,edf->secd", up_part, up_weight, preferred_element_type=jnp.float32
    )
    out_rows = lax.psum_scatter(
        out_part.astype(jnp.bfloat16), "etp", scatter_dimension=3, tiled=True
    )
    home_out = lax.all_to_all(out_rows, "expert", split_axis=0, concat_axis=0, tiled=True)
    share_width = home_out.shape[3]
    layer_sum, picked = combine(home_out.reshape(experts * CAP, share_width), slots, weights)
    dot_part = jnp.einsum("tw,tkw->tk", out_grad.astype(jnp.float32), picked) * kept.astype(
        jnp.float32
    )
    gate_value_grad = lax.psum(dot_part, "etp")
    back_rows = lax.psum_scatter(
        back_part.astype(jnp.bfloat16), "etp", scatter_dimension=3, tiled=True
    )
    home_back = lax.all_to_all(back_rows, "expert", split_axis=0, concat_axis=0, tiled=True)
    input_sum, returned = combine(home_back.reshape(experts * CAP, share_width), slots, weights)
    return (
        layer_sum.astype(jnp.bfloat16),
        input_sum.astype(jnp.bfloat16),
        gate_value_grad,
        weight_grads[0].astype(jnp.bfloat16),
        weight_grads[1].astype(jnp.bfloat16),
        down_grad.astype(jnp.bfloat16),
    )


def body(*operands):
    hidden_in, gate_weight = operands[0], operands[5]
    if lax.axis_size("expert") == 4 and lax.axis_size("etp") == 4 and hidden_in.shape[0] <= gate_weight.shape[0] * CAP:
        return gathered_body(*operands)
    return dispatched_body(*operands)


def solution(mesh):
    in_specs = (
        P(("groups", "expert"), "etp"),
        P(("groups", "expert"), "etp"),
        P(("groups", "expert"), None),
        P(("groups", "expert"), None),
        P("groups"),
        P("expert", None, "etp"),
        P("expert", None, "etp"),
        P("expert", "etp", None),
    )
    out_specs = (
        P(("groups", "expert"), "etp"),
        P(("groups", "expert"), "etp"),
        P(("groups", "expert"), None),
        P(("groups", "expert"), None, "etp"),
        P(("groups", "expert"), None, "etp"),
        P(("groups", "expert"), "etp", None),
    )
    return jax.shard_map(body, mesh=mesh, in_specs=in_specs, out_specs=out_specs, check_vma=False)
```

```python
import functools

import jax
import jax.numpy as jnp
from jax import lax
from jax.experimental import pallas as pl
from jax.experimental.pallas import tpu as pltpu
from jax.sharding import PartitionSpec as P

CAP = 16
BLK = 4
EXTRA = 16
F32 = jnp.float32
BF16 = jnp.bfloat16


def nn(a, b):
    return lax.dot_general(a, b, (((1,), (0,)), ((), ())), preferred_element_type=F32)


def nt(a, b):
    return lax.dot_general(a, b, (((1,), (1,)), ((), ())), preferred_element_type=F32)


def tn(a, b):
    return lax.dot_general(a, b, (((0,), (0,)), ((), ())), preferred_element_type=F32)


def pack_kernel(hidden_hbm, ids_hbm, gates_hbm, own_ref, ids_ref, gates_ref, sems):
    tokens, width = hidden_hbm.shape
    choose = ids_ref.shape[0]
    copies = [
        pltpu.make_async_copy(hidden_hbm, own_ref.at[pl.ds(0, tokens)], sems.at[0]),
        pltpu.make_async_copy(ids_hbm, ids_ref, sems.at[1]),
        pltpu.make_async_copy(gates_hbm, gates_ref, sems.at[2]),
    ]
    for copy in copies:
        copy.start()
    for copy in copies:
        copy.wait()
    gates = gates_ref[...]
    high = gates.astype(BF16).astype(F32)
    fill = jnp.zeros((8 - choose, tokens), F32)
    top = jnp.concatenate([jnp.concatenate([ids_ref[...].astype(F32), fill], axis=0), jnp.concatenate([high, fill], axis=0)], axis=1)
    low = jnp.concatenate([jnp.concatenate([gates - high, fill], axis=0), jnp.zeros((8, width - tokens), F32)], axis=1)
    own_ref[tokens:tokens + EXTRA, :] = jnp.concatenate([top, low], axis=0).astype(BF16)


def routing(info, choose, tokens):
    info = info.astype(F32)
    return info[0:choose, 0:tokens], info[0:choose, tokens:2 * tokens] + info[8:8 + choose, 0:tokens]


def columns(me, mask, width):
    return pl.ds(pl.multiple_of(lax.bitwise_xor(me, mask) * width, width), width)


def send_home(home_keep, home_send, me, onehot, rows, tokens, width):
    for s in range(onehot.shape[0]):
        for q in range(4):
            home = home_send if q % 2 else home_keep
            home[q // 2, s, 0:tokens, :] = tn(onehot[s], rows[s, :, columns(me, q, width)]).astype(BF16)


RING = 8
GROUP = 4


def ring(weight, slots, sems, columns=None):
    depth = slots.shape[0]

    def load(e):
        slot = lax.rem(e, depth)
        source = weight.at[e] if columns is None else weight.at[e, :, columns]
        return pltpu.make_async_copy(source, slots.at[slot], sems.at[slot])

    def start(e):
        @pl.when(e < weight.shape[0])
        def _():
            load(e).start()

    for e in range(min(depth, weight.shape[0])):
        load(jnp.int32(e)).start()
    if depth >= weight.shape[0]:
        return lambda e: None, lambda e: load(e).wait()
    return lambda e: start(e + depth), lambda e: load(e).wait()


def slot_of(slots, e):
    return slots[lax.rem(e, slots.shape[0])]


def forward_kernel(
    choose, capacity_ref, o0, o1, o2, o3, b0, b1, b2, b3, gate_ref, up_ref, down_hbm, later_ref,
    out_rows, rows_ref, act_ref, a_ref, slope_ref, silu_ref, onehot, slot_gate,
    down_ref, down_sems,
):
    sources, slots, tokens = onehot.shape
    experts = slots // CAP
    width = b0.shape[2]
    me = lax.axis_index("etp")
    first = lax.axis_index("expert") * experts
    start_down, wait_down = ring(down_hbm, down_ref, down_sems)
    row = lax.broadcasted_iota(jnp.int32, (tokens, tokens), 0)
    col = lax.broadcasted_iota(jnp.int32, (tokens, tokens), 1)
    before = jnp.where(row < col, 1.0, 0.0).astype(BF16)
    expert = lax.broadcasted_iota(jnp.int32, (experts, tokens), 0)
    mine = (first + expert).astype(F32)
    limit = jnp.zeros((experts, tokens), jnp.int32)
    for e in range(experts):
        limit = jnp.where(expert == e, capacity_ref[first + e] * BLK, limit)
    limit = limit.astype(F32)
    place = lax.broadcasted_iota(jnp.int32, (experts, CAP, tokens), 1).astype(F32)
    for s in range(sources):
        block = [o[...] for o in (o0, o1, o2, o3)] if s == 0 else [b[s - 1] for b in (b0, b1, b2, b3)]
        ids, gates = routing(block[0][tokens:tokens + EXTRA, :], choose, tokens)
        named = jnp.zeros((experts, tokens), F32)
        gate = jnp.zeros((experts, tokens), F32)
        for k in range(choose):
            hit = ids[k:k + 1, :] == mine
            named = named + jnp.where(hit, 1.0, 0.0)
            gate = gate + jnp.where(hit, gates[k:k + 1, :], 0.0)
        rank = nn(named.astype(BF16), before)
        rank = jnp.where((named > 0.5) & (rank < limit), rank, -1.0)
        chosen = jnp.where(rank[:, None, :] == place, 1.0, 0.0)
        gate_of = jnp.sum(chosen * gate[:, None, :], axis=2, keepdims=True)
        slot_gate[:, s * CAP:(s + 1) * CAP, :] = jnp.broadcast_to(gate_of, chosen.shape)
        table = chosen.reshape(slots, tokens).astype(BF16)
        onehot[s] = table
        for q in range(4):
            picked = nn(table, block[q][0:tokens, :]).astype(BF16).reshape(experts, CAP, width)
            rows_ref[:, s * CAP:(s + 1) * CAP, columns(me, q, width)] = picked

    def activate(e):
        x = rows_ref[e]
        hidden_gate = nt(x, gate_ref[e])
        hidden_up = nt(x, up_ref[e])
        sigma = jax.nn.sigmoid(hidden_gate)
        silu = hidden_gate * sigma
        activ = (silu * hidden_up).astype(BF16)
        act_ref[e] = activ
        slope_ref[e] = hidden_up * sigma * (1.0 + hidden_gate * (1.0 - sigma))
        silu_ref[e] = silu
        a_ref[e] = (activ.astype(F32) * slot_gate[e][:, 0:1]).astype(BF16)

    def project(e):
        out = nn(a_ref[e], slot_of(down_ref, e)).astype(BF16)
        at = pl.ds(pl.multiple_of(e * CAP, CAP), CAP)
        for s in range(sources):
            out_rows[s, at, :] = out[s * CAP:(s + 1) * CAP]

    def both(e):
        before, now = [e - GROUP + i for i in range(GROUP)], [e + i for i in range(GROUP)]
        for i in before:
            wait_down(i)
        for i, j in zip(before, now):
            activate(j)
            project(i)
        for i in before:
            start_down(i)

    skewed(experts, activate, wait_down, project, both)


def skewed(experts, first, wait, second, both):
    for e in range(GROUP):
        first(jnp.int32(e))

    def turn(i, _):
        both(i * GROUP)
        return 0

    lax.fori_loop(1, experts // GROUP, turn, 0)
    for e in range(experts - GROUP, experts):
        wait(jnp.int32(e))
    for e in range(experts - GROUP, experts):
        second(jnp.int32(e))


def home_kernel(onehot, rows, *refs):
    grads, (keep, send) = refs[:-2], refs[-2:]
    send_home(keep, send, lax.axis_index("etp"), onehot, rows, keep.shape[2], keep.shape[3])
    for s, grad in enumerate(grads):
        for q in range(2):
            send[2 + q, s] = grad[q]


def home_values_kernel(choose, onehot, rows, dots, own_ref, info_ref, *refs):
    keep, send = refs[-2:]
    sources, slots, tokens = onehot.shape
    experts = slots // CAP
    width = keep.shape[3]
    send_home(keep, send, lax.axis_index("etp"), onehot, rows, tokens, width)
    expert = lax.broadcasted_iota(jnp.int32, (experts, tokens), 0)
    mine = (lax.axis_index("expert") * experts + expert).astype(F32)
    for s in range(sources):
        info = own_ref[tokens:tokens + EXTRA, :] if s == 0 else info_ref[s - 1, tokens:tokens + EXTRA, :]
        ids, _ = routing(info, choose, tokens)
        chosen = onehot[s].astype(F32).reshape(experts, CAP, tokens)
        share = jnp.sum(chosen * dots[:, s * CAP:(s + 1) * CAP, :], axis=1)
        values = [jnp.sum(jnp.where(ids[k:k + 1, :] == mine, share, 0.0), axis=0, keepdims=True) for k in range(choose)]
        values = jnp.concatenate(values + [jnp.zeros((EXTRA - choose, tokens), F32)], axis=0)
        values = jnp.concatenate([values, jnp.zeros((EXTRA, width - tokens), F32)], axis=1).astype(BF16)
        for home in (keep, send):
            home[0, s, tokens:tokens + EXTRA, :] = values
            home[1, s, tokens:tokens + EXTRA, :] = values


def backward_kernel(
    a0, a1, a2, a3, near_ref,
    gate_ref, up_ref, down_hbm, act_ref, slope_ref, silu_ref, onehot, slot_gate, earlier_ref,
    back_rows, dots, rows_ref, p_ref, q_ref,
    down_ref, down_sems,
):
    sources, slots, tokens = onehot.shape
    experts = slots // CAP
    width = a0.shape[2]
    me = lax.axis_index("etp")
    start_down, wait_down = ring(down_hbm, down_ref, down_sems)
    for s, here in enumerate((a0, a1, a2, a3)):
        for q in range(4):
            block = near_ref[2 + q // 2, s] if q % 2 else here[q // 2]
            picked = nn(onehot[s], block).astype(BF16).reshape(experts, CAP, width)
            rows_ref[:, s * CAP:(s + 1) * CAP, columns(me, q, width)] = picked

    def slopes(e):
        grad = nt(rows_ref[e], slot_of(down_ref, e))
        activ = act_ref[e].astype(F32)
        dots[e] = jnp.broadcast_to(jnp.sum(activ * grad, axis=1, keepdims=True), dots.shape[1:])
        grad = grad * slot_gate[e][:, 0:1]
        p_ref[e] = (grad * slope_ref[e]).astype(BF16)
        q_ref[e] = (grad * silu_ref[e]).astype(BF16)

    def project(e):
        back = nn(p_ref[e], gate_ref[e]) + nn(q_ref[e], up_ref[e])
        back = (back * slot_gate[e][:, 0:1]).astype(BF16)
        at = pl.ds(pl.multiple_of(e * CAP, CAP), CAP)
        for s in range(sources):
            back_rows[s, at, :] = back[s * CAP:(s + 1) * CAP]

    def first(e):
        wait_down(e)
        slopes(e)
        start_down(e)

    def both(e):
        before, now = [e - GROUP + i for i in range(GROUP)], [e + i for i in range(GROUP)]
        for i in now:
            wait_down(i)
        for i, j in zip(before, now):
            slopes(j)
            project(i)
        for i in now:
            start_down(i)

    skewed(experts, first, lambda e: None, project, both)


def add_kernel(keep, came, *refs):
    near, far = refs[-2:]
    for s in range(near.shape[0]):
        far[s] = (keep[1, s].astype(F32) + came[1, s].astype(F32)).astype(BF16)
        near[s] = (keep[0, s].astype(F32) + came[0, s].astype(F32)).astype(BF16)


def chips_kernel(near, came, *refs):
    parts = refs[-near.shape[0]:]
    for s in range(near.shape[0]):
        parts[s][...] = (near[s].astype(F32) + came[s].astype(F32)).astype(BF16)


def total_kernel(count, *refs):
    total = refs[0][...].astype(F32)
    for ref in refs[1:count]:
        total = total + ref[...].astype(F32)
    rows = refs[count]
    tokens = rows.shape[0]
    rows[...] = total[0:tokens].astype(BF16)
    for values in refs[count + 1:]:
        values[...] = total[tokens:tokens + values.shape[0], 0:values.shape[1]]


BANKS = 8
TURN = 4


def product_kernel(jobs, *refs):
    lefts, rights, outs = (refs[i * len(jobs):(i + 1) * len(jobs)] for i in range(3))
    held, sems = refs[-2:]
    outs = refs[-2 - len(jobs):-2]

    def store(job, e, slot):
        return pltpu.make_async_copy(held.at[slot], outs[job].at[e], sems.at[slot])

    def turn(job, first, done, i, full):
        for pair in range(0, TURN, 2):
            places = [(first + i * TURN + j, lax.rem(done + i * TURN + j, BANKS)) for j in (pair, pair + 1)]
            if full:
                for e, slot in places:
                    store(job, e, slot).wait()
            for e, slot in places:
                held[slot] = tn(lefts[job][e], rights[job][e]).astype(BF16)
            for e, slot in places:
                store(job, e, slot).start()

    done = 0
    for job, (first, last) in enumerate(jobs):
        fresh = max(0, min(BANKS - done, last - first) // TURN)
        for i in range(fresh):
            turn(job, first, done, jnp.int32(i), False)

        def later(i, _, job=job, first=first, done=done):
            turn(job, first, done, i, True)
            return 0

        lax.fori_loop(fresh, (last - first) // TURN, later, 0)
        done = done + last - first
    for slot in range(min(done, BANKS)):
        store(0, jobs[0][0], slot).wait()


def load_kernel(source, target, token, sems):
    token[...] = jnp.zeros_like(token)
    copies = [pltpu.make_async_copy(source.at[e], target.at[e], sems.at[e]) for e in range(source.shape[0])]
    for copy in copies:
        copy.start()
    for copy in copies:
        copy.wait()


def in_vmem(weight):
    return pl.pallas_call(
        load_kernel,
        in_specs=[pl.BlockSpec(memory_space=pltpu.HBM)],
        out_specs=[pl.BlockSpec(memory_space=pltpu.VMEM)] * 2,
        out_shape=[pltpu.VMEM(weight.shape, BF16), jax.ShapeDtypeStruct((8, 128), F32)],
        scratch_shapes=[pltpu.SemaphoreType.DMA((weight.shape[0],))],
        compiler_params=pltpu.CompilerParams(vmem_limit_bytes=4 * 1024 * 1024),
        cost_estimate=pl.CostEstimate(flops=0, bytes_accessed=2 * weight.size, transcendentals=0),
    )(pltpu.with_memory_space_constraint(weight, pltpu.HBM))


def join_kernel(count, *refs):
    for i in range(count):
        refs[-1][i] = refs[i][...]


def join(arrays, *there):
    return kernel_call(
        functools.partial(join_kernel, len(arrays)),
        [jax.ShapeDtypeStruct((len(arrays),) + arrays[0].shape, arrays[0].dtype)],
        [],
        0,
        limit=2,
    )(*arrays, *there)[0]


def kernel_call(kernel, out_shape, scratch, flops, out_specs=None, limit=4, in_hbm=(), aliases={}):
    def call(*operands):
        specs = [
            pl.BlockSpec(memory_space=pltpu.HBM if i in in_hbm else pltpu.SMEM if x.ndim == 1 else pltpu.VMEM)
            for i, x in enumerate(operands)
        ]
        operands = [
            pltpu.with_memory_space_constraint(x, pltpu.HBM) if i in in_hbm else x for i, x in enumerate(operands)
        ]
        return pl.pallas_call(
            kernel,
            in_specs=specs,
            out_specs=out_specs or [pl.BlockSpec(memory_space=pltpu.VMEM)] * len(out_shape),
            out_shape=out_shape,
            scratch_shapes=scratch,
            input_output_aliases=aliases,
            compiler_params=pltpu.CompilerParams(vmem_limit_bytes=limit * 1024 * 1024),
            cost_estimate=pl.CostEstimate(flops=flops, bytes_accessed=flops // 32, transcendentals=0),
        )(*operands)

    return call


def weight_grads(jobs, begun=None, *earlier):
    count = len(jobs)
    lefts, rights = [job[0] for job in jobs], [job[1] for job in jobs]
    experts, rows, units = lefts[0].shape
    model = rights[0].shape[2]
    shape = jax.ShapeDtypeStruct((experts, units, model), BF16)
    work = sum(job[3] - job[2] for job in jobs)
    more = [] if begun is None else [begun]
    return kernel_call(
        functools.partial(product_kernel, [job[2:] for job in jobs]),
        [shape] * count,
        [pltpu.VMEM((BANKS, units, model), BF16), pltpu.SemaphoreType.DMA((BANKS,))],
        2 * work * rows * units * model,
        out_specs=[pl.BlockSpec(memory_space=pltpu.HBM)] * count,
        limit=8,
        in_hbm=(2 * count,) if more else (),
        aliases={2 * count: 0} if more else {},
    )(*lefts, *rights, *more, *earlier)


def swap(array, bit, axis="etp"):
    count = lax.axis_size(axis)
    return lax.ppermute(array, axis, [(i, i ^ bit) for i in range(count)])


def add_cores(keep, came, *earlier):
    shape = jax.ShapeDtypeStruct(keep.shape[1:], BF16)
    hbm = [2] if earlier else []
    return kernel_call(add_kernel, [shape, shape], [], 0, limit=2, in_hbm=hbm)(keep, came, *earlier)


def add_chips(near, far, *earlier):
    sources = near.shape[0]
    shape = jax.ShapeDtypeStruct(near.shape[1:], BF16)
    hbm = [2] if earlier else []
    parts = kernel_call(chips_kernel, [shape] * sources, [], 0, limit=2, in_hbm=hbm)(near, far, *earlier)
    return parts[0], [swap(parts[s], s, "expert") for s in range(1, sources)]


def gathered_body(
    hidden_in, out_grad, expert_ids, gate_values, capacity_blocks, gate_weight, up_weight, down_weight
):
    sources = lax.axis_size("expert")
    tokens, width = hidden_in.shape
    choose = expert_ids.shape[1]
    local_experts, units, model = down_weight.shape
    slots = local_experts * CAP
    rows = sources * CAP
    gate_t, gate_there = in_vmem(jnp.swapaxes(gate_weight, 1, 2))
    up_t, up_there = in_vmem(jnp.swapaxes(up_weight, 1, 2))
    product = 2 * local_experts * rows * units * model
    held = lambda *shape, kind=BF16: pltpu.VMEM(shape, kind)
    sent = lambda *shape: jax.ShapeDtypeStruct(shape, BF16)

    own = kernel_call(
        pack_kernel,
        [sent(tokens + EXTRA, width)],
        [pltpu.VMEM((choose, tokens), jnp.int32), pltpu.VMEM((choose, tokens), F32), pltpu.SemaphoreType.DMA((3,))],
        0,
        limit=2,
        in_hbm=(0, 1, 2),
    )(hidden_in, expert_ids.T, gate_values.T)[0]
    came = [swap(own, s, "expert") for s in range(1, sources)]
    own_across = swap(own, 2)
    grad_across = swap(out_grad, 2)
    came = join(came, gate_there, own_across, grad_across)
    came_across_there = swap(came, 2)
    across_near = swap(own_across, 1)
    grads = join([out_grad, grad_across], came)
    grads = [grads] + [swap(grads, s, "expert") for s in range(1, sources)]

    came_across = join([came_across_there], up_there, grads[1])[0]
    out_rows, x_rows, activ, scaled, slope, silu, onehot, slot_gate = kernel_call(
        functools.partial(forward_kernel, choose),
        [
            held(sources, slots, model),
            held(local_experts, rows, model),
            held(local_experts, rows, units),
            held(local_experts, rows, units),
            held(local_experts, rows, units, kind=F32),
            held(local_experts, rows, units, kind=F32),
            held(sources, slots, tokens),
            held(local_experts, rows, tokens, kind=F32),
        ],
        [pltpu.VMEM((RING, units, model), BF16), pltpu.SemaphoreType.DMA((RING,))],
        3 * product,
        limit=10,
        in_hbm=(11,),
    )(
        capacity_blocks,
        own, swap(own, 1), own_across, across_near,
        came, swap(came, 1), came_across, swap(came_across, 1),
        gate_t, up_t, down_weight, grads[0],
    )

    keep, send = kernel_call(
        home_kernel,
        [sent(2, sources, tokens, width), sent(4, sources, tokens, width)],
        [],
        2 * slots * sources * tokens * model,
        limit=2,
    )(onehot, out_rows, *grads)
    near = swap(send, 1)
    out_near, out_far = add_cores(keep, near)
    back_rows, dots, y_rows, gate_part, up_part = kernel_call(
        backward_kernel,
        [
            held(sources, slots, model),
            held(local_experts, rows, tokens, kind=F32),
            held(local_experts, rows, model),
            held(local_experts, rows, units),
            held(local_experts, rows, units),
        ],
        [pltpu.VMEM((RING, units, model), BF16), pltpu.SemaphoreType.DMA((RING,))],
        3 * product,
        limit=13,
        in_hbm=(7,),
    )(
        *grads, near,
        gate_t, up_t, down_weight, activ, slope, silu, onehot, slot_gate, out_near,
    )

    out_own, out_parts = add_chips(out_near, swap(out_far, 2))
    keep, send = kernel_call(
        functools.partial(home_values_kernel, choose),
        [sent(2, sources, tokens + EXTRA, width)] * 2,
        [],
        2 * slots * sources * tokens * model,
        limit=2,
    )(onehot, back_rows, dots, own, came, out_own)
    (down_grad,) = weight_grads([(scaled, y_rows, 0, local_experts)])
    back_near, back_far = add_cores(keep, swap(send, 1), down_grad)
    (up_grad,) = weight_grads([(up_part, x_rows, 0, local_experts)], None, back_near)
    (layer_out,) = kernel_call(functools.partial(total_kernel, sources), [sent(tokens, width)], [], 0, limit=2)(
        out_own, *out_parts
    )
    back_own, back_parts = add_chips(back_near, swap(back_far, 2), up_grad)
    (gate_grad,) = weight_grads([(gate_part, x_rows, 0, local_experts)], None, back_own)
    input_grad, value_grad = kernel_call(
        functools.partial(total_kernel, sources),
        [sent(tokens, width), jax.ShapeDtypeStruct((choose, tokens), F32)],
        [],
        0,
        limit=2,
    )(back_own, *back_parts)
    return (
        layer_out,
        input_grad,
        value_grad.T,
        jnp.swapaxes(gate_grad, 1, 2),
        jnp.swapaxes(up_grad, 1, 2),
        down_grad,
    )


def slot_layout(expert_ids, capacity_blocks):
    tokens_here, choose = expert_ids.shape
    experts = capacity_blocks.shape[0]
    flat_ids = expert_ids.reshape(-1)
    onehot = (flat_ids[:, None] == jnp.arange(experts, dtype=jnp.int32)[None, :]).astype(jnp.int32)
    before = jnp.cumsum(onehot, axis=0) - onehot
    ranks = jnp.sum(before * onehot, axis=1)
    limits = jnp.sum(onehot * capacity_blocks[None, :], axis=1) * BLK
    kept = ranks < limits
    slots = jnp.where(kept, flat_ids * CAP + ranks, experts * CAP)
    token_index = jnp.arange(tokens_here * choose, dtype=jnp.int32) // choose
    owners = (
        jnp.full((experts * CAP,), tokens_here, jnp.int32).at[slots].set(token_index, mode="drop")
    )
    return (kept.reshape(tokens_here, choose), slots.reshape(tokens_here, choose), owners)


def outgoing(rows, owners, experts, scale):
    padded = jnp.concatenate([rows, jnp.zeros((1, rows.shape[1]), rows.dtype)], 0)
    picked = padded[owners]
    if scale is not None:
        picked = (scale[:, None] * picked.astype(jnp.float32)).astype(jnp.bfloat16)
    return picked.reshape(experts, CAP, rows.shape[1])


def local_grads(hidden_gate, hidden_up, act_grad):
    sigma = jax.nn.sigmoid(hidden_gate)
    gate_part = (act_grad * hidden_up * sigma * (1.0 + hidden_gate * (1.0 - sigma))).astype(
        jnp.bfloat16
    )
    up_part = (act_grad * jax.nn.silu(hidden_gate)).astype(jnp.bfloat16)
    return (gate_part, up_part)


def combine(back, slots, weights):
    padded = jnp.concatenate([back, jnp.zeros((1, back.shape[1]), back.dtype)], 0)
    picked = padded[slots].astype(jnp.float32)
    return (jnp.einsum("tk,tkw->tw", weights, picked), picked)


def dispatched_body(
    hidden_in,
    out_grad,
    expert_ids,
    gate_values,
    capacity_blocks,
    gate_weight,
    up_weight,
    down_weight,
):
    experts = capacity_blocks.shape[0]
    sources = lax.axis_size("expert")
    local_experts = gate_weight.shape[0]
    kept, slots, owners = slot_layout(expert_ids, capacity_blocks)
    weights = jnp.where(kept, gate_values, 0.0)
    slot_gates = (
        jnp.zeros((experts * CAP,), jnp.float32)
        .at[slots.reshape(-1)]
        .set(weights.reshape(-1), mode="drop")
    )
    send_in = outgoing(hidden_in, owners, experts, None)
    send_grad = outgoing(out_grad, owners, experts, slot_gates)
    recv_in, recv_grad = (
        lax.all_to_all(send_in, "expert", split_axis=0, concat_axis=0, tiled=True),
        lax.all_to_all(send_grad, "expert", split_axis=0, concat_axis=0, tiled=True),
    )
    share = recv_in.shape[2]
    share_in = recv_in.reshape(sources, local_experts, CAP, share)
    share_grad = recv_grad.reshape(sources, local_experts, CAP, share)
    piece = lax.all_gather(share_in, "etp", axis=3, tiled=True)
    hidden_gate = jnp.einsum(
        "secn,enf->secf", piece, gate_weight, preferred_element_type=jnp.float32
    )
    hidden_up = jnp.einsum("secn,enf->secf", piece, up_weight, preferred_element_type=jnp.float32)
    activ = (jax.nn.silu(hidden_gate) * hidden_up).astype(jnp.bfloat16)
    piece = lax.all_gather(share_grad, "etp", axis=3, tiled=True)
    act_grad = jnp.einsum("secn,efn->secf", piece, down_weight, preferred_element_type=jnp.float32)
    columns = jnp.einsum("secf,secn->efn", activ, piece, preferred_element_type=jnp.float32)
    act_grad, down_grad = (act_grad, columns)
    gate_part, up_part = local_grads(hidden_gate, hidden_up, act_grad)
    stacked = jnp.stack([gate_part, up_part])
    weight_grads = jnp.einsum(
        "secn,gsecf->genf",
        lax.all_gather(share_in, "etp", axis=3, tiled=True),
        stacked,
        preferred_element_type=jnp.float32,
    )
    out_part = jnp.einsum("secf,efd->secd", activ, down_weight, preferred_element_type=jnp.float32)
    back_part = jnp.einsum(
        "secf,edf->secd", gate_part, gate_weight, preferred_element_type=jnp.float32
    )
    back_part = back_part + jnp.einsum(
        "secf,edf->secd", up_part, up_weight, preferred_element_type=jnp.float32
    )
    out_rows = lax.psum_scatter(
        out_part.astype(jnp.bfloat16), "etp", scatter_dimension=3, tiled=True
    )
    home_out = lax.all_to_all(out_rows, "expert", split_axis=0, concat_axis=0, tiled=True)
    share_width = home_out.shape[3]
    layer_sum, picked = combine(home_out.reshape(experts * CAP, share_width), slots, weights)
    dot_part = jnp.einsum("tw,tkw->tk", out_grad.astype(jnp.float32), picked) * kept.astype(
        jnp.float32
    )
    gate_value_grad = lax.psum(dot_part, "etp")
    back_rows = lax.psum_scatter(
        back_part.astype(jnp.bfloat16), "etp", scatter_dimension=3, tiled=True
    )
    home_back = lax.all_to_all(back_rows, "expert", split_axis=0, concat_axis=0, tiled=True)
    input_sum, returned = combine(home_back.reshape(experts * CAP, share_width), slots, weights)
    return (
        layer_sum.astype(jnp.bfloat16),
        input_sum.astype(jnp.bfloat16),
        gate_value_grad,
        weight_grads[0].astype(jnp.bfloat16),
        weight_grads[1].astype(jnp.bfloat16),
        down_grad.astype(jnp.bfloat16),
    )


def body(*operands):
    hidden_in, gate_weight = operands[0], operands[5]
    if lax.axis_size("expert") == 4 and lax.axis_size("etp") == 4 and hidden_in.shape[0] <= gate_weight.shape[0] * CAP:
        return gathered_body(*operands)
    return dispatched_body(*operands)


def solution(mesh):
    in_specs = (
        P(("groups", "expert"), "etp"),
        P(("groups", "expert"), "etp"),
        P(("groups", "expert"), None),
        P(("groups", "expert"), None),
        P("groups"),
        P("expert", None, "etp"),
        P("expert", None, "etp"),
        P("expert", "etp", None),
    )
    out_specs = (
        P(("groups", "expert"), "etp"),
        P(("groups", "expert"), "etp"),
        P(("groups", "expert"), None),
        P(("groups", "expert"), None, "etp"),
        P(("groups", "expert"), None, "etp"),
        P(("groups", "expert"), "etp", None),
    )
    return jax.shard_map(body, mesh=mesh, in_specs=in_specs, out_specs=out_specs, check_vma=False)
```

```python
import functools

import jax
import jax.numpy as jnp
from jax import lax
from jax.experimental import pallas as pl
from jax.experimental.pallas import tpu as pltpu
from jax.sharding import PartitionSpec as P

CAP = 16
BLK = 4
EXTRA = 16
F32 = jnp.float32
BF16 = jnp.bfloat16


def nn(a, b):
    return lax.dot_general(a, b, (((1,), (0,)), ((), ())), preferred_element_type=F32)


def nt(a, b):
    return lax.dot_general(a, b, (((1,), (1,)), ((), ())), preferred_element_type=F32)


def tn(a, b):
    return lax.dot_general(a, b, (((0,), (0,)), ((), ())), preferred_element_type=F32)


def pack_kernel(hidden_hbm, ids_hbm, gates_hbm, own_ref, ids_ref, gates_ref, sems):
    tokens, width = hidden_hbm.shape
    choose = ids_ref.shape[0]
    copies = [
        pltpu.make_async_copy(hidden_hbm, own_ref.at[pl.ds(0, tokens)], sems.at[0]),
        pltpu.make_async_copy(ids_hbm, ids_ref, sems.at[1]),
        pltpu.make_async_copy(gates_hbm, gates_ref, sems.at[2]),
    ]
    for copy in copies:
        copy.start()
    for copy in copies:
        copy.wait()
    gates = gates_ref[...]
    high = gates.astype(BF16).astype(F32)
    fill = jnp.zeros((8 - choose, tokens), F32)
    top = jnp.concatenate([jnp.concatenate([ids_ref[...].astype(F32), fill], axis=0), jnp.concatenate([high, fill], axis=0)], axis=1)
    low = jnp.concatenate([jnp.concatenate([gates - high, fill], axis=0), jnp.zeros((8, width - tokens), F32)], axis=1)
    own_ref[tokens:tokens + EXTRA, :] = jnp.concatenate([top, low], axis=0).astype(BF16)


def routing(info, choose, tokens):
    info = info.astype(F32)
    return info[0:choose, 0:tokens], info[0:choose, tokens:2 * tokens] + info[8:8 + choose, 0:tokens]


def columns(me, mask, width):
    return pl.ds(pl.multiple_of(lax.bitwise_xor(me, mask) * width, width), width)


def send_home(home_keep, home_send, me, onehot, rows, tokens, width):
    for s in range(onehot.shape[0]):
        for q in range(4):
            home = home_send if q % 2 else home_keep
            home[q // 2, s, 0:tokens, :] = tn(onehot[s], rows[s, :, columns(me, q, width)]).astype(BF16)


RING = 4
GROUP = 2


def ring(weight, slots, sems, columns=None):
    depth = slots.shape[0]

    def load(e):
        slot = lax.rem(e, depth)
        source = weight.at[e] if columns is None else weight.at[e, :, columns]
        return pltpu.make_async_copy(source, slots.at[slot], sems.at[slot])

    def start(e):
        @pl.when(e < weight.shape[0])
        def _():
            load(e).start()

    for e in range(min(depth, weight.shape[0])):
        load(jnp.int32(e)).start()
    if depth >= weight.shape[0]:
        return lambda e: None, lambda e: load(e).wait()
    return lambda e: start(e + depth), lambda e: load(e).wait()


def slot_of(slots, e):
    return slots[lax.rem(e, slots.shape[0])]


def forward_kernel(
    choose, capacity_ref, o0, o1, o2, o3, b0, b1, b2, b3, gate_ref, up_ref, down_hbm, later_ref,
    out_rows, rows_ref, act_ref, a_ref, slope_ref, silu_ref, onehot, slot_gate,
    down_ref, down_sems,
):
    sources, slots, tokens = onehot.shape
    experts = slots // CAP
    width = b0.shape[2]
    me = lax.axis_index("etp")
    first = lax.axis_index("expert") * experts
    start_down, wait_down = ring(down_hbm, down_ref, down_sems)
    row = lax.broadcasted_iota(jnp.int32, (tokens, tokens), 0)
    col = lax.broadcasted_iota(jnp.int32, (tokens, tokens), 1)
    before = jnp.where(row < col, 1.0, 0.0).astype(BF16)
    expert = lax.broadcasted_iota(jnp.int32, (experts, tokens), 0)
    mine = (first + expert).astype(F32)
    limit = jnp.zeros((experts, tokens), jnp.int32)
    for e in range(experts):
        limit = jnp.where(expert == e, capacity_ref[first + e] * BLK, limit)
    limit = limit.astype(F32)
    place = lax.broadcasted_iota(jnp.int32, (experts, CAP, tokens), 1).astype(F32)
    for s in range(sources):
        block = [o[...] for o in (o0, o1, o2, o3)] if s == 0 else [b[s - 1] for b in (b0, b1, b2, b3)]
        ids, gates = routing(block[0][tokens:tokens + EXTRA, :], choose, tokens)
        named = jnp.zeros((experts, tokens), F32)
        gate = jnp.zeros((experts, tokens), F32)
        for k in range(choose):
            hit = ids[k:k + 1, :] == mine
            named = named + jnp.where(hit, 1.0, 0.0)
            gate = gate + jnp.where(hit, gates[k:k + 1, :], 0.0)
        rank = nn(named.astype(BF16), before)
        rank = jnp.where((named > 0.5) & (rank < limit), rank, -1.0)
        chosen = jnp.where(rank[:, None, :] == place, 1.0, 0.0)
        gate_of = jnp.sum(chosen * gate[:, None, :], axis=2, keepdims=True)
        slot_gate[:, s * CAP:(s + 1) * CAP, :] = jnp.broadcast_to(gate_of, chosen.shape)
        table = chosen.reshape(slots, tokens).astype(BF16)
        onehot[s] = table
        for q in range(4):
            picked = nn(table, block[q][0:tokens, :]).astype(BF16).reshape(experts, CAP, width)
            rows_ref[:, s * CAP:(s + 1) * CAP, columns(me, q, width)] = picked

    def activate(e):
        x = rows_ref[e]
        hidden_gate = nt(x, gate_ref[e])
        hidden_up = nt(x, up_ref[e])
        sigma = jax.nn.sigmoid(hidden_gate)
        silu = hidden_gate * sigma
        activ = (silu * hidden_up).astype(BF16)
        act_ref[e] = activ
        slope_ref[e] = hidden_up * sigma * (1.0 + hidden_gate * (1.0 - sigma))
        silu_ref[e] = silu
        a_ref[e] = (activ.astype(F32) * slot_gate[e][:, 0:1]).astype(BF16)

    def project(e):
        out = nn(a_ref[e], slot_of(down_ref, e)).astype(BF16)
        at = pl.ds(pl.multiple_of(e * CAP, CAP), CAP)
        for s in range(sources):
            out_rows[s, at, :] = out[s * CAP:(s + 1) * CAP]

    def both(e):
        before, now = [e - GROUP + i for i in range(GROUP)], [e + i for i in range(GROUP)]
        for i in before:
            wait_down(i)
        for i, j in zip(before, now):
            activate(j)
            project(i)
        for i in before:
            start_down(i)

    skewed(experts, activate, wait_down, project, both)


def skewed(experts, first, wait, second, both):
    for e in range(GROUP):
        first(jnp.int32(e))

    def turn(i, _):
        both(i * GROUP)
        return 0

    lax.fori_loop(1, experts // GROUP, turn, 0)
    for e in range(experts - GROUP, experts):
        wait(jnp.int32(e))
    for e in range(experts - GROUP, experts):
        second(jnp.int32(e))


def home_kernel(onehot, rows, *refs):
    keep, send = refs[-2:]
    send_home(keep, send, lax.axis_index("etp"), onehot, rows, keep.shape[2], keep.shape[3])


def half(me, other, size):
    return pl.ds(pl.multiple_of(lax.bitwise_xor(me // 2, other) * size, size), size)


def half_home(me, onehot, rows, keep, send, tokens, width):
    for s in range(onehot.shape[0]):
        for q, home in enumerate((keep, send)):
            at = pl.multiple_of(lax.rem(lax.bitwise_xor(me, q), 2) * width, width)
            home[s, 0:tokens, :] = tn(onehot[s], rows[s, :, pl.ds(at, width)]).astype(BF16)


def values_kernel(choose, onehot, rows, dots, own_ref, info_ref, *refs):
    keep, send, value_ref = refs[-3:]
    sources, slots, tokens = onehot.shape
    experts = slots // CAP
    width = keep.shape[2]
    half_home(lax.axis_index("etp"), onehot, rows, keep, send, tokens, width)
    expert = lax.broadcasted_iota(jnp.int32, (experts, tokens), 0)
    mine = (lax.axis_index("expert") * experts + expert).astype(F32)
    for s in range(sources):
        info = own_ref[tokens:tokens + EXTRA, :] if s == 0 else info_ref[s - 1, tokens:tokens + EXTRA, :]
        ids, _ = routing(info, choose, tokens)
        chosen = onehot[s].astype(F32).reshape(experts, CAP, tokens)
        share = jnp.sum(chosen * dots[:, s * CAP:(s + 1) * CAP, :], axis=1)
        values = [jnp.sum(jnp.where(ids[k:k + 1, :] == mine, share, 0.0), axis=0, keepdims=True) for k in range(choose)]
        values = jnp.concatenate(values + [jnp.zeros((EXTRA - choose, tokens), F32)], axis=0)
        values = jnp.concatenate([values, jnp.zeros((EXTRA, width - tokens), F32)], axis=1).astype(BF16)
        keep[s, tokens:tokens + EXTRA, :] = values
        send[s, tokens:tokens + EXTRA, :] = values
        value_ref[s] = values


def own_kernel(gate_ref, up_ref, p_ref, q_ref, onehot, slot_gate, value_ref, earlier_ref, keep, send, back_rows):
    sources, slots, tokens = onehot.shape
    width = keep.shape[2]
    me = lax.axis_index("etp")
    here = half(me, 0, 2 * width)

    def turn(i, _):
        for e in [i * GROUP + j for j in range(GROUP)]:
            back = nn(p_ref[e], gate_ref[e, :, here]) + nn(q_ref[e], up_ref[e, :, here])
            back = (back * slot_gate[e][:, 0:1]).astype(BF16)
            at = pl.ds(pl.multiple_of(e * CAP, CAP), CAP)
            for s in range(sources):
                back_rows[s, at, :] = back[s * CAP:(s + 1) * CAP]
        return 0

    lax.fori_loop(0, slots // CAP // GROUP, turn, 0)
    half_home(me, onehot, back_rows, keep, send, tokens, width)
    for s in range(sources):
        keep[s, tokens:tokens + EXTRA, :] = value_ref[s]
        send[s, tokens:tokens + EXTRA, :] = value_ref[s]


def backward_kernel(
    a0, a1, a2, a3, n0, n1, n2, n3,
    gate_ref, up_ref, down_hbm, act_ref, slope_ref, silu_ref, onehot, slot_gate, earlier_ref,
    back_rows, dots, rows_ref, p_ref, q_ref,
    down_ref, down_sems,
):
    sources, slots, tokens = onehot.shape
    experts = slots // CAP
    width = a0.shape[2]
    me = lax.axis_index("etp")
    start_down, wait_down = ring(down_hbm, down_ref, down_sems)
    there = half(me, 1, 2 * width)
    for s, (here, near) in enumerate(((a0, n0), (a1, n1), (a2, n2), (a3, n3))):
        for q in range(4):
            block = (near if q % 2 else here)[q // 2]
            picked = nn(onehot[s], block).astype(BF16).reshape(experts, CAP, width)
            rows_ref[:, s * CAP:(s + 1) * CAP, columns(me, q, width)] = picked

    def slopes(e):
        grad = nt(rows_ref[e], slot_of(down_ref, e))
        activ = act_ref[e].astype(F32)
        dots[e] = jnp.broadcast_to(jnp.sum(activ * grad, axis=1, keepdims=True), dots.shape[1:])
        grad = grad * slot_gate[e][:, 0:1]
        p_ref[e] = (grad * slope_ref[e]).astype(BF16)
        q_ref[e] = (grad * silu_ref[e]).astype(BF16)

    def project(e):
        back = nn(p_ref[e], gate_ref[e, :, there]) + nn(q_ref[e], up_ref[e, :, there])
        back = (back * slot_gate[e][:, 0:1]).astype(BF16)
        at = pl.ds(pl.multiple_of(e * CAP, CAP), CAP)
        for s in range(sources):
            back_rows[s, at, :] = back[s * CAP:(s + 1) * CAP]

    def first(e):
        wait_down(e)
        slopes(e)
        start_down(e)

    def both(e):
        before, now = [e - GROUP + i for i in range(GROUP)], [e + i for i in range(GROUP)]
        for i in now:
            wait_down(i)
        for i, j in zip(before, now):
            slopes(j)
            project(i)
        for i in now:
            start_down(i)

    skewed(experts, first, lambda e: None, project, both)


def add_kernel(keep, came, *refs):
    near, far = refs[-2:]
    for s in range(near.shape[0]):
        far[s] = (keep[1, s].astype(F32) + came[1, s].astype(F32)).astype(BF16)
        near[s] = (keep[0, s].astype(F32) + came[0, s].astype(F32)).astype(BF16)


def pair_kernel(keep, came, *refs):
    refs[-1][...] = (keep[...].astype(F32) + came[...].astype(F32)).astype(BF16)


def chips_kernel(out_near, out_came, back_keep, back_near, back_came, *refs):
    sources, tokens = out_near.shape[:2]
    parts = refs[-sources:]
    for s in range(sources):
        parts[s][0:tokens, :] = (out_near[s].astype(F32) + out_came[s].astype(F32)).astype(BF16)
        back = back_keep[s].astype(F32) + back_near[s].astype(F32) + back_came[s].astype(F32)
        parts[s][tokens:, :] = back.astype(BF16)


def total_kernel(count, *refs):
    out_ref, back_ref, value_ref = refs[count:]
    tokens = out_ref.shape[0]
    total = refs[0][...].astype(F32)
    for ref in refs[1:count]:
        total = total + ref[...].astype(F32)
    out_ref[...] = total[0:tokens].astype(BF16)
    back_ref[...] = total[tokens:2 * tokens].astype(BF16)
    value_ref[...] = total[2 * tokens:2 * tokens + value_ref.shape[0], 0:value_ref.shape[1]]


BANKS = 8
TURN = 4


def product_kernel(jobs, *refs):
    lefts, rights, outs = (refs[i * len(jobs):(i + 1) * len(jobs)] for i in range(3))
    held, sems = refs[-2:]
    outs = refs[-2 - len(jobs):-2]

    def store(job, e, slot):
        return pltpu.make_async_copy(held.at[slot], outs[job].at[e], sems.at[slot])

    def turn(job, first, done, i, full):
        for pair in range(0, TURN, 2):
            places = [(first + i * TURN + j, lax.rem(done + i * TURN + j, BANKS)) for j in (pair, pair + 1)]
            if full:
                for e, slot in places:
                    store(job, e, slot).wait()
            for e, slot in places:
                held[slot] = tn(lefts[job][e], rights[job][e]).astype(BF16)
            for e, slot in places:
                store(job, e, slot).start()

    done = 0
    for job, (first, last) in enumerate(jobs):
        fresh = max(0, min(BANKS - done, last - first) // TURN)
        for i in range(fresh):
            turn(job, first, done, jnp.int32(i), False)

        def later(i, _, job=job, first=first, done=done):
            turn(job, first, done, i, True)
            return 0

        lax.fori_loop(fresh, (last - first) // TURN, later, 0)
        done = done + last - first
    for slot in range(min(done, BANKS)):
        store(0, jobs[0][0], slot).wait()


def load_kernel(source, target, token, sems):
    token[...] = jnp.zeros_like(token)
    copies = [pltpu.make_async_copy(source.at[e], target.at[e], sems.at[e]) for e in range(source.shape[0])]
    for copy in copies:
        copy.start()
    for copy in copies:
        copy.wait()


def in_vmem(weight):
    return pl.pallas_call(
        load_kernel,
        in_specs=[pl.BlockSpec(memory_space=pltpu.HBM)],
        out_specs=[pl.BlockSpec(memory_space=pltpu.VMEM)] * 2,
        out_shape=[pltpu.VMEM(weight.shape, BF16), jax.ShapeDtypeStruct((8, 128), F32)],
        scratch_shapes=[pltpu.SemaphoreType.DMA((weight.shape[0],))],
        compiler_params=pltpu.CompilerParams(vmem_limit_bytes=4 * 1024 * 1024),
        cost_estimate=pl.CostEstimate(flops=0, bytes_accessed=2 * weight.size, transcendentals=0),
    )(pltpu.with_memory_space_constraint(weight, pltpu.HBM))


def join_kernel(count, *refs):
    for i in range(count):
        refs[-1][i] = refs[i][...]


def join(arrays, *there):
    return kernel_call(
        functools.partial(join_kernel, len(arrays)),
        [jax.ShapeDtypeStruct((len(arrays),) + arrays[0].shape, arrays[0].dtype)],
        [],
        0,
        limit=2,
    )(*arrays, *there)[0]


def kernel_call(kernel, out_shape, scratch, flops, out_specs=None, limit=4, in_hbm=(), aliases={}):
    def call(*operands):
        specs = [
            pl.BlockSpec(memory_space=pltpu.HBM if i in in_hbm else pltpu.SMEM if x.ndim == 1 else pltpu.VMEM)
            for i, x in enumerate(operands)
        ]
        operands = [
            pltpu.with_memory_space_constraint(x, pltpu.HBM) if i in in_hbm else x for i, x in enumerate(operands)
        ]
        return pl.pallas_call(
            kernel,
            in_specs=specs,
            out_specs=out_specs or [pl.BlockSpec(memory_space=pltpu.VMEM)] * len(out_shape),
            out_shape=out_shape,
            scratch_shapes=scratch,
            input_output_aliases=aliases,
            compiler_params=pltpu.CompilerParams(vmem_limit_bytes=limit * 1024 * 1024),
            cost_estimate=pl.CostEstimate(flops=flops, bytes_accessed=flops // 32, transcendentals=0),
        )(*operands)

    return call


def weight_grads(jobs, begun=None, *earlier):
    count = len(jobs)
    lefts, rights = [job[0] for job in jobs], [job[1] for job in jobs]
    experts, rows, units = lefts[0].shape
    model = rights[0].shape[2]
    shape = jax.ShapeDtypeStruct((experts, units, model), BF16)
    work = sum(job[3] - job[2] for job in jobs)
    more = [] if begun is None else [begun]
    return kernel_call(
        functools.partial(product_kernel, [job[2:] for job in jobs]),
        [shape] * count,
        [pltpu.VMEM((BANKS, units, model), BF16), pltpu.SemaphoreType.DMA((BANKS,))],
        2 * work * rows * units * model,
        out_specs=[pl.BlockSpec(memory_space=pltpu.HBM)] * count,
        limit=8,
        in_hbm=(2 * count,) if more else (),
        aliases={2 * count: 0} if more else {},
    )(*lefts, *rights, *more, *earlier)


def swap(array, bit, axis="etp"):
    count = lax.axis_size(axis)
    return lax.ppermute(array, axis, [(i, i ^ bit) for i in range(count)])


def add_cores(keep, came, *earlier):
    shape = jax.ShapeDtypeStruct(keep.shape[1:], BF16)
    hbm = [2] if earlier else []
    return kernel_call(add_kernel, [shape, shape], [], 0, limit=2, in_hbm=hbm)(keep, came, *earlier)


def gathered_body(
    hidden_in, out_grad, expert_ids, gate_values, capacity_blocks, gate_weight, up_weight, down_weight
):
    sources = lax.axis_size("expert")
    tokens, width = hidden_in.shape
    choose = expert_ids.shape[1]
    local_experts, units, model = down_weight.shape
    slots = local_experts * CAP
    rows = sources * CAP
    gate_t, gate_there = in_vmem(jnp.swapaxes(gate_weight, 1, 2))
    up_t, up_there = in_vmem(jnp.swapaxes(up_weight, 1, 2))
    product = 2 * local_experts * rows * units * model
    held = lambda *shape, kind=BF16: pltpu.VMEM(shape, kind)
    sent = lambda *shape: jax.ShapeDtypeStruct(shape, BF16)

    own = kernel_call(
        pack_kernel,
        [sent(tokens + EXTRA, width)],
        [pltpu.VMEM((choose, tokens), jnp.int32), pltpu.VMEM((choose, tokens), F32), pltpu.SemaphoreType.DMA((3,))],
        0,
        limit=2,
        in_hbm=(0, 1, 2),
    )(hidden_in, expert_ids.T, gate_values.T)[0]
    came = [swap(own, s, "expert") for s in range(1, sources)]
    own_across = swap(own, 2)
    grad_across = swap(out_grad, 2)
    came = join(came, gate_there, own_across, grad_across)
    came_across_there = swap(came, 2)
    across_near = swap(own_across, 1)
    grads = join([out_grad, grad_across], came)
    grads = [grads] + [swap(grads, s, "expert") for s in range(1, sources)]

    came_across = join([came_across_there], up_there, grads[1])[0]
    out_rows, x_rows, activ, scaled, slope, silu, onehot, slot_gate = kernel_call(
        functools.partial(forward_kernel, choose),
        [
            held(sources, slots, model),
            held(local_experts, rows, model),
            held(local_experts, rows, units),
            held(local_experts, rows, units),
            held(local_experts, rows, units, kind=F32),
            held(local_experts, rows, units, kind=F32),
            held(sources, slots, tokens),
            held(local_experts, rows, tokens, kind=F32),
        ],
        [pltpu.VMEM((RING, units, model), BF16), pltpu.SemaphoreType.DMA((RING,))],
        3 * product,
        limit=6,
        in_hbm=(11,),
    )(
        capacity_blocks,
        own, swap(own, 1), own_across, across_near,
        came, swap(came, 1), came_across, swap(came_across, 1),
        gate_t, up_t, down_weight, grads[0],
    )

    keep, send = kernel_call(
        home_kernel, [sent(2, sources, tokens, width)] * 2, [], 2 * slots * sources * tokens * model, limit=2,
    )(onehot, out_rows, *grads)
    out_near, out_far = add_cores(keep, swap(send, 1))
    back_rows, dots, y_rows, gate_part, up_part = kernel_call(
        backward_kernel,
        [
            held(sources, slots, model // 2),
            held(local_experts, rows, tokens, kind=F32),
            held(local_experts, rows, model),
            held(local_experts, rows, units),
            held(local_experts, rows, units),
        ],
        [pltpu.VMEM((RING, units, model), BF16), pltpu.SemaphoreType.DMA((RING,))],
        3 * product,
        limit=8,
        in_hbm=(10,),
    )(
        *grads, *[swap(x, 1) for x in grads],
        gate_t, up_t, down_weight, activ, slope, silu, onehot, slot_gate, out_near,
    )

    out_came = swap(out_far, 2)
    back_sum = sent(sources, tokens + EXTRA, width)
    far_keep, far_send, values = kernel_call(
        functools.partial(values_kernel, choose),
        [back_sum, back_sum, held(sources, EXTRA, width)],
        [],
        slots * sources * tokens * model,
        limit=2,
    )(onehot, back_rows, dots, own, came, out_came)
    near_keep, near_send = kernel_call(
        own_kernel,
        [back_sum, back_sum],
        [pltpu.VMEM((sources, slots, model // 2), BF16)],
        product,
        limit=4,
    )(gate_t, up_t, gate_part, up_part, onehot, slot_gate, values, far_keep)
    (back_far,) = kernel_call(pair_kernel, [back_sum], [], 0, limit=2)(far_keep, swap(far_send, 1), near_keep)
    some = local_experts // 2
    up_grad, down_grad = weight_grads(
        [(up_part, x_rows, 0, local_experts), (scaled, y_rows, 0, some)], None, back_far
    )
    height = 2 * tokens + EXTRA
    parts = kernel_call(chips_kernel, [sent(height, width)] * sources, [], 0, limit=2, in_hbm=(5,))(
        out_near, out_came, near_keep, swap(near_send, 1), swap(back_far, 2), up_grad
    )
    down_grad, gate_grad = weight_grads(
        [(scaled, y_rows, some, local_experts), (gate_part, x_rows, 0, local_experts)], down_grad, parts[0]
    )
    layer_out, input_grad, value_grad = kernel_call(
        functools.partial(total_kernel, sources),
        [sent(tokens, width), sent(tokens, width), jax.ShapeDtypeStruct((choose, tokens), F32)],
        [],
        0,
        limit=2,
    )(parts[0], *[swap(parts[s], s, "expert") for s in range(1, sources)])
    return (
        layer_out,
        input_grad,
        value_grad.T,
        jnp.swapaxes(gate_grad, 1, 2),
        jnp.swapaxes(up_grad, 1, 2),
        down_grad,
    )


def slot_layout(expert_ids, capacity_blocks):
    tokens_here, choose = expert_ids.shape
    experts = capacity_blocks.shape[0]
    flat_ids = expert_ids.reshape(-1)
    onehot = (flat_ids[:, None] == jnp.arange(experts, dtype=jnp.int32)[None, :]).astype(jnp.int32)
    before = jnp.cumsum(onehot, axis=0) - onehot
    ranks = jnp.sum(before * onehot, axis=1)
    limits = jnp.sum(onehot * capacity_blocks[None, :], axis=1) * BLK
    kept = ranks < limits
    slots = jnp.where(kept, flat_ids * CAP + ranks, experts * CAP)
    token_index = jnp.arange(tokens_here * choose, dtype=jnp.int32) // choose
    owners = (
        jnp.full((experts * CAP,), tokens_here, jnp.int32).at[slots].set(token_index, mode="drop")
    )
    return (kept.reshape(tokens_here, choose), slots.reshape(tokens_here, choose), owners)


def outgoing(rows, owners, experts, scale):
    padded = jnp.concatenate([rows, jnp.zeros((1, rows.shape[1]), rows.dtype)], 0)
    picked = padded[owners]
    if scale is not None:
        picked = (scale[:, None] * picked.astype(jnp.float32)).astype(jnp.bfloat16)
    return picked.reshape(experts, CAP, rows.shape[1])


def local_grads(hidden_gate, hidden_up, act_grad):
    sigma = jax.nn.sigmoid(hidden_gate)
    gate_part = (act_grad * hidden_up * sigma * (1.0 + hidden_gate * (1.0 - sigma))).astype(
        jnp.bfloat16
    )
    up_part = (act_grad * jax.nn.silu(hidden_gate)).astype(jnp.bfloat16)
    return (gate_part, up_part)


def combine(back, slots, weights):
    padded = jnp.concatenate([back, jnp.zeros((1, back.shape[1]), back.dtype)], 0)
    picked = padded[slots].astype(jnp.float32)
    return (jnp.einsum("tk,tkw->tw", weights, picked), picked)


def dispatched_body(
    hidden_in,
    out_grad,
    expert_ids,
    gate_values,
    capacity_blocks,
    gate_weight,
    up_weight,
    down_weight,
):
    experts = capacity_blocks.shape[0]
    sources = lax.axis_size("expert")
    local_experts = gate_weight.shape[0]
    kept, slots, owners = slot_layout(expert_ids, capacity_blocks)
    weights = jnp.where(kept, gate_values, 0.0)
    slot_gates = (
        jnp.zeros((experts * CAP,), jnp.float32)
        .at[slots.reshape(-1)]
        .set(weights.reshape(-1), mode="drop")
    )
    send_in = outgoing(hidden_in, owners, experts, None)
    send_grad = outgoing(out_grad, owners, experts, slot_gates)
    recv_in, recv_grad = (
        lax.all_to_all(send_in, "expert", split_axis=0, concat_axis=0, tiled=True),
        lax.all_to_all(send_grad, "expert", split_axis=0, concat_axis=0, tiled=True),
    )
    share = recv_in.shape[2]
    share_in = recv_in.reshape(sources, local_experts, CAP, share)
    share_grad = recv_grad.reshape(sources, local_experts, CAP, share)
    piece = lax.all_gather(share_in, "etp", axis=3, tiled=True)
    hidden_gate = jnp.einsum(
        "secn,enf->secf", piece, gate_weight, preferred_element_type=jnp.float32
    )
    hidden_up = jnp.einsum("secn,enf->secf", piece, up_weight, preferred_element_type=jnp.float32)
    activ = (jax.nn.silu(hidden_gate) * hidden_up).astype(jnp.bfloat16)
    piece = lax.all_gather(share_grad, "etp", axis=3, tiled=True)
    act_grad = jnp.einsum("secn,efn->secf", piece, down_weight, preferred_element_type=jnp.float32)
    columns = jnp.einsum("secf,secn->efn", activ, piece, preferred_element_type=jnp.float32)
    act_grad, down_grad = (act_grad, columns)
    gate_part, up_part = local_grads(hidden_gate, hidden_up, act_grad)
    stacked = jnp.stack([gate_part, up_part])
    weight_grads = jnp.einsum(
        "secn,gsecf->genf",
        lax.all_gather(share_in, "etp", axis=3, tiled=True),
        stacked,
        preferred_element_type=jnp.float32,
    )
    out_part = jnp.einsum("secf,efd->secd", activ, down_weight, preferred_element_type=jnp.float32)
    back_part = jnp.einsum(
        "secf,edf->secd", gate_part, gate_weight, preferred_element_type=jnp.float32
    )
    back_part = back_part + jnp.einsum(
        "secf,edf->secd", up_part, up_weight, preferred_element_type=jnp.float32
    )
    out_rows = lax.psum_scatter(
        out_part.astype(jnp.bfloat16), "etp", scatter_dimension=3, tiled=True
    )
    home_out = lax.all_to_all(out_rows, "expert", split_axis=0, concat_axis=0, tiled=True)
    share_width = home_out.shape[3]
    layer_sum, picked = combine(home_out.reshape(experts * CAP, share_width), slots, weights)
    dot_part = jnp.einsum("tw,tkw->tk", out_grad.astype(jnp.float32), picked) * kept.astype(
        jnp.float32
    )
    gate_value_grad = lax.psum(dot_part, "etp")
    back_rows = lax.psum_scatter(
        back_part.astype(jnp.bfloat16), "etp", scatter_dimension=3, tiled=True
    )
    home_back = lax.all_to_all(back_rows, "expert", split_axis=0, concat_axis=0, tiled=True)
    input_sum, returned = combine(home_back.reshape(experts * CAP, share_width), slots, weights)
    return (
        layer_sum.astype(jnp.bfloat16),
        input_sum.astype(jnp.bfloat16),
        gate_value_grad,
        weight_grads[0].astype(jnp.bfloat16),
        weight_grads[1].astype(jnp.bfloat16),
        down_grad.astype(jnp.bfloat16),
    )


def body(*operands):
    hidden_in, gate_weight = operands[0], operands[5]
    if lax.axis_size("expert") == 4 and lax.axis_size("etp") == 4 and hidden_in.shape[0] <= gate_weight.shape[0] * CAP:
        return gathered_body(*operands)
    return dispatched_body(*operands)


def solution(mesh):
    in_specs = (
        P(("groups", "expert"), "etp"),
        P(("groups", "expert"), "etp"),
        P(("groups", "expert"), None),
        P(("groups", "expert"), None),
        P("groups"),
        P("expert", None, "etp"),
        P("expert", None, "etp"),
        P("expert", "etp", None),
    )
    out_specs = (
        P(("groups", "expert"), "etp"),
        P(("groups", "expert"), "etp"),
        P(("groups", "expert"), None),
        P(("groups", "expert"), None, "etp"),
        P(("groups", "expert"), None, "etp"),
        P(("groups", "expert"), "etp", None),
    )
    return jax.shard_map(body, mesh=mesh, in_specs=in_specs, out_specs=out_specs, check_vma=False)
```

```python
import functools

import jax
import jax.numpy as jnp
from jax import lax
from jax.experimental import pallas as pl
from jax.experimental.pallas import tpu as pltpu
from jax.sharding import PartitionSpec as P

CAP = 16
BLK = 4
EXTRA = 16
F32 = jnp.float32
BF16 = jnp.bfloat16


def nn(a, b):
    return lax.dot_general(a, b, (((1,), (0,)), ((), ())), preferred_element_type=F32)


def nt(a, b):
    return lax.dot_general(a, b, (((1,), (1,)), ((), ())), preferred_element_type=F32)


def tn(a, b):
    return lax.dot_general(a, b, (((0,), (0,)), ((), ())), preferred_element_type=F32)


def pack_kernel(hidden_hbm, ids_hbm, gates_hbm, own_ref, ids_ref, gates_ref, sems):
    tokens, width = hidden_hbm.shape
    choose = ids_ref.shape[0]
    copies = [
        pltpu.make_async_copy(hidden_hbm, own_ref.at[pl.ds(0, tokens)], sems.at[0]),
        pltpu.make_async_copy(ids_hbm, ids_ref, sems.at[1]),
        pltpu.make_async_copy(gates_hbm, gates_ref, sems.at[2]),
    ]
    for copy in copies:
        copy.start()
    for copy in copies:
        copy.wait()
    gates = gates_ref[...]
    high = gates.astype(BF16).astype(F32)
    fill = jnp.zeros((8 - choose, tokens), F32)
    top = jnp.concatenate([jnp.concatenate([ids_ref[...].astype(F32), fill], axis=0), jnp.concatenate([high, fill], axis=0)], axis=1)
    low = jnp.concatenate([jnp.concatenate([gates - high, fill], axis=0), jnp.zeros((8, width - tokens), F32)], axis=1)
    own_ref[tokens:tokens + EXTRA, :] = jnp.concatenate([top, low], axis=0).astype(BF16)


def routing(info, choose, tokens):
    info = info.astype(F32)
    return info[0:choose, 0:tokens], info[0:choose, tokens:2 * tokens] + info[8:8 + choose, 0:tokens]


def columns(me, mask, width):
    return pl.ds(pl.multiple_of(lax.bitwise_xor(me, mask) * width, width), width)


def send_home(home_keep, home_send, me, onehot, rows, tokens, width):
    for s in range(onehot.shape[0]):
        for q in range(4):
            home = home_send if q % 2 else home_keep
            home[q // 2, s, 0:tokens, :] = tn(onehot[s], rows[s, :, columns(me, q, width)]).astype(BF16)


RING = 8
GROUP = 4


def ring(weight, slots, sems, columns=None):
    depth = slots.shape[0]

    def load(e):
        slot = lax.rem(e, depth)
        source = weight.at[e] if columns is None else weight.at[e, :, columns]
        return pltpu.make_async_copy(source, slots.at[slot], sems.at[slot])

    def start(e):
        @pl.when(e < weight.shape[0])
        def _():
            load(e).start()

    for e in range(min(depth, weight.shape[0])):
        load(jnp.int32(e)).start()
    if depth >= weight.shape[0]:
        return lambda e: None, lambda e: load(e).wait()
    return lambda e: start(e + depth), lambda e: load(e).wait()


def slot_of(slots, e):
    return slots[lax.rem(e, slots.shape[0])]


def forward_kernel(
    choose, capacity_ref, o0, o1, o2, o3, b0, b1, b2, b3, gate_ref, up_ref, down_hbm, later_ref,
    out_rows, rows_ref, act_ref, a_ref, slope_ref, silu_ref, onehot, slot_gate,
    down_ref, down_sems,
):
    sources, slots, tokens = onehot.shape
    experts = slots // CAP
    width = b0.shape[2]
    me = lax.axis_index("etp")
    first = lax.axis_index("expert") * experts
    start_down, wait_down = ring(down_hbm, down_ref, down_sems)
    row = lax.broadcasted_iota(jnp.int32, (tokens, tokens), 0)
    col = lax.broadcasted_iota(jnp.int32, (tokens, tokens), 1)
    before = jnp.where(row < col, 1.0, 0.0).astype(BF16)
    expert = lax.broadcasted_iota(jnp.int32, (experts, tokens), 0)
    mine = (first + expert).astype(F32)
    limit = jnp.zeros((experts, tokens), jnp.int32)
    for e in range(experts):
        limit = jnp.where(expert == e, capacity_ref[first + e] * BLK, limit)
    limit = limit.astype(F32)
    place = lax.broadcasted_iota(jnp.int32, (experts, CAP, tokens), 1).astype(F32)
    for s in range(sources):
        block = [o[...] for o in (o0, o1, o2, o3)] if s == 0 else [b[s - 1] for b in (b0, b1, b2, b3)]
        ids, gates = routing(block[0][tokens:tokens + EXTRA, :], choose, tokens)
        named = jnp.zeros((experts, tokens), F32)
        gate = jnp.zeros((experts, tokens), F32)
        for k in range(choose):
            hit = ids[k:k + 1, :] == mine
            named = named + jnp.where(hit, 1.0, 0.0)
            gate = gate + jnp.where(hit, gates[k:k + 1, :], 0.0)
        rank = nn(named.astype(BF16), before)
        rank = jnp.where((named > 0.5) & (rank < limit), rank, -1.0)
        chosen = jnp.where(rank[:, None, :] == place, 1.0, 0.0)
        gate_of = jnp.sum(chosen * gate[:, None, :], axis=2, keepdims=True)
        slot_gate[:, s * CAP:(s + 1) * CAP, :] = jnp.broadcast_to(gate_of, chosen.shape)
        table = chosen.reshape(slots, tokens).astype(BF16)
        onehot[s] = table
        for q in range(4):
            picked = nn(table, block[q][0:tokens, :]).astype(BF16).reshape(experts, CAP, width)
            rows_ref[:, s * CAP:(s + 1) * CAP, columns(me, q, width)] = picked

    def activate(e):
        x = rows_ref[e]
        hidden_gate = nt(x, gate_ref[e])
        hidden_up = nt(x, up_ref[e])
        sigma = jax.nn.sigmoid(hidden_gate)
        silu = hidden_gate * sigma
        activ = (silu * hidden_up).astype(BF16)
        act_ref[e] = activ
        slope_ref[e] = hidden_up * sigma * (1.0 + hidden_gate * (1.0 - sigma))
        silu_ref[e] = silu
        a_ref[e] = (activ.astype(F32) * slot_gate[e][:, 0:1]).astype(BF16)

    def project(e):
        out = nn(a_ref[e], slot_of(down_ref, e)).astype(BF16)
        at = pl.ds(pl.multiple_of(e * CAP, CAP), CAP)
        for s in range(sources):
            out_rows[s, at, :] = out[s * CAP:(s + 1) * CAP]

    def both(e):
        before, now = [e - GROUP + i for i in range(GROUP)], [e + i for i in range(GROUP)]
        for i in before:
            wait_down(i)
        for i, j in zip(before, now):
            activate(j)
            project(i)
        for i in before:
            start_down(i)

    skewed(experts, activate, wait_down, project, both)


def skewed(experts, first, wait, second, both):
    for e in range(GROUP):
        first(jnp.int32(e))

    def turn(i, _):
        both(i * GROUP)
        return 0

    lax.fori_loop(1, experts // GROUP, turn, 0)
    for e in range(experts - GROUP, experts):
        wait(jnp.int32(e))
    for e in range(experts - GROUP, experts):
        second(jnp.int32(e))


def home_kernel(onehot, rows, *refs):
    keep, send = refs[-2:]
    send_home(keep, send, lax.axis_index("etp"), onehot, rows, keep.shape[2], keep.shape[3])


def half(me, other, size):
    return pl.ds(pl.multiple_of(lax.bitwise_xor(me // 2, other) * size, size), size)


def half_home(me, onehot, rows, keep, send, tokens, width):
    for s in range(onehot.shape[0]):
        for q, home in enumerate((keep, send)):
            at = pl.multiple_of(lax.rem(lax.bitwise_xor(me, q), 2) * width, width)
            home[s, 0:tokens, :] = tn(onehot[s], rows[s, :, pl.ds(at, width)]).astype(BF16)


def values_kernel(choose, onehot, rows, dots, own_ref, info_ref, *refs):
    keep, send, value_ref = refs[-3:]
    sources, slots, tokens = onehot.shape
    experts = slots // CAP
    width = keep.shape[2]
    half_home(lax.axis_index("etp"), onehot, rows, keep, send, tokens, width)
    expert = lax.broadcasted_iota(jnp.int32, (experts, tokens), 0)
    mine = (lax.axis_index("expert") * experts + expert).astype(F32)
    for s in range(sources):
        info = own_ref[tokens:tokens + EXTRA, :] if s == 0 else info_ref[s - 1, tokens:tokens + EXTRA, :]
        ids, _ = routing(info, choose, tokens)
        chosen = onehot[s].astype(F32).reshape(experts, CAP, tokens)
        share = jnp.sum(chosen * dots[:, s * CAP:(s + 1) * CAP, :], axis=1)
        values = [jnp.sum(jnp.where(ids[k:k + 1, :] == mine, share, 0.0), axis=0, keepdims=True) for k in range(choose)]
        values = jnp.concatenate(values + [jnp.zeros((EXTRA - choose, tokens), F32)], axis=0)
        values = jnp.concatenate([values, jnp.zeros((EXTRA, width - tokens), F32)], axis=1).astype(BF16)
        keep[s, tokens:tokens + EXTRA, :] = values
        send[s, tokens:tokens + EXTRA, :] = values
        value_ref[s] = values


def own_kernel(gate_ref, up_ref, p_ref, q_ref, onehot, slot_gate, value_ref, earlier_ref, keep, send, back_rows):
    sources, slots, tokens = onehot.shape
    width = keep.shape[2]
    me = lax.axis_index("etp")
    here = half(me, 0, 2 * width)

    def turn(i, _):
        for e in [i * GROUP + j for j in range(GROUP)]:
            back = nn(p_ref[e], gate_ref[e, :, here]) + nn(q_ref[e], up_ref[e, :, here])
            back = (back * slot_gate[e][:, 0:1]).astype(BF16)
            at = pl.ds(pl.multiple_of(e * CAP, CAP), CAP)
            for s in range(sources):
                back_rows[s, at, :] = back[s * CAP:(s + 1) * CAP]
        return 0

    lax.fori_loop(0, slots // CAP // GROUP, turn, 0)
    half_home(me, onehot, back_rows, keep, send, tokens, width)
    for s in range(sources):
        keep[s, tokens:tokens + EXTRA, :] = value_ref[s]
        send[s, tokens:tokens + EXTRA, :] = value_ref[s]


def backward_kernel(
    a0, a1, a2, a3, n0, n1, n2, n3,
    gate_ref, up_ref, down_hbm, act_ref, slope_ref, silu_ref, onehot, slot_gate, earlier_ref,
    back_rows, dots, rows_ref, p_ref, q_ref,
    down_ref, down_sems,
):
    sources, slots, tokens = onehot.shape
    experts = slots // CAP
    width = a0.shape[2]
    me = lax.axis_index("etp")
    start_down, wait_down = ring(down_hbm, down_ref, down_sems)
    there = half(me, 1, 2 * width)
    for s, (here, near) in enumerate(((a0, n0), (a1, n1), (a2, n2), (a3, n3))):
        for q in range(4):
            block = (near if q % 2 else here)[q // 2]
            picked = nn(onehot[s], block).astype(BF16).reshape(experts, CAP, width)
            rows_ref[:, s * CAP:(s + 1) * CAP, columns(me, q, width)] = picked

    def slopes(e):
        grad = nt(rows_ref[e], slot_of(down_ref, e))
        activ = act_ref[e].astype(F32)
        dots[e] = jnp.broadcast_to(jnp.sum(activ * grad, axis=1, keepdims=True), dots.shape[1:])
        grad = grad * slot_gate[e][:, 0:1]
        p_ref[e] = (grad * slope_ref[e]).astype(BF16)
        q_ref[e] = (grad * silu_ref[e]).astype(BF16)

    def project(e):
        back = nn(p_ref[e], gate_ref[e, :, there]) + nn(q_ref[e], up_ref[e, :, there])
        back = (back * slot_gate[e][:, 0:1]).astype(BF16)
        at = pl.ds(pl.multiple_of(e * CAP, CAP), CAP)
        for s in range(sources):
            back_rows[s, at, :] = back[s * CAP:(s + 1) * CAP]

    def first(e):
        wait_down(e)
        slopes(e)
        start_down(e)

    def both(e):
        before, now = [e - GROUP + i for i in range(GROUP)], [e + i for i in range(GROUP)]
        for i in now:
            wait_down(i)
        for i, j in zip(before, now):
            slopes(j)
            project(i)
        for i in now:
            start_down(i)

    skewed(experts, first, lambda e: None, project, both)


def add_kernel(keep, came, *refs):
    near, far = refs[-2:]
    for s in range(near.shape[0]):
        far[s] = (keep[1, s].astype(F32) + came[1, s].astype(F32)).astype(BF16)
        near[s] = (keep[0, s].astype(F32) + came[0, s].astype(F32)).astype(BF16)


def pair_kernel(keep, came, *refs):
    refs[-1][...] = (keep[...].astype(F32) + came[...].astype(F32)).astype(BF16)


def chips_kernel(out_near, out_came, back_keep, back_near, back_came, *refs):
    sources, tokens = out_near.shape[:2]
    parts = refs[-sources:]
    for s in range(sources):
        parts[s][0:tokens, :] = (out_near[s].astype(F32) + out_came[s].astype(F32)).astype(BF16)
        back = back_keep[s].astype(F32) + back_near[s].astype(F32) + back_came[s].astype(F32)
        parts[s][tokens:, :] = back.astype(BF16)


def total_kernel(count, *refs):
    out_ref, back_ref, value_ref = refs[count:]
    tokens = out_ref.shape[0]
    total = refs[0][...].astype(F32)
    for ref in refs[1:count]:
        total = total + ref[...].astype(F32)
    out_ref[...] = total[0:tokens].astype(BF16)
    back_ref[...] = total[tokens:2 * tokens].astype(BF16)
    value_ref[...] = total[2 * tokens:2 * tokens + value_ref.shape[0], 0:value_ref.shape[1]]


BANKS = 8
TURN = 4


def product_kernel(jobs, *refs):
    lefts, rights, outs = (refs[i * len(jobs):(i + 1) * len(jobs)] for i in range(3))
    held, sems = refs[-2:]
    outs = refs[-2 - len(jobs):-2]

    def store(job, e, slot):
        return pltpu.make_async_copy(held.at[slot], outs[job].at[e], sems.at[slot])

    def turn(job, first, done, i, full):
        for pair in range(0, TURN, 2):
            places = [(first + i * TURN + j, lax.rem(done + i * TURN + j, BANKS)) for j in (pair, pair + 1)]
            if full:
                for e, slot in places:
                    store(job, e, slot).wait()
            for e, slot in places:
                held[slot] = tn(lefts[job][e], rights[job][e]).astype(BF16)
            for e, slot in places:
                store(job, e, slot).start()

    done = 0
    for job, (first, last) in enumerate(jobs):
        fresh = max(0, min(BANKS - done, last - first) // TURN)
        for i in range(fresh):
            turn(job, first, done, jnp.int32(i), False)

        def later(i, _, job=job, first=first, done=done):
            turn(job, first, done, i, True)
            return 0

        lax.fori_loop(fresh, (last - first) // TURN, later, 0)
        done = done + last - first
    for slot in range(min(done, BANKS)):
        store(0, jobs[0][0], slot).wait()


def load_kernel(source, target, token, sems):
    token[...] = jnp.zeros_like(token)
    copies = [pltpu.make_async_copy(source.at[e], target.at[e], sems.at[e]) for e in range(source.shape[0])]
    for copy in copies:
        copy.start()
    for copy in copies:
        copy.wait()


def in_vmem(weight):
    return pl.pallas_call(
        load_kernel,
        in_specs=[pl.BlockSpec(memory_space=pltpu.HBM)],
        out_specs=[pl.BlockSpec(memory_space=pltpu.VMEM)] * 2,
        out_shape=[pltpu.VMEM(weight.shape, BF16), jax.ShapeDtypeStruct((8, 128), F32)],
        scratch_shapes=[pltpu.SemaphoreType.DMA((weight.shape[0],))],
        compiler_params=pltpu.CompilerParams(vmem_limit_bytes=4 * 1024 * 1024),
        cost_estimate=pl.CostEstimate(flops=0, bytes_accessed=2 * weight.size, transcendentals=0),
    )(pltpu.with_memory_space_constraint(weight, pltpu.HBM))


def join_kernel(count, *refs):
    for i in range(count):
        refs[-1][i] = refs[i][...]


def join(arrays, *there):
    return kernel_call(
        functools.partial(join_kernel, len(arrays)),
        [jax.ShapeDtypeStruct((len(arrays),) + arrays[0].shape, arrays[0].dtype)],
        [],
        0,
        limit=2,
    )(*arrays, *there)[0]


def kernel_call(kernel, out_shape, scratch, flops, out_specs=None, limit=4, in_hbm=(), aliases={}):
    def call(*operands):
        specs = [
            pl.BlockSpec(memory_space=pltpu.HBM if i in in_hbm else pltpu.SMEM if x.ndim == 1 else pltpu.VMEM)
            for i, x in enumerate(operands)
        ]
        operands = [
            pltpu.with_memory_space_constraint(x, pltpu.HBM) if i in in_hbm else x for i, x in enumerate(operands)
        ]
        return pl.pallas_call(
            kernel,
            in_specs=specs,
            out_specs=out_specs or [pl.BlockSpec(memory_space=pltpu.VMEM)] * len(out_shape),
            out_shape=out_shape,
            scratch_shapes=scratch,
            input_output_aliases=aliases,
            compiler_params=pltpu.CompilerParams(vmem_limit_bytes=limit * 1024 * 1024),
            cost_estimate=pl.CostEstimate(flops=flops, bytes_accessed=flops // 32, transcendentals=0),
        )(*operands)

    return call


def weight_grads(jobs, begun=None, *earlier):
    count = len(jobs)
    lefts, rights = [job[0] for job in jobs], [job[1] for job in jobs]
    experts, rows, units = lefts[0].shape
    model = rights[0].shape[2]
    shape = jax.ShapeDtypeStruct((experts, units, model), BF16)
    work = sum(job[3] - job[2] for job in jobs)
    more = [] if begun is None else [begun]
    return kernel_call(
        functools.partial(product_kernel, [job[2:] for job in jobs]),
        [shape] * count,
        [pltpu.VMEM((BANKS, units, model), BF16), pltpu.SemaphoreType.DMA((BANKS,))],
        2 * work * rows * units * model,
        out_specs=[pl.BlockSpec(memory_space=pltpu.HBM)] * count,
        limit=8,
        in_hbm=(2 * count,) if more else (),
        aliases={2 * count: 0} if more else {},
    )(*lefts, *rights, *more, *earlier)


def swap(array, bit, axis="etp"):
    count = lax.axis_size(axis)
    return lax.ppermute(array, axis, [(i, i ^ bit) for i in range(count)])


def add_cores(keep, came, *earlier):
    shape = jax.ShapeDtypeStruct(keep.shape[1:], BF16)
    hbm = [2] if earlier else []
    return kernel_call(add_kernel, [shape, shape], [], 0, limit=2, in_hbm=hbm)(keep, came, *earlier)


def gathered_body(
    hidden_in, out_grad, expert_ids, gate_values, capacity_blocks, gate_weight, up_weight, down_weight
):
    sources = lax.axis_size("expert")
    tokens, width = hidden_in.shape
    choose = expert_ids.shape[1]
    local_experts, units, model = down_weight.shape
    slots = local_experts * CAP
    rows = sources * CAP
    gate_t, gate_there = in_vmem(jnp.swapaxes(gate_weight, 1, 2))
    up_t, up_there = in_vmem(jnp.swapaxes(up_weight, 1, 2))
    product = 2 * local_experts * rows * units * model
    held = lambda *shape, kind=BF16: pltpu.VMEM(shape, kind)
    sent = lambda *shape: jax.ShapeDtypeStruct(shape, BF16)

    own = kernel_call(
        pack_kernel,
        [sent(tokens + EXTRA, width)],
        [pltpu.VMEM((choose, tokens), jnp.int32), pltpu.VMEM((choose, tokens), F32), pltpu.SemaphoreType.DMA((3,))],
        0,
        limit=2,
        in_hbm=(0, 1, 2),
    )(hidden_in, expert_ids.T, gate_values.T)[0]
    came = [swap(own, s, "expert") for s in range(1, sources)]
    own_across = swap(own, 2)
    grad_across = swap(out_grad, 2)
    came = join(came, gate_there, own_across, grad_across)
    came_across_there = swap(came, 2)
    across_near = swap(own_across, 1)
    grads = join([out_grad, grad_across], came)
    grads = [grads] + [swap(grads, s, "expert") for s in range(1, sources)]

    came_across = join([came_across_there], up_there, grads[1])[0]
    out_rows, x_rows, activ, scaled, slope, silu, onehot, slot_gate = kernel_call(
        functools.partial(forward_kernel, choose),
        [
            held(sources, slots, model),
            held(local_experts, rows, model),
            held(local_experts, rows, units),
            held(local_experts, rows, units),
            held(local_experts, rows, units, kind=F32),
            held(local_experts, rows, units, kind=F32),
            held(sources, slots, tokens),
            held(local_experts, rows, tokens, kind=F32),
        ],
        [pltpu.VMEM((RING, units, model), BF16), pltpu.SemaphoreType.DMA((RING,))],
        3 * product,
        limit=16,
        in_hbm=(11,),
    )(
        capacity_blocks,
        own, swap(own, 1), own_across, across_near,
        came, swap(came, 1), came_across, swap(came_across, 1),
        gate_t, up_t, down_weight, grads[0],
    )

    keep, send = kernel_call(
        home_kernel, [sent(2, sources, tokens, width)] * 2, [], 2 * slots * sources * tokens * model, limit=2,
    )(onehot, out_rows, *grads)
    out_near, out_far = add_cores(keep, swap(send, 1))
    back_rows, dots, y_rows, gate_part, up_part = kernel_call(
        backward_kernel,
        [
            held(sources, slots, model // 2),
            held(local_experts, rows, tokens, kind=F32),
            held(local_experts, rows, model),
            held(local_experts, rows, units),
            held(local_experts, rows, units),
        ],
        [pltpu.VMEM((RING, units, model), BF16), pltpu.SemaphoreType.DMA((RING,))],
        3 * product,
        limit=16,
        in_hbm=(10,),
    )(
        *grads, *[swap(x, 1) for x in grads],
        gate_t, up_t, down_weight, activ, slope, silu, onehot, slot_gate, out_near,
    )

    out_came = swap(out_far, 2)
    back_sum = sent(sources, tokens + EXTRA, width)
    far_keep, far_send, values = kernel_call(
        functools.partial(values_kernel, choose),
        [back_sum, back_sum, held(sources, EXTRA, width)],
        [],
        slots * sources * tokens * model,
        limit=2,
    )(onehot, back_rows, dots, own, came, out_came)
    near_keep, near_send = kernel_call(
        own_kernel,
        [back_sum, back_sum],
        [pltpu.VMEM((sources, slots, model // 2), BF16)],
        product,
        limit=16,
    )(gate_t, up_t, gate_part, up_part, onehot, slot_gate, values, far_keep)
    (back_far,) = kernel_call(pair_kernel, [back_sum], [], 0, limit=2)(far_keep, swap(far_send, 1), near_keep)
    some = local_experts // 2
    up_grad, down_grad = weight_grads(
        [(up_part, x_rows, 0, local_experts), (scaled, y_rows, 0, some)], None, back_far
    )
    height = 2 * tokens + EXTRA
    parts = kernel_call(chips_kernel, [sent(height, width)] * sources, [], 0, limit=2, in_hbm=(5,))(
        out_near, out_came, near_keep, swap(near_send, 1), swap(back_far, 2), up_grad
    )
    down_grad, gate_grad = weight_grads(
        [(scaled, y_rows, some, local_experts), (gate_part, x_rows, 0, local_experts)], down_grad, parts[0]
    )
    layer_out, input_grad, value_grad = kernel_call(
        functools.partial(total_kernel, sources),
        [sent(tokens, width), sent(tokens, width), jax.ShapeDtypeStruct((choose, tokens), F32)],
        [],
        0,
        limit=2,
    )(parts[0], *[swap(parts[s], s, "expert") for s in range(1, sources)])
    return (
        layer_out,
        input_grad,
        value_grad.T,
        jnp.swapaxes(gate_grad, 1, 2),
        jnp.swapaxes(up_grad, 1, 2),
        down_grad,
    )


def slot_layout(expert_ids, capacity_blocks):
    tokens_here, choose = expert_ids.shape
    experts = capacity_blocks.shape[0]
    flat_ids = expert_ids.reshape(-1)
    onehot = (flat_ids[:, None] == jnp.arange(experts, dtype=jnp.int32)[None, :]).astype(jnp.int32)
    before = jnp.cumsum(onehot, axis=0) - onehot
    ranks = jnp.sum(before * onehot, axis=1)
    limits = jnp.sum(onehot * capacity_blocks[None, :], axis=1) * BLK
    kept = ranks < limits
    slots = jnp.where(kept, flat_ids * CAP + ranks, experts * CAP)
    token_index = jnp.arange(tokens_here * choose, dtype=jnp.int32) // choose
    owners = (
        jnp.full((experts * CAP,), tokens_here, jnp.int32).at[slots].set(token_index, mode="drop")
    )
    return (kept.reshape(tokens_here, choose), slots.reshape(tokens_here, choose), owners)


def outgoing(rows, owners, experts, scale):
    padded = jnp.concatenate([rows, jnp.zeros((1, rows.shape[1]), rows.dtype)], 0)
    picked = padded[owners]
    if scale is not None:
        picked = (scale[:, None] * picked.astype(jnp.float32)).astype(jnp.bfloat16)
    return picked.reshape(experts, CAP, rows.shape[1])


def local_grads(hidden_gate, hidden_up, act_grad):
    sigma = jax.nn.sigmoid(hidden_gate)
    gate_part = (act_grad * hidden_up * sigma * (1.0 + hidden_gate * (1.0 - sigma))).astype(
        jnp.bfloat16
    )
    up_part = (act_grad * jax.nn.silu(hidden_gate)).astype(jnp.bfloat16)
    return (gate_part, up_part)


def combine(back, slots, weights):
    padded = jnp.concatenate([back, jnp.zeros((1, back.shape[1]), back.dtype)], 0)
    picked = padded[slots].astype(jnp.float32)
    return (jnp.einsum("tk,tkw->tw", weights, picked), picked)


def dispatched_body(
    hidden_in,
    out_grad,
    expert_ids,
    gate_values,
    capacity_blocks,
    gate_weight,
    up_weight,
    down_weight,
):
    experts = capacity_blocks.shape[0]
    sources = lax.axis_size("expert")
    local_experts = gate_weight.shape[0]
    kept, slots, owners = slot_layout(expert_ids, capacity_blocks)
    weights = jnp.where(kept, gate_values, 0.0)
    slot_gates = (
        jnp.zeros((experts * CAP,), jnp.float32)
        .at[slots.reshape(-1)]
        .set(weights.reshape(-1), mode="drop")
    )
    send_in = outgoing(hidden_in, owners, experts, None)
    send_grad = outgoing(out_grad, owners, experts, slot_gates)
    recv_in, recv_grad = (
        lax.all_to_all(send_in, "expert", split_axis=0, concat_axis=0, tiled=True),
        lax.all_to_all(send_grad, "expert", split_axis=0, concat_axis=0, tiled=True),
    )
    share = recv_in.shape[2]
    share_in = recv_in.reshape(sources, local_experts, CAP, share)
    share_grad = recv_grad.reshape(sources, local_experts, CAP, share)
    piece = lax.all_gather(share_in, "etp", axis=3, tiled=True)
    hidden_gate = jnp.einsum(
        "secn,enf->secf", piece, gate_weight, preferred_element_type=jnp.float32
    )
    hidden_up = jnp.einsum("secn,enf->secf", piece, up_weight, preferred_element_type=jnp.float32)
    activ = (jax.nn.silu(hidden_gate) * hidden_up).astype(jnp.bfloat16)
    piece = lax.all_gather(share_grad, "etp", axis=3, tiled=True)
    act_grad = jnp.einsum("secn,efn->secf", piece, down_weight, preferred_element_type=jnp.float32)
    columns = jnp.einsum("secf,secn->efn", activ, piece, preferred_element_type=jnp.float32)
    act_grad, down_grad = (act_grad, columns)
    gate_part, up_part = local_grads(hidden_gate, hidden_up, act_grad)
    stacked = jnp.stack([gate_part, up_part])
    weight_grads = jnp.einsum(
        "secn,gsecf->genf",
        lax.all_gather(share_in, "etp", axis=3, tiled=True),
        stacked,
        preferred_element_type=jnp.float32,
    )
    out_part = jnp.einsum("secf,efd->secd", activ, down_weight, preferred_element_type=jnp.float32)
    back_part = jnp.einsum(
        "secf,edf->secd", gate_part, gate_weight, preferred_element_type=jnp.float32
    )
    back_part = back_part + jnp.einsum(
        "secf,edf->secd", up_part, up_weight, preferred_element_type=jnp.float32
    )
    out_rows = lax.psum_scatter(
        out_part.astype(jnp.bfloat16), "etp", scatter_dimension=3, tiled=True
    )
    home_out = lax.all_to_all(out_rows, "expert", split_axis=0, concat_axis=0, tiled=True)
    share_width = home_out.shape[3]
    layer_sum, picked = combine(home_out.reshape(experts * CAP, share_width), slots, weights)
    dot_part = jnp.einsum("tw,tkw->tk", out_grad.astype(jnp.float32), picked) * kept.astype(
        jnp.float32
    )
    gate_value_grad = lax.psum(dot_part, "etp")
    back_rows = lax.psum_scatter(
        back_part.astype(jnp.bfloat16), "etp", scatter_dimension=3, tiled=True
    )
    home_back = lax.all_to_all(back_rows, "expert", split_axis=0, concat_axis=0, tiled=True)
    input_sum, returned = combine(home_back.reshape(experts * CAP, share_width), slots, weights)
    return (
        layer_sum.astype(jnp.bfloat16),
        input_sum.astype(jnp.bfloat16),
        gate_value_grad,
        weight_grads[0].astype(jnp.bfloat16),
        weight_grads[1].astype(jnp.bfloat16),
        down_grad.astype(jnp.bfloat16),
    )


def body(*operands):
    hidden_in, gate_weight = operands[0], operands[5]
    if lax.axis_size("expert") == 4 and lax.axis_size("etp") == 4 and hidden_in.shape[0] <= gate_weight.shape[0] * CAP:
        return gathered_body(*operands)
    return dispatched_body(*operands)


def solution(mesh):
    in_specs = (
        P(("groups", "expert"), "etp"),
        P(("groups", "expert"), "etp"),
        P(("groups", "expert"), None),
        P(("groups", "expert"), None),
        P("groups"),
        P("expert", None, "etp"),
        P("expert", None, "etp"),
        P("expert", "etp", None),
    )
    out_specs = (
        P(("groups", "expert"), "etp"),
        P(("groups", "expert"), "etp"),
        P(("groups", "expert"), None),
        P(("groups", "expert"), None, "etp"),
        P(("groups", "expert"), None, "etp"),
        P(("groups", "expert"), "etp", None),
    )
    return jax.shard_map(body, mesh=mesh, in_specs=in_specs, out_specs=out_specs, check_vma=False)
```

```python
import functools

import jax
import jax.numpy as jnp
from jax import lax
from jax.experimental import pallas as pl
from jax.experimental.pallas import tpu as pltpu
from jax.sharding import PartitionSpec as P

CAP = 16
BLK = 4
EXTRA = 16
F32 = jnp.float32
BF16 = jnp.bfloat16


def nn(a, b):
    return lax.dot_general(a, b, (((1,), (0,)), ((), ())), preferred_element_type=F32)


def nt(a, b):
    return lax.dot_general(a, b, (((1,), (1,)), ((), ())), preferred_element_type=F32)


def tn(a, b):
    return lax.dot_general(a, b, (((0,), (0,)), ((), ())), preferred_element_type=F32)


def pack_kernel(hidden_hbm, ids_hbm, gates_hbm, own_ref, ids_ref, gates_ref, sems):
    tokens, width = hidden_hbm.shape
    choose = ids_ref.shape[0]
    copies = [
        pltpu.make_async_copy(hidden_hbm, own_ref.at[pl.ds(0, tokens)], sems.at[0]),
        pltpu.make_async_copy(ids_hbm, ids_ref, sems.at[1]),
        pltpu.make_async_copy(gates_hbm, gates_ref, sems.at[2]),
    ]
    for copy in copies:
        copy.start()
    for copy in copies:
        copy.wait()
    gates = gates_ref[...]
    high = gates.astype(BF16).astype(F32)
    fill = jnp.zeros((8 - choose, tokens), F32)
    top = jnp.concatenate([jnp.concatenate([ids_ref[...].astype(F32), fill], axis=0), jnp.concatenate([high, fill], axis=0)], axis=1)
    low = jnp.concatenate([jnp.concatenate([gates - high, fill], axis=0), jnp.zeros((8, width - tokens), F32)], axis=1)
    own_ref[tokens:tokens + EXTRA, :] = jnp.concatenate([top, low], axis=0).astype(BF16)


def routing(info, choose, tokens):
    info = info.astype(F32)
    return info[0:choose, 0:tokens], info[0:choose, tokens:2 * tokens] + info[8:8 + choose, 0:tokens]


def columns(me, mask, width):
    return pl.ds(pl.multiple_of(lax.bitwise_xor(me, mask) * width, width), width)


def send_home(home_keep, home_send, me, onehot, rows, tokens, width):
    for s in range(onehot.shape[0]):
        for q in range(4):
            home = home_send if q % 2 else home_keep
            home[q // 2, s, 0:tokens, :] = tn(onehot[s], rows[s, :, columns(me, q, width)]).astype(BF16)


RING = 8
GROUP = 4


def ring(weight, slots, sems, columns=None):
    depth = slots.shape[0]

    def load(e):
        slot = lax.rem(e, depth)
        source = weight.at[e] if columns is None else weight.at[e, :, columns]
        return pltpu.make_async_copy(source, slots.at[slot], sems.at[slot])

    def start(e):
        @pl.when(e < weight.shape[0])
        def _():
            load(e).start()

    for e in range(min(depth, weight.shape[0])):
        load(jnp.int32(e)).start()
    if depth >= weight.shape[0]:
        return lambda e: None, lambda e: load(e).wait()
    return lambda e: start(e + depth), lambda e: load(e).wait()


def slot_of(slots, e):
    return slots[lax.rem(e, slots.shape[0])]


def forward_kernel(
    choose, capacity_ref, o0, o1, o2, o3, b0, b1, b2, b3, gate_ref, up_ref, down_hbm, later_ref,
    out_rows, rows_ref, act_ref, a_ref, slope_ref, silu_ref, onehot, slot_gate,
    down_ref, down_sems,
):
    sources, slots, tokens = onehot.shape
    experts = slots // CAP
    width = b0.shape[2]
    me = lax.axis_index("etp")
    first = lax.axis_index("expert") * experts
    start_down, wait_down = ring(down_hbm, down_ref, down_sems)
    row = lax.broadcasted_iota(jnp.int32, (tokens, tokens), 0)
    col = lax.broadcasted_iota(jnp.int32, (tokens, tokens), 1)
    before = jnp.where(row < col, 1.0, 0.0).astype(BF16)
    expert = lax.broadcasted_iota(jnp.int32, (experts, tokens), 0)
    mine = (first + expert).astype(F32)
    limit = jnp.zeros((experts, tokens), jnp.int32)
    for e in range(experts):
        limit = jnp.where(expert == e, capacity_ref[first + e] * BLK, limit)
    limit = limit.astype(F32)
    place = lax.broadcasted_iota(jnp.int32, (experts, CAP, tokens), 1).astype(F32)
    for s in range(sources):
        block = [o[...] for o in (o0, o1, o2, o3)] if s == 0 else [b[s - 1] for b in (b0, b1, b2, b3)]
        ids, gates = routing(block[0][tokens:tokens + EXTRA, :], choose, tokens)
        named = jnp.zeros((experts, tokens), F32)
        gate = jnp.zeros((experts, tokens), F32)
        for k in range(choose):
            hit = ids[k:k + 1, :] == mine
            named = named + jnp.where(hit, 1.0, 0.0)
            gate = gate + jnp.where(hit, gates[k:k + 1, :], 0.0)
        rank = nn(named.astype(BF16), before)
        rank = jnp.where((named > 0.5) & (rank < limit), rank, -1.0)
        chosen = jnp.where(rank[:, None, :] == place, 1.0, 0.0)
        gate_of = jnp.sum(chosen * gate[:, None, :], axis=2, keepdims=True)
        slot_gate[:, s * CAP:(s + 1) * CAP, :] = jnp.broadcast_to(gate_of, chosen.shape)
        table = chosen.reshape(slots, tokens).astype(BF16)
        onehot[s] = table
        for q in range(4):
            picked = nn(table, block[q][0:tokens, :]).astype(BF16).reshape(experts, CAP, width)
            rows_ref[:, s * CAP:(s + 1) * CAP, columns(me, q, width)] = picked

    def activate(e):
        x = rows_ref[e]
        hidden_gate = nt(x, gate_ref[e])
        hidden_up = nt(x, up_ref[e])
        sigma = jax.nn.sigmoid(hidden_gate)
        silu = hidden_gate * sigma
        activ = (silu * hidden_up).astype(BF16)
        act_ref[e] = activ
        slope_ref[e] = hidden_up * sigma * (1.0 + hidden_gate * (1.0 - sigma))
        silu_ref[e] = silu
        a_ref[e] = (activ.astype(F32) * slot_gate[e][:, 0:1]).astype(BF16)

    def project(e):
        out = nn(a_ref[e], slot_of(down_ref, e)).astype(BF16)
        at = pl.ds(pl.multiple_of(e * CAP, CAP), CAP)
        for s in range(sources):
            out_rows[s, at, :] = out[s * CAP:(s + 1) * CAP]

    def both(e):
        before, now = [e - GROUP + i for i in range(GROUP)], [e + i for i in range(GROUP)]
        for i in before:
            wait_down(i)
        for i, j in zip(before, now):
            activate(j)
            project(i)
        for i in before:
            start_down(i)

    skewed(experts, activate, wait_down, project, both)


def skewed(experts, first, wait, second, both):
    for e in range(GROUP):
        first(jnp.int32(e))

    def turn(i, _):
        both(i * GROUP)
        return 0

    lax.fori_loop(1, experts // GROUP, turn, 0)
    for e in range(experts - GROUP, experts):
        wait(jnp.int32(e))
    for e in range(experts - GROUP, experts):
        second(jnp.int32(e))


def home_kernel(onehot, rows, *refs):
    keep, send = refs[-2:]
    send_home(keep, send, lax.axis_index("etp"), onehot, rows, keep.shape[2], keep.shape[3])


def half(me, other, size):
    return pl.ds(pl.multiple_of(lax.bitwise_xor(me // 2, other) * size, size), size)


def half_home(me, onehot, rows, keep, send, tokens, width):
    for s in range(onehot.shape[0]):
        for q, home in enumerate((keep, send)):
            at = pl.multiple_of(lax.rem(lax.bitwise_xor(me, q), 2) * width, width)
            home[s, 0:tokens, :] = tn(onehot[s], rows[s, :, pl.ds(at, width)]).astype(BF16)


def values_kernel(choose, onehot, rows, dots, own_ref, info_ref, *refs):
    keep, send, value_ref = refs[-3:]
    sources, slots, tokens = onehot.shape
    experts = slots // CAP
    width = keep.shape[2]
    half_home(lax.axis_index("etp"), onehot, rows, keep, send, tokens, width)
    expert = lax.broadcasted_iota(jnp.int32, (experts, tokens), 0)
    mine = (lax.axis_index("expert") * experts + expert).astype(F32)
    for s in range(sources):
        info = own_ref[tokens:tokens + EXTRA, :] if s == 0 else info_ref[s - 1, tokens:tokens + EXTRA, :]
        ids, _ = routing(info, choose, tokens)
        chosen = onehot[s].astype(F32).reshape(experts, CAP, tokens)
        share = jnp.sum(chosen * dots[:, s * CAP:(s + 1) * CAP, :], axis=1)
        values = [jnp.sum(jnp.where(ids[k:k + 1, :] == mine, share, 0.0), axis=0, keepdims=True) for k in range(choose)]
        values = jnp.concatenate(values + [jnp.zeros((EXTRA - choose, tokens), F32)], axis=0)
        values = jnp.concatenate([values, jnp.zeros((EXTRA, width - tokens), F32)], axis=1).astype(BF16)
        keep[s, tokens:tokens + EXTRA, :] = values
        send[s, tokens:tokens + EXTRA, :] = values
        value_ref[s] = values


def own_kernel(gate_ref, up_ref, p_ref, q_ref, onehot, slot_gate, value_ref, earlier_ref, keep, send, back_rows):
    sources, slots, tokens = onehot.shape
    width = keep.shape[2]
    me = lax.axis_index("etp")
    here = half(me, 0, 2 * width)

    def turn(i, _):
        for e in [i * GROUP + j for j in range(GROUP)]:
            back = nn(p_ref[e], gate_ref[e, :, here]) + nn(q_ref[e], up_ref[e, :, here])
            back = (back * slot_gate[e][:, 0:1]).astype(BF16)
            at = pl.ds(pl.multiple_of(e * CAP, CAP), CAP)
            for s in range(sources):
                back_rows[s, at, :] = back[s * CAP:(s + 1) * CAP]
        return 0

    lax.fori_loop(0, slots // CAP // GROUP, turn, 0)
    half_home(me, onehot, back_rows, keep, send, tokens, width)
    for s in range(sources):
        keep[s, tokens:tokens + EXTRA, :] = value_ref[s]
        send[s, tokens:tokens + EXTRA, :] = value_ref[s]


def backward_kernel(
    a01, a23, n01, n23,
    gate_ref, up_ref, down_hbm, act_ref, slope_ref, silu_ref, onehot, slot_gate, earlier_ref,
    back_rows, dots, rows_ref, p_ref, q_ref,
    down_ref, down_sems,
):
    sources, slots, tokens = onehot.shape
    experts = slots // CAP
    width = a01.shape[3]
    me = lax.axis_index("etp")
    start_down, wait_down = ring(down_hbm, down_ref, down_sems)
    there = half(me, 1, 2 * width)
    for s in range(sources):
        here, near = ((a01, n01), (a23, n23))[s // 2]
        for q in range(4):
            block = (near if q % 2 else here)[s % 2, q // 2]
            picked = nn(onehot[s], block).astype(BF16).reshape(experts, CAP, width)
            rows_ref[:, s * CAP:(s + 1) * CAP, columns(me, q, width)] = picked

    def slopes(e):
        grad = nt(rows_ref[e], slot_of(down_ref, e))
        activ = act_ref[e].astype(F32)
        dots[e] = jnp.broadcast_to(jnp.sum(activ * grad, axis=1, keepdims=True), dots.shape[1:])
        grad = grad * slot_gate[e][:, 0:1]
        p_ref[e] = (grad * slope_ref[e]).astype(BF16)
        q_ref[e] = (grad * silu_ref[e]).astype(BF16)

    def project(e):
        back = nn(p_ref[e], gate_ref[e, :, there]) + nn(q_ref[e], up_ref[e, :, there])
        back = (back * slot_gate[e][:, 0:1]).astype(BF16)
        at = pl.ds(pl.multiple_of(e * CAP, CAP), CAP)
        for s in range(sources):
            back_rows[s, at, :] = back[s * CAP:(s + 1) * CAP]

    def first(e):
        wait_down(e)
        slopes(e)
        start_down(e)

    def both(e):
        before, now = [e - GROUP + i for i in range(GROUP)], [e + i for i in range(GROUP)]
        for i in now:
            wait_down(i)
        for i, j in zip(before, now):
            slopes(j)
            project(i)
        for i in now:
            start_down(i)

    skewed(experts, first, lambda e: None, project, both)


def add_kernel(keep, came, *refs):
    near, far = refs[-2:]
    for s in range(near.shape[0]):
        far[s] = (keep[1, s].astype(F32) + came[1, s].astype(F32)).astype(BF16)
        near[s] = (keep[0, s].astype(F32) + came[0, s].astype(F32)).astype(BF16)


def pair_kernel(keep, came, *refs):
    refs[-1][...] = (keep[...].astype(F32) + came[...].astype(F32)).astype(BF16)


def chips_kernel(out_near, out_came, back_keep, back_near, back_came, *refs):
    sources, tokens = out_near.shape[:2]
    parts = refs[-sources:]
    for s in range(sources):
        parts[s][0:tokens, :] = (out_near[s].astype(F32) + out_came[s].astype(F32)).astype(BF16)
        back = back_keep[s].astype(F32) + back_near[s].astype(F32) + back_came[s].astype(F32)
        parts[s][tokens:, :] = back.astype(BF16)


def total_kernel(count, *refs):
    out_ref, back_ref, value_ref = refs[count:]
    tokens = out_ref.shape[0]
    total = refs[0][...].astype(F32)
    for ref in refs[1:count]:
        total = total + ref[...].astype(F32)
    out_ref[...] = total[0:tokens].astype(BF16)
    back_ref[...] = total[tokens:2 * tokens].astype(BF16)
    value_ref[...] = total[2 * tokens:2 * tokens + value_ref.shape[0], 0:value_ref.shape[1]]


BANKS = 8
TURN = 4


def product_kernel(jobs, *refs):
    lefts, rights, outs = (refs[i * len(jobs):(i + 1) * len(jobs)] for i in range(3))
    held, sems = refs[-2:]
    outs = refs[-2 - len(jobs):-2]

    def store(job, e, slot):
        return pltpu.make_async_copy(held.at[slot], outs[job].at[e], sems.at[slot])

    def turn(job, first, done, i, full):
        for pair in range(0, TURN, 2):
            places = [(first + i * TURN + j, lax.rem(done + i * TURN + j, BANKS)) for j in (pair, pair + 1)]
            if full:
                for e, slot in places:
                    store(job, e, slot).wait()
            for e, slot in places:
                held[slot] = tn(lefts[job][e], rights[job][e]).astype(BF16)
            for e, slot in places:
                store(job, e, slot).start()

    done = 0
    for job, (first, last) in enumerate(jobs):
        fresh = max(0, min(BANKS - done, last - first) // TURN)
        for i in range(fresh):
            turn(job, first, done, jnp.int32(i), False)

        def later(i, _, job=job, first=first, done=done):
            turn(job, first, done, i, True)
            return 0

        lax.fori_loop(fresh, (last - first) // TURN, later, 0)
        done = done + last - first
    for slot in range(min(done, BANKS)):
        store(0, jobs[0][0], slot).wait()


def load_kernel(source, target, token, sems):
    token[...] = jnp.zeros_like(token)
    copies = [pltpu.make_async_copy(source.at[e], target.at[e], sems.at[e]) for e in range(source.shape[0])]
    for copy in copies:
        copy.start()
    for copy in copies:
        copy.wait()


def in_vmem(weight):
    return pl.pallas_call(
        load_kernel,
        in_specs=[pl.BlockSpec(memory_space=pltpu.HBM)],
        out_specs=[pl.BlockSpec(memory_space=pltpu.VMEM)] * 2,
        out_shape=[pltpu.VMEM(weight.shape, BF16), jax.ShapeDtypeStruct((8, 128), F32)],
        scratch_shapes=[pltpu.SemaphoreType.DMA((weight.shape[0],))],
        compiler_params=pltpu.CompilerParams(vmem_limit_bytes=4 * 1024 * 1024),
        cost_estimate=pl.CostEstimate(flops=0, bytes_accessed=2 * weight.size, transcendentals=0),
    )(pltpu.with_memory_space_constraint(weight, pltpu.HBM))


def join_kernel(count, *refs):
    for i in range(count):
        refs[-1][i] = refs[i][...]


def join(arrays, *there):
    return kernel_call(
        functools.partial(join_kernel, len(arrays)),
        [jax.ShapeDtypeStruct((len(arrays),) + arrays[0].shape, arrays[0].dtype)],
        [],
        0,
        limit=2,
    )(*arrays, *there)[0]


def kernel_call(kernel, out_shape, scratch, flops, out_specs=None, limit=4, in_hbm=(), aliases={}):
    def call(*operands):
        specs = [
            pl.BlockSpec(memory_space=pltpu.HBM if i in in_hbm else pltpu.SMEM if x.ndim == 1 else pltpu.VMEM)
            for i, x in enumerate(operands)
        ]
        operands = [
            pltpu.with_memory_space_constraint(x, pltpu.HBM) if i in in_hbm else x for i, x in enumerate(operands)
        ]
        return pl.pallas_call(
            kernel,
            in_specs=specs,
            out_specs=out_specs or [pl.BlockSpec(memory_space=pltpu.VMEM)] * len(out_shape),
            out_shape=out_shape,
            scratch_shapes=scratch,
            input_output_aliases=aliases,
            compiler_params=pltpu.CompilerParams(vmem_limit_bytes=limit * 1024 * 1024),
            cost_estimate=pl.CostEstimate(flops=flops, bytes_accessed=flops // 32, transcendentals=0),
        )(*operands)

    return call


def weight_grads(jobs, begun=None, *earlier):
    count = len(jobs)
    lefts, rights = [job[0] for job in jobs], [job[1] for job in jobs]
    experts, rows, units = lefts[0].shape
    model = rights[0].shape[2]
    shape = jax.ShapeDtypeStruct((experts, units, model), BF16)
    work = sum(job[3] - job[2] for job in jobs)
    more = [] if begun is None else [begun]
    return kernel_call(
        functools.partial(product_kernel, [job[2:] for job in jobs]),
        [shape] * count,
        [pltpu.VMEM((BANKS, units, model), BF16), pltpu.SemaphoreType.DMA((BANKS,))],
        2 * work * rows * units * model,
        out_specs=[pl.BlockSpec(memory_space=pltpu.HBM)] * count,
        limit=8,
        in_hbm=(2 * count,) if more else (),
        aliases={2 * count: 0} if more else {},
    )(*lefts, *rights, *more, *earlier)


def swap(array, bit, axis="etp"):
    count = lax.axis_size(axis)
    return lax.ppermute(array, axis, [(i, i ^ bit) for i in range(count)])


def add_cores(keep, came, *earlier):
    shape = jax.ShapeDtypeStruct(keep.shape[1:], BF16)
    hbm = [2] if earlier else []
    return kernel_call(add_kernel, [shape, shape], [], 0, limit=2, in_hbm=hbm)(keep, came, *earlier)


def gathered_body(
    hidden_in, out_grad, expert_ids, gate_values, capacity_blocks, gate_weight, up_weight, down_weight
):
    sources = lax.axis_size("expert")
    tokens, width = hidden_in.shape
    choose = expert_ids.shape[1]
    local_experts, units, model = down_weight.shape
    slots = local_experts * CAP
    rows = sources * CAP
    gate_t, gate_there = in_vmem(jnp.swapaxes(gate_weight, 1, 2))
    up_t, up_there = in_vmem(jnp.swapaxes(up_weight, 1, 2))
    product = 2 * local_experts * rows * units * model
    held = lambda *shape, kind=BF16: pltpu.VMEM(shape, kind)
    sent = lambda *shape: jax.ShapeDtypeStruct(shape, BF16)

    own = kernel_call(
        pack_kernel,
        [sent(tokens + EXTRA, width)],
        [pltpu.VMEM((choose, tokens), jnp.int32), pltpu.VMEM((choose, tokens), F32), pltpu.SemaphoreType.DMA((3,))],
        0,
        limit=2,
        in_hbm=(0, 1, 2),
    )(hidden_in, expert_ids.T, gate_values.T)[0]
    came = [swap(own, s, "expert") for s in range(1, sources)]
    own_across = swap(own, 2)
    grad_across = swap(out_grad, 2)
    came = join(came, gate_there, own_across, grad_across)
    came_across_there = swap(came, 2)
    across_near = swap(own_across, 1)
    grads = join([out_grad, grad_across], came)
    near_grads = join([grads, swap(grads, 1, "expert")])
    far_grads = swap(near_grads, 2, "expert")

    came_across = join([came_across_there], up_there, near_grads)[0]
    out_rows, x_rows, activ, scaled, slope, silu, onehot, slot_gate = kernel_call(
        functools.partial(forward_kernel, choose),
        [
            held(sources, slots, model),
            held(local_experts, rows, model),
            held(local_experts, rows, units),
            held(local_experts, rows, units),
            held(local_experts, rows, units, kind=F32),
            held(local_experts, rows, units, kind=F32),
            held(sources, slots, tokens),
            held(local_experts, rows, tokens, kind=F32),
        ],
        [pltpu.VMEM((RING, units, model), BF16), pltpu.SemaphoreType.DMA((RING,))],
        3 * product,
        limit=16,
        in_hbm=(11,),
    )(
        capacity_blocks,
        own, swap(own, 1), own_across, across_near,
        came, swap(came, 1), came_across, swap(came_across, 1),
        gate_t, up_t, down_weight, near_grads,
    )

    keep, send = kernel_call(
        home_kernel, [sent(2, sources, tokens, width)] * 2, [], 2 * slots * sources * tokens * model, limit=2,
    )(onehot, out_rows, far_grads)
    out_near, out_far = add_cores(keep, swap(send, 1))
    back_rows, dots, y_rows, gate_part, up_part = kernel_call(
        backward_kernel,
        [
            held(sources, slots, model // 2),
            held(local_experts, rows, tokens, kind=F32),
            held(local_experts, rows, model),
            held(local_experts, rows, units),
            held(local_experts, rows, units),
        ],
        [pltpu.VMEM((RING, units, model), BF16), pltpu.SemaphoreType.DMA((RING,))],
        3 * product,
        limit=16,
        in_hbm=(6,),
    )(
        near_grads, far_grads, swap(near_grads, 1), swap(far_grads, 1),
        gate_t, up_t, down_weight, activ, slope, silu, onehot, slot_gate, out_near,
    )

    out_came = swap(out_far, 2)
    back_sum = sent(sources, tokens + EXTRA, width)
    far_keep, far_send, values = kernel_call(
        functools.partial(values_kernel, choose),
        [back_sum, back_sum, held(sources, EXTRA, width)],
        [],
        slots * sources * tokens * model,
        limit=2,
    )(onehot, back_rows, dots, own, came, out_came)
    near_keep, near_send = kernel_call(
        own_kernel,
        [back_sum, back_sum],
        [pltpu.VMEM((sources, slots, model // 2), BF16)],
        product,
        limit=16,
    )(gate_t, up_t, gate_part, up_part, onehot, slot_gate, values, far_keep)
    (back_far,) = kernel_call(pair_kernel, [back_sum], [], 0, limit=2)(far_keep, swap(far_send, 1), near_keep)
    some = local_experts // 2
    up_grad, down_grad = weight_grads(
        [(up_part, x_rows, 0, local_experts), (scaled, y_rows, 0, some)], None, back_far
    )
    height = 2 * tokens + EXTRA
    parts = kernel_call(chips_kernel, [sent(height, width)] * sources, [], 0, limit=2, in_hbm=(5,))(
        out_near, out_came, near_keep, swap(near_send, 1), swap(back_far, 2), up_grad
    )
    down_grad, gate_grad = weight_grads(
        [(scaled, y_rows, some, local_experts), (gate_part, x_rows, 0, local_experts)], down_grad, parts[0]
    )
    layer_out, input_grad, value_grad = kernel_call(
        functools.partial(total_kernel, sources),
        [sent(tokens, width), sent(tokens, width), jax.ShapeDtypeStruct((choose, tokens), F32)],
        [],
        0,
        limit=2,
    )(parts[0], *[swap(parts[s], s, "expert") for s in range(1, sources)])
    return (
        layer_out,
        input_grad,
        value_grad.T,
        jnp.swapaxes(gate_grad, 1, 2),
        jnp.swapaxes(up_grad, 1, 2),
        down_grad,
    )


def slot_layout(expert_ids, capacity_blocks):
    tokens_here, choose = expert_ids.shape
    experts = capacity_blocks.shape[0]
    flat_ids = expert_ids.reshape(-1)
    onehot = (flat_ids[:, None] == jnp.arange(experts, dtype=jnp.int32)[None, :]).astype(jnp.int32)
    before = jnp.cumsum(onehot, axis=0) - onehot
    ranks = jnp.sum(before * onehot, axis=1)
    limits = jnp.sum(onehot * capacity_blocks[None, :], axis=1) * BLK
    kept = ranks < limits
    slots = jnp.where(kept, flat_ids * CAP + ranks, experts * CAP)
    token_index = jnp.arange(tokens_here * choose, dtype=jnp.int32) // choose
    owners = (
        jnp.full((experts * CAP,), tokens_here, jnp.int32).at[slots].set(token_index, mode="drop")
    )
    return (kept.reshape(tokens_here, choose), slots.reshape(tokens_here, choose), owners)


def outgoing(rows, owners, experts, scale):
    padded = jnp.concatenate([rows, jnp.zeros((1, rows.shape[1]), rows.dtype)], 0)
    picked = padded[owners]
    if scale is not None:
        picked = (scale[:, None] * picked.astype(jnp.float32)).astype(jnp.bfloat16)
    return picked.reshape(experts, CAP, rows.shape[1])


def local_grads(hidden_gate, hidden_up, act_grad):
    sigma = jax.nn.sigmoid(hidden_gate)
    gate_part = (act_grad * hidden_up * sigma * (1.0 + hidden_gate * (1.0 - sigma))).astype(
        jnp.bfloat16
    )
    up_part = (act_grad * jax.nn.silu(hidden_gate)).astype(jnp.bfloat16)
    return (gate_part, up_part)


def combine(back, slots, weights):
    padded = jnp.concatenate([back, jnp.zeros((1, back.shape[1]), back.dtype)], 0)
    picked = padded[slots].astype(jnp.float32)
    return (jnp.einsum("tk,tkw->tw", weights, picked), picked)


def dispatched_body(
    hidden_in,
    out_grad,
    expert_ids,
    gate_values,
    capacity_blocks,
    gate_weight,
    up_weight,
    down_weight,
):
    experts = capacity_blocks.shape[0]
    sources = lax.axis_size("expert")
    local_experts = gate_weight.shape[0]
    kept, slots, owners = slot_layout(expert_ids, capacity_blocks)
    weights = jnp.where(kept, gate_values, 0.0)
    slot_gates = (
        jnp.zeros((experts * CAP,), jnp.float32)
        .at[slots.reshape(-1)]
        .set(weights.reshape(-1), mode="drop")
    )
    send_in = outgoing(hidden_in, owners, experts, None)
    send_grad = outgoing(out_grad, owners, experts, slot_gates)
    recv_in, recv_grad = (
        lax.all_to_all(send_in, "expert", split_axis=0, concat_axis=0, tiled=True),
        lax.all_to_all(send_grad, "expert", split_axis=0, concat_axis=0, tiled=True),
    )
    share = recv_in.shape[2]
    share_in = recv_in.reshape(sources, local_experts, CAP, share)
    share_grad = recv_grad.reshape(sources, local_experts, CAP, share)
    piece = lax.all_gather(share_in, "etp", axis=3, tiled=True)
    hidden_gate = jnp.einsum(
        "secn,enf->secf", piece, gate_weight, preferred_element_type=jnp.float32
    )
    hidden_up = jnp.einsum("secn,enf->secf", piece, up_weight, preferred_element_type=jnp.float32)
    activ = (jax.nn.silu(hidden_gate) * hidden_up).astype(jnp.bfloat16)
    piece = lax.all_gather(share_grad, "etp", axis=3, tiled=True)
    act_grad = jnp.einsum("secn,efn->secf", piece, down_weight, preferred_element_type=jnp.float32)
    columns = jnp.einsum("secf,secn->efn", activ, piece, preferred_element_type=jnp.float32)
    act_grad, down_grad = (act_grad, columns)
    gate_part, up_part = local_grads(hidden_gate, hidden_up, act_grad)
    stacked = jnp.stack([gate_part, up_part])
    weight_grads = jnp.einsum(
        "secn,gsecf->genf",
        lax.all_gather(share_in, "etp", axis=3, tiled=True),
        stacked,
        preferred_element_type=jnp.float32,
    )
    out_part = jnp.einsum("secf,efd->secd", activ, down_weight, preferred_element_type=jnp.float32)
    back_part = jnp.einsum(
        "secf,edf->secd", gate_part, gate_weight, preferred_element_type=jnp.float32
    )
    back_part = back_part + jnp.einsum(
        "secf,edf->secd", up_part, up_weight, preferred_element_type=jnp.float32
    )
    out_rows = lax.psum_scatter(
        out_part.astype(jnp.bfloat16), "etp", scatter_dimension=3, tiled=True
    )
    home_out = lax.all_to_all(out_rows, "expert", split_axis=0, concat_axis=0, tiled=True)
    share_width = home_out.shape[3]
    layer_sum, picked = combine(home_out.reshape(experts * CAP, share_width), slots, weights)
    dot_part = jnp.einsum("tw,tkw->tk", out_grad.astype(jnp.float32), picked) * kept.astype(
        jnp.float32
    )
    gate_value_grad = lax.psum(dot_part, "etp")
    back_rows = lax.psum_scatter(
        back_part.astype(jnp.bfloat16), "etp", scatter_dimension=3, tiled=True
    )
    home_back = lax.all_to_all(back_rows, "expert", split_axis=0, concat_axis=0, tiled=True)
    input_sum, returned = combine(home_back.reshape(experts * CAP, share_width), slots, weights)
    return (
        layer_sum.astype(jnp.bfloat16),
        input_sum.astype(jnp.bfloat16),
        gate_value_grad,
        weight_grads[0].astype(jnp.bfloat16),
        weight_grads[1].astype(jnp.bfloat16),
        down_grad.astype(jnp.bfloat16),
    )


def body(*operands):
    hidden_in, gate_weight = operands[0], operands[5]
    if lax.axis_size("expert") == 4 and lax.axis_size("etp") == 4 and hidden_in.shape[0] <= gate_weight.shape[0] * CAP:
        return gathered_body(*operands)
    return dispatched_body(*operands)


def solution(mesh):
    in_specs = (
        P(("groups", "expert"), "etp"),
        P(("groups", "expert"), "etp"),
        P(("groups", "expert"), None),
        P(("groups", "expert"), None),
        P("groups"),
        P("expert", None, "etp"),
        P("expert", None, "etp"),
        P("expert", "etp", None),
    )
    out_specs = (
        P(("groups", "expert"), "etp"),
        P(("groups", "expert"), "etp"),
        P(("groups", "expert"), None),
        P(("groups", "expert"), None, "etp"),
        P(("groups", "expert"), None, "etp"),
        P(("groups", "expert"), "etp", None),
    )
    return jax.shard_map(body, mesh=mesh, in_specs=in_specs, out_specs=out_specs, check_vma=False)
```

```python
import functools

import jax
import jax.numpy as jnp
from jax import lax
from jax.experimental import pallas as pl
from jax.experimental.pallas import tpu as pltpu
from jax.sharding import PartitionSpec as P

CAP = 16
BLK = 4
EXTRA = 16
F32 = jnp.float32
BF16 = jnp.bfloat16


def nn(a, b):
    return lax.dot_general(a, b, (((1,), (0,)), ((), ())), preferred_element_type=F32)


def nt(a, b):
    return lax.dot_general(a, b, (((1,), (1,)), ((), ())), preferred_element_type=F32)


def tn(a, b):
    return lax.dot_general(a, b, (((0,), (0,)), ((), ())), preferred_element_type=F32)


def pack_kernel(hidden_hbm, ids_hbm, gates_hbm, own_ref, ids_ref, gates_ref, sems):
    tokens, width = hidden_hbm.shape
    choose = ids_ref.shape[0]
    copies = [
        pltpu.make_async_copy(hidden_hbm, own_ref.at[pl.ds(0, tokens)], sems.at[0]),
        pltpu.make_async_copy(ids_hbm, ids_ref, sems.at[1]),
        pltpu.make_async_copy(gates_hbm, gates_ref, sems.at[2]),
    ]
    for copy in copies:
        copy.start()
    for copy in copies:
        copy.wait()
    gates = gates_ref[...]
    high = gates.astype(BF16).astype(F32)
    fill = jnp.zeros((8 - choose, tokens), F32)
    top = jnp.concatenate([jnp.concatenate([ids_ref[...].astype(F32), fill], axis=0), jnp.concatenate([high, fill], axis=0)], axis=1)
    low = jnp.concatenate([jnp.concatenate([gates - high, fill], axis=0), jnp.zeros((8, width - tokens), F32)], axis=1)
    own_ref[tokens:tokens + EXTRA, :] = jnp.concatenate([top, low], axis=0).astype(BF16)


def routing(info, choose, tokens):
    info = info.astype(F32)
    return info[0:choose, 0:tokens], info[0:choose, tokens:2 * tokens] + info[8:8 + choose, 0:tokens]


def columns(me, mask, width):
    return pl.ds(pl.multiple_of(lax.bitwise_xor(me, mask) * width, width), width)


def send_home(home_keep, home_send, me, onehot, rows, tokens, width):
    for s in range(onehot.shape[0]):
        for q in range(4):
            home = home_send if q % 2 else home_keep
            home[q // 2, s, 0:tokens, :] = tn(onehot[s], rows[s, :, columns(me, q, width)]).astype(BF16)


RING = 8
GROUP = 4


def ring(weight, slots, sems, columns=None):
    depth = slots.shape[0]

    def load(e):
        slot = lax.rem(e, depth)
        source = weight.at[e] if columns is None else weight.at[e, :, columns]
        return pltpu.make_async_copy(source, slots.at[slot], sems.at[slot])

    def start(e):
        @pl.when(e < weight.shape[0])
        def _():
            load(e).start()

    for e in range(min(depth, weight.shape[0])):
        load(jnp.int32(e)).start()
    if depth >= weight.shape[0]:
        return lambda e: None, lambda e: load(e).wait()
    return lambda e: start(e + depth), lambda e: load(e).wait()


def slot_of(slots, e):
    return slots[lax.rem(e, slots.shape[0])]


def forward_kernel(
    choose, capacity_ref, o0, o1, o2, o3, b0, b1, b2, b3, gate_ref, up_ref, down_hbm, later_ref,
    out_rows, rows_ref, act_ref, a_ref, slope_ref, silu_ref, onehot, slot_gate,
    down_ref, down_sems,
):
    sources, slots, tokens = onehot.shape
    experts = slots // CAP
    width = b0.shape[2]
    me = lax.axis_index("etp")
    first = lax.axis_index("expert") * experts
    start_down, wait_down = ring(down_hbm, down_ref, down_sems)
    row = lax.broadcasted_iota(jnp.int32, (tokens, tokens), 0)
    col = lax.broadcasted_iota(jnp.int32, (tokens, tokens), 1)
    before = jnp.where(row < col, 1.0, 0.0).astype(BF16)
    expert = lax.broadcasted_iota(jnp.int32, (experts, tokens), 0)
    mine = (first + expert).astype(F32)
    limit = jnp.zeros((experts, tokens), jnp.int32)
    for e in range(experts):
        limit = jnp.where(expert == e, capacity_ref[first + e] * BLK, limit)
    limit = limit.astype(F32)
    place = lax.broadcasted_iota(jnp.int32, (experts, CAP, tokens), 1).astype(F32)
    for s in range(sources):
        block = [o[...] for o in (o0, o1, o2, o3)] if s == 0 else [b[s - 1] for b in (b0, b1, b2, b3)]
        ids, gates = routing(block[0][tokens:tokens + EXTRA, :], choose, tokens)
        named = jnp.zeros((experts, tokens), F32)
        gate = jnp.zeros((experts, tokens), F32)
        for k in range(choose):
            hit = ids[k:k + 1, :] == mine
            named = named + jnp.where(hit, 1.0, 0.0)
            gate = gate + jnp.where(hit, gates[k:k + 1, :], 0.0)
        rank = nn(named.astype(BF16), before)
        rank = jnp.where((named > 0.5) & (rank < limit), rank, -1.0)
        chosen = jnp.where(rank[:, None, :] == place, 1.0, 0.0)
        gate_of = jnp.sum(chosen * gate[:, None, :], axis=2, keepdims=True)
        slot_gate[:, s * CAP:(s + 1) * CAP, :] = jnp.broadcast_to(gate_of, chosen.shape)
        table = chosen.reshape(slots, tokens).astype(BF16)
        onehot[s] = table
        for q in range(4):
            picked = nn(table, block[q][0:tokens, :]).astype(BF16).reshape(experts, CAP, width)
            rows_ref[:, s * CAP:(s + 1) * CAP, columns(me, q, width)] = picked

    def activate(e):
        x = rows_ref[e]
        hidden_gate = nt(x, gate_ref[e])
        hidden_up = nt(x, up_ref[e])
        sigma = jax.nn.sigmoid(hidden_gate)
        silu = hidden_gate * sigma
        activ = (silu * hidden_up).astype(BF16)
        act_ref[e] = activ
        slope_ref[e] = hidden_up * sigma * (1.0 + hidden_gate * (1.0 - sigma))
        silu_ref[e] = silu
        a_ref[e] = (activ.astype(F32) * slot_gate[e][:, 0:1]).astype(BF16)

    def project(e):
        out = nn(a_ref[e], slot_of(down_ref, e)).astype(BF16)
        at = pl.ds(pl.multiple_of(e * CAP, CAP), CAP)
        for s in range(sources):
            out_rows[s, at, :] = out[s * CAP:(s + 1) * CAP]

    def both(e):
        before, now = [e - GROUP + i for i in range(GROUP)], [e + i for i in range(GROUP)]
        for i in before:
            wait_down(i)
        for i, j in zip(before, now):
            activate(j)
            project(i)
        for i in before:
            start_down(i)

    skewed(experts, activate, wait_down, project, both)


def skewed(experts, first, wait, second, both):
    for e in range(GROUP):
        first(jnp.int32(e))

    def turn(i, _):
        both(i * GROUP)
        return 0

    lax.fori_loop(1, experts // GROUP, turn, 0)
    for e in range(experts - GROUP, experts):
        wait(jnp.int32(e))
    for e in range(experts - GROUP, experts):
        second(jnp.int32(e))


def home_kernel(onehot, rows, *refs):
    keep, send = refs[-2:]
    send_home(keep, send, lax.axis_index("etp"), onehot, rows, keep.shape[2], keep.shape[3])


def half(me, other, size):
    return pl.ds(pl.multiple_of(lax.bitwise_xor(me // 2, other) * size, size), size)


def half_home(me, onehot, rows, keep, send, tokens, width):
    for s in range(onehot.shape[0]):
        for q, home in enumerate((keep, send)):
            at = pl.multiple_of(lax.rem(lax.bitwise_xor(me, q), 2) * width, width)
            home[s, 0:tokens, :] = tn(onehot[s], rows[s, :, pl.ds(at, width)]).astype(BF16)


def values_kernel(choose, onehot, rows, dots, own_ref, info_ref, *refs):
    keep, send, value_ref = refs[-3:]
    sources, slots, tokens = onehot.shape
    experts = slots // CAP
    width = keep.shape[2]
    half_home(lax.axis_index("etp"), onehot, rows, keep, send, tokens, width)
    expert = lax.broadcasted_iota(jnp.int32, (experts, tokens), 0)
    mine = (lax.axis_index("expert") * experts + expert).astype(F32)
    for s in range(sources):
        info = own_ref[tokens:tokens + EXTRA, :] if s == 0 else info_ref[s - 1, tokens:tokens + EXTRA, :]
        ids, _ = routing(info, choose, tokens)
        chosen = onehot[s].astype(F32).reshape(experts, CAP, tokens)
        share = jnp.sum(chosen * dots[:, s * CAP:(s + 1) * CAP, :], axis=1)
        values = [jnp.sum(jnp.where(ids[k:k + 1, :] == mine, share, 0.0), axis=0, keepdims=True) for k in range(choose)]
        values = jnp.concatenate(values + [jnp.zeros((EXTRA - choose, tokens), F32)], axis=0)
        values = jnp.concatenate([values, jnp.zeros((EXTRA, width - tokens), F32)], axis=1).astype(BF16)
        keep[s, tokens:tokens + EXTRA, :] = values
        send[s, tokens:tokens + EXTRA, :] = values
        value_ref[s] = values


def own_kernel(gate_ref, up_ref, p_ref, q_ref, onehot, slot_gate, value_ref, earlier_ref, keep, send, back_rows):
    sources, slots, tokens = onehot.shape
    width = keep.shape[2]
    me = lax.axis_index("etp")
    here = half(me, 0, 2 * width)

    def turn(i, _):
        for e in [i * GROUP + j for j in range(GROUP)]:
            back = nn(p_ref[e], gate_ref[e, :, here]) + nn(q_ref[e], up_ref[e, :, here])
            back = (back * slot_gate[e][:, 0:1]).astype(BF16)
            at = pl.ds(pl.multiple_of(e * CAP, CAP), CAP)
            for s in range(sources):
                back_rows[s, at, :] = back[s * CAP:(s + 1) * CAP]
        return 0

    lax.fori_loop(0, slots // CAP // GROUP, turn, 0)
    half_home(me, onehot, back_rows, keep, send, tokens, width)
    for s in range(sources):
        keep[s, tokens:tokens + EXTRA, :] = value_ref[s]
        send[s, tokens:tokens + EXTRA, :] = value_ref[s]


def backward_kernel(
    a01, a23, n01, n23,
    gate_ref, up_ref, down_hbm, act_ref, slope_ref, silu_ref, onehot, slot_gate, earlier_ref,
    back_rows, dots, rows_ref, p_ref, q_ref,
    down_ref, down_sems,
):
    sources, slots, tokens = onehot.shape
    experts = slots // CAP
    width = a01.shape[3]
    me = lax.axis_index("etp")
    start_down, wait_down = ring(down_hbm, down_ref, down_sems)
    there = half(me, 1, 2 * width)
    for s in range(sources):
        here, near = ((a01, n01), (a23, n23))[s // 2]
        for q in range(4):
            block = (near if q % 2 else here)[s % 2, q // 2]
            picked = nn(onehot[s], block).astype(BF16).reshape(experts, CAP, width)
            rows_ref[:, s * CAP:(s + 1) * CAP, columns(me, q, width)] = picked

    def slopes(e):
        grad = nt(rows_ref[e], slot_of(down_ref, e))
        activ = act_ref[e].astype(F32)
        dots[e] = jnp.broadcast_to(jnp.sum(activ * grad, axis=1, keepdims=True), dots.shape[1:])
        grad = grad * slot_gate[e][:, 0:1]
        p_ref[e] = (grad * slope_ref[e]).astype(BF16)
        q_ref[e] = (grad * silu_ref[e]).astype(BF16)

    def project(e):
        back = nn(p_ref[e], gate_ref[e, :, there]) + nn(q_ref[e], up_ref[e, :, there])
        back = (back * slot_gate[e][:, 0:1]).astype(BF16)
        at = pl.ds(pl.multiple_of(e * CAP, CAP), CAP)
        for s in range(sources):
            back_rows[s, at, :] = back[s * CAP:(s + 1) * CAP]

    def first(e):
        wait_down(e)
        slopes(e)
        start_down(e)

    def both(e):
        before, now = [e - GROUP + i for i in range(GROUP)], [e + i for i in range(GROUP)]
        for i in now:
            wait_down(i)
        for i, j in zip(before, now):
            slopes(j)
            project(i)
        for i in now:
            start_down(i)

    skewed(experts, first, lambda e: None, project, both)


def add_kernel(keep, came, *refs):
    near, far = refs[-2:]
    for s in range(near.shape[0]):
        far[s] = (keep[1, s].astype(F32) + came[1, s].astype(F32)).astype(BF16)
        near[s] = (keep[0, s].astype(F32) + came[0, s].astype(F32)).astype(BF16)


def pair_kernel(keep, came, *refs):
    refs[-1][...] = (keep[...].astype(F32) + came[...].astype(F32)).astype(BF16)


def pairs_kernel(near, came, *refs):
    for s in range(near.shape[0]):
        refs[-2 + s % 2][s // 2] = (near[s].astype(F32) + came[s].astype(F32)).astype(BF16)


def chips_kernel(out_even, out_came, back_keep, back_near, back_came, *refs):
    sources, tokens = back_keep.shape[0], out_even.shape[1]
    parts = refs[-sources:]
    for s in range(sources):
        back = back_keep[s].astype(F32) + back_near[s].astype(F32) + back_came[s].astype(F32)
        start = 0
        if s % 2 == 0:
            parts[s][0:tokens, :] = (out_even[s // 2].astype(F32) + out_came[s // 2].astype(F32)).astype(BF16)
            start = tokens
        parts[s][start:, :] = back.astype(BF16)


def total_kernel(p0, p1, p2, p3, out_ref, back_ref, value_ref):
    tokens = out_ref.shape[0]
    both = p0[...].astype(F32) + p2[...].astype(F32)
    out_ref[...] = both[0:tokens].astype(BF16)
    back = both[tokens:] + p1[...].astype(F32) + p3[...].astype(F32)
    back_ref[...] = back[0:tokens].astype(BF16)
    value_ref[...] = back[tokens:tokens + value_ref.shape[0], 0:value_ref.shape[1]]


BANKS = 8
TURN = 4


def product_kernel(jobs, *refs):
    lefts, rights, outs = (refs[i * len(jobs):(i + 1) * len(jobs)] for i in range(3))
    held, sems = refs[-2:]
    outs = refs[-2 - len(jobs):-2]

    def store(job, e, slot):
        return pltpu.make_async_copy(held.at[slot], outs[job].at[e], sems.at[slot])

    def turn(job, first, done, i, full):
        for pair in range(0, TURN, 2):
            places = [(first + i * TURN + j, lax.rem(done + i * TURN + j, BANKS)) for j in (pair, pair + 1)]
            if full:
                for e, slot in places:
                    store(job, e, slot).wait()
            for e, slot in places:
                held[slot] = tn(lefts[job][e], rights[job][e]).astype(BF16)
            for e, slot in places:
                store(job, e, slot).start()

    done = 0
    for job, (first, last) in enumerate(jobs):
        fresh = max(0, min(BANKS - done, last - first) // TURN)
        for i in range(fresh):
            turn(job, first, done, jnp.int32(i), False)

        def later(i, _, job=job, first=first, done=done):
            turn(job, first, done, i, True)
            return 0

        lax.fori_loop(fresh, (last - first) // TURN, later, 0)
        done = done + last - first
    for slot in range(min(done, BANKS)):
        store(0, jobs[0][0], slot).wait()


def load_kernel(source, target, token, sems):
    token[...] = jnp.zeros_like(token)
    copies = [pltpu.make_async_copy(source.at[e], target.at[e], sems.at[e]) for e in range(source.shape[0])]
    for copy in copies:
        copy.start()
    for copy in copies:
        copy.wait()


def in_vmem(weight):
    return pl.pallas_call(
        load_kernel,
        in_specs=[pl.BlockSpec(memory_space=pltpu.HBM)],
        out_specs=[pl.BlockSpec(memory_space=pltpu.VMEM)] * 2,
        out_shape=[pltpu.VMEM(weight.shape, BF16), jax.ShapeDtypeStruct((8, 128), F32)],
        scratch_shapes=[pltpu.SemaphoreType.DMA((weight.shape[0],))],
        compiler_params=pltpu.CompilerParams(vmem_limit_bytes=4 * 1024 * 1024),
        cost_estimate=pl.CostEstimate(flops=0, bytes_accessed=2 * weight.size, transcendentals=0),
    )(pltpu.with_memory_space_constraint(weight, pltpu.HBM))


def join_kernel(count, *refs):
    for i in range(count):
        refs[-1][i] = refs[i][...]


def join(arrays, *there):
    return kernel_call(
        functools.partial(join_kernel, len(arrays)),
        [jax.ShapeDtypeStruct((len(arrays),) + arrays[0].shape, arrays[0].dtype)],
        [],
        0,
        limit=2,
    )(*arrays, *there)[0]


def kernel_call(kernel, out_shape, scratch, flops, out_specs=None, limit=4, in_hbm=(), aliases={}):
    def call(*operands):
        specs = [
            pl.BlockSpec(memory_space=pltpu.HBM if i in in_hbm else pltpu.SMEM if x.ndim == 1 else pltpu.VMEM)
            for i, x in enumerate(operands)
        ]
        operands = [
            pltpu.with_memory_space_constraint(x, pltpu.HBM) if i in in_hbm else x for i, x in enumerate(operands)
        ]
        return pl.pallas_call(
            kernel,
            in_specs=specs,
            out_specs=out_specs or [pl.BlockSpec(memory_space=pltpu.VMEM)] * len(out_shape),
            out_shape=out_shape,
            scratch_shapes=scratch,
            input_output_aliases=aliases,
            compiler_params=pltpu.CompilerParams(vmem_limit_bytes=limit * 1024 * 1024),
            cost_estimate=pl.CostEstimate(flops=flops, bytes_accessed=flops // 32, transcendentals=0),
        )(*operands)

    return call


def weight_grads(jobs, begun=None, *earlier):
    count = len(jobs)
    lefts, rights = [job[0] for job in jobs], [job[1] for job in jobs]
    experts, rows, units = lefts[0].shape
    model = rights[0].shape[2]
    shape = jax.ShapeDtypeStruct((experts, units, model), BF16)
    work = sum(job[3] - job[2] for job in jobs)
    more = [] if begun is None else [begun]
    return kernel_call(
        functools.partial(product_kernel, [job[2:] for job in jobs]),
        [shape] * count,
        [pltpu.VMEM((BANKS, units, model), BF16), pltpu.SemaphoreType.DMA((BANKS,))],
        2 * work * rows * units * model,
        out_specs=[pl.BlockSpec(memory_space=pltpu.HBM)] * count,
        limit=8,
        in_hbm=(2 * count,) if more else (),
        aliases={2 * count: 0} if more else {},
    )(*lefts, *rights, *more, *earlier)


def swap(array, bit, axis="etp"):
    count = lax.axis_size(axis)
    return lax.ppermute(array, axis, [(i, i ^ bit) for i in range(count)])


def add_cores(keep, came, *earlier):
    shape = jax.ShapeDtypeStruct(keep.shape[1:], BF16)
    hbm = [2] if earlier else []
    return kernel_call(add_kernel, [shape, shape], [], 0, limit=2, in_hbm=hbm)(keep, came, *earlier)


def gathered_body(
    hidden_in, out_grad, expert_ids, gate_values, capacity_blocks, gate_weight, up_weight, down_weight
):
    sources = lax.axis_size("expert")
    tokens, width = hidden_in.shape
    choose = expert_ids.shape[1]
    local_experts, units, model = down_weight.shape
    slots = local_experts * CAP
    rows = sources * CAP
    gate_t, gate_there = in_vmem(jnp.swapaxes(gate_weight, 1, 2))
    up_t, up_there = in_vmem(jnp.swapaxes(up_weight, 1, 2))
    product = 2 * local_experts * rows * units * model
    held = lambda *shape, kind=BF16: pltpu.VMEM(shape, kind)
    sent = lambda *shape: jax.ShapeDtypeStruct(shape, BF16)

    own = kernel_call(
        pack_kernel,
        [sent(tokens + EXTRA, width)],
        [pltpu.VMEM((choose, tokens), jnp.int32), pltpu.VMEM((choose, tokens), F32), pltpu.SemaphoreType.DMA((3,))],
        0,
        limit=2,
        in_hbm=(0, 1, 2),
    )(hidden_in, expert_ids.T, gate_values.T)[0]
    came = [swap(own, s, "expert") for s in range(1, sources)]
    own_across = swap(own, 2)
    grad_across = swap(out_grad, 2)
    came = join(came, gate_there, own_across, grad_across)
    came_across_there = swap(came, 2)
    across_near = swap(own_across, 1)
    grads = join([out_grad, grad_across], came)
    near_grads = join([grads, swap(grads, 1, "expert")])
    far_grads = swap(near_grads, 2, "expert")

    came_across = join([came_across_there], up_there, near_grads)[0]
    out_rows, x_rows, activ, scaled, slope, silu, onehot, slot_gate = kernel_call(
        functools.partial(forward_kernel, choose),
        [
            held(sources, slots, model),
            held(local_experts, rows, model),
            held(local_experts, rows, units),
            held(local_experts, rows, units),
            held(local_experts, rows, units, kind=F32),
            held(local_experts, rows, units, kind=F32),
            held(sources, slots, tokens),
            held(local_experts, rows, tokens, kind=F32),
        ],
        [pltpu.VMEM((RING, units, model), BF16), pltpu.SemaphoreType.DMA((RING,))],
        3 * product,
        limit=16,
        in_hbm=(11,),
    )(
        capacity_blocks,
        own, swap(own, 1), own_across, across_near,
        came, swap(came, 1), came_across, swap(came_across, 1),
        gate_t, up_t, down_weight, near_grads,
    )

    keep, send = kernel_call(
        home_kernel, [sent(2, sources, tokens, width)] * 2, [], 2 * slots * sources * tokens * model, limit=2,
    )(onehot, out_rows, far_grads)
    out_near, out_far = add_cores(keep, swap(send, 1))
    back_rows, dots, y_rows, gate_part, up_part = kernel_call(
        backward_kernel,
        [
            held(sources, slots, model // 2),
            held(local_experts, rows, tokens, kind=F32),
            held(local_experts, rows, model),
            held(local_experts, rows, units),
            held(local_experts, rows, units),
        ],
        [pltpu.VMEM((RING, units, model), BF16), pltpu.SemaphoreType.DMA((RING,))],
        3 * product,
        limit=16,
        in_hbm=(6,),
    )(
        near_grads, far_grads, swap(near_grads, 1), swap(far_grads, 1),
        gate_t, up_t, down_weight, activ, slope, silu, onehot, slot_gate, out_near,
    )

    pair = sent(2, tokens, width)
    out_even, out_odd = kernel_call(pairs_kernel, [pair, pair], [], 0, limit=2)(out_near, swap(out_far, 2))
    out_came = swap(out_odd, 1, "expert")
    back_sum = sent(sources, tokens + EXTRA, width)
    far_keep, far_send, values = kernel_call(
        functools.partial(values_kernel, choose),
        [back_sum, back_sum, held(sources, EXTRA, width)],
        [],
        slots * sources * tokens * model,
        limit=2,
    )(onehot, back_rows, dots, own, came, out_even)
    near_keep, near_send = kernel_call(
        own_kernel,
        [back_sum, back_sum],
        [pltpu.VMEM((sources, slots, model // 2), BF16)],
        product,
        limit=16,
    )(gate_t, up_t, gate_part, up_part, onehot, slot_gate, values, far_keep)
    (back_far,) = kernel_call(pair_kernel, [back_sum], [], 0, limit=2)(far_keep, swap(far_send, 1), near_keep)
    some = local_experts // 2
    up_grad, down_grad = weight_grads(
        [(up_part, x_rows, 0, local_experts), (scaled, y_rows, 0, some)], None, back_far
    )
    height = 2 * tokens + EXTRA
    heights = [sent(height - tokens * (s % 2), width) for s in range(sources)]
    parts = kernel_call(chips_kernel, heights, [], 0, limit=2, in_hbm=(5,))(
        out_even, out_came, near_keep, swap(near_send, 1), swap(back_far, 2), up_grad
    )
    down_grad, gate_grad = weight_grads(
        [(scaled, y_rows, some, local_experts), (gate_part, x_rows, 0, local_experts)], down_grad, parts[0]
    )
    layer_out, input_grad, value_grad = kernel_call(
        total_kernel,
        [sent(tokens, width), sent(tokens, width), jax.ShapeDtypeStruct((choose, tokens), F32)],
        [],
        0,
        limit=2,
    )(parts[0], *[swap(parts[s], s, "expert") for s in range(1, sources)])
    return (
        layer_out,
        input_grad,
        value_grad.T,
        jnp.swapaxes(gate_grad, 1, 2),
        jnp.swapaxes(up_grad, 1, 2),
        down_grad,
    )


def slot_layout(expert_ids, capacity_blocks):
    tokens_here, choose = expert_ids.shape
    experts = capacity_blocks.shape[0]
    flat_ids = expert_ids.reshape(-1)
    onehot = (flat_ids[:, None] == jnp.arange(experts, dtype=jnp.int32)[None, :]).astype(jnp.int32)
    before = jnp.cumsum(onehot, axis=0) - onehot
    ranks = jnp.sum(before * onehot, axis=1)
    limits = jnp.sum(onehot * capacity_blocks[None, :], axis=1) * BLK
    kept = ranks < limits
    slots = jnp.where(kept, flat_ids * CAP + ranks, experts * CAP)
    token_index = jnp.arange(tokens_here * choose, dtype=jnp.int32) // choose
    owners = (
        jnp.full((experts * CAP,), tokens_here, jnp.int32).at[slots].set(token_index, mode="drop")
    )
    return (kept.reshape(tokens_here, choose), slots.reshape(tokens_here, choose), owners)


def outgoing(rows, owners, experts, scale):
    padded = jnp.concatenate([rows, jnp.zeros((1, rows.shape[1]), rows.dtype)], 0)
    picked = padded[owners]
    if scale is not None:
        picked = (scale[:, None] * picked.astype(jnp.float32)).astype(jnp.bfloat16)
    return picked.reshape(experts, CAP, rows.shape[1])


def local_grads(hidden_gate, hidden_up, act_grad):
    sigma = jax.nn.sigmoid(hidden_gate)
    gate_part = (act_grad * hidden_up * sigma * (1.0 + hidden_gate * (1.0 - sigma))).astype(
        jnp.bfloat16
    )
    up_part = (act_grad * jax.nn.silu(hidden_gate)).astype(jnp.bfloat16)
    return (gate_part, up_part)


def combine(back, slots, weights):
    padded = jnp.concatenate([back, jnp.zeros((1, back.shape[1]), back.dtype)], 0)
    picked = padded[slots].astype(jnp.float32)
    return (jnp.einsum("tk,tkw->tw", weights, picked), picked)


def dispatched_body(
    hidden_in,
    out_grad,
    expert_ids,
    gate_values,
    capacity_blocks,
    gate_weight,
    up_weight,
    down_weight,
):
    experts = capacity_blocks.shape[0]
    sources = lax.axis_size("expert")
    local_experts = gate_weight.shape[0]
    kept, slots, owners = slot_layout(expert_ids, capacity_blocks)
    weights = jnp.where(kept, gate_values, 0.0)
    slot_gates = (
        jnp.zeros((experts * CAP,), jnp.float32)
        .at[slots.reshape(-1)]
        .set(weights.reshape(-1), mode="drop")
    )
    send_in = outgoing(hidden_in, owners, experts, None)
    send_grad = outgoing(out_grad, owners, experts, slot_gates)
    recv_in, recv_grad = (
        lax.all_to_all(send_in, "expert", split_axis=0, concat_axis=0, tiled=True),
        lax.all_to_all(send_grad, "expert", split_axis=0, concat_axis=0, tiled=True),
    )
    share = recv_in.shape[2]
    share_in = recv_in.reshape(sources, local_experts, CAP, share)
    share_grad = recv_grad.reshape(sources, local_experts, CAP, share)
    piece = lax.all_gather(share_in, "etp", axis=3, tiled=True)
    hidden_gate = jnp.einsum(
        "secn,enf->secf", piece, gate_weight, preferred_element_type=jnp.float32
    )
    hidden_up = jnp.einsum("secn,enf->secf", piece, up_weight, preferred_element_type=jnp.float32)
    activ = (jax.nn.silu(hidden_gate) * hidden_up).astype(jnp.bfloat16)
    piece = lax.all_gather(share_grad, "etp", axis=3, tiled=True)
    act_grad = jnp.einsum("secn,efn->secf", piece, down_weight, preferred_element_type=jnp.float32)
    columns = jnp.einsum("secf,secn->efn", activ, piece, preferred_element_type=jnp.float32)
    act_grad, down_grad = (act_grad, columns)
    gate_part, up_part = local_grads(hidden_gate, hidden_up, act_grad)
    stacked = jnp.stack([gate_part, up_part])
    weight_grads = jnp.einsum(
        "secn,gsecf->genf",
        lax.all_gather(share_in, "etp", axis=3, tiled=True),
        stacked,
        preferred_element_type=jnp.float32,
    )
    out_part = jnp.einsum("secf,efd->secd", activ, down_weight, preferred_element_type=jnp.float32)
    back_part = jnp.einsum(
        "secf,edf->secd", gate_part, gate_weight, preferred_element_type=jnp.float32
    )
    back_part = back_part + jnp.einsum(
        "secf,edf->secd", up_part, up_weight, preferred_element_type=jnp.float32
    )
    out_rows = lax.psum_scatter(
        out_part.astype(jnp.bfloat16), "etp", scatter_dimension=3, tiled=True
    )
    home_out = lax.all_to_all(out_rows, "expert", split_axis=0, concat_axis=0, tiled=True)
    share_width = home_out.shape[3]
    layer_sum, picked = combine(home_out.reshape(experts * CAP, share_width), slots, weights)
    dot_part = jnp.einsum("tw,tkw->tk", out_grad.astype(jnp.float32), picked) * kept.astype(
        jnp.float32
    )
    gate_value_grad = lax.psum(dot_part, "etp")
    back_rows = lax.psum_scatter(
        back_part.astype(jnp.bfloat16), "etp", scatter_dimension=3, tiled=True
    )
    home_back = lax.all_to_all(back_rows, "expert", split_axis=0, concat_axis=0, tiled=True)
    input_sum, returned = combine(home_back.reshape(experts * CAP, share_width), slots, weights)
    return (
        layer_sum.astype(jnp.bfloat16),
        input_sum.astype(jnp.bfloat16),
        gate_value_grad,
        weight_grads[0].astype(jnp.bfloat16),
        weight_grads[1].astype(jnp.bfloat16),
        down_grad.astype(jnp.bfloat16),
    )


def body(*operands):
    hidden_in, gate_weight = operands[0], operands[5]
    if lax.axis_size("expert") == 4 and lax.axis_size("etp") == 4 and hidden_in.shape[0] <= gate_weight.shape[0] * CAP:
        return gathered_body(*operands)
    return dispatched_body(*operands)


def solution(mesh):
    in_specs = (
        P(("groups", "expert"), "etp"),
        P(("groups", "expert"), "etp"),
        P(("groups", "expert"), None),
        P(("groups", "expert"), None),
        P("groups"),
        P("expert", None, "etp"),
        P("expert", None, "etp"),
        P("expert", "etp", None),
    )
    out_specs = (
        P(("groups", "expert"), "etp"),
        P(("groups", "expert"), "etp"),
        P(("groups", "expert"), None),
        P(("groups", "expert"), None, "etp"),
        P(("groups", "expert"), None, "etp"),
        P(("groups", "expert"), "etp", None),
    )
    return jax.shard_map(body, mesh=mesh, in_specs=in_specs, out_specs=out_specs, check_vma=False)
```
